32 devices in a mesh: dp: 4 (over z), expert: 8 (over y, x, core).
Axes of the slice: x: 2, y: 2, z: 4, core: 2. Of those that a mesh axis runs over, the one named last changes fastest.
Arguments:
- tokens: bfloat16 [4096, 2048], P(('dp', 'expert')), may hold values from -6 to 6
- attn_gain: bfloat16 [2048], P('dp'), may hold values from 0.5 to 1.5
- qkv_weight: bfloat16 [2048, 6144], P('dp'), may hold values from -0.125 to 0.125
- qkv_bias: bfloat16 [3, 2048], P(None, 'dp'), may hold values from -3 to 3
- out_weight: bfloat16 [2048, 2048], P('dp'), may hold values from -0.5 to 0.5
- ffn_gain: bfloat16 [2048], P('dp'), may hold values from 0.5 to 1.5
- router_weight: bfloat16 [2048, 8], P('dp'), may hold values from -0.0625 to 0.0625
- shared_gate_weight: bfloat16 [2048], P('dp'), may hold values from -0.125 to 0.125
- shared_weight: bfloat16 [5632, 3, 2048], P('dp'), may hold values from -0.125 to 0.125
- expert_up: bfloat16 [8, 1408, 2, 2048], P('expert', None, None, 'dp'), may hold values from -0.125 to 0.125
- expert_down: bfloat16 [8, 1408, 2048], P('expert', None, 'dp'), may hold values from -1.25 to 1.25
- routes: int32 [4096, 4], P(('dp', 'expert')), may hold values from 0 to 7, all different within a row; in each aligned block of 128 rows (0 to 127, 128 to 255, ...) at most 128 rows name the same one
- segment_ids: int32 [32, 128], P(('dp', 'expert')), may hold values from 0 to 3, never falling along the last dimension, each value on 1 to 48 neighbouring positions
- cotangent: bfloat16 [4096, 2048], P(('dp', 'expert')), may hold values from -6 to 6
Outputs:
- output: bfloat16 [4096, 2048], P(('dp', 'expert'))
- tokens_grad: float32 [4096, 2048], P(('dp', 'expert'))
- attn_gain_grad: float32 [2048], P('dp')
- qkv_weight_grad: float32 [2048, 6144], P('dp')
- qkv_bias_grad: float32 [3, 2048], P(None, 'dp')
- out_weight_grad: float32 [2048, 2048], P('dp')
- ffn_gain_grad: float32 [2048], P('dp')
- router_weight_grad: float32 [2048, 8], P('dp')
- shared_gate_weight_grad: float32 [2048], P('dp')
- shared_weight_grad: float32 [5632, 3, 2048], P('dp')
- expert_up_grad: float32 [8, 1408, 2, 2048], P('expert', None, None, 'dp')
- expert_down_grad: float32 [8, 1408, 2048], P('expert', None, 'dp')
The draws below stay inside these ranges and needn't reach their ends.
Inputs may be any that keep to these rules, and one draw needn't show every extreme that they name: `routes`: each row names 4 different experts. Within the rows of one sequence (an aligned block of 128 rows) no expert is named more than 128 times, and in every draw some expert is named exactly 128 times in some block. `segment_ids`: along a sequence the document ids never fall; each document holds 1 to 48 positions, and some document holds exactly 48.
All inputs are finite; a program needn't handle non-finite values.
Results may differ from the reference program's by a relative error of at most 0.02.
Values may be sent and summed in bfloat16 or wider, within the bound.
A program may use at most 384 MiB of HBM per device.

```python
import math
import jax
import jax.numpy as jnp
import numpy as np
from jax import lax

D = 2048
HEADS = 16
HEAD = 128
SH = 5632
F = 1408
TOP = 4
TOK_DEV = 128
SEGS = 4
EXPERTS = 8
SEQS = 32
TOKENS = 4096
CAP = 128
DOC_MOST = 48


def shard_levels(key, extent, cuts, smallest, high):
    factor_of, own = 1.0, jax.random.fold_in(key, 6)
    for dim, shards_of in cuts:
        heights = jnp.exp(jax.random.uniform(jax.random.fold_in(own, dim), (shards_of,), jnp.float32, smallest / len(cuts), high / len(cuts)))
        factor_of = factor_of * jnp.repeat(heights, extent[dim] // shards_of).reshape([-1 if axis == dim else 1 for axis in range(len(extent))])
    return factor_of


def length_profile(number_of, total, most, lean):
    weights = [(1 << 20) // math.isqrt(standing ** lean) + 1 for standing in range(2, number_of + 1)]
    surplus, given = total - most - (number_of - 1), [1] * (number_of - 1)
    while surplus > 0:
        candidates = [i for i in range(number_of - 1) if given[i] < most]
        pool, left = sum([weights[i] for i in candidates]), surplus
        for i in candidates:
            extra = min(most - given[i], max(1, left * weights[i] // pool), surplus)
            given[i] = given[i] + extra
            surplus = surplus - extra
    return np.array([most] + given)


def uneven_parts(key, amount, total, limit, skew):
    if amount == 2:
        one = jax.random.randint(key, (), max(1, total - limit), min(limit, total - 1) + 1)
        return jnp.stack([one, total - one])
    tallies = jnp.asarray(length_profile(amount, total, limit, skew), jnp.int32)
    twos = (amount - 1) // 2
    source_of, taker = tallies[1:1 + 2 * twos:2], tallies[2:2 + 2 * twos:2]
    slack = jnp.minimum(source_of - 1, limit - taker)
    moved = jax.random.randint(jax.random.fold_in(key, 1), (twos,), 0, 1 << 20) % (slack + 1)
    tallies = tallies.at[1:1 + 2 * twos:2].set(source_of - moved).at[2:2 + 2 * twos:2].set(taker + moved)
    return tallies[jax.random.permutation(jax.random.fold_in(key, 2), amount)]


def routed_block(stream_key, own, number, rows, amount, top, most, lean):
    ranking = jax.random.permutation(stream_key, amount)
    packed, common = portions_of(amount, rows * top, most, lean, True), portions_of(amount, rows * top, most, lean, False)
    places = jnp.arange(amount)

    def named(sizes, rotation):
        used = int((sizes > 0).sum())
        fixed = max(1, used // 4)
        passed = fixed + (places - fixed + rotation * (used - fixed)) % max(1, amount - fixed)
        return jnp.zeros((amount,), jnp.int32).at[ranking[jnp.where(places < fixed, places, passed)]].set(jnp.asarray(sizes, jnp.int32))

    sizes = jnp.where(number % 4 == 0, named(packed, number // 4), named(common, number - number // 4 - 1))
    mixed = jax.random.permutation(jax.random.fold_in(own, 3), amount)
    giver, taker = mixed[0:amount // 2 * 2:2], mixed[1:amount // 2 * 2:2]
    room = jnp.minimum(sizes[giver] - 1, most - sizes[taker]) // 2
    room = jnp.where((giver == ranking[0]) | (taker == ranking[0]) | (sizes[taker] == 0), 0, jnp.maximum(room, 0))
    passed = jax.random.randint(jax.random.fold_in(own, 4), (amount // 2,), 0, 1 << 20) % (room + 1)
    sizes = sizes.at[giver].add(-passed).at[taker].add(passed)
    labels = jnp.searchsorted(jnp.cumsum(sizes), jnp.arange(rows * top), side="right").astype(jnp.int32)
    grid = labels.reshape(top, rows).T
    grid = grid[jax.random.permutation(jax.random.fold_in(own, 1), rows)]
    rotation = jax.random.randint(jax.random.fold_in(own, 2), (rows, 1), 0, top)
    return jnp.take_along_axis(grid, (jnp.arange(top)[None, :] + rotation) % top, axis=1)


def portions_of(number_of, total, bound, slope, full):
    loads = [(1 << 20) // math.isqrt(grade ** slope) + 1 for grade in range(1, number_of + 1)]
    largest = bound if full else min(bound, max(-(-total // number_of), total * loads[0] // sum(loads)))
    least = 1 if total - largest >= number_of - 1 else 0
    counts, spare = [largest] + [least] * (number_of - 1), total - largest - least * (number_of - 1)
    while spare > 0:
        candidates = [i for i in range(1, number_of) if counts[i] < largest] or [i for i in range(1, number_of) if counts[i] < bound]
        pool, remaining = sum([loads[i] for i in candidates]), spare
        for i in candidates:
            addition = min(bound - counts[i], max(1, remaining * loads[i] // pool), spare)
            counts[i] = counts[i] + addition
            spare = spare - addition
    return np.array(counts)


def scatter_about(rng, shape, spread, reach, shards=(), held_as=jnp.bfloat16):
    level = shard_levels(rng, shape, shards, -0.22, 0.18) if shards else 1.0
    values = jax.random.normal(rng, shape, jnp.float32) * spread * level
    return jnp.minimum(jnp.maximum(values, -reach), reach).astype(held_as)


def setup_inputs(seed: int = 0) -> dict:
    key_of = jax.random.split(jax.random.key(seed), 15)
    tokens = scatter_about(key_of[0], (TOKENS, D), 1.0, 6.0, ((0, 32),))
    attn_gain = jnp.clip(1.0 + 0.1 * jax.random.normal(key_of[1], (D,), jnp.float32), 0.5, 1.5).astype(jnp.bfloat16)
    qkv_weight = scatter_about(key_of[2], (D, 3 * D), D ** -0.5, 0.125, ((0, 4),))
    qkv_bias = scatter_about(key_of[3], (3, D), 0.5, 3.0, ((1, 4),))
    out_weight = scatter_about(key_of[4], (D, D), (D // 16) ** -0.5, 0.5, ((0, 4),))
    ffn_gain = jnp.clip(1.0 + 0.1 * jax.random.normal(key_of[5], (D,), jnp.float32), 0.5, 1.5).astype(jnp.bfloat16)
    router_weight = scatter_about(key_of[6], (D, EXPERTS), (4 * D) ** -0.5, 0.0625, ((0, 4),))
    shared_gate_weight = scatter_about(key_of[7], (D,), D ** -0.5, 0.125, ((0, 4),))
    shared_weight = scatter_about(key_of[8], (SH, 3, D), D ** -0.5, 0.125, ((0, 4),))
    expert_up = scatter_about(key_of[9], (EXPERTS, F, 2, D), D ** -0.5, 0.125, ((0, 8), (3, 4)))
    expert_down = scatter_about(key_of[10], (EXPERTS, F, D), (max(F // 64, 1)) ** -0.5, 1.25, ((0, 8), (2, 4)))
    routes_keys = jax.random.split(jax.random.fold_in(key_of[11], 1), TOKENS // TOK_DEV)
    routes_turns = jax.random.permutation(jax.random.fold_in(key_of[11], 3), TOKENS // TOK_DEV)
    routes = jax.vmap(lambda own, number: routed_block(jax.random.fold_in(key_of[11], 2), own, number, TOK_DEV, EXPERTS, TOP, CAP, 2))(routes_keys, routes_turns).reshape((TOKENS, TOP))
    segment_ids = jax.vmap(lambda own: jnp.searchsorted(jnp.cumsum(uneven_parts(own, SEGS, TOK_DEV, DOC_MOST, 1)), jnp.arange(TOK_DEV), side="right"))(jax.random.split(key_of[12], SEQS)).reshape((SEQS, TOK_DEV)).astype(jnp.int32)
    cotangent = scatter_about(key_of[13], (TOKENS, D), 1.0, 6.0, ((0, 32),))
    return {"tokens": tokens, "attn_gain": attn_gain, "qkv_weight": qkv_weight, "qkv_bias": qkv_bias, "out_weight": out_weight, "ffn_gain": ffn_gain, "router_weight": router_weight, "shared_gate_weight": shared_gate_weight, "shared_weight": shared_weight, "expert_up": expert_up, "expert_down": expert_down, "routes": routes, "segment_ids": segment_ids, "cotangent": cotangent}


EPS = 1e-06
THETA = 1000000.0
NEGATIVE = -1e+30
full_precision = lax.Precision.HIGHEST

@jax.custom_vjp
def low(v):
    return lax.optimization_barrier(v.astype(jnp.bfloat16)).astype(jnp.float32)

@jax.custom_vjp
def low_back(v):
    return v

def low_keep(v):
    return (low(v), None)

def low_pass(kept, grad):
    return (grad,)

def back_keep(v):
    return (v, None)

def back_low(kept, grad):
    return (low(grad),)
low.defvjp(low_keep, low_pass)
low_back.defvjp(back_keep, back_low)

def rms_scale(values):
    return lax.rsqrt(lax.optimization_barrier(jnp.mean(values * values, axis=-1, keepdims=True)) + EPS)

def route_slots(block_routes, num_experts):
    flat_routes = block_routes.reshape(-1)
    onehot = (flat_routes[:, None] == jnp.arange(num_experts, dtype=jnp.int32)[None, :]).astype(jnp.int32)
    before = jnp.cumsum(onehot, axis=0, dtype=jnp.int32) - onehot
    return lax.optimization_barrier(jnp.sum(before * onehot, axis=1, dtype=jnp.int32)).reshape(block_routes.shape)

def rope_tables(length, head_width):
    indices = jnp.arange(head_width // 2).astype(jnp.float32)
    frequency = jnp.exp(indices * (-2.0 * math.log(THETA) / head_width))
    angles = jnp.arange(length).astype(jnp.float32)[:, None] * frequency[None, :]
    return (jnp.cos(angles), jnp.sin(angles))

def rotate(values, cosine_table, sine_table):
    half_width = values.shape[-1] // 2
    lower_half = values[..., :half_width]
    upper_half = values[..., half_width:]
    cos_rows = cosine_table[:, None, :]
    sin_rows = sine_table[:, None, :]
    return jnp.concatenate([lower_half * cos_rows - upper_half * sin_rows, upper_half * cos_rows + lower_half * sin_rows], axis=-1)

def expert_rows(operands):
    rows, weight_up, weight_down = operands
    gate_up = low_back(jnp.einsum('rd,fgd->rgf', rows, weight_up, precision=full_precision))
    hidden = low(jax.nn.silu(gate_up[:, 0]) * gate_up[:, 1])
    return low_back(low(jnp.dot(hidden, weight_down, precision=full_precision)))

def reference(tokens, attn_gain, qkv_weight, qkv_bias, out_weight, ffn_gain, router_weight, shared_gate_weight, shared_weight, expert_up, expert_down, routes, segment_ids, cotangent):
    block_routes = routes.reshape(SEQS, TOK_DEV, TOP)
    slot_index = jax.vmap(route_slots, in_axes=(0, None))(block_routes, EXPERTS)
    block_base = (jnp.arange(SEQS, dtype=jnp.int32) * (EXPERTS * CAP))[:, None, None]
    target = (block_base + block_routes * CAP + slot_index).reshape(-1).astype(jnp.int32)
    total_slots = SEQS * EXPERTS * CAP
    route_count = TOKENS * TOP
    slot_table = jnp.full((total_slots,), route_count, dtype=jnp.int32).at[target].set(jnp.arange(route_count, dtype=jnp.int32))
    slot_filled = (slot_table < route_count)[:, None]
    slot_token = jnp.minimum(slot_table // TOP, TOKENS - 1).astype(jnp.int32)
    route_hot = (routes[:, :, None] == jnp.arange(EXPERTS, dtype=jnp.int32)[None, None, :]).astype(jnp.float32)
    same_doc = segment_ids[:, :, None] == segment_ids[:, None, :]
    causal = jnp.arange(TOK_DEV)[:, None] >= jnp.arange(TOK_DEV)[None, :]
    allowed = (same_doc & causal[None])[:, None, :, :]
    cosine_table, sine_table = rope_tables(TOK_DEV, HEAD)
    score_scale = HEAD ** (-0.5)

    def forward(resid_in, gain_one, w_qkv, b_qkv, w_out, gain_two, w_router, w_sgate, w_shared, w_up, w_down):
        normed_one = low(resid_in * rms_scale(resid_in) * gain_one)
        qkv_rows = low_back(jnp.dot(normed_one, w_qkv, precision=full_precision) + b_qkv.reshape(-1))
        qkv_rows = qkv_rows.reshape(SEQS, TOK_DEV, 3, HEADS, HEAD)
        query_rows = low(rotate(qkv_rows[:, :, 0], cosine_table, sine_table))
        key_rows = low(rotate(qkv_rows[:, :, 1], cosine_table, sine_table))
        value_rows = low(qkv_rows[:, :, 2])
        scores = low_back(jnp.einsum('bthd,bshd->bhts', query_rows, key_rows, precision=full_precision) * score_scale)
        scores = jnp.where(allowed, scores, NEGATIVE)
        probs_low = low(jax.nn.softmax(scores, axis=-1))
        mixed_heads = low(low_back(jnp.einsum('bhts,bshd->bthd', probs_low, value_rows, precision=full_precision)))
        attn_out = low_back(jnp.dot(mixed_heads.reshape(TOKENS, D), w_out, precision=full_precision))
        hidden_state = resid_in + attn_out
        normed_two = low(hidden_state * rms_scale(hidden_state) * gain_two)
        logits = low_back(jnp.dot(normed_two, w_router, precision=full_precision))
        router_probs = jax.nn.softmax(logits, axis=-1)
        gate_values = lax.optimization_barrier(jnp.sum(route_hot * router_probs[:, None, :], axis=-1))
        sent_rows = low_back(jnp.where(slot_filled, normed_two[slot_token], 0.0))
        sent_rows = sent_rows.reshape(SEQS, EXPERTS, CAP, D).transpose(1, 0, 2, 3).reshape(EXPERTS, SEQS * CAP, D)
        returned = lax.map(jax.checkpoint(expert_rows), (sent_rows, w_up, w_down))
        returned = returned.reshape(EXPERTS, SEQS, CAP, D).transpose(1, 0, 2, 3).reshape(total_slots, D)
        picked = returned[target].reshape(TOKENS, TOP, D)
        expert_sum = lax.optimization_barrier(jnp.sum(gate_values[:, :, None] * picked, axis=1))
        shared_gu = low_back(jnp.einsum('td,fgd->tgf', normed_two, w_shared[:, 0:2], precision=full_precision))
        shared_act = low(jax.nn.silu(shared_gu[:, 0]) * shared_gu[:, 1])
        shared_out = low_back(jnp.dot(shared_act, w_shared[:, 2], precision=full_precision))
        gate_logit = low_back(jnp.dot(normed_two, w_sgate, precision=full_precision))
        return hidden_state + expert_sum + jax.nn.sigmoid(gate_logit)[:, None] * shared_out
    block_out, pullback = jax.vjp(forward, tokens.astype(jnp.float32), attn_gain.astype(jnp.float32), qkv_weight.astype(jnp.float32), qkv_bias.astype(jnp.float32), out_weight.astype(jnp.float32), ffn_gain.astype(jnp.float32), router_weight.astype(jnp.float32), shared_gate_weight.astype(jnp.float32), shared_weight.astype(jnp.float32), expert_up.astype(jnp.float32), expert_down.astype(jnp.float32))
    grads = pullback(cotangent.astype(jnp.float32))
    return (block_out.astype(jnp.bfloat16), grads[0], grads[1], grads[2], grads[3], grads[4], grads[5], grads[6], grads[7], grads[8], grads[9], grads[10])
```

```python
import math

import jax
import jax.numpy as jnp
from jax import lax
from jax.sharding import PartitionSpec as P

HEADS = 16
HEAD = 128


EPS = 1e-06
THETA = 1000000.0
NEGATIVE = -1e30


def rms_scale(values):
    return lax.rsqrt(jnp.mean(values * values, axis=-1, keepdims=True) + EPS)


def rope_tables(length, head_width):
    indices = jnp.arange(head_width // 2).astype(jnp.float32)
    frequency = jnp.exp(indices * (-2.0 * math.log(THETA) / head_width))
    angles = jnp.arange(length).astype(jnp.float32)[:, None] * frequency[None, :]
    return (jnp.cos(angles), jnp.sin(angles))


def rotate(values, cosine_table, sine_table):
    half_width = values.shape[-1] // 2
    lower_half = values[..., :half_width]
    upper_half = values[..., half_width:]
    cos_rows = cosine_table[:, None, :]
    sin_rows = sine_table[:, None, :]
    return jnp.concatenate(
        [
            lower_half * cos_rows - upper_half * sin_rows,
            upper_half * cos_rows + lower_half * sin_rows,
        ],
        axis=-1,
    )


def unrotate(values, cosine_table, sine_table):
    half_width = values.shape[-1] // 2
    lower_half = values[..., :half_width]
    upper_half = values[..., half_width:]
    cos_rows = cosine_table[:, None, :]
    sin_rows = sine_table[:, None, :]
    return jnp.concatenate(
        [
            lower_half * cos_rows + upper_half * sin_rows,
            upper_half * cos_rows - lower_half * sin_rows,
        ],
        axis=-1,
    )


def norm_back(values, scale_rows, gain_row, upstream):
    scaled = gain_row * upstream
    gain_grad = jnp.sum(upstream * values * scale_rows, axis=0)
    input_grad = scale_rows * scaled - values * scale_rows**3 * jnp.mean(
        scaled * values, axis=-1, keepdims=True
    )
    return (gain_grad, input_grad)


def silu_parts(gate):
    logistic = jax.nn.sigmoid(gate)
    silu = gate * logistic
    return (silu, logistic * (1.0 + gate * (1.0 - logistic)))


def gather_all(rows):
    rows = lax.all_gather(rows, "dp", axis=0, tiled=True)
    return lax.all_gather(rows, "expert", axis=0, tiled=True)


def scatter_all(rows):
    rows = lax.psum_scatter(rows, "expert", scatter_dimension=0, tiled=True)
    return lax.psum_scatter(rows, "dp", scatter_dimension=0, tiled=True)


def shards(
    tokens,
    attn_gain,
    qkv_weight,
    qkv_bias,
    out_weight,
    ffn_gain,
    router_weight,
    shared_gate_weight,
    shared_weight,
    expert_up,
    expert_down,
    routes,
    segment_ids,
    cotangent,
):
    num_dp = lax.axis_size("dp")
    num_expert = lax.axis_size("expert")
    me_expert = lax.axis_index("expert")
    seq_len, model_width = tokens.shape
    shard_width = qkv_weight.shape[0]
    head_count = HEADS // num_expert
    head_width = head_count * HEAD
    plane_rows = seq_len * num_expert
    units = shared_weight.shape[0] // num_expert
    score_scale = HEAD ** (-0.5)

    small = jnp.concatenate(
        [
            attn_gain[None],
            ffn_gain[None],
            shared_gate_weight[None],
            qkv_bias,
            router_weight.T,
        ],
        axis=0,
    )
    small = lax.all_gather(small, "dp", axis=1, tiled=True)
    gain_one = small[0].astype(jnp.float32)
    gain_two = small[1].astype(jnp.float32)
    bias_cols = lax.dynamic_slice_in_dim(small[3:6], me_expert * head_width, head_width, 1)
    w_route = jnp.concatenate([small[6:], small[2:3]], axis=0)

    plane_tokens = lax.all_gather(tokens, "expert", axis=0, tiled=True)
    plane_docs = lax.all_gather(segment_ids, "expert", axis=0, tiled=True)
    cols_qkv = lax.dynamic_slice_in_dim(
        qkv_weight.reshape(shard_width, 3, model_width), me_expert * head_width, head_width, 2
    ).reshape(shard_width, 3 * head_width)
    cols_out = lax.dynamic_slice_in_dim(out_weight, me_expert * head_width, head_width, 1)
    attn_weights = lax.all_gather(
        jnp.concatenate([cols_qkv, cols_out], axis=1), "dp", axis=0, tiled=True
    )
    w_qkv = attn_weights[:, : 3 * head_width]
    w_out = lax.all_to_all(
        attn_weights[:, 3 * head_width :], "expert", split_axis=0, concat_axis=1, tiled=True
    )

    expert_full = jnp.concatenate([expert_up[0], expert_down[0][:, None, :]], axis=1)
    expert_units = lax.all_to_all(expert_full, "dp", split_axis=0, concat_axis=2, tiled=True)
    shared_units = lax.dynamic_slice_in_dim(shared_weight, me_expert * units, units, 0)
    mlp_weight = jnp.concatenate([expert_units, shared_units], axis=0)
    routed_units = expert_units.shape[0]
    all_units = routed_units + units

    all_cot = gather_all(cotangent)
    all_routes = gather_all(routes)

    plane_resid = plane_tokens.astype(jnp.float32)
    normed_one = (plane_resid * rms_scale(plane_resid) * gain_one).astype(jnp.bfloat16)
    qkv_rows = jnp.dot(normed_one, w_qkv, preferred_element_type=jnp.float32) + bias_cols.reshape(
        -1
    ).astype(jnp.float32)
    qkv_rows = qkv_rows.reshape(num_expert, seq_len, 3, head_count, HEAD)
    cosine_table, sine_table = rope_tables(seq_len, HEAD)
    query_rows = rotate(qkv_rows[:, :, 0], cosine_table, sine_table).astype(jnp.bfloat16)
    key_rows = rotate(qkv_rows[:, :, 1], cosine_table, sine_table).astype(jnp.bfloat16)
    value_rows = qkv_rows[:, :, 2].astype(jnp.bfloat16)
    positions = jnp.arange(seq_len)
    allowed = (
        (plane_docs[:, :, None] == plane_docs[:, None, :])
        & (positions[:, None] >= positions[None, :])[None]
    )[:, None]
    scores = (
        jnp.einsum("bthd,bshd->bhts", query_rows, key_rows, preferred_element_type=jnp.float32)
        * score_scale
    )
    scores = jnp.where(allowed, scores, NEGATIVE)
    exp_scores = jnp.exp(scores - jnp.max(scores, axis=-1, keepdims=True))
    attn_probs = exp_scores / jnp.sum(exp_scores, axis=-1, keepdims=True)
    probs_low = attn_probs.astype(jnp.bfloat16)
    mixed_heads = (
        jnp.einsum("bhts,bshd->bthd", probs_low, value_rows, preferred_element_type=jnp.float32)
        .reshape(plane_rows, head_width)
        .astype(jnp.bfloat16)
    )
    attn_part = jnp.dot(mixed_heads, w_out, preferred_element_type=jnp.float32)
    attn_out = lax.psum_scatter(
        attn_part.astype(jnp.bfloat16), "expert", scatter_dimension=0, tiled=True
    )

    resid_in = tokens.astype(jnp.float32)
    hidden_state = resid_in + attn_out.astype(jnp.float32)
    rms_two = rms_scale(hidden_state)
    normed_two = (hidden_state * rms_two * gain_two).astype(jnp.bfloat16)

    all_normed = gather_all(normed_two)
    all_logits = jnp.einsum(
        "td,ed->te", all_normed, w_route, preferred_element_type=jnp.float32
    )
    all_probs = jax.nn.softmax(all_logits[:, :num_expert], axis=-1)
    all_named = jnp.any(all_routes == me_expert, axis=1)
    my_prob = jnp.sum(
        jnp.where(jnp.arange(num_expert)[None, :] == me_expert, all_probs, 0.0), axis=1
    )
    gate_routed = jnp.where(all_named, my_prob, 0.0)
    gate_shared = jax.nn.sigmoid(all_logits[:, num_expert])
    is_routed = (jnp.arange(all_units) < routed_units)[None, :]
    row_gate = jnp.where(is_routed, gate_routed[:, None], gate_shared[:, None])

    gate_up = jnp.einsum(
        "td,fgd->gtf", all_normed, mlp_weight[:, :2], preferred_element_type=jnp.float32
    )
    silu, d_silu = silu_parts(gate_up[0])
    act = silu * gate_up[1]
    raw_act_grad = jnp.einsum(
        "td,fd->tf", all_cot, mlp_weight[:, 2], preferred_element_type=jnp.float32
    )
    gated_act = (row_gate * act).astype(jnp.bfloat16)
    act_dots = act * raw_act_grad
    d_gate_routed = jnp.where(
        all_named, jnp.sum(jnp.where(is_routed, act_dots, 0.0), axis=1), 0.0
    )
    d_gate_shared = jnp.sum(jnp.where(is_routed, 0.0, act_dots), axis=1)
    act_grad = raw_act_grad * row_gate
    d_gate_up = jnp.stack([act_grad * gate_up[1] * d_silu, act_grad * silu], axis=0).astype(
        jnp.bfloat16
    )
    d_rows = jnp.einsum(
        "gtf,fgd->td", d_gate_up, mlp_weight[:, :2], preferred_element_type=jnp.float32
    ).astype(jnp.bfloat16)
    gate_cols = jnp.concatenate(
        [
            jnp.where(
                jnp.arange(num_expert)[None, :] == me_expert, d_gate_routed[:, None], 0.0
            ),
            d_gate_shared[:, None],
        ],
        axis=1,
    )
    d_gate_cols = scatter_all(gate_cols)
    d_rows_sum = scatter_all(d_rows).astype(jnp.float32)

    up_grad = jnp.einsum(
        "gtf,td->fgd", d_gate_up, all_normed, preferred_element_type=jnp.float32
    ).astype(jnp.bfloat16)
    down_grad = jnp.einsum(
        "tf,td->fd", gated_act, all_cot, preferred_element_type=jnp.float32
    ).astype(jnp.bfloat16)
    out_rows = jnp.dot(gated_act, mlp_weight[:, 2], preferred_element_type=jnp.float32).astype(
        jnp.bfloat16
    )
    output = (hidden_state + scatter_all(out_rows).astype(jnp.float32)).astype(jnp.bfloat16)
    mlp_grad = jnp.concatenate([up_grad, down_grad[:, None, :]], axis=1)
    expert_grad = lax.all_to_all(
        mlp_grad[:routed_units], "dp", split_axis=2, concat_axis=0, tiled=True
    ).astype(jnp.float32)
    shared_grad = lax.all_gather(
        mlp_grad[routed_units:], "expert", axis=0, tiled=True
    ).astype(jnp.float32)

    back_grad = cotangent.astype(jnp.float32)
    logits = jnp.einsum("td,ed->te", normed_two, w_route, preferred_element_type=jnp.float32)
    router_probs = jax.nn.softmax(logits[:, :num_expert], axis=-1)
    logistic_gate = jax.nn.sigmoid(logits[:, num_expert:])
    d_router_probs = d_gate_cols[:, :num_expert]
    d_logits = router_probs * (
        d_router_probs - jnp.sum(router_probs * d_router_probs, axis=-1, keepdims=True)
    )
    d_gate_logit = d_gate_cols[:, num_expert:] * logistic_gate * (1.0 - logistic_gate)
    d_route = jnp.concatenate([d_logits, d_gate_logit], axis=1).astype(jnp.bfloat16)
    route_grad = jnp.einsum("td,te->ed", normed_two, d_route, preferred_element_type=jnp.float32)
    d_normed = d_rows_sum + jnp.dot(d_route, w_route, preferred_element_type=jnp.float32)
    ffn_gain_grad, d_hidden = norm_back(hidden_state, rms_two, gain_two, d_normed)
    d_hidden = back_grad + d_hidden

    d_attn_out = lax.all_gather(d_hidden.astype(jnp.bfloat16), "expert", axis=0, tiled=True)
    out_grad = jnp.einsum(
        "td,te->de", mixed_heads, d_attn_out, preferred_element_type=jnp.float32
    ).astype(jnp.bfloat16)
    out_grad = lax.all_to_all(out_grad, "expert", split_axis=1, concat_axis=0, tiled=True)
    d_mixed = (
        jnp.einsum("te,de->td", d_attn_out, w_out, preferred_element_type=jnp.float32)
        .astype(jnp.bfloat16)
        .reshape(num_expert, seq_len, head_count, HEAD)
    )
    values_grad = jnp.einsum(
        "bhts,bthd->bshd", probs_low, d_mixed, preferred_element_type=jnp.float32
    )
    d_probs = jnp.einsum("bthd,bshd->bhts", d_mixed, value_rows, preferred_element_type=jnp.float32)
    d_scores = (
        attn_probs * (d_probs - jnp.sum(attn_probs * d_probs, axis=-1, keepdims=True))
    ).astype(jnp.bfloat16)
    d_query = unrotate(
        jnp.einsum("bhts,bshd->bthd", d_scores, key_rows, preferred_element_type=jnp.float32)
        * score_scale,
        cosine_table,
        sine_table,
    )
    d_keys = unrotate(
        jnp.einsum("bhts,bthd->bshd", d_scores, query_rows, preferred_element_type=jnp.float32)
        * score_scale,
        cosine_table,
        sine_table,
    )
    d_qkv = (
        jnp.stack([d_query, d_keys, values_grad], axis=2)
        .reshape(plane_rows, 3 * head_width)
        .astype(jnp.bfloat16)
    )
    bias_part = jnp.sum(d_qkv.astype(jnp.float32), axis=0).reshape(3, head_width)
    bias_grad = lax.dynamic_update_slice_in_dim(
        jnp.zeros((3, model_width), jnp.float32), bias_part, me_expert * head_width, 1
    )
    d_normed_one = lax.psum_scatter(
        jnp.einsum("te,de->td", d_qkv, w_qkv, preferred_element_type=jnp.float32).astype(
            jnp.bfloat16
        ),
        "expert",
        scatter_dimension=0,
        tiled=True,
    ).astype(jnp.float32)
    qkv_grad = jnp.einsum(
        "td,te->de", normed_one, d_qkv, preferred_element_type=jnp.float32
    ).astype(jnp.bfloat16)
    attn_grad = lax.psum_scatter(
        jnp.concatenate([qkv_grad, out_grad], axis=1), "dp", scatter_dimension=0, tiled=True
    )
    attn_grad = lax.all_gather(attn_grad, "expert", axis=0).astype(jnp.float32)
    qkv_weight_grad = (
        attn_grad[:, :, : 3 * head_width]
        .reshape(num_expert, shard_width, 3, head_width)
        .transpose(1, 2, 0, 3)
        .reshape(shard_width, 3 * model_width)
    )
    out_weight_grad = (
        attn_grad[:, :, 3 * head_width :].transpose(1, 0, 2).reshape(shard_width, model_width)
    )
    attn_gain_grad, d_input = norm_back(resid_in, rms_scale(resid_in), gain_one, d_normed_one)
    tokens_grad = d_hidden + d_input

    small_grad = jnp.concatenate(
        [attn_gain_grad[None], ffn_gain_grad[None], bias_grad, route_grad], axis=0
    )
    small_grad = lax.psum_scatter(small_grad, "dp", scatter_dimension=1, tiled=True)
    small_grad = lax.psum(small_grad, "expert")
    return (
        output,
        tokens_grad,
        small_grad[0],
        qkv_weight_grad,
        small_grad[2:5],
        out_weight_grad,
        small_grad[1],
        small_grad[5 : 5 + num_expert].T,
        small_grad[5 + num_expert],
        shared_grad,
        expert_grad[None, :, :2],
        expert_grad[None, :, 2],
    )


def solution(mesh):
    return jax.shard_map(
        shards,
        mesh=mesh,
        in_specs=(
            P(("dp", "expert"), None),
            P("dp"),
            P("dp", None),
            P(None, "dp"),
            P("dp", None),
            P("dp"),
            P("dp", None),
            P("dp"),
            P("dp", None, None),
            P("expert", None, None, "dp"),
            P("expert", None, "dp"),
            P(("dp", "expert"), None),
            P(("dp", "expert"), None),
            P(("dp", "expert"), None),
        ),
        out_specs=(
            P(("dp", "expert"), None),
            P(("dp", "expert"), None),
            P("dp"),
            P("dp", None),
            P(None, "dp"),
            P("dp", None),
            P("dp"),
            P("dp", None),
            P("dp"),
            P("dp", None, None),
            P("expert", None, None, "dp"),
            P("expert", None, "dp"),
        ),
        check_vma=False,
    )
```

```python
import functools
import math

import jax
import jax.numpy as jnp
from jax import lax
from jax.experimental import pallas as pl
from jax.experimental.pallas import tpu as pltpu
from jax.sharding import PartitionSpec as P

HEADS = 16
HEAD = 128


EPS = 1e-06
THETA = 1000000.0
NEGATIVE = -1e30


def rms_scale(values):
    return lax.rsqrt(jnp.mean(values * values, axis=-1, keepdims=True) + EPS)


def rope_tables(length, head_width):
    indices = jnp.arange(head_width // 2).astype(jnp.float32)
    frequency = jnp.exp(indices * (-2.0 * math.log(THETA) / head_width))
    angles = jnp.arange(length).astype(jnp.float32)[:, None] * frequency[None, :]
    return (jnp.cos(angles), jnp.sin(angles))


def rotate(values, cosine_table, sine_table):
    half_width = values.shape[-1] // 2
    lower_half = values[..., :half_width]
    upper_half = values[..., half_width:]
    cos_rows = cosine_table[:, None, :]
    sin_rows = sine_table[:, None, :]
    return jnp.concatenate(
        [
            lower_half * cos_rows - upper_half * sin_rows,
            upper_half * cos_rows + lower_half * sin_rows,
        ],
        axis=-1,
    )


def unrotate(values, cosine_table, sine_table):
    half_width = values.shape[-1] // 2
    lower_half = values[..., :half_width]
    upper_half = values[..., half_width:]
    cos_rows = cosine_table[:, None, :]
    sin_rows = sine_table[:, None, :]
    return jnp.concatenate(
        [
            lower_half * cos_rows + upper_half * sin_rows,
            upper_half * cos_rows - lower_half * sin_rows,
        ],
        axis=-1,
    )


def norm_back(values, scale_rows, gain_row, upstream):
    scaled = gain_row * upstream
    gain_grad = jnp.sum(upstream * values * scale_rows, axis=0)
    input_grad = scale_rows * scaled - values * scale_rows**3 * jnp.mean(
        scaled * values, axis=-1, keepdims=True
    )
    return (gain_grad, input_grad)


MESH = pl.DeviceIdType.MESH
NT = (((1,), (1,)), ((), ()))


def flip(index, step):
    return index + step - 2 * step * lax.rem(lax.div(index, step), 2)


def flip_pair(index, turn):
    return index + lax.rem(turn, 2) * (1 - 2 * lax.rem(index, 2)) + lax.div(turn, 2) * (
        2 - 4 * lax.rem(lax.div(index, 2), 2)
    )


def send(source, target, send_sem, recv_sem, device):
    return pltpu.make_async_remote_copy(
        src_ref=source,
        dst_ref=target,
        send_sem=send_sem,
        recv_sem=recv_sem,
        device_id=device,
        device_id_type=MESH,
    )


def greet(devices):
    barrier = pltpu.get_barrier_semaphore()
    for device in devices:
        pl.semaphore_signal(barrier, inc=1, device_id=device, device_id_type=MESH)
    pl.semaphore_wait(barrier, len(devices))


def mlp_kernel(
    routed_units,
    x_own,
    g_own,
    cot,
    w_gu,
    w_d,
    x_all,
    out_part,
    dx_own,
    dg_own,
    acc_gu,
    acc_d,
    g_all,
    x_tile,
    c_tile,
    gu_buf,
    h_buf,
    dgu_buf,
    act_buf,
    out_buf,
    dx_buf,
    dg_buf,
    sib_x,
    sib_g,
    cross_x,
    cross_g,
    sum_x,
    sum_g,
    far_x,
    far_g,
    ag_send,
    ag_recv,
    gs_send,
    gs_recv,
    rs_send,
    rs_recv,
    rg_send,
    rg_recv,
    local_sem,
):
    me_z = lax.axis_index("dp")
    me_e = lax.axis_index("expert")
    core = lax.rem(me_e, 2)
    me_x = lax.rem(lax.div(me_e, 2), 2)
    me_y = lax.div(me_e, 4)
    sib = flip(me_e, 1)
    nbr = {1: sib, 2: flip(me_e, 2), 4: flip(me_e, 4), 6: flip(flip(me_e, 2), 4)}
    nbr[3], nbr[5], nbr[7] = flip(nbr[2], 1), flip(nbr[4], 1), flip(nbr[6], 1)
    units, width = w_d.shape
    rows = x_own.shape[0]
    tile = 4 * rows
    chunk = 256

    def z_of(turn):
        return flip_pair(me_z, turn)

    plane_step = {1: 1, 2: 2, 3: 4, 4: 6}
    on_step = {5: 2, 6: 4, 7: 6}

    def gather_send(turn, channel):
        if channel == 0:
            block, device = (me_z, me_e), (z_of(turn), me_e)
        elif channel in plane_step:
            block, device = (z_of(turn), me_e), (me_z, nbr[plane_step[channel]])
        else:
            block, device = (z_of(turn), nbr[on_step[channel]]), (me_z, sib)
        return (
            send(x_all.at[block], x_all.at[block], ag_send.at[turn, channel], ag_recv.at[turn, channel], device),
            send(g_all.at[block], g_all.at[block], gs_send.at[turn, channel], gs_recv.at[turn, channel], device),
        )

    def gather_wait(turn, channel):
        if channel == 0:
            block = (z_of(turn), me_e)
        elif channel in plane_step:
            block = (z_of(turn), nbr[plane_step[channel]])
        else:
            block = (z_of(turn), nbr[on_step[channel] + 1])
        for buffer, sems in ((x_all, (ag_send, ag_recv)), (g_all, (gs_send, gs_recv))):
            send(
                buffer.at[block],
                buffer.at[block],
                sems[0].at[turn, channel],
                sems[1].at[turn, channel],
                (me_z, sib),
            ).wait_recv()

    def start(copies):
        for copy in copies:
            copy.start()

    def spread(turn):
        for channel in (4, 2, 3, 1):
            start(gather_send(turn, channel))

    def pass_on(turn):
        for channel in (2, 3, 4):
            gather_wait(turn, channel)
            start(gather_send(turn, channel + 3))

    def scatter_send(turn, channel):
        par = lax.rem(turn, 2)
        if channel < 2:
            group = me_y if channel == 0 else 1 - me_y
            source, target, device = (par, 1 - core, group), (par, channel), (me_z, sib)
            buffers = (dx_buf, sib_x), (dg_buf, sib_g)
        elif channel < 5:
            group = me_y if channel == 2 else 1 - me_y
            column = me_x if channel == 3 else 1 - me_x
            source, target = (par, core, group, column), (turn, channel - 2)
            device = (me_z, nbr[(2, 4, 6)[channel - 2]])
            buffers = (dx_buf, cross_x), (dg_buf, cross_g)
        else:
            source, target, device = (turn,), (turn,), (z_of(turn), me_e)
            buffers = (sum_x, far_x), (sum_g, far_g)
        (x_from, x_to), (g_from, g_to) = buffers
        return (
            send(x_from.at[source], x_to.at[target], rs_send.at[turn, channel], rs_recv.at[turn, channel], device),
            send(g_from.at[source], g_to.at[target], rg_send.at[turn, channel], rg_recv.at[turn, channel], device),
        )

    def wait_recv(copies):
        for copy in copies:
            copy.wait_recv()

    def wait_send(copies):
        for copy in copies:
            copy.wait_send()

    def pair_sum(turn, half):
        par = lax.rem(turn, 2)
        wait_recv(scatter_send(turn, half))
        group = me_y if half == 0 else 1 - me_y
        for column in range(2):

            @pl.loop(0, rows, step=32)
            def _(row):
                span = pl.ds(pl.multiple_of(row, 32), 32)
                dx_buf[par, core, group, column, span, :] = (
                    dx_buf[par, core, group, column, span, :].astype(jnp.float32)
                    + sib_x[par, half, column, span, :].astype(jnp.float32)
                ).astype(jnp.bfloat16)

            dg_buf[par, core, group, column] = (
                dg_buf[par, core, group, column] + sib_g[par, half, column]
            )
        if half == 0:
            start(scatter_send(turn, 2))
        else:
            start(scatter_send(turn, 4))
            start(scatter_send(turn, 3))

    def plane_sum(turn):
        par = lax.rem(turn, 2)
        for channel in (2, 3, 4):
            wait_recv(scatter_send(turn, channel))

        @pl.loop(0, rows, step=32)
        def _(row):
            span = pl.ds(pl.multiple_of(row, 32), 32)
            total = dx_buf[par, core, me_y, me_x, span, :].astype(jnp.float32)
            for k in range(3):
                total = total + cross_x[turn, k, span, :].astype(jnp.float32)
            sum_x[turn, span, :] = total.astype(jnp.bfloat16)

        total = dg_buf[par, core, me_y, me_x]
        for k in range(3):
            total = total + cross_g[turn, k]
        sum_g[turn] = total

        @pl.when(turn > 0)
        def _():
            start(scatter_send(turn, 5))

        for channel in range(5):
            wait_send(scatter_send(turn, channel))

    greet(
        [(z_of(turn), me_e) for turn in (1, 2, 3)]
        + [(me_z, nbr[step]) for step in (1, 2, 4, 6)]
    )
    own = pltpu.make_async_copy(x_own, x_all.at[me_z, me_e], local_sem.at[0])
    own.start()
    g_all[me_z, me_e] = g_own[...]
    own.wait()
    spread(0)
    for turn in (1, 2, 3):
        start(gather_send(turn, 0))

    @pl.loop(0, 2 * units, step=48)
    def _(row):
        acc_gu[pl.ds(pl.multiple_of(row, 16), 48), :] = jnp.zeros((48, width), jnp.float32)

    @pl.loop(0, units, step=48)
    def _(row):
        acc_d[pl.ds(pl.multiple_of(row, 16), 48), :] = jnp.zeros((48, width), jnp.float32)

    pass_on(0)

    def step(index, carry):
        turn, half = lax.div(index, 2), lax.rem(index, 2)
        par = lax.rem(turn, 2)
        where = z_of(turn)
        group = lax.rem(me_y + half, 2)
        block = pl.ds(pl.multiple_of(group * 4, 4), 4)

        c_load = pltpu.make_async_copy(cot.at[block, where], c_tile, local_sem.at[1])
        c_load.start()

        @pl.when(half == 0)
        def _():
            gather_wait(turn, 1)
            gather_wait(turn, 5)

        @pl.when(half == 1)
        def _():
            gather_wait(turn, 6)
            gather_wait(turn, 7)

        x_load = pltpu.make_async_copy(x_all.at[where, block], x_tile, local_sem.at[0])
        x_load.start()
        x_load.wait()
        c_load.wait()
        for j in range(2):
            xs = x_tile[2 * j : 2 * j + 2].reshape(2 * rows, width)
            cs = c_tile[2 * j : 2 * j + 2].reshape(2 * rows, width)
            gu_buf[:, 2 * rows * j : 2 * rows * (j + 1)] = lax.dot_general(
                w_gu[...], xs, NT, preferred_element_type=jnp.float32
            )
            h_buf[:, 2 * rows * j : 2 * rows * (j + 1)] = lax.dot_general(
                w_d[...], cs, NT, preferred_element_type=jnp.float32
            )

        def gates(row):
            return jnp.concatenate(
                [g_all[where, group * 4 + j, pl.ds(row, 1), :] for j in range(4)], axis=1
            )

        gate_routed = gates(me_e)
        gate_shared = gates(8)
        dots = []
        for low, high, gate in (
            (0, routed_units, gate_routed),
            (routed_units, units, gate_shared),
        ):
            part = high - low
            piece = 16

            def units_step(k, dot, low=low, gate=gate):
                at = pl.multiple_of(low + k * piece, 16)
                g = gu_buf[pl.ds(at, piece), :]
                u = gu_buf[pl.ds(pl.multiple_of(units + at, 16), piece), :]
                h = h_buf[pl.ds(at, piece), :]
                logistic = jax.nn.sigmoid(g)
                silu = g * logistic
                act = silu * u
                act_buf[pl.ds(at, piece), :] = (act * gate).astype(jnp.bfloat16)
                d_act = h * gate
                dgu_buf[pl.ds(at, piece), :] = (
                    d_act * u * (logistic * (1.0 + g * (1.0 - logistic)))
                ).astype(jnp.bfloat16)
                dgu_buf[pl.ds(pl.multiple_of(units + at, 16), piece), :] = (d_act * silu).astype(
                    jnp.bfloat16
                )
                return dot + jnp.sum(act * h, axis=0, keepdims=True)

            dots.append(
                lax.fori_loop(0, part // piece, units_step, jnp.zeros((1, tile), jnp.float32))
            )
        line = lax.broadcasted_iota(jnp.int32, (16, tile), 0)
        d_gates = jnp.where(line == me_e, dots[0], 0.0) + jnp.where(line == 8, dots[1], 0.0)
        for j in range(4):
            dg_buf[par, j % 2, group, j // 2] = d_gates[:, j * rows : (j + 1) * rows]

        xs = x_tile[...].reshape(tile, width)
        cs = c_tile[...].reshape(tile, width)
        for n in range(width // chunk):
            cols = slice(n * chunk, (n + 1) * chunk)
            acc_gu[:, cols] += jnp.dot(
                dgu_buf[...], x_tile[:, :, cols].reshape(tile, chunk), preferred_element_type=jnp.float32
            )
            acc_d[:, cols] += jnp.dot(
                act_buf[...], c_tile[:, :, cols].reshape(tile, chunk), preferred_element_type=jnp.float32
            )

        out_store = pltpu.make_async_copy(out_buf, out_part.at[block, where], local_sem.at[2])

        @pl.when(index > 0)
        def _():
            out_store.wait()

        dgu_t = dgu_buf[...].T
        act_t = act_buf[...].T
        for n in range(width // chunk):
            cols = slice(n * chunk, (n + 1) * chunk)
            dx = jnp.dot(dgu_t, w_gu[:, cols], preferred_element_type=jnp.float32).astype(jnp.bfloat16)
            out = jnp.dot(act_t, w_d[:, cols], preferred_element_type=jnp.float32).astype(jnp.bfloat16)
            for j in range(4):
                dx_buf[par, j % 2, group, j // 2, :, cols] = dx[j * rows : (j + 1) * rows]
                out_buf[j, :, cols] = out[j * rows : (j + 1) * rows]
        out_store.start()

        @pl.when(half == 0)
        def _():
            start(scatter_send(turn, 0))

            @pl.when(turn < 3)
            def _():
                gather_wait(turn + 1, 0)
                spread(turn + 1)

            @pl.when(turn > 0)
            def _():
                pair_sum(turn - 1, 1)

        @pl.when(half == 1)
        def _():
            start(scatter_send(turn, 1))
            pair_sum(turn, 0)

            @pl.when(turn < 3)
            def _():
                pass_on(turn + 1)

            @pl.when(turn > 0)
            def _():
                plane_sum(turn - 1)

        return carry

    lax.fori_loop(0, 8, step, 0)
    pair_sum(3, 1)
    plane_sum(3)
    pltpu.make_async_copy(out_buf, out_part.at[pl.ds(0, 4), me_z], local_sem.at[2]).wait()
    for turn in (1, 2, 3):
        wait_recv(
            (
                send(sum_x.at[turn], far_x.at[turn], rs_send.at[turn, 5], rs_recv.at[turn, 5], (me_z, sib)),
                send(sum_g.at[turn], far_g.at[turn], rg_send.at[turn, 5], rg_recv.at[turn, 5], (me_z, sib)),
            )
        )

    @pl.loop(0, rows, step=32)
    def _(row):
        span = pl.ds(pl.multiple_of(row, 32), 32)
        total = sum_x[0, span, :].astype(jnp.float32)
        for turn in (1, 2, 3):
            total = total + far_x[turn, span, :].astype(jnp.float32)
        dx_own[span, :] = total

    dg_own[...] = sum_g[0] + far_g[1] + far_g[2] + far_g[3]
    for turn in range(4):
        if turn > 0:
            wait_send(gather_send(turn, 0))
            wait_send(scatter_send(turn, 5))
        for channel in range(1, 8):
            wait_send(gather_send(turn, channel))


def mlp_call(normed_own, gates_own, all_cot, w_gu, w_d, routed_units):
    num_expert, num_dp, rows, width = all_cot.shape
    units = w_d.shape[0]
    low, full = jnp.bfloat16, jnp.float32
    any_space = pl.BlockSpec(memory_space=pl.ANY)
    vmem = pl.BlockSpec(memory_space=pltpu.VMEM)
    dma = pltpu.SemaphoreType.DMA
    flops = 18 * num_expert * num_dp * rows * units * width
    return pl.pallas_call(
        functools.partial(mlp_kernel, routed_units),
        out_shape=(
            jax.ShapeDtypeStruct((num_dp, num_expert, rows, width), low),
            jax.ShapeDtypeStruct((num_expert, num_dp, rows, width), low),
            jax.ShapeDtypeStruct((rows, width), full),
            jax.ShapeDtypeStruct((16, rows), full),
            jax.ShapeDtypeStruct((2 * units, width), full),
            jax.ShapeDtypeStruct((units, width), full),
        ),
        in_specs=[any_space, vmem, any_space, vmem, vmem],
        out_specs=(any_space, any_space, vmem, vmem, vmem, vmem),
        scratch_shapes=[
            pltpu.VMEM((num_dp, num_expert, 16, rows), full),
            pltpu.VMEM((4, rows, width), low),
            pltpu.VMEM((4, rows, width), low),
            pltpu.VMEM((2 * units, 4 * rows), full),
            pltpu.VMEM((units, 4 * rows), full),
            pltpu.VMEM((2 * units, 4 * rows), low),
            pltpu.VMEM((units, 4 * rows), low),
            pltpu.VMEM((4, rows, width), low),
            pltpu.VMEM((2, 2, 2, 2, rows, width), low),
            pltpu.VMEM((2, 2, 2, 2, 16, rows), full),
            pltpu.VMEM((2, 2, 2, rows, width), low),
            pltpu.VMEM((2, 2, 2, 16, rows), full),
            pltpu.VMEM((4, 3, rows, width), low),
            pltpu.VMEM((4, 3, 16, rows), full),
            pltpu.VMEM((4, rows, width), low),
            pltpu.VMEM((4, 16, rows), full),
            pltpu.VMEM((4, rows, width), low),
            pltpu.VMEM((4, 16, rows), full),
            dma((4, 8)),
            dma((4, 8)),
            dma((4, 8)),
            dma((4, 8)),
            dma((4, 6)),
            dma((4, 6)),
            dma((4, 6)),
            dma((4, 6)),
            dma((3,)),
        ],
        compiler_params=pltpu.CompilerParams(
            collective_id=0, has_side_effects=True, vmem_limit_bytes=63 * 2**20
        ),
        cost_estimate=pl.CostEstimate(flops=flops, bytes_accessed=80 * 2**20, transcendentals=0),
    )(normed_own, gates_own, all_cot, w_gu, w_d)


def silu_parts(gate):
    logistic = jax.nn.sigmoid(gate)
    silu = gate * logistic
    return (silu, logistic * (1.0 + gate * (1.0 - logistic)))


def gather_all(rows):
    rows = lax.all_gather(rows, "dp", axis=0, tiled=True)
    return lax.all_gather(rows, "expert", axis=0, tiled=True)


def scatter_all(rows):
    rows = lax.psum_scatter(rows, "expert", scatter_dimension=0, tiled=True)
    return lax.psum_scatter(rows, "dp", scatter_dimension=0, tiled=True)


def shards(
    tokens,
    attn_gain,
    qkv_weight,
    qkv_bias,
    out_weight,
    ffn_gain,
    router_weight,
    shared_gate_weight,
    shared_weight,
    expert_up,
    expert_down,
    routes,
    segment_ids,
    cotangent,
):
    num_dp = lax.axis_size("dp")
    num_expert = lax.axis_size("expert")
    me_expert = lax.axis_index("expert")
    seq_len, model_width = tokens.shape
    shard_width = qkv_weight.shape[0]
    head_count = HEADS // num_expert
    head_width = head_count * HEAD
    plane_rows = seq_len * num_expert
    units = shared_weight.shape[0] // num_expert
    score_scale = HEAD ** (-0.5)

    small = jnp.concatenate(
        [
            attn_gain[None],
            ffn_gain[None],
            shared_gate_weight[None],
            qkv_bias,
            router_weight.T,
        ],
        axis=0,
    )
    small = lax.all_gather(small, "dp", axis=1, tiled=True)
    gain_one = small[0].astype(jnp.float32)
    gain_two = small[1].astype(jnp.float32)
    bias_cols = lax.dynamic_slice_in_dim(small[3:6], me_expert * head_width, head_width, 1)
    w_route = jnp.concatenate([small[6:], small[2:3]], axis=0)

    plane_tokens = lax.all_gather(tokens, "expert", axis=0, tiled=True)
    plane_docs = lax.all_gather(segment_ids, "expert", axis=0, tiled=True)
    cols_qkv = lax.dynamic_slice_in_dim(
        qkv_weight.reshape(shard_width, 3, model_width), me_expert * head_width, head_width, 2
    ).reshape(shard_width, 3 * head_width)
    cols_out = lax.dynamic_slice_in_dim(out_weight, me_expert * head_width, head_width, 1)
    attn_weights = lax.all_gather(
        jnp.concatenate([cols_qkv, cols_out], axis=1), "dp", axis=0, tiled=True
    )
    w_qkv = attn_weights[:, : 3 * head_width]
    w_out = lax.all_to_all(
        attn_weights[:, 3 * head_width :], "expert", split_axis=0, concat_axis=1, tiled=True
    )

    expert_full = jnp.concatenate([expert_up[0], expert_down[0][:, None, :]], axis=1)
    expert_units = lax.all_to_all(expert_full, "dp", split_axis=0, concat_axis=2, tiled=True)
    shared_units = lax.dynamic_slice_in_dim(shared_weight, me_expert * units, units, 0)
    mlp_weight = jnp.concatenate([expert_units, shared_units], axis=0)
    routed_units = expert_units.shape[0]
    all_units = routed_units + units

    all_cot = gather_all(cotangent)
    all_routes = gather_all(routes)

    plane_resid = plane_tokens.astype(jnp.float32)
    normed_one = (plane_resid * rms_scale(plane_resid) * gain_one).astype(jnp.bfloat16)
    qkv_rows = jnp.dot(normed_one, w_qkv, preferred_element_type=jnp.float32) + bias_cols.reshape(
        -1
    ).astype(jnp.float32)
    qkv_rows = qkv_rows.reshape(num_expert, seq_len, 3, head_count, HEAD)
    cosine_table, sine_table = rope_tables(seq_len, HEAD)
    query_rows = rotate(qkv_rows[:, :, 0], cosine_table, sine_table).astype(jnp.bfloat16)
    key_rows = rotate(qkv_rows[:, :, 1], cosine_table, sine_table).astype(jnp.bfloat16)
    value_rows = qkv_rows[:, :, 2].astype(jnp.bfloat16)
    positions = jnp.arange(seq_len)
    allowed = (
        (plane_docs[:, :, None] == plane_docs[:, None, :])
        & (positions[:, None] >= positions[None, :])[None]
    )[:, None]
    scores = (
        jnp.einsum("bthd,bshd->bhts", query_rows, key_rows, preferred_element_type=jnp.float32)
        * score_scale
    )
    scores = jnp.where(allowed, scores, NEGATIVE)
    exp_scores = jnp.exp(scores - jnp.max(scores, axis=-1, keepdims=True))
    attn_probs = exp_scores / jnp.sum(exp_scores, axis=-1, keepdims=True)
    probs_low = attn_probs.astype(jnp.bfloat16)
    mixed_heads = (
        jnp.einsum("bhts,bshd->bthd", probs_low, value_rows, preferred_element_type=jnp.float32)
        .reshape(plane_rows, head_width)
        .astype(jnp.bfloat16)
    )
    attn_part = jnp.dot(mixed_heads, w_out, preferred_element_type=jnp.float32)
    attn_out = lax.psum_scatter(
        attn_part.astype(jnp.bfloat16), "expert", scatter_dimension=0, tiled=True
    )

    resid_in = tokens.astype(jnp.float32)
    hidden_state = resid_in + attn_out.astype(jnp.float32)
    rms_two = rms_scale(hidden_state)
    normed_two = (hidden_state * rms_two * gain_two).astype(jnp.bfloat16)

    all_normed = gather_all(normed_two)
    all_logits = jnp.einsum(
        "td,ed->te", all_normed, w_route, preferred_element_type=jnp.float32
    )
    all_probs = jax.nn.softmax(all_logits[:, :num_expert], axis=-1)
    all_named = jnp.any(all_routes == me_expert, axis=1)
    my_prob = jnp.sum(
        jnp.where(jnp.arange(num_expert)[None, :] == me_expert, all_probs, 0.0), axis=1
    )
    gate_routed = jnp.where(all_named, my_prob, 0.0)
    gate_shared = jax.nn.sigmoid(all_logits[:, num_expert])
    is_routed = (jnp.arange(all_units) < routed_units)[None, :]
    row_gate = jnp.where(is_routed, gate_routed[:, None], gate_shared[:, None])

    gate_up = jnp.einsum(
        "td,fgd->gtf", all_normed, mlp_weight[:, :2], preferred_element_type=jnp.float32
    )
    silu, d_silu = silu_parts(gate_up[0])
    act = silu * gate_up[1]
    raw_act_grad = jnp.einsum(
        "td,fd->tf", all_cot, mlp_weight[:, 2], preferred_element_type=jnp.float32
    )
    gated_act = (row_gate * act).astype(jnp.bfloat16)
    act_dots = act * raw_act_grad
    d_gate_routed = jnp.where(
        all_named, jnp.sum(jnp.where(is_routed, act_dots, 0.0), axis=1), 0.0
    )
    d_gate_shared = jnp.sum(jnp.where(is_routed, 0.0, act_dots), axis=1)
    act_grad = raw_act_grad * row_gate
    d_gate_up = jnp.stack([act_grad * gate_up[1] * d_silu, act_grad * silu], axis=0).astype(
        jnp.bfloat16
    )
    d_rows = jnp.einsum(
        "gtf,fgd->td", d_gate_up, mlp_weight[:, :2], preferred_element_type=jnp.float32
    ).astype(jnp.bfloat16)
    gate_cols = jnp.concatenate(
        [
            jnp.where(
                jnp.arange(num_expert)[None, :] == me_expert, d_gate_routed[:, None], 0.0
            ),
            d_gate_shared[:, None],
        ],
        axis=1,
    )
    d_gate_cols = scatter_all(gate_cols)
    d_rows_sum = scatter_all(d_rows).astype(jnp.float32)

    up_grad = jnp.einsum(
        "gtf,td->fgd", d_gate_up, all_normed, preferred_element_type=jnp.float32
    ).astype(jnp.bfloat16)
    down_grad = jnp.einsum(
        "tf,td->fd", gated_act, all_cot, preferred_element_type=jnp.float32
    ).astype(jnp.bfloat16)
    out_rows = jnp.dot(gated_act, mlp_weight[:, 2], preferred_element_type=jnp.float32).astype(
        jnp.bfloat16
    )
    output = (hidden_state + scatter_all(out_rows).astype(jnp.float32)).astype(jnp.bfloat16)
    mlp_grad = jnp.concatenate([up_grad, down_grad[:, None, :]], axis=1)
    expert_grad = lax.all_to_all(
        mlp_grad[:routed_units], "dp", split_axis=2, concat_axis=0, tiled=True
    ).astype(jnp.float32)
    shared_grad = lax.all_gather(
        mlp_grad[routed_units:], "expert", axis=0, tiled=True
    ).astype(jnp.float32)

    back_grad = cotangent.astype(jnp.float32)
    logits = jnp.einsum("td,ed->te", normed_two, w_route, preferred_element_type=jnp.float32)
    router_probs = jax.nn.softmax(logits[:, :num_expert], axis=-1)
    logistic_gate = jax.nn.sigmoid(logits[:, num_expert:])
    d_router_probs = d_gate_cols[:, :num_expert]
    d_logits = router_probs * (
        d_router_probs - jnp.sum(router_probs * d_router_probs, axis=-1, keepdims=True)
    )
    d_gate_logit = d_gate_cols[:, num_expert:] * logistic_gate * (1.0 - logistic_gate)
    d_route = jnp.concatenate([d_logits, d_gate_logit], axis=1).astype(jnp.bfloat16)
    route_grad = jnp.einsum("td,te->ed", normed_two, d_route, preferred_element_type=jnp.float32)
    d_normed = d_rows_sum + jnp.dot(d_route, w_route, preferred_element_type=jnp.float32)
    ffn_gain_grad, d_hidden = norm_back(hidden_state, rms_two, gain_two, d_normed)
    d_hidden = back_grad + d_hidden

    d_attn_out = lax.all_gather(d_hidden.astype(jnp.bfloat16), "expert", axis=0, tiled=True)
    out_grad = jnp.einsum(
        "td,te->de", mixed_heads, d_attn_out, preferred_element_type=jnp.float32
    ).astype(jnp.bfloat16)
    out_grad = lax.all_to_all(out_grad, "expert", split_axis=1, concat_axis=0, tiled=True)
    d_mixed = (
        jnp.einsum("te,de->td", d_attn_out, w_out, preferred_element_type=jnp.float32)
        .astype(jnp.bfloat16)
        .reshape(num_expert, seq_len, head_count, HEAD)
    )
    values_grad = jnp.einsum(
        "bhts,bthd->bshd", probs_low, d_mixed, preferred_element_type=jnp.float32
    )
    d_probs = jnp.einsum("bthd,bshd->bhts", d_mixed, value_rows, preferred_element_type=jnp.float32)
    d_scores = (
        attn_probs * (d_probs - jnp.sum(attn_probs * d_probs, axis=-1, keepdims=True))
    ).astype(jnp.bfloat16)
    d_query = unrotate(
        jnp.einsum("bhts,bshd->bthd", d_scores, key_rows, preferred_element_type=jnp.float32)
        * score_scale,
        cosine_table,
        sine_table,
    )
    d_keys = unrotate(
        jnp.einsum("bhts,bthd->bshd", d_scores, query_rows, preferred_element_type=jnp.float32)
        * score_scale,
        cosine_table,
        sine_table,
    )
    d_qkv = (
        jnp.stack([d_query, d_keys, values_grad], axis=2)
        .reshape(plane_rows, 3 * head_width)
        .astype(jnp.bfloat16)
    )
    bias_part = jnp.sum(d_qkv.astype(jnp.float32), axis=0).reshape(3, head_width)
    bias_grad = lax.dynamic_update_slice_in_dim(
        jnp.zeros((3, model_width), jnp.float32), bias_part, me_expert * head_width, 1
    )
    d_normed_one = lax.psum_scatter(
        jnp.einsum("te,de->td", d_qkv, w_qkv, preferred_element_type=jnp.float32).astype(
            jnp.bfloat16
        ),
        "expert",
        scatter_dimension=0,
        tiled=True,
    ).astype(jnp.float32)
    qkv_grad = jnp.einsum(
        "td,te->de", normed_one, d_qkv, preferred_element_type=jnp.float32
    ).astype(jnp.bfloat16)
    attn_grad = lax.psum_scatter(
        jnp.concatenate([qkv_grad, out_grad], axis=1), "dp", scatter_dimension=0, tiled=True
    )
    attn_grad = lax.all_gather(attn_grad, "expert", axis=0).astype(jnp.float32)
    qkv_weight_grad = (
        attn_grad[:, :, : 3 * head_width]
        .reshape(num_expert, shard_width, 3, head_width)
        .transpose(1, 2, 0, 3)
        .reshape(shard_width, 3 * model_width)
    )
    out_weight_grad = (
        attn_grad[:, :, 3 * head_width :].transpose(1, 0, 2).reshape(shard_width, model_width)
    )
    attn_gain_grad, d_input = norm_back(resid_in, rms_scale(resid_in), gain_one, d_normed_one)
    tokens_grad = d_hidden + d_input

    small_grad = jnp.concatenate(
        [attn_gain_grad[None], ffn_gain_grad[None], bias_grad, route_grad], axis=0
    )
    small_grad = lax.psum_scatter(small_grad, "dp", scatter_dimension=1, tiled=True)
    small_grad = lax.psum(small_grad, "expert")
    return (
        output,
        tokens_grad,
        small_grad[0],
        qkv_weight_grad,
        small_grad[2:5],
        out_weight_grad,
        small_grad[1],
        small_grad[5 : 5 + num_expert].T,
        small_grad[5 + num_expert],
        shared_grad,
        expert_grad[None, :, :2],
        expert_grad[None, :, 2],
    )


def fast_shards(
    tokens,
    attn_gain,
    qkv_weight,
    qkv_bias,
    out_weight,
    ffn_gain,
    router_weight,
    shared_gate_weight,
    shared_weight,
    expert_up,
    expert_down,
    routes,
    segment_ids,
    cotangent,
):
    num_dp = lax.axis_size("dp")
    num_expert = lax.axis_size("expert")
    me_expert = lax.axis_index("expert")
    seq_len, model_width = tokens.shape
    shard_width = qkv_weight.shape[0]
    head_count = HEADS // num_expert
    head_width = head_count * HEAD
    plane_rows = seq_len * num_expert
    units = shared_weight.shape[0] // num_expert
    score_scale = HEAD ** (-0.5)

    small = jnp.concatenate(
        [
            attn_gain[None],
            ffn_gain[None],
            shared_gate_weight[None],
            qkv_bias,
            router_weight.T,
        ],
        axis=0,
    )
    small = lax.all_gather(small, "dp", axis=1, tiled=True)
    gain_one = small[0].astype(jnp.float32)
    gain_two = small[1].astype(jnp.float32)
    bias_cols = lax.dynamic_slice_in_dim(small[3:6], me_expert * head_width, head_width, 1)
    w_route = jnp.concatenate([small[6:], small[2:3]], axis=0)

    plane_tokens = lax.all_gather(tokens, "expert", axis=0, tiled=True)
    plane_docs = lax.all_gather(segment_ids, "expert", axis=0, tiled=True)
    cols_qkv = lax.dynamic_slice_in_dim(
        qkv_weight.reshape(shard_width, 3, model_width), me_expert * head_width, head_width, 2
    ).reshape(shard_width, 3 * head_width)
    cols_out = lax.dynamic_slice_in_dim(out_weight, me_expert * head_width, head_width, 1)
    attn_weights = lax.all_gather(
        jnp.concatenate([cols_qkv, cols_out], axis=1), "dp", axis=0, tiled=True
    )
    w_qkv = attn_weights[:, : 3 * head_width]
    w_out = lax.all_to_all(
        attn_weights[:, 3 * head_width :], "expert", split_axis=0, concat_axis=1, tiled=True
    )

    expert_full = jnp.concatenate([expert_up[0], expert_down[0][:, None, :]], axis=1)
    expert_units = lax.all_to_all(expert_full, "dp", split_axis=0, concat_axis=2, tiled=True)
    shared_units = lax.dynamic_slice_in_dim(shared_weight, me_expert * units, units, 0)
    mlp_weight = jnp.concatenate([expert_units, shared_units], axis=0)
    routed_units = expert_units.shape[0]
    all_units = routed_units + units

    all_cot = gather_all(cotangent)

    plane_resid = plane_tokens.astype(jnp.float32)
    normed_one = (plane_resid * rms_scale(plane_resid) * gain_one).astype(jnp.bfloat16)
    qkv_rows = jnp.dot(normed_one, w_qkv, preferred_element_type=jnp.float32) + bias_cols.reshape(
        -1
    ).astype(jnp.float32)
    qkv_rows = qkv_rows.reshape(num_expert, seq_len, 3, head_count, HEAD)
    cosine_table, sine_table = rope_tables(seq_len, HEAD)
    query_rows = rotate(qkv_rows[:, :, 0], cosine_table, sine_table).astype(jnp.bfloat16)
    key_rows = rotate(qkv_rows[:, :, 1], cosine_table, sine_table).astype(jnp.bfloat16)
    value_rows = qkv_rows[:, :, 2].astype(jnp.bfloat16)
    positions = jnp.arange(seq_len)
    allowed = (
        (plane_docs[:, :, None] == plane_docs[:, None, :])
        & (positions[:, None] >= positions[None, :])[None]
    )[:, None]
    scores = (
        jnp.einsum("bthd,bshd->bhts", query_rows, key_rows, preferred_element_type=jnp.float32)
        * score_scale
    )
    scores = jnp.where(allowed, scores, NEGATIVE)
    exp_scores = jnp.exp(scores - jnp.max(scores, axis=-1, keepdims=True))
    attn_probs = exp_scores / jnp.sum(exp_scores, axis=-1, keepdims=True)
    probs_low = attn_probs.astype(jnp.bfloat16)
    mixed_heads = (
        jnp.einsum("bhts,bshd->bthd", probs_low, value_rows, preferred_element_type=jnp.float32)
        .reshape(plane_rows, head_width)
        .astype(jnp.bfloat16)
    )
    attn_part = jnp.dot(mixed_heads, w_out, preferred_element_type=jnp.float32)
    attn_out = lax.psum_scatter(
        attn_part.astype(jnp.bfloat16), "expert", scatter_dimension=0, tiled=True
    )

    resid_in = tokens.astype(jnp.float32)
    hidden_state = resid_in + attn_out.astype(jnp.float32)
    rms_two = rms_scale(hidden_state)
    normed_two = (hidden_state * rms_two * gain_two).astype(jnp.bfloat16)

    logits = jnp.einsum("td,ed->te", normed_two, w_route, preferred_element_type=jnp.float32)
    router_probs = jax.nn.softmax(logits[:, :num_expert], axis=-1)
    logistic_gate = jax.nn.sigmoid(logits[:, num_expert:])
    named = jnp.any(routes[:, :, None] == jnp.arange(num_expert)[None, None, :], axis=1)
    gates = jnp.concatenate([jnp.where(named, router_probs, 0.0), logistic_gate], axis=1).T
    gates = jnp.pad(gates, ((0, 16 - gates.shape[0]), (0, 0)))
    w_gu = mlp_weight[:, :2].transpose(1, 0, 2).reshape(2 * all_units, model_width)
    w_d = mlp_weight[:, 2]
    _, out_rows, d_rows_sum, d_gate_rows, gu_grad, down_grad = mlp_call(
        normed_two,
        gates,
        all_cot.reshape(num_expert, num_dp, seq_len, model_width),
        w_gu,
        w_d,
        routed_units,
    )
    out_rows = out_rows.reshape(num_expert * num_dp * seq_len, model_width)
    output = (hidden_state + scatter_all(out_rows).astype(jnp.float32)).astype(jnp.bfloat16)
    d_gate_cols = d_gate_rows[: num_expert + 1].T
    d_gate_cols = jnp.where(
        jnp.concatenate([named, jnp.ones((seq_len, 1), bool)], axis=1), d_gate_cols, 0.0
    )
    up_grad = gu_grad.reshape(2, all_units, model_width).transpose(1, 0, 2).astype(jnp.bfloat16)
    down_grad = down_grad.astype(jnp.bfloat16)
    mlp_grad = jnp.concatenate([up_grad, down_grad[:, None, :]], axis=1)
    expert_grad = lax.all_to_all(
        mlp_grad[:routed_units], "dp", split_axis=2, concat_axis=0, tiled=True
    ).astype(jnp.float32)
    shared_grad = lax.all_gather(
        mlp_grad[routed_units:], "expert", axis=0, tiled=True
    ).astype(jnp.float32)

    back_grad = cotangent.astype(jnp.float32)
    d_router_probs = d_gate_cols[:, :num_expert]
    d_logits = router_probs * (
        d_router_probs - jnp.sum(router_probs * d_router_probs, axis=-1, keepdims=True)
    )
    d_gate_logit = d_gate_cols[:, num_expert:] * logistic_gate * (1.0 - logistic_gate)
    d_route = jnp.concatenate([d_logits, d_gate_logit], axis=1).astype(jnp.bfloat16)
    route_grad = jnp.einsum("td,te->ed", normed_two, d_route, preferred_element_type=jnp.float32)
    d_normed = d_rows_sum + jnp.dot(d_route, w_route, preferred_element_type=jnp.float32)
    ffn_gain_grad, d_hidden = norm_back(hidden_state, rms_two, gain_two, d_normed)
    d_hidden = back_grad + d_hidden

    d_attn_out = lax.all_gather(d_hidden.astype(jnp.bfloat16), "expert", axis=0, tiled=True)
    out_grad = jnp.einsum(
        "td,te->de", mixed_heads, d_attn_out, preferred_element_type=jnp.float32
    ).astype(jnp.bfloat16)
    out_grad = lax.all_to_all(out_grad, "expert", split_axis=1, concat_axis=0, tiled=True)
    d_mixed = (
        jnp.einsum("te,de->td", d_attn_out, w_out, preferred_element_type=jnp.float32)
        .astype(jnp.bfloat16)
        .reshape(num_expert, seq_len, head_count, HEAD)
    )
    values_grad = jnp.einsum(
        "bhts,bthd->bshd", probs_low, d_mixed, preferred_element_type=jnp.float32
    )
    d_probs = jnp.einsum("bthd,bshd->bhts", d_mixed, value_rows, preferred_element_type=jnp.float32)
    d_scores = (
        attn_probs * (d_probs - jnp.sum(attn_probs * d_probs, axis=-1, keepdims=True))
    ).astype(jnp.bfloat16)
    d_query = unrotate(
        jnp.einsum("bhts,bshd->bthd", d_scores, key_rows, preferred_element_type=jnp.float32)
        * score_scale,
        cosine_table,
        sine_table,
    )
    d_keys = unrotate(
        jnp.einsum("bhts,bthd->bshd", d_scores, query_rows, preferred_element_type=jnp.float32)
        * score_scale,
        cosine_table,
        sine_table,
    )
    d_qkv = (
        jnp.stack([d_query, d_keys, values_grad], axis=2)
        .reshape(plane_rows, 3 * head_width)
        .astype(jnp.bfloat16)
    )
    bias_part = jnp.sum(d_qkv.astype(jnp.float32), axis=0).reshape(3, head_width)
    bias_grad = lax.dynamic_update_slice_in_dim(
        jnp.zeros((3, model_width), jnp.float32), bias_part, me_expert * head_width, 1
    )
    d_normed_one = lax.psum_scatter(
        jnp.einsum("te,de->td", d_qkv, w_qkv, preferred_element_type=jnp.float32).astype(
            jnp.bfloat16
        ),
        "expert",
        scatter_dimension=0,
        tiled=True,
    ).astype(jnp.float32)
    qkv_grad = jnp.einsum(
        "td,te->de", normed_one, d_qkv, preferred_element_type=jnp.float32
    ).astype(jnp.bfloat16)
    attn_grad = lax.psum_scatter(
        jnp.concatenate([qkv_grad, out_grad], axis=1), "dp", scatter_dimension=0, tiled=True
    )
    attn_grad = lax.all_gather(attn_grad, "expert", axis=0).astype(jnp.float32)
    qkv_weight_grad = (
        attn_grad[:, :, : 3 * head_width]
        .reshape(num_expert, shard_width, 3, head_width)
        .transpose(1, 2, 0, 3)
        .reshape(shard_width, 3 * model_width)
    )
    out_weight_grad = (
        attn_grad[:, :, 3 * head_width :].transpose(1, 0, 2).reshape(shard_width, model_width)
    )
    attn_gain_grad, d_input = norm_back(resid_in, rms_scale(resid_in), gain_one, d_normed_one)
    tokens_grad = d_hidden + d_input

    small_grad = jnp.concatenate(
        [attn_gain_grad[None], ffn_gain_grad[None], bias_grad, route_grad], axis=0
    )
    small_grad = lax.psum_scatter(small_grad, "dp", scatter_dimension=1, tiled=True)
    small_grad = lax.psum(small_grad, "expert")
    return (
        output,
        tokens_grad,
        small_grad[0],
        qkv_weight_grad,
        small_grad[2:5],
        out_weight_grad,
        small_grad[1],
        small_grad[5 : 5 + num_expert].T,
        small_grad[5 + num_expert],
        shared_grad,
        expert_grad[None, :, :2],
        expert_grad[None, :, 2],
    )


def solution(mesh):
    cube = mesh.shape["expert"] == 8 and mesh.shape["dp"] == 4
    return jax.shard_map(
        fast_shards if cube else shards,
        mesh=mesh,
        in_specs=(
            P(("dp", "expert"), None),
            P("dp"),
            P("dp", None),
            P(None, "dp"),
            P("dp", None),
            P("dp"),
            P("dp", None),
            P("dp"),
            P("dp", None, None),
            P("expert", None, None, "dp"),
            P("expert", None, "dp"),
            P(("dp", "expert"), None),
            P(("dp", "expert"), None),
            P(("dp", "expert"), None),
        ),
        out_specs=(
            P(("dp", "expert"), None),
            P(("dp", "expert"), None),
            P("dp"),
            P("dp", None),
            P(None, "dp"),
            P("dp", None),
            P("dp"),
            P("dp", None),
            P("dp"),
            P("dp", None, None),
            P("expert", None, None, "dp"),
            P("expert", None, "dp"),
        ),
        check_vma=False,
    )
```

```python
import functools
import math

import jax
import jax.numpy as jnp
from jax import lax
from jax.experimental import pallas as pl
from jax.experimental.pallas import tpu as pltpu
from jax.sharding import PartitionSpec as P

HEADS = 16
HEAD = 128


EPS = 1e-06
THETA = 1000000.0
NEGATIVE = -1e30


def rms_scale(values):
    return lax.rsqrt(jnp.mean(values * values, axis=-1, keepdims=True) + EPS)


def rope_tables(length, head_width):
    indices = jnp.arange(head_width // 2).astype(jnp.float32)
    frequency = jnp.exp(indices * (-2.0 * math.log(THETA) / head_width))
    angles = jnp.arange(length).astype(jnp.float32)[:, None] * frequency[None, :]
    return (jnp.cos(angles), jnp.sin(angles))


def rotate(values, cosine_table, sine_table):
    half_width = values.shape[-1] // 2
    lower_half = values[..., :half_width]
    upper_half = values[..., half_width:]
    cos_rows = cosine_table[:, None, :]
    sin_rows = sine_table[:, None, :]
    return jnp.concatenate(
        [
            lower_half * cos_rows - upper_half * sin_rows,
            upper_half * cos_rows + lower_half * sin_rows,
        ],
        axis=-1,
    )


def unrotate(values, cosine_table, sine_table):
    half_width = values.shape[-1] // 2
    lower_half = values[..., :half_width]
    upper_half = values[..., half_width:]
    cos_rows = cosine_table[:, None, :]
    sin_rows = sine_table[:, None, :]
    return jnp.concatenate(
        [
            lower_half * cos_rows + upper_half * sin_rows,
            upper_half * cos_rows - lower_half * sin_rows,
        ],
        axis=-1,
    )


def norm_back(values, scale_rows, gain_row, upstream):
    scaled = gain_row * upstream
    gain_grad = jnp.sum(upstream * values * scale_rows, axis=0)
    input_grad = scale_rows * scaled - values * scale_rows**3 * jnp.mean(
        scaled * values, axis=-1, keepdims=True
    )
    return (gain_grad, input_grad)


MESH = pl.DeviceIdType.MESH
NT = (((1,), (1,)), ((), ()))


def flip(index, step):
    return index + step - 2 * step * lax.rem(lax.div(index, step), 2)


def flip_pair(index, turn):
    return index + lax.rem(turn, 2) * (1 - 2 * lax.rem(index, 2)) + lax.div(turn, 2) * (
        2 - 4 * lax.rem(lax.div(index, 2), 2)
    )


def send(source, target, send_sem, recv_sem, device):
    return pltpu.make_async_remote_copy(
        src_ref=source,
        dst_ref=target,
        send_sem=send_sem,
        recv_sem=recv_sem,
        device_id=device,
        device_id_type=MESH,
    )


def greet(devices):
    barrier = pltpu.get_barrier_semaphore()
    for device in devices:
        pl.semaphore_signal(barrier, inc=1, device_id=device, device_id_type=MESH)
    pl.semaphore_wait(barrier, len(devices))

TN = (((0,), (0,)), ((), ()))


class PlaneGather:
    def __init__(self, region, send_sem, recv_sem, me_z, me_e, nbr):
        self.sems = send_sem, recv_sem
        self.region, self.me_z, self.nbr = region, me_z, nbr
        out = {1: (me_e, None, 1), 2: (me_e, None, 2), 3: (me_e, None, 4)}
        out.update({4: (nbr[2], 0, 4), 5: (nbr[4], 1, 2), 6: (nbr[2], None, 1), 7: (nbr[4], None, 1)})
        out.update({8: (nbr[6], 0, 1), 9: (nbr[6], 1, 1)})
        self.out = out
        self.into = {
            1: (nbr[1], None), 2: (nbr[2], None), 3: (nbr[4], None), 4: (nbr[6], 0), 5: (nbr[6], 1),
            6: (nbr[3], None), 7: (nbr[5], None), 8: (nbr[7], 0), 9: (nbr[7], 1),
        }

    def copy(self, channel):
        owner, half, step = self.out[channel]
        ref = self.region(owner, half)
        return send(
            ref, ref, self.sems[0].at[channel], self.sems[1].at[channel], (self.me_z, self.nbr[step])
        )

    def start(self, *channels):
        for channel in channels:
            self.copy(channel).start()

    def wait(self, *channels):
        for channel in channels:
            ref = self.region(*self.into[channel])
            send(
                ref, ref, self.sems[0].at[channel], self.sems[1].at[channel], (self.me_z, self.nbr[1])
            ).wait_recv()

    def begin(self):
        self.start(2, 3, 1)

    def relay(self):
        self.wait(2)
        self.start(4, 6)
        self.wait(3)
        self.start(5, 7)

    def relay_far(self):
        self.wait(4)
        self.start(8)
        self.wait(5)
        self.start(9)

    def finish(self):
        self.wait(1, 6, 7, 8, 9)

    def drain(self):
        for channel in range(1, 10):
            self.copy(channel).wait_send()


def add_rows(target, source, rows):
    @pl.loop(0, rows, step=32)
    def _(row):
        span = pl.ds(pl.multiple_of(row, 32), 32)
        target[span, :] = target[span, :] + source[span, :]


class PlaneScatter:
    def __init__(self, theirs, own, sib, relayed, crossed, sems, place, me_z, nbr):
        self.theirs, self.own, self.sib, self.relayed, self.crossed = theirs, own, sib, relayed, crossed
        self.sems, self.me_z, self.nbr = sems, me_z, nbr
        y, x = place
        self.own_block, self.far_block = 2 * y + x, 2 * (1 - y) + 1 - x
        self.x_block, self.y_block = 2 * y + 1 - x, 2 * (1 - y) + x
        self.rows = crossed.shape[1]

    def copy(self, channel):
        half = self.rows // 2
        low, high = pl.ds(0, half), pl.ds(half, half)
        own, x_block, y_block, far_block = self.own, self.x_block, self.y_block, self.far_block
        if channel == 0:
            source, target, step = self.theirs, self.sib, 1
        elif channel == 1:
            source, target, step = own.at[far_block, low], self.relayed.at[0], 2
        elif channel == 2:
            source, target, step = own.at[far_block, high], self.relayed.at[1], 4
        elif channel == 3:
            source, target, step = own.at[x_block, low], self.crossed.at[0, low], 2
        elif channel == 4:
            source, target, step = own.at[y_block, high], self.crossed.at[1, high], 4
        elif channel == 5:
            source, target, step = own.at[y_block, low], self.crossed.at[1, low], 4
        else:
            source, target, step = own.at[x_block, high], self.crossed.at[0, high], 2
        return send(
            source,
            target,
            self.sems[0].at[channel],
            self.sems[1].at[channel],
            (self.me_z, self.nbr[step]),
        )

    def first(self):
        self.copy(0).start()

    def second(self):
        self.copy(0).wait_recv()
        own, sib = self.own, self.sib
        add_rows(own.at[self.far_block], sib.at[self.far_block], self.rows)
        self.copy(1).start()
        self.copy(2).start()
        add_rows(own.at[self.x_block], sib.at[self.x_block], self.rows)
        self.copy(3).start()
        add_rows(own.at[self.y_block], sib.at[self.y_block], self.rows)
        self.copy(4).start()
        add_rows(own.at[self.own_block], sib.at[self.own_block], self.rows)

    def third(self):
        half = self.rows // 2
        self.copy(1).wait_recv()
        add_rows(self.own.at[self.y_block, pl.ds(0, half)], self.relayed.at[0], half)
        self.copy(2).wait_recv()
        add_rows(self.own.at[self.x_block, pl.ds(half, half)], self.relayed.at[1], half)
        self.copy(5).start()
        self.copy(6).start()

    def fourth(self, store):
        for channel in (3, 4, 5, 6):
            self.copy(channel).wait_recv()

        @pl.loop(0, self.rows, step=32)
        def _(row):
            span = pl.ds(pl.multiple_of(row, 32), 32)
            store(
                span,
                self.own[self.own_block, span, :].astype(jnp.float32)
                + self.crossed[0, span, :].astype(jnp.float32)
                + self.crossed[1, span, :].astype(jnp.float32),
            )

    def drain(self):
        for channel in range(7):
            self.copy(channel).wait_send()


class TileScatter(PlaneScatter):
    def copy(self, channel):
        if channel not in (0, 7):
            return super().copy(channel)
        part = channel // 7
        return send(
            self.theirs.at[part],
            self.sib.at[part],
            self.sems[0].at[channel],
            self.sems[1].at[channel],
            (self.me_z, self.nbr[1]),
        )

    def sum_near(self):
        self.copy(0).wait_recv()
        own, near = self.own, self.sib.at[0]
        add_rows(own.at[self.x_block], near.at[lax.rem(self.x_block, 2)], self.rows)
        self.copy(3).start()
        add_rows(own.at[self.own_block], near.at[lax.rem(self.own_block, 2)], self.rows)

    def sum_far(self):
        self.copy(7).wait_recv()
        own, other = self.own, self.sib.at[1]
        add_rows(own.at[self.far_block], other.at[lax.rem(self.far_block, 2)], self.rows)
        self.copy(1).start()
        self.copy(2).start()
        add_rows(own.at[self.y_block], other.at[lax.rem(self.y_block, 2)], self.rows)
        self.copy(4).start()

    def drain(self):
        for channel in range(1, 7):
            self.copy(channel).wait_send()


class ChainGather:
    def __init__(self, region, send_sem, recv_sem, me_z, me_e):
        self.region, self.sems, self.me_z, self.me_e = region, (send_sem, recv_sem), me_z, me_e

    def copy(self, way, hop):
        step = 1 - 2 * way
        ref = self.region(jnp.clip(self.me_z - step * hop, 0, 3))
        return send(
            ref,
            ref,
            self.sems[0].at[way, hop],
            self.sems[1].at[way, hop],
            (jnp.clip(self.me_z + step, 0, 3), self.me_e),
        )

    def sends(self, way, hop):
        z = self.me_z
        return (z < 3) & (z >= hop) if way == 0 else (z > 0) & (z <= 3 - hop)

    def takes(self, way, hop):
        z = self.me_z
        return z > hop if way == 0 else z < 3 - hop

    def begin(self):
        for way in range(2):
            pl.when(self.sends(way, 0))(self.copy(way, 0).start)

    def hop(self, hop):
        for way in range(2):
            step = 1 - 2 * way
            ref = self.region(jnp.clip(self.me_z - step * (hop + 1), 0, 3))
            arrived = send(
                ref,
                ref,
                self.sems[0].at[way, hop],
                self.sems[1].at[way, hop],
                (jnp.clip(self.me_z - step, 0, 3), self.me_e),
            )
            pl.when(self.takes(way, hop))(arrived.wait_recv)
            if hop < 2:
                pl.when(self.sends(way, hop + 1))(self.copy(way, hop + 1).start)

    def drain(self):
        for hop in range(3):
            for way in range(2):
                pl.when(self.sends(way, hop))(self.copy(way, hop).wait_send)


class ChainScatter:
    def __init__(self, part, landing, add, sems, me_z, me_e):
        self.part, self.landing, self.add = part, landing, add
        self.sems, self.me_z, self.me_e = sems, me_z, me_e

    def copy(self, way, hop, source, owner):
        slot = 4 if way == 1 and hop == 2 else owner
        return send(
            source,
            self.landing.at[slot],
            self.sems[0].at[way, hop],
            self.sems[1].at[way, hop],
            (jnp.clip(self.me_z + 1 - 2 * way, 0, 3), self.me_e),
        )

    def steps(self, hop):
        for way in range(2):
            place = self.me_z if way == 0 else 3 - self.me_z
            owner = jnp.clip(3 - hop + place if way == 0 else hop - place, 0, 3)
            yield way, place, owner

    def hop(self, hop):
        for way, place, owner in self.steps(hop):

            @pl.when(place == 0)
            def _(way=way, owner=owner):
                self.copy(way, hop, self.part(owner), owner).start()

            @pl.when((place > 0) & (place <= hop))
            def _(way=way, owner=owner):
                here = self.landing.at[owner]
                self.copy(way, hop - 1, here, owner).wait_recv()
                self.add(owner, owner)
                self.copy(way, hop, here, owner).start()

    def last(self, low, middle, high):
        up = self.copy(0, 2, self.landing.at[self.me_z], self.me_z)
        down = self.copy(1, 2, self.landing.at[4], 4)
        pl.when(self.me_z > 0)(up.wait_recv)
        pl.when(self.me_z < 3)(down.wait_recv)
        pl.when(self.me_z == 0)(low)
        pl.when((self.me_z > 0) & (self.me_z < 3))(middle)
        pl.when(self.me_z == 3)(high)

    def drain(self):
        for hop in range(3):
            for way, place, owner in self.steps(hop):
                pl.when(place <= hop)(self.copy(way, hop, self.part(owner), owner).wait_send)


def mlp_kernel(
    routed_units,
    _x_in,
    g_all,
    cot,
    w_all,
    up_weight,
    down_weight,
    shared_weight,
    x_all,
    out_part,
    dx_own,
    dg_own,
    d_routed,
    shared_all,
    expert_all,
    w_gu,
    w_d,
    acc_gu,
    acc_d,
    stage,
    x_tile,
    c_tile,
    gu_buf,
    h_buf,
    dgu_buf,
    act_buf,
    out_buf,
    theirs,
    own,
    sib_x,
    relayed,
    crossed,
    sum_x,
    far_x,
    dg_all,
    dg_in,
    dg_sum,
    dg_far,
    a_send,
    a_recv,
    z_send,
    z_recv,
    r_send,
    r_recv,
    fz_send,
    fz_recv,
    dp_send,
    dp_recv,
    dz_send,
    dz_recv,
    local_sem,
):
    me_z = lax.axis_index("dp")
    me_e = lax.axis_index("expert")
    core = lax.rem(me_e, 2)
    me_x = lax.rem(lax.div(me_e, 2), 2)
    me_y = lax.div(me_e, 4)
    nbr = {1: flip(me_e, 1), 2: flip(me_e, 2), 4: flip(me_e, 4)}
    nbr[6] = flip(nbr[2], 4)
    nbr[3], nbr[5], nbr[7] = flip(nbr[2], 1), flip(nbr[4], 1), flip(nbr[6], 1)
    units, width = w_d.shape
    rows = x_all.shape[2]
    tile = 4 * rows
    chunk = 256

    def z_of(turn):
        return flip_pair(me_z, turn)

    def gather(turn):
        where = z_of(turn)

        def region(owner, half):
            if half is None:
                return x_all.at[where, owner]
            return x_all.at[where, owner, pl.ds(half * (rows // 2), rows // 2)]

        return PlaneGather(region, a_send.at[turn], a_recv.at[turn], me_z, me_e, nbr)

    def z_copy(turn, here):
        block = (z_of(turn) if here else me_z, me_e)
        return send(
            x_all.at[block], x_all.at[block], z_send.at[turn], z_recv.at[turn], (z_of(turn), me_e)
        )

    def slot_of(turn):
        return turn - 2 * lax.div(turn, 3)

    def scatter(turn):
        par = lax.rem(turn, 2)
        return TileScatter(
            theirs,
            own.at[slot_of(turn)],
            sib_x.at[par],
            relayed.at[par],
            crossed.at[slot_of(turn)],
            (r_send.at[turn], r_recv.at[turn]),
            (me_y, me_x),
            me_z,
            nbr,
        )

    def far_send(turn):
        return send(
            sum_x.at[turn], far_x.at[turn - 1], fz_send.at[turn], fz_recv.at[turn], (z_of(turn), me_e)
        )

    def plane_sum(turn):
        sums = scatter(turn)

        def store(span, total):
            sum_x[turn, span, :] = total.astype(jnp.bfloat16)

        sums.fourth(store)
        pl.when(turn > 0)(lambda: far_send(turn).start())
        sums.drain()

    greet([(z_of(turn), me_e) for turn in (1, 2, 3)] + [(me_z, nbr[k]) for k in range(1, 8)])
    z_copy(1, False).start()
    shard_width = width // 4
    shared_units = units - routed_units

    def lanes(index):
        return pl.ds(pl.multiple_of(index * shard_width, shard_width), shard_width)

    def lines(index, amount):
        return pl.ds(pl.multiple_of(index * amount, 16), amount)

    w_loads = []
    for part in range(3):
        target, base = (w_d, 0) if part == 2 else (w_gu, part * units)
        routed = pl.ds(base, routed_units)
        own_units = lines(me_z, routed_units)
        pairs = [
            (w_all.at[part, :, lanes(z_of(turn))], target.at[routed, lanes(z_of(turn))])
            for turn in (1, 2, 3)
        ]
        pairs.append(
            (
                down_weight.at[own_units] if part == 2 else up_weight.at[part, own_units],
                target.at[routed, lanes(me_z)],
            )
        )
        pairs.append(
            (
                shared_weight.at[part, lines(me_e, shared_units)],
                target.at[pl.ds(base + routed_units, shared_units)],
            )
        )
        for source, place in pairs:
            w_loads.append(
                pltpu.make_async_copy(source, place, local_sem.at[3 + len(w_loads)])
            )
    for copy in w_loads:
        copy.start()

    @pl.loop(0, 2 * units, step=48)
    def _(row):
        acc_gu[pl.ds(pl.multiple_of(row, 16), 48), :] = jnp.zeros((48, width), jnp.float32)

    @pl.loop(0, units, step=48)
    def _(row):
        acc_d[pl.ds(pl.multiple_of(row, 16), 48), :] = jnp.zeros((48, width), jnp.float32)

    def group_of(half):
        return lax.rem(me_y + half, 2)

    def place_of(index):
        turn = lax.rem(lax.div(index + 1, 2), 4)
        ends = 1 - lax.div(index + 6, 7) + lax.div(index, 7)
        return turn, lax.rem(index + 1 + ends, 2)

    def load(index):
        turn, half = place_of(index)
        block = pl.ds(pl.multiple_of(group_of(half) * 4, 4), 4)
        return (
            pltpu.make_async_copy(x_all.at[z_of(turn), block], x_tile, local_sem.at[0]),
            pltpu.make_async_copy(cot.at[block, z_of(turn)], c_tile, local_sem.at[1]),
        )


    for copy in load(0):
        copy.start()
    for copy in w_loads:
        copy.wait()

    def step(index, carry):
        turn, half = place_of(index)
        slot = slot_of(turn)
        pair, odd = lax.div(index, 2), lax.rem(index, 2)
        where = z_of(turn)
        group = group_of(half)
        block = pl.ds(pl.multiple_of(group * 4, 4), 4)

        for copy in load(index):
            copy.wait()
        for j in range(2):
            xs = x_tile[2 * j : 2 * j + 2].reshape(2 * rows, width)
            cs = c_tile[2 * j : 2 * j + 2].reshape(2 * rows, width)
            gu_buf[:, 2 * rows * j : 2 * rows * (j + 1)] = lax.dot_general(
                w_gu[...], xs, NT, preferred_element_type=jnp.float32
            )
            h_buf[:, 2 * rows * j : 2 * rows * (j + 1)] = lax.dot_general(
                w_d[...], cs, NT, preferred_element_type=jnp.float32
            )

        def gates(row):
            return jnp.concatenate(
                [g_all[group * 4 + j, where, pl.ds(row, 1), :] for j in range(4)], axis=1
            )

        dots = []
        for low, high, gate in (
            (0, routed_units, gates(me_e)),
            (routed_units, units, gates(8)),
        ):
            piece = 16

            def units_step(k, dot, low=low, gate=gate):
                at = pl.multiple_of(low + k * piece, 16)
                g = gu_buf[pl.ds(at, piece), :]
                u = gu_buf[pl.ds(pl.multiple_of(units + at, 16), piece), :]
                h = h_buf[pl.ds(at, piece), :]
                logistic = jax.nn.sigmoid(g)
                silu = g * logistic
                act = silu * u
                act_buf[pl.ds(at, piece), :] = (act * gate).astype(jnp.bfloat16)
                d_act = h * gate
                dgu_buf[pl.ds(at, piece), :] = (
                    d_act * u * (logistic * (1.0 + g * (1.0 - logistic)))
                ).astype(jnp.bfloat16)
                dgu_buf[pl.ds(pl.multiple_of(units + at, 16), piece), :] = (d_act * silu).astype(
                    jnp.bfloat16
                )
                return dot + jnp.sum(act * h, axis=0, keepdims=True)

            dots.append(
                lax.fori_loop(
                    0, (high - low) // piece, units_step, jnp.zeros((1, tile), jnp.float32)
                )
            )
        line = lax.broadcasted_iota(jnp.int32, (8, tile), 0)
        d_gates = jnp.where(line == 0, dots[0], 0.0) + jnp.where(line == 1, dots[1], 0.0)
        for j in range(4):
            dg_all[group * 4 + j, where] = d_gates[:, j * rows : (j + 1) * rows]

        @pl.when(index == 0)
        def _():
            z_copy(1, True).wait_recv()
            gather(1).begin()
            z_copy(2, False).start()

        @pl.when((odd == 1) & (index < 7))
        def _():
            gather(pair + 1).relay_far()

        @pl.when((odd == 1) & (index < 5))
        def _():
            z_copy(pair + 2, True).wait_recv()
            gather(pair + 2).begin()
            pl.when(index == 1)(lambda: z_copy(3, False).start())

        @pl.when((odd == 1) & (index > 4))
        def _():
            plane_sum(pair - 1)

        for n in range(width // chunk):
            cols = slice(n * chunk, (n + 1) * chunk)
            acc_gu[:, cols] += jnp.dot(
                dgu_buf[...], x_tile[:, :, cols].reshape(tile, chunk), preferred_element_type=jnp.float32
            )
            acc_d[:, cols] += jnp.dot(
                act_buf[...], c_tile[:, :, cols].reshape(tile, chunk), preferred_element_type=jnp.float32
            )

        @pl.when((odd == 0) & (index < 6))
        def _():
            gather(pair + 1).relay()
            gather(pair + 1).wait(1, 6)

        @pl.when((odd == 1) & (index < 7))
        def _():
            gather(pair + 1).wait(7, 8, 9)

        @pl.when(index < 7)
        def _():
            for copy in load(index + 1):
                copy.start()

        out_store = pltpu.make_async_copy(out_buf, out_part.at[block, where], local_sem.at[2])

        @pl.when(index > 0)
        def _():
            out_store.wait()

        @pl.when((odd == 1) & (index < 7))
        def _():
            scatter(turn - 1).copy(0).wait_send()

        @pl.when((odd == 0) & (index > 2))
        def _():
            scatter(turn - 1).copy(7).wait_send()

        @pl.when(index == 7)
        def _():
            scatter(3).copy(7).wait_send()

        dgu_t = dgu_buf[...].T
        act_t = act_buf[...].T
        for n in range(width // chunk):
            cols = slice(n * chunk, (n + 1) * chunk)
            dx = jnp.dot(dgu_t, w_gu[:, cols], preferred_element_type=jnp.float32).astype(jnp.bfloat16)
            out = jnp.dot(act_t, w_d[:, cols], preferred_element_type=jnp.float32).astype(jnp.bfloat16)
            for column in range(2):
                core_0 = dx[2 * column * rows : (2 * column + 1) * rows]
                core_1 = dx[(2 * column + 1) * rows : (2 * column + 2) * rows]
                own[slot, 2 * group + column, :, cols] = jnp.where(core == 0, core_0, core_1)
                theirs[half, column, :, cols] = jnp.where(core == 0, core_1, core_0)
            for j in range(4):
                out_buf[j, :, cols] = out[j * rows : (j + 1) * rows]
        out_store.start()

        @pl.when(odd == 1)
        def _():
            pl.when(index == 1)(lambda: scatter(0).sum_near())
            pl.when(index > 2)(lambda: scatter(pair).sum_far())

        @pl.when((odd == 0) & (index > 0))
        def _():
            pl.when(index > 2)(lambda: scatter(pair - 1).third())
            scatter(pair).sum_near()

        pl.when(half == 0)(lambda: scatter(turn).copy(0).start())
        pl.when(half == 1)(lambda: scatter(turn).copy(7).start())
        return carry

    lax.fori_loop(0, 8, step, 0)

    def dp_copy(step, here):
        return send(
            dg_all.at[nbr[step]],
            dg_in.at[nbr[step] if here else me_e],
            dp_send.at[step],
            dp_recv.at[step],
            (me_z, nbr[step]),
        )

    for step_to in range(1, 8):
        dp_copy(step_to, False).start()
    dg_in[me_e] = dg_all[me_e]
    scatter(3).third()
    scatter(0).sum_far()

    depth = stage.shape[1]
    stores = []

    def write_out(part):
        for piece in range(units // depth):
            row, slot = piece * depth, len(stores) % 2
            if len(stores) > 1:
                for copy in stores[-2]:
                    copy.wait()
            if part == 2:
                stage[slot] = acc_d[row : row + depth].astype(jnp.bfloat16)
            else:
                at = part * units + row
                stage[slot] = acc_gu[at : at + depth].astype(jnp.bfloat16)
            if row < routed_units:
                pairs = [
                    (stage.at[slot], d_routed.at[part, pl.ds(row, depth)]),
                    (
                        stage.at[slot, :, lanes(me_z)],
                        expert_all.at[
                            part, pl.ds(pl.multiple_of(me_z * routed_units + row, 16), depth)
                        ],
                    ),
                ]
            else:
                at = pl.multiple_of(me_e * shared_units + row - routed_units, 16)
                pairs = [(stage.at[slot], shared_all.at[part, pl.ds(at, depth)])]
            stores.append(
                [
                    pltpu.make_async_copy(source, place, local_sem.at[2 * slot + 3 + k])
                    for k, (source, place) in enumerate(pairs)
                ]
            )
            for copy in stores[-1]:
                copy.start()

    write_out(0)
    plane_sum(3)
    scatter(0).third()
    for step_to in range(1, 8):
        dp_copy(step_to, True).wait_recv()
    total_shared = dg_in[0, :, 1:2, :]
    for source in range(1, 8):
        total_shared = total_shared + dg_in[source, :, 1:2, :]
    dg_sum[...] = jnp.concatenate(
        [dg_in[source, :, 0:1, :] for source in range(8)]
        + [total_shared, jnp.zeros((4, 7, rows), jnp.float32)],
        axis=1,
    )

    def dz_copy(turn):
        return send(
            dg_sum.at[z_of(turn)],
            dg_far.at[turn - 1],
            dz_send.at[turn],
            dz_recv.at[turn],
            (z_of(turn), me_e),
        )

    for turn in (1, 2, 3):
        dz_copy(turn).start()
    write_out(1)
    plane_sum(0)
    write_out(2)
    pltpu.make_async_copy(out_buf, out_part.at[pl.ds(0, 4), me_z], local_sem.at[2]).wait()
    for turn in (1, 2, 3):
        dz_copy(turn).wait_recv()
    dg_own[...] = dg_sum[me_z] + dg_far[0] + dg_far[1] + dg_far[2]
    for turn in (1, 2, 3):
        far_send(turn).wait_recv()

    @pl.loop(0, rows, step=32)
    def _(row):
        span = pl.ds(pl.multiple_of(row, 32), 32)
        total = sum_x[0, span, :].astype(jnp.float32)
        for turn in range(3):
            total = total + far_x[turn, span, :].astype(jnp.float32)
        dx_own[span, :] = total

    for copy in stores[-2] + stores[-1]:
        copy.wait()
    scatter(3).copy(0).wait_send()
    scatter(0).copy(7).wait_send()
    for turn in (1, 2, 3):
        z_copy(turn, False).wait_send()
        dz_copy(turn).wait_send()
        far_send(turn).wait_send()
    for step_to in range(1, 8):
        dp_copy(step_to, False).wait_send()
    for turn in (1, 2, 3):
        gather(turn).drain()


def mlp_call(x_all, gates_all, all_cot, w_all, up_weight, down_weight, shared_weight):
    num_expert, num_dp, rows, width = all_cot.shape
    routed_units = w_all.shape[1]
    units = routed_units + shared_weight.shape[1] // num_expert
    low, full = jnp.bfloat16, jnp.float32
    shape = jax.ShapeDtypeStruct
    any_space = pl.BlockSpec(memory_space=pl.ANY)
    vmem = pl.BlockSpec(memory_space=pltpu.VMEM)
    dma = pltpu.SemaphoreType.DMA
    flops = 18 * num_expert * num_dp * rows * units * width
    return pl.pallas_call(
        functools.partial(mlp_kernel, routed_units),
        out_shape=(
            shape((num_dp, num_expert, rows, width), low),
            shape((num_expert, num_dp, rows, width), low),
            shape((rows, width), full),
            shape((16, rows), full),
            shape((3, routed_units, width), low),
            shape(shared_weight.shape, low),
            shape((3, num_dp * routed_units, width // num_dp), low),
        ),
        in_specs=[any_space, vmem] + [any_space] * 5,
        input_output_aliases={0: 0},
        out_specs=(any_space, any_space, vmem, vmem, any_space, any_space, any_space),
        scratch_shapes=[
            pltpu.VMEM((2 * units, width), low),
            pltpu.VMEM((units, width), low),
            pltpu.VMEM((2 * units, width), full),
            pltpu.VMEM((units, width), full),
            pltpu.VMEM((2, units - routed_units, width), low),
            pltpu.VMEM((4, rows, width), low),
            pltpu.VMEM((4, rows, width), low),
            pltpu.VMEM((2 * units, 4 * rows), full),
            pltpu.VMEM((units, 4 * rows), full),
            pltpu.VMEM((2 * units, 4 * rows), low),
            pltpu.VMEM((units, 4 * rows), low),
            pltpu.VMEM((4, rows, width), low),
            pltpu.VMEM((2, 2, rows, width), low),
            pltpu.VMEM((3, 4, rows, width), low),
            pltpu.VMEM((2, 2, 2, rows, width), low),
            pltpu.VMEM((2, 2, rows // 2, width), low),
            pltpu.VMEM((3, 2, rows, width), low),
            pltpu.VMEM((4, rows, width), low),
            pltpu.VMEM((3, rows, width), low),
            pltpu.VMEM((num_expert, num_dp, 8, rows), full),
            pltpu.VMEM((num_expert, num_dp, 8, rows), full),
            pltpu.VMEM((num_dp, 16, rows), full),
            pltpu.VMEM((3, 16, rows), full),
            dma((4, 10)),
            dma((4, 10)),
            dma((4,)),
            dma((4,)),
            dma((4, 8)),
            dma((4, 8)),
            dma((4,)),
            dma((4,)),
            dma((8,)),
            dma((8,)),
            dma((4,)),
            dma((4,)),
            dma((18,)),
        ],
        compiler_params=pltpu.CompilerParams(
            collective_id=0, has_side_effects=True, vmem_limit_bytes=63 * 2**20
        ),
        cost_estimate=pl.CostEstimate(flops=flops, bytes_accessed=80 * 2**20, transcendentals=0),
    )(x_all, gates_all, all_cot, w_all, up_weight, down_weight, shared_weight)


def swap_halves(values):
    half = values.shape[-1] // 2
    return jnp.concatenate([values[:, half:], values[:, :half]], axis=1)


def tail_kernel(
    mixed,
    qkv,
    probs,
    normed,
    w_qkv,
    w_out,
    tables,
    tokens,
    params,
    d_rows,
    d_gates,
    named,
    router_probs,
    normed_two,
    hidden,
    cotangent,
    out_part,
    d_routed,
    _shared_in,
    _expert_in,
    output,
    tokens_grad,
    small_out,
    attn_all,
    shared_all,
    expert_all,
    rows_all,
    normed_part,
    d_mixed,
    d_qkv,
    out_grad,
    grads,
    grads_in,
    out_in,
    grads_sum,
    n_sib,
    n_relayed,
    n_crossed,
    f_own,
    f_sib,
    f_relayed,
    f_crossed,
    f_sum,
    f_far,
    d_normed,
    small,
    small_far,
    small_plane,
    e_send,
    e_recv,
    a_send,
    a_recv,
    o_send,
    o_recv,
    z_send,
    z_recv,
    y_send,
    y_recv,
    n_send,
    n_recv,
    f_send,
    f_recv,
    fz_send,
    fz_recv,
    s_send,
    s_recv,
    g_send,
    g_recv,
    h_send,
    h_recv,
    t_send,
    t_recv,
    p_send,
    p_recv,
    local_sem,
):
    me_z = lax.axis_index("dp")
    me_e = lax.axis_index("expert")
    core = lax.rem(me_e, 2)
    me_x = lax.rem(lax.div(me_e, 2), 2)
    me_y = lax.div(me_e, 4)
    nbr = {1: flip(me_e, 1), 2: flip(me_e, 2), 4: flip(me_e, 4)}
    nbr[6] = flip(nbr[2], 4)
    nbr[3], nbr[5], nbr[7] = flip(nbr[2], 1), flip(nbr[4], 1), flip(nbr[6], 1)
    far = {turn: flip_pair(me_z, turn) for turn in (1, 2, 3)}
    where = {0: me_z, **far}
    rows, width = tokens.shape
    head_width = mixed.shape[1]
    shard_width = width // 4
    routed_units = d_routed.shape[1]
    units = shared_all.shape[1] // 8
    heads = head_width // HEAD
    sequences = 8
    score_scale = HEAD ** (-0.5)

    greet([(far[turn], me_e) for turn in (1, 2, 3)] + [(me_z, nbr[k]) for k in range(1, 8)])

    def lanes(index, amount):
        return pl.ds(pl.multiple_of(index * amount, amount), amount)

    def expert_send(part, turn):
        return send(
            d_routed.at[part, :, lanes(far[turn], shard_width)],
            expert_all.at[part, pl.ds(pl.multiple_of(me_z * routed_units, 16), routed_units)],
            e_send.at[part, turn],
            e_recv.at[part, turn],
            (far[turn], me_e),
        )

    def expert_wait(part, turn):
        here = expert_all.at[part, pl.ds(pl.multiple_of(far[turn] * routed_units, 16), routed_units)]
        send(here, here, e_send.at[part, turn], e_recv.at[part, turn], (far[turn], me_e)).wait_recv()

    split = units // 32 * 16

    def shared_region(owner, half):
        base = pl.multiple_of(owner * units, 16)
        if half is None:
            return shared_all.at[:, pl.ds(base, units)]
        if half == 0:
            return shared_all.at[:, pl.ds(base, split)]
        return shared_all.at[:, pl.ds(pl.multiple_of(base + split, 16), units - split)]

    shared = PlaneGather(shared_region, s_send, s_recv, me_z, me_e, nbr)

    def rows_region(owner, half):
        if half is None:
            return rows_all.at[owner]
        return rows_all.at[owner, pl.ds(half * (rows // 2), rows // 2)]

    gather = PlaneGather(rows_region, a_send, a_recv, me_z, me_e, nbr)
    forward = {
        turn: PlaneScatter(
            out_part.at[:, 1 - core, where[turn]],
            f_own.at[turn % 2],
            f_sib.at[turn],
            f_relayed.at[turn],
            f_crossed.at[turn],
            (f_send.at[turn], f_recv.at[turn]),
            (me_y, me_x),
            me_z,
            nbr,
        )
        for turn in range(4)
    }

    def forward_load(turn):
        return pltpu.make_async_copy(
            out_part.at[:, core, where[turn]], f_own.at[turn % 2], local_sem.at[3 + turn % 2]
        )

    def far_send(turn):
        return send(
            f_sum.at[turn], f_far.at[turn - 1], fz_send.at[turn], fz_recv.at[turn], (where[turn], me_e)
        )

    def forward_last(turn):
        def store(span, total):
            f_sum[turn, span, :] = total.astype(jnp.bfloat16)

        forward[turn].fourth(store)
        if turn:
            far_send(turn).start()

    forward_load(1).start()
    forward_load(2).start()
    forward[1].first()
    forward[2].first()

    top, gate = router_probs[:8], router_probs[8:9]
    d_top = d_gates[:8] * named[...]
    d_logits = top * (d_top - jnp.sum(top * d_top, axis=0, keepdims=True))
    line = lax.broadcasted_iota(jnp.int32, (8, rows), 0)
    d_rest = jnp.where(line == 0, d_gates[8:9] * gate * (1.0 - gate), 0.0)
    d_route = jnp.concatenate([d_logits, d_rest], axis=0).astype(jnp.bfloat16)
    small[...] = jnp.dot(d_route, normed_two[...], preferred_element_type=jnp.float32)
    d_normed[...] = d_rows[...] + lax.dot_general(
        d_route, params[...], TN, preferred_element_type=jnp.float32
    )
    gains = params[...].astype(jnp.float32)

    def norm_back_rows(value, up, gain):
        scale = lax.rsqrt(jnp.mean(value * value, axis=-1, keepdims=True) + EPS)
        scaled = gain * up
        grad = scale * scaled - value * (scale * scale * scale) * jnp.mean(
            scaled * value, axis=-1, keepdims=True
        )
        return grad, jnp.sum(up * value * scale, axis=0, keepdims=True)

    def hidden_step(index, gain_sum):
        span = pl.ds(pl.multiple_of(index * 16, 16), 16)
        grad, term = norm_back_rows(hidden[span, :], d_normed[span, :], gains[10:11])
        grad = cotangent[span, :].astype(jnp.float32) + grad
        tokens_grad[span, :] = grad
        rows_all[me_e, span, :] = grad.astype(jnp.bfloat16)
        return gain_sum + term

    small[10:11, :] = lax.fori_loop(0, rows // 16, hidden_step, jnp.zeros((1, width), jnp.float32))
    gather.begin()
    for part in range(3):
        for turn in (1, 2, 3):
            expert_send(part, turn).start()
    gather.relay()
    forward_load(1).wait()
    forward[1].second()
    gather.relay_far()
    gather.finish()
    forward[1].third()
    forward[3].first()
    forward[0].first()

    all_rows = sequences * rows
    d_mixed[...] = lax.dot_general(
        rows_all[...].reshape(all_rows, width), w_out[...], NT, preferred_element_type=jnp.float32
    ).astype(jnp.bfloat16)
    for n in range(4):
        cols = slice(n * shard_width, (n + 1) * shard_width)
        out_grad[:, cols] = lax.dot_general(
            mixed[...],
            rows_all[:, :, cols].reshape(all_rows, shard_width),
            TN,
            preferred_element_type=jnp.float32,
        ).astype(jnp.bfloat16)
    span_out = pl.ds(pl.multiple_of(me_e * head_width, head_width), head_width)

    def out_send(step):
        return send(
            out_grad.at[:, lanes(nbr[step], head_width)],
            grads.at[3, span_out],
            o_send.at[step],
            o_recv.at[step],
            (me_z, nbr[step]),
        )

    for step in range(1, 8):
        out_send(step).start()
    grads[3, span_out, :] = out_grad[:, lanes(me_e, head_width)]
    forward_load(2).wait()
    forward[2].second()
    forward_last(1)

    def chain_of(first, amount, landing, sems):
        def part(owner):
            return grads.at[
                pl.ds(first, amount), pl.ds(pl.multiple_of(owner * shard_width, shard_width), shard_width)
            ]

        def add(slot, owner):
            for index in range(amount):

                @pl.loop(0, shard_width, step=64)
                def _(row, index=index):
                    span = pl.ds(pl.multiple_of(row, 64), 64)
                    theirs = pl.ds(pl.multiple_of(owner * shard_width + row, 64), 64)
                    landing[slot, index, span, :] = (
                        landing[slot, index, span, :] + grads[first + index, theirs, :]
                    )

        def total(*slots):
            for index in range(amount):

                @pl.loop(0, shard_width, step=64)
                def _(row, index=index):
                    span = pl.ds(pl.multiple_of(row, 64), 64)
                    own = pl.ds(pl.multiple_of(me_z * shard_width + row, 64), 64)
                    value = grads[first + index, own, :].astype(jnp.float32)
                    for slot in slots:
                        value = value + landing[slot, index, span, :].astype(jnp.float32)
                    grads_sum[first + index, span, :] = value.astype(jnp.bfloat16)

        chain = ChainScatter(part, landing, add, sems, me_z, me_e)
        last = (lambda: total(4), lambda: total(me_z, 4), lambda: total(me_z))
        return chain, lambda: chain.last(*last)

    chain, chain_last = chain_of(0, 3, grads_in, (z_send, z_recv))
    out_chain, out_chain_last = chain_of(3, 1, out_in, (y_send, y_recv))

    def projections_of(first, amount, sems, place):
        def region(owner, half):
            cols = lanes(owner, head_width)
            if half is None:
                return attn_all.at[pl.ds(first, amount), :, cols]
            return attn_all.at[
                pl.ds(first, amount), pl.ds(half * (shard_width // 2), shard_width // 2), cols
            ]

        own = pltpu.make_async_copy(
            grads_sum.at[pl.ds(first, amount)], region(me_e, None), local_sem.at[place]
        )
        return own, PlaneGather(region, *sems, me_z, me_e, nbr)

    qkv_own, projections = projections_of(0, 3, (g_send, g_recv), 2)
    out_own, out_projection = projections_of(3, 1, (h_send, h_recv), 7)

    def sequence(index, carry):
        span = pl.ds(pl.multiple_of(index * rows, rows), rows)
        for head in range(heads):
            cols = slice(head * HEAD, (head + 1) * HEAD)
            query, key, value = qkv[0, span, cols], qkv[1, span, cols], qkv[2, span, cols]
            up = d_mixed[span, cols]
            weights = probs[index * heads + head]
            values_grad = lax.dot_general(
                weights.astype(jnp.bfloat16), up, TN, preferred_element_type=jnp.float32
            )
            d_probs = lax.dot_general(up, value, NT, preferred_element_type=jnp.float32)
            d_scores = (
                weights * (d_probs - jnp.sum(weights * d_probs, axis=-1, keepdims=True))
            ).astype(jnp.bfloat16)
            d_query = jnp.dot(d_scores, key, preferred_element_type=jnp.float32) * score_scale
            d_key = (
                lax.dot_general(d_scores, query, TN, preferred_element_type=jnp.float32)
                * score_scale
            )
            d_query = d_query * tables[0] - swap_halves(d_query) * tables[1]
            d_key = d_key * tables[0] - swap_halves(d_key) * tables[1]
            for part, value_of in enumerate((d_query, d_key, values_grad)):
                base = part * head_width + head * HEAD
                d_qkv[span, base : base + HEAD] = value_of.astype(jnp.bfloat16)
        return carry

    def normed_load(n):
        return pltpu.make_async_copy(
            normed.at[:, n * 256 : (n + 1) * 256], normed_part.at[n % 2], local_sem.at[5 + n % 2]
        )

    normed_load(0).start()
    lax.fori_loop(0, sequences // 2, sequence, 0)
    for step in range(1, 8):
        here = grads.at[3, pl.ds(pl.multiple_of(nbr[step] * head_width, head_width), head_width)]
        send(here, here, o_send.at[step], o_recv.at[step], (me_z, nbr[step])).wait_recv()
    out_chain.hop(0)
    shared.begin()
    forward[2].third()
    lax.fori_loop(sequences // 2, sequences, sequence, 0)

    for n in range(width // 256):
        cols = slice(n * 256, (n + 1) * 256)
        if n < width // 256 - 1:
            normed_load(n + 1).start()
        normed_load(n).wait()
        term = lax.dot_general(
            normed_part[n % 2], d_qkv[...], TN, preferred_element_type=jnp.float32
        ).astype(jnp.bfloat16)
        for part in range(3):
            grads[part, cols, :] = term[:, part * head_width : (part + 1) * head_width]
    chain.hop(0)
    out_chain.hop(1)
    gather.drain()

    for n in range(width // 256):
        cols = slice(n * 256, (n + 1) * 256)
        term = lax.dot_general(
            d_qkv[...], w_qkv[cols, : 3 * head_width], NT, preferred_element_type=jnp.float32
        ).astype(jnp.bfloat16)
        for owner in range(8):
            mine = lax.rem(owner + core + 1, 2)
            rows_all[4 * mine + owner // 2, :, cols] = term[owner * rows : (owner + 1) * rows]
    back = PlaneScatter(
        rows_all.at[pl.ds(0, 4)],
        rows_all.at[pl.ds(4, 4)],
        n_sib,
        n_relayed,
        n_crossed,
        (n_send, n_recv),
        (me_y, me_x),
        me_z,
        nbr,
    )
    back.first()
    bias_terms = jnp.sum(d_qkv[...].astype(jnp.float32), axis=0, keepdims=True)
    for part in range(3):
        small[11 + part : 12 + part, lanes(me_e, head_width)] = bias_terms[
            :, part * head_width : (part + 1) * head_width
        ]
    forward_last(2)
    forward[1].drain()
    forward_load(3).start()
    back.second()
    back.third()
    out_chain.hop(2)
    shared.relay()
    chain.hop(1)
    out_chain_last()
    out_own.start()
    out_own.wait()
    out_projection.begin()
    forward_load(3).wait()
    forward[3].second()

    def keep(span, total):
        d_normed[span, :] = total

    back.fourth(keep)

    def norm_step(index, gain_sum):
        span = pl.ds(pl.multiple_of(index * 16, 16), 16)
        grad, term = norm_back_rows(
            tokens[span, :].astype(jnp.float32), d_normed[span, :], gains[9:10]
        )
        tokens_grad[span, :] = tokens_grad[span, :] + grad
        return gain_sum + term

    small[9:10, :] = lax.fori_loop(0, rows // 16, norm_step, jnp.zeros((1, width), jnp.float32))

    def small_send(turn):
        return send(
            small.at[:, lanes(far[turn], shard_width)],
            small_far.at[turn],
            t_send.at[turn],
            t_recv.at[turn],
            (far[turn], me_e),
        )

    for turn in (1, 2, 3):
        small_send(turn).start()
    forward[2].drain()
    forward_load(0).start()
    forward[3].third()
    forward_load(0).wait()
    forward[0].second()
    out_projection.relay()
    chain.hop(2)
    out_projection.relay_far()
    for turn in (1, 2, 3):
        small_send(turn).wait_recv()
    small_plane[me_e] = (
        small[:, lanes(me_z, shard_width)] + small_far[1] + small_far[2] + small_far[3]
    )

    def plane_send(step):
        return send(
            small_plane.at[me_e],
            small_plane.at[me_e],
            p_send.at[step],
            p_recv.at[step],
            (me_z, nbr[step]),
        )

    for step in range(1, 8):
        plane_send(step).start()
    forward_last(3)
    shared.relay_far()
    forward[0].third()
    for step in range(1, 8):
        here = small_plane.at[nbr[step]]
        send(here, here, p_send.at[step], p_recv.at[step], (me_z, nbr[step])).wait_recv()
    total = small_plane[0]
    for index in range(1, 8):
        total = total + small_plane[index]
    small_out[...] = total

    chain_last()
    qkv_own.start()
    qkv_own.wait()
    projections.begin()
    forward_last(0)
    projections.relay()
    for turn in (1, 2, 3):
        far_send(turn).wait_recv()

    @pl.loop(0, rows, step=32)
    def _(row):
        span = pl.ds(pl.multiple_of(row, 32), 32)
        total = f_sum[0, span, :].astype(jnp.float32)
        for turn in (1, 2, 3):
            total = total + f_far[turn - 1, span, :].astype(jnp.float32)
        output[span, :] = (hidden[span, :] + total).astype(jnp.bfloat16)

    projections.relay_far()
    shared.finish()
    projections.finish()
    out_projection.finish()
    for turn in (1, 2, 3):
        for part in range(3):
            expert_wait(part, turn)
            expert_send(part, turn).wait_send()
        small_send(turn).wait_send()
        far_send(turn).wait_send()
    for step in range(1, 8):
        out_send(step).wait_send()
        plane_send(step).wait_send()
    for turn in (3, 0):
        forward[turn].drain()
    chain.drain()
    out_chain.drain()
    out_projection.drain()
    back.drain()
    shared.drain()
    projections.drain()


def tail_call(
    mixed, qkv, probs, normed, w_qkv, w_out, tables, tokens, params, d_rows, d_gates, named, router_probs,
    normed_two, hidden, cotangent, out_part, d_routed, shared_all, expert_all,
):
    rows, width = tokens.shape
    head_width = mixed.shape[1]
    shard_width = width // 4
    low, full = jnp.bfloat16, jnp.float32
    shape = jax.ShapeDtypeStruct
    any_space = pl.BlockSpec(memory_space=pl.ANY)
    vmem = pl.BlockSpec(memory_space=pltpu.VMEM)
    dma = pltpu.SemaphoreType.DMA
    return pl.pallas_call(
        tail_kernel,
        out_shape=(
            shape((rows, width), low),
            shape((rows, width), full),
            shape((16, shard_width), full),
            shape((4, shard_width, width), low),
            shape(shared_all.shape, low),
            shape(expert_all.shape, low),
        ),
        in_specs=[vmem] * 3 + [any_space] + [vmem] * 12 + [any_space] * 4,
        input_output_aliases={18: 4, 19: 5},
        out_specs=(vmem, vmem, vmem, any_space, any_space, any_space),
        scratch_shapes=[
            pltpu.VMEM((8, rows, width), low),
            pltpu.VMEM((2, 8 * rows, 256), low),
            pltpu.VMEM((8 * rows, head_width), low),
            pltpu.VMEM((8 * rows, 3 * head_width), low),
            pltpu.VMEM((head_width, width), low),
            pltpu.VMEM((4, width, head_width), low),
            pltpu.VMEM((5, 3, shard_width, head_width), low),
            pltpu.VMEM((5, 1, shard_width, head_width), low),
            pltpu.VMEM((4, shard_width, head_width), low),
            pltpu.VMEM((4, rows, width), low),
            pltpu.VMEM((2, rows // 2, width), low),
            pltpu.VMEM((2, rows, width), low),
            pltpu.VMEM((2, 4, rows, width), low),
            pltpu.VMEM((4, 4, rows, width), low),
            pltpu.VMEM((4, 2, rows // 2, width), low),
            pltpu.VMEM((4, 2, rows, width), low),
            pltpu.VMEM((4, rows, width), low),
            pltpu.VMEM((3, rows, width), low),
            pltpu.VMEM((rows, width), full),
            pltpu.VMEM((16, width), full),
            pltpu.VMEM((4, 16, shard_width), full),
            pltpu.VMEM((8, 16, shard_width), full),
            dma((3, 4)),
            dma((3, 4)),
            dma((10,)),
            dma((10,)),
            dma((8,)),
            dma((8,)),
            dma((2, 3)),
            dma((2, 3)),
            dma((2, 3)),
            dma((2, 3)),
            dma((7,)),
            dma((7,)),
            dma((4, 7)),
            dma((4, 7)),
            dma((4,)),
            dma((4,)),
            dma((10,)),
            dma((10,)),
            dma((10,)),
            dma((10,)),
            dma((10,)),
            dma((10,)),
            dma((4,)),
            dma((4,)),
            dma((8,)),
            dma((8,)),
            dma((8,)),
        ],
        compiler_params=pltpu.CompilerParams(
            collective_id=1, has_side_effects=True, vmem_limit_bytes=63 * 2**20
        ),
        cost_estimate=pl.CostEstimate(
            flops=24 * 8 * rows * width * head_width, bytes_accessed=80 * 2**20, transcendentals=0
        ),
    )(
        mixed, qkv, probs, normed, w_qkv, w_out, tables, tokens, params, d_rows, d_gates, named, router_probs,
        normed_two, hidden, cotangent, out_part, d_routed, shared_all, expert_all,
    )


def front_kernel(
    tokens,
    docs,
    params,
    named,
    tables,
    cotangent,
    qkv_weight,
    out_weight,
    up_weight,
    down_weight,
    qkv,
    probs,
    mixed,
    normed,
    hidden,
    normed_two,
    gates_all,
    router_probs,
    params_all,
    weights_out,
    w_out_out,
    cot_all,
    w_all,
    x_all,
    rows_all,
    weights,
    w_out,
    params_in,
    docs_all,
    gates_in,
    qkv_part,
    n_sib,
    n_relayed,
    n_crossed,
    a_send,
    a_recv,
    w_send,
    w_recv,
    p_send,
    p_recv,
    d_send,
    d_recv,
    o_send,
    o_recv,
    n_send,
    n_recv,
    c_send,
    c_recv,
    k_send,
    k_recv,
    e_send,
    e_recv,
    x_send,
    x_recv,
    y_send,
    y_recv,
    g_send,
    g_recv,
    local_sem,
):
    me_z = lax.axis_index("dp")
    me_e = lax.axis_index("expert")
    core = lax.rem(me_e, 2)
    me_x = lax.rem(lax.div(me_e, 2), 2)
    me_y = lax.div(me_e, 4)
    nbr = {1: flip(me_e, 1), 2: flip(me_e, 2), 4: flip(me_e, 4)}
    nbr[6] = flip(nbr[2], 4)
    nbr[3], nbr[5], nbr[7] = flip(nbr[2], 1), flip(nbr[4], 1), flip(nbr[6], 1)
    far = {turn: flip_pair(me_z, turn) for turn in (1, 2, 3)}
    rows, width = tokens.shape
    shard_width = qkv_weight.shape[0]
    head_width = w_out.shape[0]
    heads = head_width // HEAD
    routed_units = down_weight.shape[0] // 4
    sequences = 8
    score_scale = HEAD ** (-0.5)

    def lanes(index, amount):
        return pl.ds(pl.multiple_of(index * amount, amount), amount)

    def lines(index, amount, grain=16):
        return pl.ds(pl.multiple_of(index * amount, grain), amount)

    my_lines = lines(me_z, shard_width)
    own = [
        pltpu.make_async_copy(
            qkv_weight.at[:, pl.ds(pl.multiple_of(part * width + me_e * head_width, head_width), head_width)],
            weights.at[my_lines, part * head_width : (part + 1) * head_width],
            local_sem.at[part],
        )
        for part in range(3)
    ]
    own.append(
        pltpu.make_async_copy(
            out_weight.at[:, lanes(me_e, head_width)],
            weights.at[my_lines, 3 * head_width : 4 * head_width],
            local_sem.at[3],
        )
    )
    own.append(pltpu.make_async_copy(tokens, rows_all.at[me_e], local_sem.at[4]))
    own.append(pltpu.make_async_copy(cotangent, cot_all.at[me_e, me_z], local_sem.at[5]))
    for copy in own:
        copy.start()
    params_in[me_z] = params[...]
    docs_all[me_e] = docs[...]
    greet([(far[turn], me_e) for turn in (1, 2, 3)] + [(me_z, nbr[k]) for k in range(1, 8)])
    for copy in own:
        copy.wait()

    attn_weights = ChainGather(
        lambda z: weights.at[lines(z, shard_width)], w_send, w_recv, me_z, me_e
    )
    attn_weights.begin()
    cot_chain = ChainGather(lambda z: cot_all.at[me_e, z], k_send, k_recv, me_z, me_e)
    cot_chain.begin()

    def cot_gather(place, z):
        def region(owner, half):
            if half is None:
                return cot_all.at[owner, z]
            return cot_all.at[owner, z, pl.ds(half * (rows // 2), rows // 2)]

        return PlaneGather(region, c_send.at[place], c_recv.at[place], me_z, me_e, nbr)

    cot_own = cot_gather(6, me_z)

    def cot_step(hop, name):
        for way in range(2):
            z = jnp.clip(me_z - (1 - 2 * way) * (hop + 1), 0, 3)
            pl.when(cot_chain.takes(way, hop))(getattr(cot_gather(way * 3 + hop, z), name))

    def expert_copy(part, turn, here):
        source = down_weight if part == 2 else up_weight.at[part]
        z = far[turn] if here else me_z
        target = w_all.at[part, :, lanes(z, shard_width)]
        return send(
            target if here else source.at[lines(far[turn], routed_units)],
            target,
            e_send.at[part, turn],
            e_recv.at[part, turn],
            (far[turn], me_e),
        )

    def rows_region(owner, half):
        if half is None:
            return rows_all.at[owner]
        return rows_all.at[owner, pl.ds(half * (rows // 2), rows // 2)]

    gather = PlaneGather(rows_region, a_send, a_recv, me_z, me_e, nbr)

    def params_send(turn):
        return send(
            params_in.at[me_z], params_in.at[me_z], p_send.at[turn], p_recv.at[turn], (far[turn], me_e)
        )

    def docs_send(step):
        return send(
            docs_all.at[me_e], docs_all.at[me_e], d_send.at[step], d_recv.at[step], (me_z, nbr[step])
        )

    for turn in (1, 2, 3):
        params_send(turn).start()
    gather.begin()
    for step in range(1, 8):
        docs_send(step).start()
    cot_own.begin()
    gather.relay()
    cot_chain.hop(0)
    cot_step(0, "begin")
    gather.relay_far()
    cot_own.relay()
    for turn in (1, 2, 3):
        here = params_in.at[far[turn]]
        send(here, here, p_send.at[turn], p_recv.at[turn], (far[turn], me_e)).wait_recv()
    params_all[...] = jnp.concatenate([params_in[z] for z in range(4)], axis=1)
    gather.finish()
    attn_weights.hop(0)
    cot_own.relay_far()
    cot_chain.hop(1)
    cot_step(0, "relay")
    cot_step(1, "begin")

    def norm_rows(value, gain):
        scale = lax.rsqrt(jnp.mean(value * value, axis=-1, keepdims=True) + EPS)
        return (value * scale * gain).astype(jnp.bfloat16)

    params_full = params_all[...].astype(jnp.float32)
    gain_one, gain_two = params_full[9:10], params_full[10:11]
    bias = params_all[:, lanes(me_e, head_width)].astype(jnp.float32)[11:14]

    for owner in range(8):

        @pl.loop(0, rows, step=16)
        def _(row, owner=owner):
            span = pl.ds(pl.multiple_of(row, 16), 16)
            normed[pl.ds(pl.multiple_of(owner * rows + row, 16), 16), :] = norm_rows(
                rows_all[owner, span, :].astype(jnp.float32), gain_one
            )

    cot_step(0, "relay_far")
    attn_weights.hop(1)
    for part in range(3):
        for turn in (1, 2, 3):
            expert_copy(part, turn, False).start()
    cot_chain.hop(2)

    cot_step(1, "relay")
    cot_step(2, "begin")
    attn_weights.hop(2)

    def out_send(step):
        return send(
            weights.at[lines(nbr[step], head_width), 3 * head_width : 4 * head_width],
            w_out.at[:, lanes(me_e, head_width)],
            o_send.at[step],
            o_recv.at[step],
            (me_z, nbr[step]),
        )

    for step in range(1, 8):
        out_send(step).start()
    w_out[:, lanes(me_e, head_width)] = weights[lines(me_e, head_width), 3 * head_width :]
    weights_store = pltpu.make_async_copy(weights, weights_out, local_sem.at[0])
    weights_store.start()

    for part in range(3):
        cols = slice(part * head_width, (part + 1) * head_width)
        qkv_part[...] = (
            jnp.dot(normed[...], weights[:, cols], preferred_element_type=jnp.float32)
            + bias[part : part + 1]
        )
        if part == 2:
            qkv[part] = qkv_part[...].astype(jnp.bfloat16)
        else:

            @pl.loop(0, sequences)
            def _(index, part=part):
                span = pl.ds(pl.multiple_of(index * rows, rows), rows)
                for head in range(heads):
                    at = slice(head * HEAD, (head + 1) * HEAD)
                    value = qkv_part[span, at]
                    qkv[part, span, at] = (
                        value * tables[0] + swap_halves(value) * tables[1]
                    ).astype(jnp.bfloat16)

    order = lax.broadcasted_iota(jnp.int32, (rows, rows), 0) >= lax.broadcasted_iota(
        jnp.int32, (rows, rows), 1
    )

    def sequence(index, carry):
        span = pl.ds(pl.multiple_of(index * rows, rows), rows)
        doc = jnp.broadcast_to(docs_all[index, 0:1, :], (rows, rows))
        allowed = (doc == doc.T) & order
        for head in range(heads):
            at = slice(head * HEAD, (head + 1) * HEAD)
            scores = (
                lax.dot_general(
                    qkv[0, span, at], qkv[1, span, at], NT, preferred_element_type=jnp.float32
                )
                * score_scale
            )
            scores = jnp.where(allowed, scores, NEGATIVE)
            exp_scores = jnp.exp(scores - jnp.max(scores, axis=-1, keepdims=True))
            weight = exp_scores / jnp.sum(exp_scores, axis=-1, keepdims=True)
            probs[index * heads + head] = weight
            mixed[span, at] = jnp.dot(
                weight.astype(jnp.bfloat16), qkv[2, span, at], preferred_element_type=jnp.float32
            ).astype(jnp.bfloat16)
        return carry

    cot_step(1, "relay_far")
    cot_step(2, "relay")
    for step in range(1, 8):
        here = docs_all.at[nbr[step]]
        send(here, here, d_send.at[step], d_recv.at[step], (me_z, nbr[step])).wait_recv()
    lax.fori_loop(0, sequences // 2, sequence, 0)
    cot_step(2, "relay_far")
    lax.fori_loop(sequences // 2, sequences, sequence, 0)
    gather.drain()

    for step in range(1, 8):
        here = w_out.at[:, lanes(nbr[step], head_width)]
        send(here, here, o_send.at[step], o_recv.at[step], (me_z, nbr[step])).wait_recv()
    for n in range(width // shard_width):
        cols = slice(n * shard_width, (n + 1) * shard_width)
        term = jnp.dot(mixed[...], w_out[:, cols], preferred_element_type=jnp.float32).astype(
            jnp.bfloat16
        )
        for owner in range(8):
            mine = lax.rem(owner + core + 1, 2)
            rows_all[4 * mine + owner // 2, :, cols] = term[owner * rows : (owner + 1) * rows]
    sums = PlaneScatter(
        rows_all.at[pl.ds(0, 4)],
        rows_all.at[pl.ds(4, 4)],
        n_sib,
        n_relayed,
        n_crossed,
        (n_send, n_recv),
        (me_y, me_x),
        me_z,
        nbr,
    )
    sums.first()
    out_store = pltpu.make_async_copy(w_out, w_out_out, local_sem.at[1])
    out_store.start()
    sums.second()

    sums.third()

    def keep(span, total):
        hidden[span, :] = total + tokens[span, :].astype(jnp.float32)

    sums.fourth(keep)

    @pl.loop(0, rows, step=16)
    def _(row):
        span = pl.ds(pl.multiple_of(row, 16), 16)
        normed_two[span, :] = norm_rows(hidden[span, :], gain_two)

    logits = lax.dot_general(
        params_all[...], normed_two[...], NT, preferred_element_type=jnp.float32
    )
    top = jnp.exp(logits[:8] - jnp.max(logits[:8], axis=0, keepdims=True))
    top = top / jnp.sum(top, axis=0, keepdims=True)
    line = lax.broadcasted_iota(jnp.int32, (8, rows), 0)
    rest = jnp.where(line == 0, jax.nn.sigmoid(logits[8:]), 0.0)
    router_probs[...] = jnp.concatenate([top, rest], axis=0)
    x_own = pltpu.make_async_copy(normed_two, x_all.at[me_z, me_e], local_sem.at[2])
    x_own.start()
    gates_in[me_e, me_z] = jnp.concatenate([top * named[...], rest], axis=0)

    def gates_far(turn, z):
        here = gates_in.at[me_e, z]
        return send(here, here, y_send.at[turn], y_recv.at[turn], (far[turn], me_e))

    def gates_near(step, owner):
        here = gates_in.at[owner]
        return send(here, here, g_send.at[step], g_recv.at[step], (me_z, nbr[step]))

    for turn in (1, 2, 3):
        gates_far(turn, me_z).start()

    def x_region(owner, half):
        if half is None:
            return x_all.at[me_z, owner]
        return x_all.at[me_z, owner, pl.ds(half * (rows // 2), rows // 2)]

    x_gather = PlaneGather(x_region, x_send, x_recv, me_z, me_e, nbr)
    x_own.wait()
    x_gather.begin()
    for turn in (1, 2, 3):
        gates_far(turn, far[turn]).wait_recv()
    for step in range(1, 8):
        gates_near(step, me_e).start()
    x_gather.relay()
    x_gather.relay_far()
    for step in range(1, 8):
        gates_near(step, nbr[step]).wait_recv()
    gates_all[...] = gates_in[...]
    x_gather.finish()

    cot_own.finish()
    for hop in range(3):
        cot_step(hop, "finish")
    for turn in (1, 2, 3):
        for part in range(3):
            expert_copy(part, turn, True).wait_recv()
            expert_copy(part, turn, False).wait_send()
        params_send(turn).wait_send()
        gates_far(turn, me_z).wait_send()
    for step in range(1, 8):
        docs_send(step).wait_send()
        gates_near(step, me_e).wait_send()
        out_send(step).wait_send()
    weights_store.wait()
    out_store.wait()
    attn_weights.drain()
    cot_chain.drain()
    sums.drain()
    x_gather.drain()
    cot_own.drain()
    for hop in range(3):
        cot_step(hop, "drain")


def front_call(
    tokens, docs, params, named, tables, cotangent, qkv_weight, out_weight, up_weight, down_weight
):
    rows, width = tokens.shape
    shard_width = qkv_weight.shape[0]
    head_width = width // 8
    pairs = 8 * head_width // HEAD
    routed_units = down_weight.shape[0] // 4
    low, full = jnp.bfloat16, jnp.float32
    shape = jax.ShapeDtypeStruct
    any_space = pl.BlockSpec(memory_space=pl.ANY)
    vmem = pl.BlockSpec(memory_space=pltpu.VMEM)
    dma = pltpu.SemaphoreType.DMA
    return pl.pallas_call(
        front_kernel,
        out_shape=(
            shape((3, 8 * rows, head_width), low),
            shape((pairs, rows, rows), full),
            shape((8 * rows, head_width), low),
            shape((8 * rows, width), low),
            shape((rows, width), full),
            shape((rows, width), low),
            shape((8, 4, 16, rows), full),
            shape((16, rows), full),
            shape((16, width), low),
            shape((width, 4 * head_width), low),
            shape((head_width, width), low),
            shape((8, 4, rows, width), low),
            shape((3, routed_units, width), low),
            shape((4, 8, rows, width), low),
        ),
        in_specs=[vmem] * 6 + [any_space] * 4,
        out_specs=tuple([vmem] * 9 + [any_space] * 5),
        scratch_shapes=[
            pltpu.VMEM((8, rows, width), low),
            pltpu.VMEM((width, 4 * head_width), low),
            pltpu.VMEM((head_width, width), low),
            pltpu.VMEM((4, 16, shard_width), low),
            pltpu.VMEM((8, 8, rows), full),
            pltpu.VMEM((8, 4, 16, rows), full),
            pltpu.VMEM((8 * rows, head_width), full),
            pltpu.VMEM((4, rows, width), low),
            pltpu.VMEM((2, rows // 2, width), low),
            pltpu.VMEM((2, rows, width), low),
            dma((10,)),
            dma((10,)),
            dma((2, 3)),
            dma((2, 3)),
            dma((4,)),
            dma((4,)),
            dma((8,)),
            dma((8,)),
            dma((8,)),
            dma((8,)),
            dma((7,)),
            dma((7,)),
            dma((7, 10)),
            dma((7, 10)),
            dma((2, 3)),
            dma((2, 3)),
            dma((3, 4)),
            dma((3, 4)),
            dma((10,)),
            dma((10,)),
            dma((4,)),
            dma((4,)),
            dma((8,)),
            dma((8,)),
            dma((6,)),
        ],
        compiler_params=pltpu.CompilerParams(
            collective_id=2, has_side_effects=True, vmem_limit_bytes=60 * 2**20
        ),
        cost_estimate=pl.CostEstimate(
            flops=8 * 8 * rows * width * head_width, bytes_accessed=80 * 2**20, transcendentals=0
        ),
    )(
        tokens, docs, params, named, tables, cotangent, qkv_weight, out_weight, up_weight, down_weight
    )


def widen_kernel(attn_all, shared_all, expert_all, qkv, out, shared, up, down):
    for part in range(3):
        width = attn_all.shape[2]
        qkv[:, part * width : (part + 1) * width] = attn_all[part].astype(jnp.float32)
        shared[part] = shared_all[part].astype(jnp.float32)
    out[...] = attn_all[3].astype(jnp.float32)
    for part in range(2):
        up[:, part, :] = expert_all[part].astype(jnp.float32)
    down[...] = expert_all[2].astype(jnp.float32)


def widen_call(attn_all, shared_all, expert_all):
    steps = 8
    _, depth, width = attn_all.shape
    units, routed, cols = shared_all.shape[1], expert_all.shape[1], expert_all.shape[2]
    full = jnp.float32
    shape = jax.ShapeDtypeStruct
    return pl.pallas_call(
        widen_kernel,
        grid=(steps,),
        out_shape=(
            shape((depth, 3 * width), full),
            shape((depth, width), full),
            shape(shared_all.shape, full),
            shape((routed, 2, cols), full),
            shape((routed, cols), full),
        ),
        in_specs=[
            pl.BlockSpec((4, depth // steps, width), lambda i: (0, i, 0)),
            pl.BlockSpec((3, units // steps, width), lambda i: (0, i, 0)),
            pl.BlockSpec((3, routed // steps, cols), lambda i: (0, i, 0)),
        ],
        out_specs=(
            pl.BlockSpec((depth // steps, 3 * width), lambda i: (i, 0)),
            pl.BlockSpec((depth // steps, width), lambda i: (i, 0)),
            pl.BlockSpec((3, units // steps, width), lambda i: (0, i, 0)),
            pl.BlockSpec((routed // steps, 2, cols), lambda i: (i, 0, 0)),
            pl.BlockSpec((routed // steps, cols), lambda i: (i, 0)),
        ),
        compiler_params=pltpu.CompilerParams(vmem_limit_bytes=60 * 2**20),
        cost_estimate=pl.CostEstimate(flops=0, bytes_accessed=96 * 2**20, transcendentals=0),
    )(attn_all, shared_all, expert_all)


def silu_parts(gate):
    logistic = jax.nn.sigmoid(gate)
    silu = gate * logistic
    return (silu, logistic * (1.0 + gate * (1.0 - logistic)))


def gather_all(rows):
    rows = lax.all_gather(rows, "dp", axis=0, tiled=True)
    return lax.all_gather(rows, "expert", axis=0, tiled=True)


def scatter_all(rows):
    rows = lax.psum_scatter(rows, "expert", scatter_dimension=0, tiled=True)
    return lax.psum_scatter(rows, "dp", scatter_dimension=0, tiled=True)


def shards(
    tokens,
    attn_gain,
    qkv_weight,
    qkv_bias,
    out_weight,
    ffn_gain,
    router_weight,
    shared_gate_weight,
    shared_weight,
    expert_up,
    expert_down,
    routes,
    segment_ids,
    cotangent,
):
    num_dp = lax.axis_size("dp")
    num_expert = lax.axis_size("expert")
    me_expert = lax.axis_index("expert")
    seq_len, model_width = tokens.shape
    shard_width = qkv_weight.shape[0]
    head_count = HEADS // num_expert
    head_width = head_count * HEAD
    plane_rows = seq_len * num_expert
    units = shared_weight.shape[0] // num_expert
    score_scale = HEAD ** (-0.5)

    small = jnp.concatenate(
        [
            attn_gain[None],
            ffn_gain[None],
            shared_gate_weight[None],
            qkv_bias,
            router_weight.T,
        ],
        axis=0,
    )
    small = lax.all_gather(small, "dp", axis=1, tiled=True)
    gain_one = small[0].astype(jnp.float32)
    gain_two = small[1].astype(jnp.float32)
    bias_cols = lax.dynamic_slice_in_dim(small[3:6], me_expert * head_width, head_width, 1)
    w_route = jnp.concatenate([small[6:], small[2:3]], axis=0)

    plane_tokens = lax.all_gather(tokens, "expert", axis=0, tiled=True)
    plane_docs = lax.all_gather(segment_ids, "expert", axis=0, tiled=True)
    cols_qkv = lax.dynamic_slice_in_dim(
        qkv_weight.reshape(shard_width, 3, model_width), me_expert * head_width, head_width, 2
    ).reshape(shard_width, 3 * head_width)
    cols_out = lax.dynamic_slice_in_dim(out_weight, me_expert * head_width, head_width, 1)
    attn_weights = lax.all_gather(
        jnp.concatenate([cols_qkv, cols_out], axis=1), "dp", axis=0, tiled=True
    )
    w_qkv = attn_weights[:, : 3 * head_width]
    w_out = lax.all_to_all(
        attn_weights[:, 3 * head_width :], "expert", split_axis=0, concat_axis=1, tiled=True
    )

    expert_full = jnp.concatenate([expert_up[0], expert_down[0][:, None, :]], axis=1)
    expert_units = lax.all_to_all(expert_full, "dp", split_axis=0, concat_axis=2, tiled=True)
    shared_units = lax.dynamic_slice_in_dim(shared_weight, me_expert * units, units, 0)
    mlp_weight = jnp.concatenate([expert_units, shared_units], axis=0)
    routed_units = expert_units.shape[0]
    all_units = routed_units + units

    all_cot = gather_all(cotangent)
    all_routes = gather_all(routes)

    plane_resid = plane_tokens.astype(jnp.float32)
    normed_one = (plane_resid * rms_scale(plane_resid) * gain_one).astype(jnp.bfloat16)
    qkv_rows = jnp.dot(normed_one, w_qkv, preferred_element_type=jnp.float32) + bias_cols.reshape(
        -1
    ).astype(jnp.float32)
    qkv_rows = qkv_rows.reshape(num_expert, seq_len, 3, head_count, HEAD)
    cosine_table, sine_table = rope_tables(seq_len, HEAD)
    query_rows = rotate(qkv_rows[:, :, 0], cosine_table, sine_table).astype(jnp.bfloat16)
    key_rows = rotate(qkv_rows[:, :, 1], cosine_table, sine_table).astype(jnp.bfloat16)
    value_rows = qkv_rows[:, :, 2].astype(jnp.bfloat16)
    positions = jnp.arange(seq_len)
    allowed = (
        (plane_docs[:, :, None] == plane_docs[:, None, :])
        & (positions[:, None] >= positions[None, :])[None]
    )[:, None]
    scores = (
        jnp.einsum("bthd,bshd->bhts", query_rows, key_rows, preferred_element_type=jnp.float32)
        * score_scale
    )
    scores = jnp.where(allowed, scores, NEGATIVE)
    exp_scores = jnp.exp(scores - jnp.max(scores, axis=-1, keepdims=True))
    attn_probs = exp_scores / jnp.sum(exp_scores, axis=-1, keepdims=True)
    probs_low = attn_probs.astype(jnp.bfloat16)
    mixed_heads = (
        jnp.einsum("bhts,bshd->bthd", probs_low, value_rows, preferred_element_type=jnp.float32)
        .reshape(plane_rows, head_width)
        .astype(jnp.bfloat16)
    )
    attn_part = jnp.dot(mixed_heads, w_out, preferred_element_type=jnp.float32)
    attn_out = lax.psum_scatter(
        attn_part.astype(jnp.bfloat16), "expert", scatter_dimension=0, tiled=True
    )

    resid_in = tokens.astype(jnp.float32)
    hidden_state = resid_in + attn_out.astype(jnp.float32)
    rms_two = rms_scale(hidden_state)
    normed_two = (hidden_state * rms_two * gain_two).astype(jnp.bfloat16)

    all_normed = gather_all(normed_two)
    all_logits = jnp.einsum(
        "td,ed->te", all_normed, w_route, preferred_element_type=jnp.float32
    )
    all_probs = jax.nn.softmax(all_logits[:, :num_expert], axis=-1)
    all_named = jnp.any(all_routes == me_expert, axis=1)
    my_prob = jnp.sum(
        jnp.where(jnp.arange(num_expert)[None, :] == me_expert, all_probs, 0.0), axis=1
    )
    gate_routed = jnp.where(all_named, my_prob, 0.0)
    gate_shared = jax.nn.sigmoid(all_logits[:, num_expert])
    is_routed = (jnp.arange(all_units) < routed_units)[None, :]
    row_gate = jnp.where(is_routed, gate_routed[:, None], gate_shared[:, None])

    gate_up = jnp.einsum(
        "td,fgd->gtf", all_normed, mlp_weight[:, :2], preferred_element_type=jnp.float32
    )
    silu, d_silu = silu_parts(gate_up[0])
    act = silu * gate_up[1]
    raw_act_grad = jnp.einsum(
        "td,fd->tf", all_cot, mlp_weight[:, 2], preferred_element_type=jnp.float32
    )
    gated_act = (row_gate * act).astype(jnp.bfloat16)
    act_dots = act * raw_act_grad
    d_gate_routed = jnp.where(
        all_named, jnp.sum(jnp.where(is_routed, act_dots, 0.0), axis=1), 0.0
    )
    d_gate_shared = jnp.sum(jnp.where(is_routed, 0.0, act_dots), axis=1)
    act_grad = raw_act_grad * row_gate
    d_gate_up = jnp.stack([act_grad * gate_up[1] * d_silu, act_grad * silu], axis=0).astype(
        jnp.bfloat16
    )
    d_rows = jnp.einsum(
        "gtf,fgd->td", d_gate_up, mlp_weight[:, :2], preferred_element_type=jnp.float32
    ).astype(jnp.bfloat16)
    gate_cols = jnp.concatenate(
        [
            jnp.where(
                jnp.arange(num_expert)[None, :] == me_expert, d_gate_routed[:, None], 0.0
            ),
            d_gate_shared[:, None],
        ],
        axis=1,
    )
    d_gate_cols = scatter_all(gate_cols)
    d_rows_sum = scatter_all(d_rows).astype(jnp.float32)

    up_grad = jnp.einsum(
        "gtf,td->fgd", d_gate_up, all_normed, preferred_element_type=jnp.float32
    ).astype(jnp.bfloat16)
    down_grad = jnp.einsum(
        "tf,td->fd", gated_act, all_cot, preferred_element_type=jnp.float32
    ).astype(jnp.bfloat16)
    out_rows = jnp.dot(gated_act, mlp_weight[:, 2], preferred_element_type=jnp.float32).astype(
        jnp.bfloat16
    )
    output = (hidden_state + scatter_all(out_rows).astype(jnp.float32)).astype(jnp.bfloat16)
    mlp_grad = jnp.concatenate([up_grad, down_grad[:, None, :]], axis=1)
    expert_grad = lax.all_to_all(
        mlp_grad[:routed_units], "dp", split_axis=2, concat_axis=0, tiled=True
    ).astype(jnp.float32)
    shared_grad = lax.all_gather(
        mlp_grad[routed_units:], "expert", axis=0, tiled=True
    ).astype(jnp.float32)

    back_grad = cotangent.astype(jnp.float32)
    logits = jnp.einsum("td,ed->te", normed_two, w_route, preferred_element_type=jnp.float32)
    router_probs = jax.nn.softmax(logits[:, :num_expert], axis=-1)
    logistic_gate = jax.nn.sigmoid(logits[:, num_expert:])
    d_router_probs = d_gate_cols[:, :num_expert]
    d_logits = router_probs * (
        d_router_probs - jnp.sum(router_probs * d_router_probs, axis=-1, keepdims=True)
    )
    d_gate_logit = d_gate_cols[:, num_expert:] * logistic_gate * (1.0 - logistic_gate)
    d_route = jnp.concatenate([d_logits, d_gate_logit], axis=1).astype(jnp.bfloat16)
    route_grad = jnp.einsum("td,te->ed", normed_two, d_route, preferred_element_type=jnp.float32)
    d_normed = d_rows_sum + jnp.dot(d_route, w_route, preferred_element_type=jnp.float32)
    ffn_gain_grad, d_hidden = norm_back(hidden_state, rms_two, gain_two, d_normed)
    d_hidden = back_grad + d_hidden

    d_attn_out = lax.all_gather(d_hidden.astype(jnp.bfloat16), "expert", axis=0, tiled=True)
    out_grad = jnp.einsum(
        "td,te->de", mixed_heads, d_attn_out, preferred_element_type=jnp.float32
    ).astype(jnp.bfloat16)
    out_grad = lax.all_to_all(out_grad, "expert", split_axis=1, concat_axis=0, tiled=True)
    d_mixed = (
        jnp.einsum("te,de->td", d_attn_out, w_out, preferred_element_type=jnp.float32)
        .astype(jnp.bfloat16)
        .reshape(num_expert, seq_len, head_count, HEAD)
    )
    values_grad = jnp.einsum(
        "bhts,bthd->bshd", probs_low, d_mixed, preferred_element_type=jnp.float32
    )
    d_probs = jnp.einsum("bthd,bshd->bhts", d_mixed, value_rows, preferred_element_type=jnp.float32)
    d_scores = (
        attn_probs * (d_probs - jnp.sum(attn_probs * d_probs, axis=-1, keepdims=True))
    ).astype(jnp.bfloat16)
    d_query = unrotate(
        jnp.einsum("bhts,bshd->bthd", d_scores, key_rows, preferred_element_type=jnp.float32)
        * score_scale,
        cosine_table,
        sine_table,
    )
    d_keys = unrotate(
        jnp.einsum("bhts,bthd->bshd", d_scores, query_rows, preferred_element_type=jnp.float32)
        * score_scale,
        cosine_table,
        sine_table,
    )
    d_qkv = (
        jnp.stack([d_query, d_keys, values_grad], axis=2)
        .reshape(plane_rows, 3 * head_width)
        .astype(jnp.bfloat16)
    )
    bias_part = jnp.sum(d_qkv.astype(jnp.float32), axis=0).reshape(3, head_width)
    bias_grad = lax.dynamic_update_slice_in_dim(
        jnp.zeros((3, model_width), jnp.float32), bias_part, me_expert * head_width, 1
    )
    d_normed_one = lax.psum_scatter(
        jnp.einsum("te,de->td", d_qkv, w_qkv, preferred_element_type=jnp.float32).astype(
            jnp.bfloat16
        ),
        "expert",
        scatter_dimension=0,
        tiled=True,
    ).astype(jnp.float32)
    qkv_grad = jnp.einsum(
        "td,te->de", normed_one, d_qkv, preferred_element_type=jnp.float32
    ).astype(jnp.bfloat16)
    attn_grad = lax.psum_scatter(
        jnp.concatenate([qkv_grad, out_grad], axis=1), "dp", scatter_dimension=0, tiled=True
    )
    attn_grad = lax.all_gather(attn_grad, "expert", axis=0).astype(jnp.float32)
    qkv_weight_grad = (
        attn_grad[:, :, : 3 * head_width]
        .reshape(num_expert, shard_width, 3, head_width)
        .transpose(1, 2, 0, 3)
        .reshape(shard_width, 3 * model_width)
    )
    out_weight_grad = (
        attn_grad[:, :, 3 * head_width :].transpose(1, 0, 2).reshape(shard_width, model_width)
    )
    attn_gain_grad, d_input = norm_back(resid_in, rms_scale(resid_in), gain_one, d_normed_one)
    tokens_grad = d_hidden + d_input

    small_grad = jnp.concatenate(
        [attn_gain_grad[None], ffn_gain_grad[None], bias_grad, route_grad], axis=0
    )
    small_grad = lax.psum_scatter(small_grad, "dp", scatter_dimension=1, tiled=True)
    small_grad = lax.psum(small_grad, "expert")
    return (
        output,
        tokens_grad,
        small_grad[0],
        qkv_weight_grad,
        small_grad[2:5],
        out_weight_grad,
        small_grad[1],
        small_grad[5 : 5 + num_expert].T,
        small_grad[5 + num_expert],
        shared_grad,
        expert_grad[None, :, :2],
        expert_grad[None, :, 2],
    )


def fast_shards(
    tokens,
    attn_gain,
    qkv_weight,
    qkv_bias,
    out_weight,
    ffn_gain,
    router_weight,
    shared_gate_weight,
    shared_weight,
    expert_up,
    expert_down,
    routes,
    segment_ids,
    cotangent,
):
    num_dp = lax.axis_size("dp")
    num_expert = lax.axis_size("expert")
    seq_len, model_width = tokens.shape
    up_weight = expert_up[0].transpose(1, 0, 2)
    low, full = jnp.bfloat16, jnp.float32

    params = jnp.concatenate(
        [
            router_weight.T,
            shared_gate_weight[None],
            attn_gain[None],
            ffn_gain[None],
            qkv_bias,
            jnp.zeros((16 - 6 - num_expert, attn_gain.shape[0]), low),
        ],
        axis=0,
    )
    named = jnp.any(routes[:, :, None] == jnp.arange(num_expert)[None, None, :], axis=1)
    named = named.T.astype(full)
    cosine_table, sine_table = rope_tables(seq_len, HEAD)
    tables = jnp.stack(
        [
            jnp.concatenate([cosine_table, cosine_table], axis=1),
            jnp.concatenate([-sine_table, sine_table], axis=1),
        ]
    )
    (
        qkv,
        probs,
        mixed,
        normed_one,
        hidden_state,
        normed_two,
        gates_all,
        router_probs,
        params,
        attn_weights,
        w_out,
        all_cot,
        mlp_weight,
        x_all,
    ) = front_call(
        tokens,
        jnp.broadcast_to(segment_ids.astype(full), (8, seq_len)),
        params,
        named,
        tables,
        cotangent,
        qkv_weight,
        out_weight,
        up_weight,
        expert_down[0],
    )

    _, out_part, d_rows, d_gates, d_routed, shared_grad, expert_grad = mlp_call(
        x_all,
        gates_all,
        all_cot,
        mlp_weight,
        up_weight,
        expert_down[0],
        shared_weight.transpose(1, 0, 2),
    )

    output, tokens_grad, small_grad, attn_grad, shared_grad, expert_grad = tail_call(
        mixed,
        qkv,
        probs,
        normed_one,
        attn_weights,
        w_out,
        tables,
        tokens,
        params,
        d_rows,
        d_gates,
        named,
        router_probs,
        normed_two,
        hidden_state,
        cotangent,
        out_part.reshape(num_expert // 2, 2, num_dp, seq_len, model_width),
        d_routed,
        shared_grad,
        expert_grad,
    )
    qkv_grad, out_grad, shared_grad, up_grad, down_grad = widen_call(
        attn_grad, shared_grad, expert_grad
    )
    return (
        output,
        tokens_grad,
        small_grad[num_expert + 1],
        qkv_grad,
        small_grad[num_expert + 3 : num_expert + 6],
        out_grad,
        small_grad[num_expert + 2],
        small_grad[:num_expert].T,
        small_grad[num_expert],
        shared_grad.transpose(1, 0, 2),
        up_grad[None],
        down_grad[None],
    )


def solution(mesh):
    cube = mesh.shape["expert"] == 8 and mesh.shape["dp"] == 4
    return jax.shard_map(
        fast_shards if cube else shards,
        mesh=mesh,
        in_specs=(
            P(("dp", "expert"), None),
            P("dp"),
            P("dp", None),
            P(None, "dp"),
            P("dp", None),
            P("dp"),
            P("dp", None),
            P("dp"),
            P("dp", None, None),
            P("expert", None, None, "dp"),
            P("expert", None, "dp"),
            P(("dp", "expert"), None),
            P(("dp", "expert"), None),
            P(("dp", "expert"), None),
        ),
        out_specs=(
            P(("dp", "expert"), None),
            P(("dp", "expert"), None),
            P("dp"),
            P("dp", None),
            P(None, "dp"),
            P("dp", None),
            P("dp"),
            P("dp", None),
            P("dp"),
            P("dp", None, None),
            P("expert", None, None, "dp"),
            P("expert", None, "dp"),
        ),
        check_vma=False,
    )
```

```python
import functools
import math

import jax
import jax.numpy as jnp
import numpy as np
from jax import lax
from jax.experimental import pallas as pl
from jax.experimental.pallas import tpu as pltpu
from jax.sharding import PartitionSpec as P

HEADS = 16
HEAD = 128


EPS = 1e-06
THETA = 1000000.0
NEGATIVE = -1e30


def rms_scale(values):
    return lax.rsqrt(jnp.mean(values * values, axis=-1, keepdims=True) + EPS)


def rope_tables(length, head_width):
    indices = jnp.arange(head_width // 2).astype(jnp.float32)
    frequency = jnp.exp(indices * (-2.0 * math.log(THETA) / head_width))
    angles = jnp.arange(length).astype(jnp.float32)[:, None] * frequency[None, :]
    return (jnp.cos(angles), jnp.sin(angles))


def rotate(values, cosine_table, sine_table):
    half_width = values.shape[-1] // 2
    lower_half = values[..., :half_width]
    upper_half = values[..., half_width:]
    cos_rows = cosine_table[:, None, :]
    sin_rows = sine_table[:, None, :]
    return jnp.concatenate(
        [
            lower_half * cos_rows - upper_half * sin_rows,
            upper_half * cos_rows + lower_half * sin_rows,
        ],
        axis=-1,
    )


def unrotate(values, cosine_table, sine_table):
    half_width = values.shape[-1] // 2
    lower_half = values[..., :half_width]
    upper_half = values[..., half_width:]
    cos_rows = cosine_table[:, None, :]
    sin_rows = sine_table[:, None, :]
    return jnp.concatenate(
        [
            lower_half * cos_rows + upper_half * sin_rows,
            upper_half * cos_rows - lower_half * sin_rows,
        ],
        axis=-1,
    )


def norm_back(values, scale_rows, gain_row, upstream):
    scaled = gain_row * upstream
    gain_grad = jnp.sum(upstream * values * scale_rows, axis=0)
    input_grad = scale_rows * scaled - values * scale_rows**3 * jnp.mean(
        scaled * values, axis=-1, keepdims=True
    )
    return (gain_grad, input_grad)


MESH = pl.DeviceIdType.MESH
NT = (((1,), (1,)), ((), ()))


def flip(index, step):
    return index + step - 2 * step * lax.rem(lax.div(index, step), 2)


def flip_pair(index, turn):
    return index + lax.rem(turn, 2) * (1 - 2 * lax.rem(index, 2)) + lax.div(turn, 2) * (
        2 - 4 * lax.rem(lax.div(index, 2), 2)
    )


def send(source, target, send_sem, recv_sem, device):
    return pltpu.make_async_remote_copy(
        src_ref=source,
        dst_ref=target,
        send_sem=send_sem,
        recv_sem=recv_sem,
        device_id=device,
        device_id_type=MESH,
    )


def greet(devices):
    barrier = pltpu.get_barrier_semaphore()
    for device in devices:
        pl.semaphore_signal(barrier, inc=1, device_id=device, device_id_type=MESH)
    pl.semaphore_wait(barrier, len(devices))

TN = (((0,), (0,)), ((), ()))


class PlaneGather:
    def __init__(self, region, send_sem, recv_sem, me_z, me_e, nbr):
        self.sems = send_sem, recv_sem
        self.region, self.me_z, self.nbr = region, me_z, nbr
        out = {1: (me_e, None, 1), 2: (me_e, None, 2), 3: (me_e, None, 4)}
        out.update({4: (nbr[2], 0, 4), 5: (nbr[4], 1, 2), 6: (nbr[2], None, 1), 7: (nbr[4], None, 1)})
        out.update({8: (nbr[6], 0, 1), 9: (nbr[6], 1, 1)})
        self.out = out
        self.into = {
            1: (nbr[1], None), 2: (nbr[2], None), 3: (nbr[4], None), 4: (nbr[6], 0), 5: (nbr[6], 1),
            6: (nbr[3], None), 7: (nbr[5], None), 8: (nbr[7], 0), 9: (nbr[7], 1),
        }

    def copy(self, channel):
        owner, half, step = self.out[channel]
        ref = self.region(owner, half)
        return send(
            ref, ref, self.sems[0].at[channel], self.sems[1].at[channel], (self.me_z, self.nbr[step])
        )

    def start(self, *channels):
        for channel in channels:
            self.copy(channel).start()

    def wait(self, *channels):
        for channel in channels:
            ref = self.region(*self.into[channel])
            send(
                ref, ref, self.sems[0].at[channel], self.sems[1].at[channel], (self.me_z, self.nbr[1])
            ).wait_recv()

    def begin(self):
        self.start(2, 3, 1)

    def relay(self):
        self.wait(2)
        self.start(4, 6)
        self.wait(3)
        self.start(5, 7)

    def relay_far(self):
        self.wait(4)
        self.start(8)
        self.wait(5)
        self.start(9)

    def finish(self):
        self.wait(1, 6, 7, 8, 9)

    def drain(self):
        for channel in range(1, 10):
            self.copy(channel).wait_send()


def add_rows(target, source, rows):
    @pl.loop(0, rows, step=32)
    def _(row):
        span = pl.ds(pl.multiple_of(row, 32), 32)
        target[span, :] = target[span, :] + source[span, :]


class PlaneScatter:
    def __init__(self, theirs, own, sib, relayed, crossed, sems, place, me_z, nbr):
        self.theirs, self.own, self.sib, self.relayed, self.crossed = theirs, own, sib, relayed, crossed
        self.sems, self.me_z, self.nbr = sems, me_z, nbr
        y, x = place
        self.own_block, self.far_block = 2 * y + x, 2 * (1 - y) + 1 - x
        self.x_block, self.y_block = 2 * y + 1 - x, 2 * (1 - y) + x
        self.rows = crossed.shape[1]

    def copy(self, channel):
        half = self.rows // 2
        low, high = pl.ds(0, half), pl.ds(half, half)
        own, x_block, y_block, far_block = self.own, self.x_block, self.y_block, self.far_block
        if channel == 0:
            source, target, step = self.theirs, self.sib, 1
        elif channel == 1:
            source, target, step = own.at[far_block, low], self.relayed.at[0], 2
        elif channel == 2:
            source, target, step = own.at[far_block, high], self.relayed.at[1], 4
        elif channel == 3:
            source, target, step = own.at[x_block, low], self.crossed.at[0, low], 2
        elif channel == 4:
            source, target, step = own.at[y_block, high], self.crossed.at[1, high], 4
        elif channel == 5:
            source, target, step = own.at[y_block, low], self.crossed.at[1, low], 4
        else:
            source, target, step = own.at[x_block, high], self.crossed.at[0, high], 2
        return send(
            source,
            target,
            self.sems[0].at[channel],
            self.sems[1].at[channel],
            (self.me_z, self.nbr[step]),
        )

    def first(self):
        self.copy(0).start()

    def second(self):
        self.copy(0).wait_recv()
        own, sib = self.own, self.sib
        add_rows(own.at[self.far_block], sib.at[self.far_block], self.rows)
        self.copy(1).start()
        self.copy(2).start()
        add_rows(own.at[self.x_block], sib.at[self.x_block], self.rows)
        self.copy(3).start()
        add_rows(own.at[self.y_block], sib.at[self.y_block], self.rows)
        self.copy(4).start()
        add_rows(own.at[self.own_block], sib.at[self.own_block], self.rows)

    def third(self):
        half = self.rows // 2
        self.copy(1).wait_recv()
        add_rows(self.own.at[self.y_block, pl.ds(0, half)], self.relayed.at[0], half)
        self.copy(2).wait_recv()
        add_rows(self.own.at[self.x_block, pl.ds(half, half)], self.relayed.at[1], half)
        self.copy(5).start()
        self.copy(6).start()

    def fourth(self, store):
        for channel in (3, 4, 5, 6):
            self.copy(channel).wait_recv()

        @pl.loop(0, self.rows, step=32)
        def _(row):
            span = pl.ds(pl.multiple_of(row, 32), 32)
            store(
                span,
                self.own[self.own_block, span, :].astype(jnp.float32)
                + self.crossed[0, span, :].astype(jnp.float32)
                + self.crossed[1, span, :].astype(jnp.float32),
            )

    def drain(self):
        for channel in range(7):
            self.copy(channel).wait_send()


class TileScatter(PlaneScatter):
    def copy(self, channel):
        if channel not in (0, 7):
            return super().copy(channel)
        part = channel // 7
        return send(
            self.theirs.at[part],
            self.sib.at[part],
            self.sems[0].at[channel],
            self.sems[1].at[channel],
            (self.me_z, self.nbr[1]),
        )

    def sum_near(self):
        self.copy(0).wait_recv()
        own, near = self.own, self.sib.at[0]
        add_rows(own.at[self.x_block], near.at[lax.rem(self.x_block, 2)], self.rows)
        self.copy(3).start()
        add_rows(own.at[self.own_block], near.at[lax.rem(self.own_block, 2)], self.rows)

    def sum_far(self):
        self.copy(7).wait_recv()
        own, other = self.own, self.sib.at[1]
        add_rows(own.at[self.far_block], other.at[lax.rem(self.far_block, 2)], self.rows)
        self.copy(1).start()
        self.copy(2).start()
        add_rows(own.at[self.y_block], other.at[lax.rem(self.y_block, 2)], self.rows)
        self.copy(4).start()

    def drain(self):
        for channel in range(1, 7):
            self.copy(channel).wait_send()


class ChainGather:
    def __init__(self, region, send_sem, recv_sem, me_z, me_e):
        self.region, self.sems, self.me_z, self.me_e = region, (send_sem, recv_sem), me_z, me_e

    def copy(self, way, hop):
        step = 1 - 2 * way
        ref = self.region(jnp.clip(self.me_z - step * hop, 0, 3))
        return send(
            ref,
            ref,
            self.sems[0].at[way, hop],
            self.sems[1].at[way, hop],
            (jnp.clip(self.me_z + step, 0, 3), self.me_e),
        )

    def sends(self, way, hop):
        z = self.me_z
        return (z < 3) & (z >= hop) if way == 0 else (z > 0) & (z <= 3 - hop)

    def takes(self, way, hop):
        z = self.me_z
        return z > hop if way == 0 else z < 3 - hop

    def begin(self):
        for way in range(2):
            pl.when(self.sends(way, 0))(self.copy(way, 0).start)

    def hop(self, hop):
        for way in range(2):
            step = 1 - 2 * way
            ref = self.region(jnp.clip(self.me_z - step * (hop + 1), 0, 3))
            arrived = send(
                ref,
                ref,
                self.sems[0].at[way, hop],
                self.sems[1].at[way, hop],
                (jnp.clip(self.me_z - step, 0, 3), self.me_e),
            )
            pl.when(self.takes(way, hop))(arrived.wait_recv)
            if hop < 2:
                pl.when(self.sends(way, hop + 1))(self.copy(way, hop + 1).start)

    def drain(self):
        for hop in range(3):
            for way in range(2):
                pl.when(self.sends(way, hop))(self.copy(way, hop).wait_send)


class ChainScatter:
    def __init__(self, part, landing, add, sems, me_z, me_e):
        self.part, self.landing, self.add = part, landing, add
        self.sems, self.me_z, self.me_e = sems, me_z, me_e

    def copy(self, way, hop, source, owner):
        slot = 4 if way == 1 and hop == 2 else owner
        return send(
            source,
            self.landing.at[slot],
            self.sems[0].at[way, hop],
            self.sems[1].at[way, hop],
            (jnp.clip(self.me_z + 1 - 2 * way, 0, 3), self.me_e),
        )

    def steps(self, hop):
        for way in range(2):
            place = self.me_z if way == 0 else 3 - self.me_z
            owner = jnp.clip(3 - hop + place if way == 0 else hop - place, 0, 3)
            yield way, place, owner

    def hop(self, hop):
        for way, place, owner in self.steps(hop):

            @pl.when(place == 0)
            def _(way=way, owner=owner):
                self.copy(way, hop, self.part(owner), owner).start()

            @pl.when((place > 0) & (place <= hop))
            def _(way=way, owner=owner):
                here = self.landing.at[owner]
                self.copy(way, hop - 1, here, owner).wait_recv()
                self.add(owner, owner)
                self.copy(way, hop, here, owner).start()

    def last(self, low, middle, high):
        up = self.copy(0, 2, self.landing.at[self.me_z], self.me_z)
        down = self.copy(1, 2, self.landing.at[4], 4)
        pl.when(self.me_z > 0)(up.wait_recv)
        pl.when(self.me_z < 3)(down.wait_recv)
        pl.when(self.me_z == 0)(low)
        pl.when((self.me_z > 0) & (self.me_z < 3))(middle)
        pl.when(self.me_z == 3)(high)

    def drain(self):
        for hop in range(3):
            for way, place, owner in self.steps(hop):
                pl.when(place <= hop)(self.copy(way, hop, self.part(owner), owner).wait_send)


def named_of(routes):
    expert = lax.broadcasted_iota(jnp.int32, (8, routes.shape[1]), 0)
    hits = jnp.zeros(expert.shape, jnp.float32)
    for way in range(routes.shape[0]):
        hits = hits + jnp.where(routes[way : way + 1, :] == expert, 1.0, 0.0)
    return hits


def mlp_kernel(
    routed_units,
    _x_in,
    g_all,
    cot,
    w_all,
    up_weight,
    down_weight,
    shared_weight,
    x_all,
    out_part,
    dx_own,
    dg_own,
    d_routed,
    shared_all,
    expert_all,
    w_gu,
    w_d,
    acc_gu,
    acc_d,
    stage,
    x_tile,
    c_tile,
    gu_buf,
    h_buf,
    dgu_buf,
    act_buf,
    out_buf,
    theirs,
    own,
    sib_x,
    relayed,
    crossed,
    sum_x,
    far_x,
    dg_all,
    dg_in,
    dg_sum,
    dg_far,
    a_send,
    a_recv,
    z_send,
    z_recv,
    r_send,
    r_recv,
    fz_send,
    fz_recv,
    dp_send,
    dp_recv,
    dz_send,
    dz_recv,
    local_sem,
):
    me_z = lax.axis_index("dp")
    me_e = lax.axis_index("expert")
    core = lax.rem(me_e, 2)
    me_x = lax.rem(lax.div(me_e, 2), 2)
    me_y = lax.div(me_e, 4)
    nbr = {1: flip(me_e, 1), 2: flip(me_e, 2), 4: flip(me_e, 4)}
    nbr[6] = flip(nbr[2], 4)
    nbr[3], nbr[5], nbr[7] = flip(nbr[2], 1), flip(nbr[4], 1), flip(nbr[6], 1)
    units, width = w_d.shape
    rows = x_all.shape[2]
    tile = 4 * rows
    chunk = 256

    def z_of(turn):
        return flip_pair(me_z, turn)

    def gather(turn):
        where = z_of(turn)

        def region(owner, half):
            if half is None:
                return x_all.at[where, owner]
            return x_all.at[where, owner, pl.ds(half * (rows // 2), rows // 2)]

        return PlaneGather(region, a_send.at[turn], a_recv.at[turn], me_z, me_e, nbr)

    def z_copy(turn, here):
        block = (z_of(turn) if here else me_z, me_e)
        return send(
            x_all.at[block], x_all.at[block], z_send.at[turn], z_recv.at[turn], (z_of(turn), me_e)
        )

    def slot_of(turn):
        return turn - 2 * lax.div(turn, 3)

    def scatter(turn):
        par = lax.rem(turn, 2)
        return TileScatter(
            theirs,
            own.at[slot_of(turn)],
            sib_x.at[par],
            relayed.at[par],
            crossed.at[slot_of(turn)],
            (r_send.at[turn], r_recv.at[turn]),
            (me_y, me_x),
            me_z,
            nbr,
        )

    def far_send(turn):
        return send(
            sum_x.at[turn], far_x.at[turn - 1], fz_send.at[turn], fz_recv.at[turn], (z_of(turn), me_e)
        )

    def plane_sum(turn):
        sums = scatter(turn)

        def store(span, total):
            sum_x[turn, span, :] = total.astype(jnp.bfloat16)

        sums.fourth(store)
        pl.when(turn > 0)(lambda: far_send(turn).start())
        sums.drain()

    greet([(z_of(turn), me_e) for turn in (1, 2, 3)] + [(me_z, nbr[k]) for k in range(1, 8)])
    z_copy(1, False).start()
    shard_width = width // 4
    shared_units = units - routed_units

    def lanes(index):
        return pl.ds(pl.multiple_of(index * shard_width, shard_width), shard_width)

    def lines(index, amount):
        return pl.ds(pl.multiple_of(index * amount, 16), amount)

    w_loads = []
    for part in range(3):
        target, base = (w_d, 0) if part == 2 else (w_gu, part * units)
        routed = pl.ds(base, routed_units)
        own_units = lines(me_z, routed_units)
        pairs = [
            (w_all.at[part, :, lanes(z_of(turn))], target.at[routed, lanes(z_of(turn))])
            for turn in (1, 2, 3)
        ]
        pairs.append(
            (
                down_weight.at[own_units] if part == 2 else up_weight.at[part, own_units],
                target.at[routed, lanes(me_z)],
            )
        )
        pairs.append(
            (
                shared_weight.at[part, lines(me_e, shared_units)],
                target.at[pl.ds(base + routed_units, shared_units)],
            )
        )
        for source, place in pairs:
            w_loads.append(
                pltpu.make_async_copy(source, place, local_sem.at[3 + len(w_loads)])
            )
    for copy in w_loads:
        copy.start()

    @pl.loop(0, 2 * units, step=48)
    def _(row):
        acc_gu[pl.ds(pl.multiple_of(row, 16), 48), :] = jnp.zeros((48, width), jnp.float32)

    @pl.loop(0, units, step=48)
    def _(row):
        acc_d[pl.ds(pl.multiple_of(row, 16), 48), :] = jnp.zeros((48, width), jnp.float32)

    def group_of(half):
        return lax.rem(me_y + half, 2)

    def place_of(index):
        turn = lax.rem(lax.div(index + 1, 2), 4)
        ends = 1 - lax.div(index + 6, 7) + lax.div(index, 7)
        return turn, lax.rem(index + 1 + ends, 2)

    def load(index):
        turn, half = place_of(index)
        block = pl.ds(pl.multiple_of(group_of(half) * 4, 4), 4)
        return (
            pltpu.make_async_copy(x_all.at[z_of(turn), block], x_tile, local_sem.at[0]),
            pltpu.make_async_copy(cot.at[block, z_of(turn)], c_tile, local_sem.at[1]),
        )


    for copy in load(0):
        copy.start()
    for copy in w_loads:
        copy.wait()

    def step(index, carry):
        turn, half = place_of(index)
        slot = slot_of(turn)
        pair, odd = lax.div(index, 2), lax.rem(index, 2)
        where = z_of(turn)
        group = group_of(half)
        block = pl.ds(pl.multiple_of(group * 4, 4), 4)

        for copy in load(index):
            copy.wait()
        for j in range(2):
            xs = x_tile[2 * j : 2 * j + 2].reshape(2 * rows, width)
            cs = c_tile[2 * j : 2 * j + 2].reshape(2 * rows, width)
            gu_buf[:, 2 * rows * j : 2 * rows * (j + 1)] = lax.dot_general(
                w_gu[...], xs, NT, preferred_element_type=jnp.float32
            )
            h_buf[:, 2 * rows * j : 2 * rows * (j + 1)] = lax.dot_general(
                w_d[...], cs, NT, preferred_element_type=jnp.float32
            )

        def gates(row):
            return jnp.concatenate(
                [g_all[group * 4 + j, where, pl.ds(row, 1), :] for j in range(4)], axis=1
            )

        dots = []
        for low, high, gate in (
            (0, routed_units, gates(me_e)),
            (routed_units, units, gates(8)),
        ):
            piece = 16

            def units_step(k, dot, low=low, gate=gate):
                at = pl.multiple_of(low + k * piece, 16)
                g = gu_buf[pl.ds(at, piece), :]
                u = gu_buf[pl.ds(pl.multiple_of(units + at, 16), piece), :]
                h = h_buf[pl.ds(at, piece), :]
                logistic = jax.nn.sigmoid(g)
                silu = g * logistic
                act = silu * u
                act_buf[pl.ds(at, piece), :] = (act * gate).astype(jnp.bfloat16)
                d_act = h * gate
                dgu_buf[pl.ds(at, piece), :] = (
                    d_act * u * (logistic * (1.0 + g * (1.0 - logistic)))
                ).astype(jnp.bfloat16)
                dgu_buf[pl.ds(pl.multiple_of(units + at, 16), piece), :] = (d_act * silu).astype(
                    jnp.bfloat16
                )
                return dot + jnp.sum(act * h, axis=0, keepdims=True)

            dots.append(
                lax.fori_loop(
                    0, (high - low) // piece, units_step, jnp.zeros((1, tile), jnp.float32)
                )
            )
        line = lax.broadcasted_iota(jnp.int32, (8, tile), 0)
        d_gates = jnp.where(line == 0, dots[0], 0.0) + jnp.where(line == 1, dots[1], 0.0)
        for j in range(4):
            dg_all[group * 4 + j, where] = d_gates[:, j * rows : (j + 1) * rows]

        @pl.when(index == 0)
        def _():
            z_copy(1, True).wait_recv()
            gather(1).begin()
            z_copy(2, False).start()

        @pl.when((odd == 1) & (index < 7))
        def _():
            gather(pair + 1).relay_far()

        @pl.when((odd == 1) & (index < 5))
        def _():
            z_copy(pair + 2, True).wait_recv()
            gather(pair + 2).begin()
            pl.when(index == 1)(lambda: z_copy(3, False).start())

        @pl.when((odd == 1) & (index > 4))
        def _():
            plane_sum(pair - 1)

        for n in range(width // chunk):
            cols = slice(n * chunk, (n + 1) * chunk)
            acc_gu[:, cols] += jnp.dot(
                dgu_buf[...], x_tile[:, :, cols].reshape(tile, chunk), preferred_element_type=jnp.float32
            )
            acc_d[:, cols] += jnp.dot(
                act_buf[...], c_tile[:, :, cols].reshape(tile, chunk), preferred_element_type=jnp.float32
            )

        @pl.when((odd == 0) & (index < 6))
        def _():
            gather(pair + 1).relay()
            gather(pair + 1).wait(1, 6)

        @pl.when((odd == 1) & (index < 7))
        def _():
            gather(pair + 1).wait(7, 8, 9)

        @pl.when(index < 7)
        def _():
            for copy in load(index + 1):
                copy.start()

        out_store = pltpu.make_async_copy(out_buf, out_part.at[block, where], local_sem.at[2])

        @pl.when(index > 0)
        def _():
            out_store.wait()

        @pl.when((odd == 1) & (index < 7))
        def _():
            scatter(turn - 1).copy(0).wait_send()

        @pl.when((odd == 0) & (index > 2))
        def _():
            scatter(turn - 1).copy(7).wait_send()

        @pl.when(index == 7)
        def _():
            scatter(3).copy(7).wait_send()

        dgu_t = dgu_buf[...].T
        act_t = act_buf[...].T
        for n in range(width // chunk):
            cols = slice(n * chunk, (n + 1) * chunk)
            dx = jnp.dot(dgu_t, w_gu[:, cols], preferred_element_type=jnp.float32).astype(jnp.bfloat16)
            out = jnp.dot(act_t, w_d[:, cols], preferred_element_type=jnp.float32).astype(jnp.bfloat16)
            for column in range(2):
                core_0 = dx[2 * column * rows : (2 * column + 1) * rows]
                core_1 = dx[(2 * column + 1) * rows : (2 * column + 2) * rows]
                own[slot, 2 * group + column, :, cols] = jnp.where(core == 0, core_0, core_1)
                theirs[half, column, :, cols] = jnp.where(core == 0, core_1, core_0)
            for j in range(4):
                out_buf[j, :, cols] = out[j * rows : (j + 1) * rows]
        out_store.start()

        @pl.when(odd == 1)
        def _():
            pl.when(index == 1)(lambda: scatter(0).sum_near())
            pl.when(index > 2)(lambda: scatter(pair).sum_far())

        @pl.when((odd == 0) & (index > 0))
        def _():
            pl.when(index > 2)(lambda: scatter(pair - 1).third())
            scatter(pair).sum_near()

        pl.when(half == 0)(lambda: scatter(turn).copy(0).start())
        pl.when(half == 1)(lambda: scatter(turn).copy(7).start())
        return carry

    lax.fori_loop(0, 8, step, 0)

    def dp_copy(step, here):
        return send(
            dg_all.at[nbr[step]],
            dg_in.at[nbr[step] if here else me_e],
            dp_send.at[step],
            dp_recv.at[step],
            (me_z, nbr[step]),
        )

    for step_to in range(1, 8):
        dp_copy(step_to, False).start()
    dg_in[me_e] = dg_all[me_e]
    scatter(3).third()
    scatter(0).sum_far()

    depth = stage.shape[1]
    stores = []

    def write_out(part):
        for piece in range(units // depth):
            row, slot = piece * depth, len(stores) % 2
            if len(stores) > 1:
                for copy in stores[-2]:
                    copy.wait()
            if part == 2:
                stage[slot] = acc_d[row : row + depth].astype(jnp.bfloat16)
            else:
                at = part * units + row
                stage[slot] = acc_gu[at : at + depth].astype(jnp.bfloat16)
            if row < routed_units:
                pairs = [
                    (stage.at[slot], d_routed.at[part, pl.ds(row, depth)]),
                    (
                        stage.at[slot, :, lanes(me_z)],
                        expert_all.at[
                            part, pl.ds(pl.multiple_of(me_z * routed_units + row, 16), depth)
                        ],
                    ),
                ]
            else:
                at = pl.multiple_of(me_e * shared_units + row - routed_units, 16)
                pairs = [(stage.at[slot], shared_all.at[part, pl.ds(at, depth)])]
            stores.append(
                [
                    pltpu.make_async_copy(source, place, local_sem.at[2 * slot + 3 + k])
                    for k, (source, place) in enumerate(pairs)
                ]
            )
            for copy in stores[-1]:
                copy.start()

    write_out(0)
    plane_sum(3)
    scatter(0).third()
    for step_to in range(1, 8):
        dp_copy(step_to, True).wait_recv()
    total_shared = dg_in[0, :, 1:2, :]
    for source in range(1, 8):
        total_shared = total_shared + dg_in[source, :, 1:2, :]
    dg_sum[...] = jnp.concatenate(
        [dg_in[source, :, 0:1, :] for source in range(8)]
        + [total_shared, jnp.zeros((4, 7, rows), jnp.float32)],
        axis=1,
    )

    def dz_copy(turn):
        return send(
            dg_sum.at[z_of(turn)],
            dg_far.at[turn - 1],
            dz_send.at[turn],
            dz_recv.at[turn],
            (z_of(turn), me_e),
        )

    for turn in (1, 2, 3):
        dz_copy(turn).start()
    write_out(1)
    plane_sum(0)
    write_out(2)
    pltpu.make_async_copy(out_buf, out_part.at[pl.ds(0, 4), me_z], local_sem.at[2]).wait()
    for turn in (1, 2, 3):
        dz_copy(turn).wait_recv()
    dg_own[...] = dg_sum[me_z] + dg_far[0] + dg_far[1] + dg_far[2]
    for turn in (1, 2, 3):
        far_send(turn).wait_recv()

    @pl.loop(0, rows, step=32)
    def _(row):
        span = pl.ds(pl.multiple_of(row, 32), 32)
        total = sum_x[0, span, :].astype(jnp.float32)
        for turn in range(3):
            total = total + far_x[turn, span, :].astype(jnp.float32)
        dx_own[span, :] = total

    for copy in stores[-2] + stores[-1]:
        copy.wait()
    scatter(3).copy(0).wait_send()
    scatter(0).copy(7).wait_send()
    for turn in (1, 2, 3):
        z_copy(turn, False).wait_send()
        dz_copy(turn).wait_send()
        far_send(turn).wait_send()
    for step_to in range(1, 8):
        dp_copy(step_to, False).wait_send()
    for turn in (1, 2, 3):
        gather(turn).drain()


def mlp_call(x_all, gates_all, all_cot, w_all, up_weight, down_weight, shared_weight):
    num_expert, num_dp, rows, width = all_cot.shape
    routed_units = w_all.shape[1]
    units = routed_units + shared_weight.shape[1] // num_expert
    low, full = jnp.bfloat16, jnp.float32
    shape = jax.ShapeDtypeStruct
    any_space = pl.BlockSpec(memory_space=pl.ANY)
    vmem = pl.BlockSpec(memory_space=pltpu.VMEM)
    dma = pltpu.SemaphoreType.DMA
    flops = 18 * num_expert * num_dp * rows * units * width
    return pl.pallas_call(
        functools.partial(mlp_kernel, routed_units),
        out_shape=(
            shape((num_dp, num_expert, rows, width), low),
            shape((num_expert, num_dp, rows, width), low),
            shape((rows, width), full),
            shape((16, rows), full),
            shape((3, routed_units, width), low),
            shape(shared_weight.shape, low),
            shape((3, num_dp * routed_units, width // num_dp), low),
        ),
        in_specs=[any_space, vmem] + [any_space] * 5,
        input_output_aliases={0: 0},
        out_specs=(any_space, any_space, vmem, vmem, any_space, any_space, any_space),
        scratch_shapes=[
            pltpu.VMEM((2 * units, width), low),
            pltpu.VMEM((units, width), low),
            pltpu.VMEM((2 * units, width), full),
            pltpu.VMEM((units, width), full),
            pltpu.VMEM((2, units - routed_units, width), low),
            pltpu.VMEM((4, rows, width), low),
            pltpu.VMEM((4, rows, width), low),
            pltpu.VMEM((2 * units, 4 * rows), full),
            pltpu.VMEM((units, 4 * rows), full),
            pltpu.VMEM((2 * units, 4 * rows), low),
            pltpu.VMEM((units, 4 * rows), low),
            pltpu.VMEM((4, rows, width), low),
            pltpu.VMEM((2, 2, rows, width), low),
            pltpu.VMEM((3, 4, rows, width), low),
            pltpu.VMEM((2, 2, 2, rows, width), low),
            pltpu.VMEM((2, 2, rows // 2, width), low),
            pltpu.VMEM((3, 2, rows, width), low),
            pltpu.VMEM((4, rows, width), low),
            pltpu.VMEM((3, rows, width), low),
            pltpu.VMEM((num_expert, num_dp, 8, rows), full),
            pltpu.VMEM((num_expert, num_dp, 8, rows), full),
            pltpu.VMEM((num_dp, 16, rows), full),
            pltpu.VMEM((3, 16, rows), full),
            dma((4, 10)),
            dma((4, 10)),
            dma((4,)),
            dma((4,)),
            dma((4, 8)),
            dma((4, 8)),
            dma((4,)),
            dma((4,)),
            dma((8,)),
            dma((8,)),
            dma((4,)),
            dma((4,)),
            dma((18,)),
        ],
        compiler_params=pltpu.CompilerParams(
            collective_id=0, has_side_effects=True, vmem_limit_bytes=63 * 2**20
        ),
        cost_estimate=pl.CostEstimate(flops=flops, bytes_accessed=80 * 2**20, transcendentals=0),
    )(x_all, gates_all, all_cot, w_all, up_weight, down_weight, shared_weight)


def swap_halves(values):
    half = values.shape[-1] // 2
    return jnp.concatenate([values[:, half:], values[:, :half]], axis=1)


def tail_kernel(
    mixed,
    qkv,
    probs,
    normed,
    w_qkv,
    w_out,
    tables,
    tokens,
    params,
    d_rows,
    d_gates,
    routes,
    router_probs,
    normed_two,
    hidden,
    cotangent,
    out_part,
    d_routed,
    _shared_in,
    _expert_in,
    output,
    tokens_grad,
    small_out,
    attn_all,
    shared_all,
    expert_all,
    rows_all,
    normed_part,
    d_mixed,
    d_qkv,
    out_grad,
    grads,
    grads_in,
    out_in,
    grads_sum,
    n_sib,
    n_relayed,
    n_crossed,
    f_own,
    f_sib,
    f_relayed,
    f_crossed,
    f_sum,
    f_far,
    d_normed,
    small,
    small_far,
    small_plane,
    e_send,
    e_recv,
    a_send,
    a_recv,
    o_send,
    o_recv,
    z_send,
    z_recv,
    y_send,
    y_recv,
    n_send,
    n_recv,
    f_send,
    f_recv,
    fz_send,
    fz_recv,
    s_send,
    s_recv,
    g_send,
    g_recv,
    h_send,
    h_recv,
    t_send,
    t_recv,
    p_send,
    p_recv,
    local_sem,
):
    me_z = lax.axis_index("dp")
    me_e = lax.axis_index("expert")
    core = lax.rem(me_e, 2)
    me_x = lax.rem(lax.div(me_e, 2), 2)
    me_y = lax.div(me_e, 4)
    nbr = {1: flip(me_e, 1), 2: flip(me_e, 2), 4: flip(me_e, 4)}
    nbr[6] = flip(nbr[2], 4)
    nbr[3], nbr[5], nbr[7] = flip(nbr[2], 1), flip(nbr[4], 1), flip(nbr[6], 1)
    far = {turn: flip_pair(me_z, turn) for turn in (1, 2, 3)}
    where = {0: me_z, **far}
    rows, width = tokens.shape
    head_width = mixed.shape[1]
    shard_width = width // 4
    routed_units = d_routed.shape[1]
    units = shared_all.shape[1] // 8
    heads = head_width // HEAD
    sequences = 8
    score_scale = HEAD ** (-0.5)

    greet([(far[turn], me_e) for turn in (1, 2, 3)] + [(me_z, nbr[k]) for k in range(1, 8)])

    def lanes(index, amount):
        return pl.ds(pl.multiple_of(index * amount, amount), amount)

    def expert_send(part, turn):
        return send(
            d_routed.at[part, :, lanes(far[turn], shard_width)],
            expert_all.at[part, pl.ds(pl.multiple_of(me_z * routed_units, 16), routed_units)],
            e_send.at[part, turn],
            e_recv.at[part, turn],
            (far[turn], me_e),
        )

    def expert_wait(part, turn):
        here = expert_all.at[part, pl.ds(pl.multiple_of(far[turn] * routed_units, 16), routed_units)]
        send(here, here, e_send.at[part, turn], e_recv.at[part, turn], (far[turn], me_e)).wait_recv()

    split = units // 32 * 16

    def shared_region(owner, half):
        base = pl.multiple_of(owner * units, 16)
        if half is None:
            return shared_all.at[:, pl.ds(base, units)]
        if half == 0:
            return shared_all.at[:, pl.ds(base, split)]
        return shared_all.at[:, pl.ds(pl.multiple_of(base + split, 16), units - split)]

    shared = PlaneGather(shared_region, s_send, s_recv, me_z, me_e, nbr)

    def rows_region(owner, half):
        if half is None:
            return rows_all.at[owner]
        return rows_all.at[owner, pl.ds(half * (rows // 2), rows // 2)]

    gather = PlaneGather(rows_region, a_send, a_recv, me_z, me_e, nbr)
    forward = {
        turn: PlaneScatter(
            out_part.at[:, 1 - core, where[turn]],
            f_own.at[turn % 2],
            f_sib.at[turn],
            f_relayed.at[turn],
            f_crossed.at[turn],
            (f_send.at[turn], f_recv.at[turn]),
            (me_y, me_x),
            me_z,
            nbr,
        )
        for turn in range(4)
    }

    def forward_load(turn):
        return pltpu.make_async_copy(
            out_part.at[:, core, where[turn]], f_own.at[turn % 2], local_sem.at[3 + turn % 2]
        )

    def far_send(turn):
        return send(
            f_sum.at[turn], f_far.at[turn - 1], fz_send.at[turn], fz_recv.at[turn], (where[turn], me_e)
        )

    def forward_last(turn):
        def store(span, total):
            f_sum[turn, span, :] = total.astype(jnp.bfloat16)

        forward[turn].fourth(store)
        if turn:
            far_send(turn).start()

    forward_load(1).start()
    forward_load(2).start()
    forward[1].first()
    forward[2].first()

    top, gate = router_probs[:8], router_probs[8:9]
    d_top = d_gates[:8] * named_of(routes)
    d_logits = top * (d_top - jnp.sum(top * d_top, axis=0, keepdims=True))
    line = lax.broadcasted_iota(jnp.int32, (8, rows), 0)
    d_rest = jnp.where(line == 0, d_gates[8:9] * gate * (1.0 - gate), 0.0)
    d_route = jnp.concatenate([d_logits, d_rest], axis=0).astype(jnp.bfloat16)
    small[...] = jnp.dot(d_route, normed_two[...], preferred_element_type=jnp.float32)
    d_normed[...] = d_rows[...] + lax.dot_general(
        d_route, params[...], TN, preferred_element_type=jnp.float32
    )
    gains = params[...].astype(jnp.float32)

    def norm_back_rows(value, up, gain):
        scale = lax.rsqrt(jnp.mean(value * value, axis=-1, keepdims=True) + EPS)
        scaled = gain * up
        grad = scale * scaled - value * (scale * scale * scale) * jnp.mean(
            scaled * value, axis=-1, keepdims=True
        )
        return grad, jnp.sum(up * value * scale, axis=0, keepdims=True)

    def hidden_step(index, gain_sum):
        span = pl.ds(pl.multiple_of(index * 16, 16), 16)
        grad, term = norm_back_rows(hidden[span, :], d_normed[span, :], gains[10:11])
        grad = cotangent[span, :].astype(jnp.float32) + grad
        tokens_grad[span, :] = grad
        rows_all[me_e, span, :] = grad.astype(jnp.bfloat16)
        return gain_sum + term

    small[10:11, :] = lax.fori_loop(0, rows // 16, hidden_step, jnp.zeros((1, width), jnp.float32))
    gather.begin()
    for part in range(3):
        for turn in (1, 2, 3):
            expert_send(part, turn).start()
    gather.relay()
    forward_load(1).wait()
    forward[1].second()
    gather.relay_far()
    gather.finish()
    forward[1].third()
    forward[3].first()
    forward[0].first()

    all_rows = sequences * rows
    d_mixed[...] = lax.dot_general(
        rows_all[...].reshape(all_rows, width), w_out[...], NT, preferred_element_type=jnp.float32
    ).astype(jnp.bfloat16)
    for n in range(4):
        cols = slice(n * shard_width, (n + 1) * shard_width)
        out_grad[:, cols] = lax.dot_general(
            mixed[...],
            rows_all[:, :, cols].reshape(all_rows, shard_width),
            TN,
            preferred_element_type=jnp.float32,
        ).astype(jnp.bfloat16)
    span_out = pl.ds(pl.multiple_of(me_e * head_width, head_width), head_width)

    def out_send(step):
        return send(
            out_grad.at[:, lanes(nbr[step], head_width)],
            grads.at[3, span_out],
            o_send.at[step],
            o_recv.at[step],
            (me_z, nbr[step]),
        )

    for step in range(1, 8):
        out_send(step).start()
    grads[3, span_out, :] = out_grad[:, lanes(me_e, head_width)]
    forward_load(2).wait()
    forward[2].second()
    forward_last(1)

    def chain_of(first, amount, landing, sems):
        def part(owner):
            return grads.at[
                pl.ds(first, amount), pl.ds(pl.multiple_of(owner * shard_width, shard_width), shard_width)
            ]

        def add(slot, owner):
            for index in range(amount):

                @pl.loop(0, shard_width, step=64)
                def _(row, index=index):
                    span = pl.ds(pl.multiple_of(row, 64), 64)
                    theirs = pl.ds(pl.multiple_of(owner * shard_width + row, 64), 64)
                    landing[slot, index, span, :] = (
                        landing[slot, index, span, :] + grads[first + index, theirs, :]
                    )

        def total(*slots):
            for index in range(amount):

                @pl.loop(0, shard_width, step=64)
                def _(row, index=index):
                    span = pl.ds(pl.multiple_of(row, 64), 64)
                    own = pl.ds(pl.multiple_of(me_z * shard_width + row, 64), 64)
                    value = grads[first + index, own, :].astype(jnp.float32)
                    for slot in slots:
                        value = value + landing[slot, index, span, :].astype(jnp.float32)
                    grads_sum[first + index, span, :] = value.astype(jnp.bfloat16)

        chain = ChainScatter(part, landing, add, sems, me_z, me_e)
        last = (lambda: total(4), lambda: total(me_z, 4), lambda: total(me_z))
        return chain, lambda: chain.last(*last)

    chain, chain_last = chain_of(0, 3, grads_in, (z_send, z_recv))
    out_chain, out_chain_last = chain_of(3, 1, out_in, (y_send, y_recv))

    def projections_of(first, amount, sems, place):
        def region(owner, half):
            cols = lanes(owner, head_width)
            if half is None:
                return attn_all.at[pl.ds(first, amount), :, cols]
            return attn_all.at[
                pl.ds(first, amount), pl.ds(half * (shard_width // 2), shard_width // 2), cols
            ]

        own = pltpu.make_async_copy(
            grads_sum.at[pl.ds(first, amount)], region(me_e, None), local_sem.at[place]
        )
        return own, PlaneGather(region, *sems, me_z, me_e, nbr)

    qkv_own, projections = projections_of(0, 3, (g_send, g_recv), 2)
    out_own, out_projection = projections_of(3, 1, (h_send, h_recv), 7)

    def sequence(index, carry):
        span = pl.ds(pl.multiple_of(index * rows, rows), rows)
        for head in range(heads):
            cols = slice(head * HEAD, (head + 1) * HEAD)
            query, key, value = qkv[0, span, cols], qkv[1, span, cols], qkv[2, span, cols]
            up = d_mixed[span, cols]
            weights = probs[index * heads + head]
            values_grad = lax.dot_general(
                weights.astype(jnp.bfloat16), up, TN, preferred_element_type=jnp.float32
            )
            d_probs = lax.dot_general(up, value, NT, preferred_element_type=jnp.float32)
            d_scores = (
                weights * (d_probs - jnp.sum(weights * d_probs, axis=-1, keepdims=True))
            ).astype(jnp.bfloat16)
            d_query = jnp.dot(d_scores, key, preferred_element_type=jnp.float32) * score_scale
            d_key = (
                lax.dot_general(d_scores, query, TN, preferred_element_type=jnp.float32)
                * score_scale
            )
            d_query = d_query * tables[0] - swap_halves(d_query) * tables[1]
            d_key = d_key * tables[0] - swap_halves(d_key) * tables[1]
            for part, value_of in enumerate((d_query, d_key, values_grad)):
                base = part * head_width + head * HEAD
                d_qkv[span, base : base + HEAD] = value_of.astype(jnp.bfloat16)
        return carry

    def normed_load(n):
        return pltpu.make_async_copy(
            normed.at[:, n * 256 : (n + 1) * 256], normed_part.at[n % 2], local_sem.at[5 + n % 2]
        )

    normed_load(0).start()
    lax.fori_loop(0, sequences // 2, sequence, 0)
    for step in range(1, 8):
        here = grads.at[3, pl.ds(pl.multiple_of(nbr[step] * head_width, head_width), head_width)]
        send(here, here, o_send.at[step], o_recv.at[step], (me_z, nbr[step])).wait_recv()
    out_chain.hop(0)
    shared.begin()
    forward[2].third()
    lax.fori_loop(sequences // 2, sequences, sequence, 0)

    for n in range(width // 256):
        cols = slice(n * 256, (n + 1) * 256)
        if n < width // 256 - 1:
            normed_load(n + 1).start()
        normed_load(n).wait()
        term = lax.dot_general(
            normed_part[n % 2], d_qkv[...], TN, preferred_element_type=jnp.float32
        ).astype(jnp.bfloat16)
        for part in range(3):
            grads[part, cols, :] = term[:, part * head_width : (part + 1) * head_width]
    chain.hop(0)
    out_chain.hop(1)
    gather.drain()

    for n in range(width // 256):
        cols = slice(n * 256, (n + 1) * 256)
        term = lax.dot_general(
            d_qkv[...], w_qkv[cols, : 3 * head_width], NT, preferred_element_type=jnp.float32
        ).astype(jnp.bfloat16)
        for owner in range(8):
            mine = lax.rem(owner + core + 1, 2)
            rows_all[4 * mine + owner // 2, :, cols] = term[owner * rows : (owner + 1) * rows]
    back = PlaneScatter(
        rows_all.at[pl.ds(0, 4)],
        rows_all.at[pl.ds(4, 4)],
        n_sib,
        n_relayed,
        n_crossed,
        (n_send, n_recv),
        (me_y, me_x),
        me_z,
        nbr,
    )
    def keep(span, total):
        d_normed[span, :] = total

    def norm_step(index, gain_sum):
        span = pl.ds(pl.multiple_of(index * 16, 16), 16)
        grad, term = norm_back_rows(
            tokens[span, :].astype(jnp.float32), d_normed[span, :], gains[9:10]
        )
        tokens_grad[span, :] = tokens_grad[span, :] + grad
        return gain_sum + term

    def small_send(turn):
        return send(
            small.at[:, lanes(far[turn], shard_width)],
            small_far.at[turn],
            t_send.at[turn],
            t_recv.at[turn],
            (far[turn], me_e),
        )

    def plane_send(step):
        return send(
            small_plane.at[me_e],
            small_plane.at[me_e],
            p_send.at[step],
            p_recv.at[step],
            (me_z, nbr[step]),
        )

    back.first()
    bias_terms = jnp.sum(d_qkv[...].astype(jnp.float32), axis=0, keepdims=True)
    for part in range(3):
        small[11 + part : 12 + part, lanes(me_e, head_width)] = bias_terms[
            :, part * head_width : (part + 1) * head_width
        ]
    back.second()
    out_chain.hop(2)
    chain.hop(1)
    out_chain_last()
    out_own.start()
    out_own.wait()
    out_projection.begin()
    back.third()
    out_projection.relay()
    chain.hop(2)
    out_projection.relay_far()
    shared.relay()
    back.fourth(keep)
    small[9:10, :] = lax.fori_loop(0, rows // 16, norm_step, jnp.zeros((1, width), jnp.float32))
    for turn in (1, 2, 3):
        small_send(turn).start()
    forward_last(2)
    forward[1].drain()
    forward_load(3).start()
    forward_load(3).wait()
    forward[3].second()
    forward[2].drain()
    forward_load(0).start()
    chain_last()
    qkv_own.start()
    qkv_own.wait()
    projections.begin()
    forward[3].third()
    forward_load(0).wait()
    forward[0].second()
    for turn in (1, 2, 3):
        small_send(turn).wait_recv()
    small_plane[me_e] = (
        small[:, lanes(me_z, shard_width)] + small_far[1] + small_far[2] + small_far[3]
    )
    for step in range(1, 8):
        plane_send(step).start()
    shared.relay_far()
    projections.relay()
    forward_last(3)
    forward[0].third()
    for step in range(1, 8):
        here = small_plane.at[nbr[step]]
        send(here, here, p_send.at[step], p_recv.at[step], (me_z, nbr[step])).wait_recv()
    total = small_plane[0]
    for index in range(1, 8):
        total = total + small_plane[index]
    small_out[...] = total
    forward_last(0)
    for turn in (1, 2, 3):
        far_send(turn).wait_recv()

    @pl.loop(0, rows, step=32)
    def _(row):
        span = pl.ds(pl.multiple_of(row, 32), 32)
        total = f_sum[0, span, :].astype(jnp.float32)
        for turn in (1, 2, 3):
            total = total + f_far[turn - 1, span, :].astype(jnp.float32)
        output[span, :] = (hidden[span, :] + total).astype(jnp.bfloat16)

    projections.relay_far()
    shared.finish()
    projections.finish()
    out_projection.finish()
    for turn in (1, 2, 3):
        for part in range(3):
            expert_wait(part, turn)
            expert_send(part, turn).wait_send()
        small_send(turn).wait_send()
        far_send(turn).wait_send()
    for step in range(1, 8):
        out_send(step).wait_send()
        plane_send(step).wait_send()
    for turn in (3, 0):
        forward[turn].drain()
    chain.drain()
    out_chain.drain()
    out_projection.drain()
    back.drain()
    shared.drain()
    projections.drain()


def tail_call(
    mixed, qkv, probs, normed, w_qkv, w_out, tables, tokens, params, d_rows, d_gates, routes, router_probs,
    normed_two, hidden, cotangent, out_part, d_routed, shared_all, expert_all,
):
    rows, width = tokens.shape
    head_width = mixed.shape[1]
    shard_width = width // 4
    low, full = jnp.bfloat16, jnp.float32
    shape = jax.ShapeDtypeStruct
    any_space = pl.BlockSpec(memory_space=pl.ANY)
    vmem = pl.BlockSpec(memory_space=pltpu.VMEM)
    dma = pltpu.SemaphoreType.DMA
    return pl.pallas_call(
        tail_kernel,
        out_shape=(
            shape((rows, width), low),
            shape((rows, width), full),
            shape((16, shard_width), full),
            shape((4, shard_width, width), low),
            shape(shared_all.shape, low),
            shape(expert_all.shape, low),
        ),
        in_specs=[vmem] * 3 + [any_space] + [vmem] * 12 + [any_space] * 4,
        input_output_aliases={18: 4, 19: 5},
        out_specs=(vmem, vmem, vmem, any_space, any_space, any_space),
        scratch_shapes=[
            pltpu.VMEM((8, rows, width), low),
            pltpu.VMEM((2, 8 * rows, 256), low),
            pltpu.VMEM((8 * rows, head_width), low),
            pltpu.VMEM((8 * rows, 3 * head_width), low),
            pltpu.VMEM((head_width, width), low),
            pltpu.VMEM((4, width, head_width), low),
            pltpu.VMEM((5, 3, shard_width, head_width), low),
            pltpu.VMEM((5, 1, shard_width, head_width), low),
            pltpu.VMEM((4, shard_width, head_width), low),
            pltpu.VMEM((4, rows, width), low),
            pltpu.VMEM((2, rows // 2, width), low),
            pltpu.VMEM((2, rows, width), low),
            pltpu.VMEM((2, 4, rows, width), low),
            pltpu.VMEM((4, 4, rows, width), low),
            pltpu.VMEM((4, 2, rows // 2, width), low),
            pltpu.VMEM((4, 2, rows, width), low),
            pltpu.VMEM((4, rows, width), low),
            pltpu.VMEM((3, rows, width), low),
            pltpu.VMEM((rows, width), full),
            pltpu.VMEM((16, width), full),
            pltpu.VMEM((4, 16, shard_width), full),
            pltpu.VMEM((8, 16, shard_width), full),
            dma((3, 4)),
            dma((3, 4)),
            dma((10,)),
            dma((10,)),
            dma((8,)),
            dma((8,)),
            dma((2, 3)),
            dma((2, 3)),
            dma((2, 3)),
            dma((2, 3)),
            dma((7,)),
            dma((7,)),
            dma((4, 7)),
            dma((4, 7)),
            dma((4,)),
            dma((4,)),
            dma((10,)),
            dma((10,)),
            dma((10,)),
            dma((10,)),
            dma((10,)),
            dma((10,)),
            dma((4,)),
            dma((4,)),
            dma((8,)),
            dma((8,)),
            dma((8,)),
        ],
        compiler_params=pltpu.CompilerParams(
            collective_id=1, has_side_effects=True, vmem_limit_bytes=63 * 2**20
        ),
        cost_estimate=pl.CostEstimate(
            flops=24 * 8 * rows * width * head_width, bytes_accessed=80 * 2**20, transcendentals=0
        ),
    )(
        mixed, qkv, probs, normed, w_qkv, w_out, tables, tokens, params, d_rows, d_gates, routes, router_probs,
        normed_two, hidden, cotangent, out_part, d_routed, shared_all, expert_all,
    )


def front_kernel(
    tokens,
    docs,
    routes,
    router,
    gate_vector,
    gain_in,
    gain_out,
    bias_in,
    tables,
    cotangent,
    qkv_weight,
    out_weight,
    up_weight,
    down_weight,
    qkv,
    probs,
    mixed,
    normed,
    hidden,
    normed_two,
    gates_all,
    router_probs,
    params_all,
    weights_out,
    w_out_out,
    cot_all,
    w_all,
    x_all,
    rows_all,
    weights,
    w_out,
    params_in,
    docs_all,
    gates_in,
    qkv_part,
    n_sib,
    n_relayed,
    n_crossed,
    a_send,
    a_recv,
    w_send,
    w_recv,
    p_send,
    p_recv,
    d_send,
    d_recv,
    o_send,
    o_recv,
    n_send,
    n_recv,
    c_send,
    c_recv,
    k_send,
    k_recv,
    e_send,
    e_recv,
    x_send,
    x_recv,
    y_send,
    y_recv,
    g_send,
    g_recv,
    local_sem,
):
    me_z = lax.axis_index("dp")
    me_e = lax.axis_index("expert")
    core = lax.rem(me_e, 2)
    me_x = lax.rem(lax.div(me_e, 2), 2)
    me_y = lax.div(me_e, 4)
    nbr = {1: flip(me_e, 1), 2: flip(me_e, 2), 4: flip(me_e, 4)}
    nbr[6] = flip(nbr[2], 4)
    nbr[3], nbr[5], nbr[7] = flip(nbr[2], 1), flip(nbr[4], 1), flip(nbr[6], 1)
    far = {turn: flip_pair(me_z, turn) for turn in (1, 2, 3)}
    rows, width = tokens.shape
    shard_width = qkv_weight.shape[0]
    head_width = w_out.shape[0]
    heads = head_width // HEAD
    routed_units = down_weight.shape[0] // 4
    sequences = 8
    score_scale = HEAD ** (-0.5)

    def lanes(index, amount):
        return pl.ds(pl.multiple_of(index * amount, amount), amount)

    def lines(index, amount, grain=16):
        return pl.ds(pl.multiple_of(index * amount, grain), amount)

    my_lines = lines(me_z, shard_width)
    own = [
        pltpu.make_async_copy(
            qkv_weight.at[:, pl.ds(pl.multiple_of(part * width + me_e * head_width, head_width), head_width)],
            weights.at[my_lines, part * head_width : (part + 1) * head_width],
            local_sem.at[part],
        )
        for part in range(3)
    ]
    own.append(
        pltpu.make_async_copy(
            out_weight.at[:, lanes(me_e, head_width)],
            weights.at[my_lines, 3 * head_width : 4 * head_width],
            local_sem.at[3],
        )
    )
    own.append(pltpu.make_async_copy(tokens, rows_all.at[me_e], local_sem.at[4]))
    own.append(pltpu.make_async_copy(cotangent, cot_all.at[me_e, me_z], local_sem.at[5]))
    for copy in own:
        copy.start()
    shards = [router[...]] + [ref[...].reshape(1, shard_width) for ref in (gate_vector, gain_in, gain_out)]
    shards = [part.astype(jnp.float32) for part in shards + [bias_in[...]]]
    shards.append(jnp.zeros((2, shard_width), jnp.float32))
    params_in[me_z] = jnp.concatenate(shards, axis=0).astype(jnp.bfloat16)
    docs_all[me_e] = jnp.broadcast_to(docs[...].astype(jnp.float32), docs_all.shape[1:])
    greet([(far[turn], me_e) for turn in (1, 2, 3)] + [(me_z, nbr[k]) for k in range(1, 8)])
    for copy in own:
        copy.wait()

    attn_weights = ChainGather(
        lambda z: weights.at[lines(z, shard_width)], w_send, w_recv, me_z, me_e
    )
    attn_weights.begin()
    cot_chain = ChainGather(lambda z: cot_all.at[me_e, z], k_send, k_recv, me_z, me_e)
    cot_chain.begin()

    def cot_gather(place, z):
        def region(owner, half):
            if half is None:
                return cot_all.at[owner, z]
            return cot_all.at[owner, z, pl.ds(half * (rows // 2), rows // 2)]

        return PlaneGather(region, c_send.at[place], c_recv.at[place], me_z, me_e, nbr)

    cot_own = cot_gather(6, me_z)

    def cot_step(hop, name):
        for way in range(2):
            z = jnp.clip(me_z - (1 - 2 * way) * (hop + 1), 0, 3)
            pl.when(cot_chain.takes(way, hop))(getattr(cot_gather(way * 3 + hop, z), name))

    def expert_copy(part, turn, here):
        source = down_weight if part == 2 else up_weight.at[part]
        z = far[turn] if here else me_z
        target = w_all.at[part, :, lanes(z, shard_width)]
        return send(
            target if here else source.at[lines(far[turn], routed_units)],
            target,
            e_send.at[part, turn],
            e_recv.at[part, turn],
            (far[turn], me_e),
        )

    ends = (me_z == 0) | (me_z == 3)

    def expert_start(turn, from_ends):
        @pl.when(ends if from_ends else jnp.logical_not(ends))
        def _():
            for part in range(3):
                expert_copy(part, turn, False).start()

    def rows_region(owner, half):
        if half is None:
            return rows_all.at[owner]
        return rows_all.at[owner, pl.ds(half * (rows // 2), rows // 2)]

    gather = PlaneGather(rows_region, a_send, a_recv, me_z, me_e, nbr)

    def params_send(turn):
        return send(
            params_in.at[me_z], params_in.at[me_z], p_send.at[turn], p_recv.at[turn], (far[turn], me_e)
        )

    def docs_send(step):
        return send(
            docs_all.at[me_e], docs_all.at[me_e], d_send.at[step], d_recv.at[step], (me_z, nbr[step])
        )

    for turn in (1, 2, 3):
        params_send(turn).start()
    gather.begin()
    for step in range(1, 8):
        docs_send(step).start()
    cot_own.begin()
    gather.relay()
    cot_chain.hop(0)
    cot_step(0, "begin")
    gather.relay_far()
    cot_own.relay()
    for turn in (1, 2, 3):
        here = params_in.at[far[turn]]
        send(here, here, p_send.at[turn], p_recv.at[turn], (far[turn], me_e)).wait_recv()
    params_all[...] = jnp.concatenate([params_in[z] for z in range(4)], axis=1)
    gather.finish()
    attn_weights.hop(0)
    cot_own.relay_far()
    cot_chain.hop(1)
    cot_step(0, "relay")
    cot_step(1, "begin")

    def norm_rows(value, gain):
        scale = lax.rsqrt(jnp.mean(value * value, axis=-1, keepdims=True) + EPS)
        return (value * scale * gain).astype(jnp.bfloat16)

    params_full = params_all[...].astype(jnp.float32)
    gain_one, gain_two = params_full[9:10], params_full[10:11]
    bias = params_all[:, lanes(me_e, head_width)].astype(jnp.float32)[11:14]

    for owner in range(8):

        @pl.loop(0, rows, step=16)
        def _(row, owner=owner):
            span = pl.ds(pl.multiple_of(row, 16), 16)
            normed[pl.ds(pl.multiple_of(owner * rows + row, 16), 16), :] = norm_rows(
                rows_all[owner, span, :].astype(jnp.float32), gain_one
            )

    cot_step(0, "relay_far")
    attn_weights.hop(1)
    expert_start(1, True)
    expert_start(2, True)
    expert_start(3, False)
    cot_chain.hop(2)

    cot_step(1, "relay")
    cot_step(2, "begin")
    attn_weights.hop(2)
    expert_start(1, False)
    expert_start(2, False)
    expert_start(3, True)

    def out_send(step):
        return send(
            weights.at[lines(nbr[step], head_width), 3 * head_width : 4 * head_width],
            w_out.at[:, lanes(me_e, head_width)],
            o_send.at[step],
            o_recv.at[step],
            (me_z, nbr[step]),
        )

    for step in range(1, 8):
        out_send(step).start()
    w_out[:, lanes(me_e, head_width)] = weights[lines(me_e, head_width), 3 * head_width :]
    weights_store = pltpu.make_async_copy(weights, weights_out, local_sem.at[0])
    weights_store.start()

    for part in range(3):
        cols = slice(part * head_width, (part + 1) * head_width)
        qkv_part[...] = (
            jnp.dot(normed[...], weights[:, cols], preferred_element_type=jnp.float32)
            + bias[part : part + 1]
        )
        if part == 2:
            qkv[part] = qkv_part[...].astype(jnp.bfloat16)
        else:

            @pl.loop(0, sequences)
            def _(index, part=part):
                span = pl.ds(pl.multiple_of(index * rows, rows), rows)
                for head in range(heads):
                    at = slice(head * HEAD, (head + 1) * HEAD)
                    value = qkv_part[span, at]
                    qkv[part, span, at] = (
                        value * tables[0] + swap_halves(value) * tables[1]
                    ).astype(jnp.bfloat16)

    order = lax.broadcasted_iota(jnp.int32, (rows, rows), 0) >= lax.broadcasted_iota(
        jnp.int32, (rows, rows), 1
    )

    def sequence(index, carry):
        span = pl.ds(pl.multiple_of(index * rows, rows), rows)
        doc = jnp.broadcast_to(docs_all[index, 0:1, :], (rows, rows))
        allowed = (doc == doc.T) & order
        for head in range(heads):
            at = slice(head * HEAD, (head + 1) * HEAD)
            scores = (
                lax.dot_general(
                    qkv[0, span, at], qkv[1, span, at], NT, preferred_element_type=jnp.float32
                )
                * score_scale
            )
            scores = jnp.where(allowed, scores, NEGATIVE)
            exp_scores = jnp.exp(scores - jnp.max(scores, axis=-1, keepdims=True))
            weight = exp_scores / jnp.sum(exp_scores, axis=-1, keepdims=True)
            probs[index * heads + head] = weight
            mixed[span, at] = jnp.dot(
                weight.astype(jnp.bfloat16), qkv[2, span, at], preferred_element_type=jnp.float32
            ).astype(jnp.bfloat16)
        return carry

    cot_step(1, "relay_far")
    cot_step(2, "relay")
    for step in range(1, 8):
        here = docs_all.at[nbr[step]]
        send(here, here, d_send.at[step], d_recv.at[step], (me_z, nbr[step])).wait_recv()
    lax.fori_loop(0, sequences // 2, sequence, 0)
    cot_step(2, "relay_far")
    lax.fori_loop(sequences // 2, sequences, sequence, 0)
    gather.drain()

    for step in range(1, 8):
        here = w_out.at[:, lanes(nbr[step], head_width)]
        send(here, here, o_send.at[step], o_recv.at[step], (me_z, nbr[step])).wait_recv()
    for n in range(width // shard_width):
        cols = slice(n * shard_width, (n + 1) * shard_width)
        term = jnp.dot(mixed[...], w_out[:, cols], preferred_element_type=jnp.float32).astype(
            jnp.bfloat16
        )
        for owner in range(8):
            mine = lax.rem(owner + core + 1, 2)
            rows_all[4 * mine + owner // 2, :, cols] = term[owner * rows : (owner + 1) * rows]
    sums = PlaneScatter(
        rows_all.at[pl.ds(0, 4)],
        rows_all.at[pl.ds(4, 4)],
        n_sib,
        n_relayed,
        n_crossed,
        (n_send, n_recv),
        (me_y, me_x),
        me_z,
        nbr,
    )
    sums.first()
    out_store = pltpu.make_async_copy(w_out, w_out_out, local_sem.at[1])
    out_store.start()
    sums.second()

    sums.third()

    def keep(span, total):
        hidden[span, :] = total + tokens[span, :].astype(jnp.float32)

    sums.fourth(keep)

    @pl.loop(0, rows, step=16)
    def _(row):
        span = pl.ds(pl.multiple_of(row, 16), 16)
        normed_two[span, :] = norm_rows(hidden[span, :], gain_two)

    logits = lax.dot_general(
        params_all[...], normed_two[...], NT, preferred_element_type=jnp.float32
    )
    top = jnp.exp(logits[:8] - jnp.max(logits[:8], axis=0, keepdims=True))
    top = top / jnp.sum(top, axis=0, keepdims=True)
    line = lax.broadcasted_iota(jnp.int32, (8, rows), 0)
    rest = jnp.where(line == 0, jax.nn.sigmoid(logits[8:]), 0.0)
    router_probs[...] = jnp.concatenate([top, rest], axis=0)
    x_own = pltpu.make_async_copy(normed_two, x_all.at[me_z, me_e], local_sem.at[2])
    x_own.start()
    gates_in[me_e, me_z] = jnp.concatenate([top * named_of(routes), rest], axis=0)

    def gates_far(turn, z):
        here = gates_in.at[me_e, z]
        return send(here, here, y_send.at[turn], y_recv.at[turn], (far[turn], me_e))

    def gates_near(step, owner):
        here = gates_in.at[owner]
        return send(here, here, g_send.at[step], g_recv.at[step], (me_z, nbr[step]))

    for turn in (1, 2, 3):
        gates_far(turn, me_z).start()

    def x_region(owner, half):
        if half is None:
            return x_all.at[me_z, owner]
        return x_all.at[me_z, owner, pl.ds(half * (rows // 2), rows // 2)]

    x_gather = PlaneGather(x_region, x_send, x_recv, me_z, me_e, nbr)
    x_own.wait()
    x_gather.begin()
    for turn in (1, 2, 3):
        gates_far(turn, far[turn]).wait_recv()
    for step in range(1, 8):
        gates_near(step, me_e).start()
    x_gather.relay()
    x_gather.relay_far()
    for step in range(1, 8):
        gates_near(step, nbr[step]).wait_recv()
    gates_all[...] = gates_in[...]
    x_gather.finish()

    cot_own.finish()
    for hop in range(3):
        cot_step(hop, "finish")
    for turn in (1, 2, 3):
        for part in range(3):
            expert_copy(part, turn, True).wait_recv()
            expert_copy(part, turn, False).wait_send()
        params_send(turn).wait_send()
        gates_far(turn, me_z).wait_send()
    for step in range(1, 8):
        docs_send(step).wait_send()
        gates_near(step, me_e).wait_send()
        out_send(step).wait_send()
    weights_store.wait()
    out_store.wait()
    attn_weights.drain()
    cot_chain.drain()
    sums.drain()
    x_gather.drain()
    cot_own.drain()
    for hop in range(3):
        cot_step(hop, "drain")


def front_call(
    tokens, docs, routes, router, gate_vector, gain_in, gain_out, bias_in, tables, cotangent, qkv_weight,
    out_weight, up_weight, down_weight,
):
    rows, width = tokens.shape
    shard_width = qkv_weight.shape[0]
    head_width = width // 8
    pairs = 8 * head_width // HEAD
    routed_units = down_weight.shape[0] // 4
    low, full = jnp.bfloat16, jnp.float32
    shape = jax.ShapeDtypeStruct
    any_space = pl.BlockSpec(memory_space=pl.ANY)
    vmem = pl.BlockSpec(memory_space=pltpu.VMEM)
    dma = pltpu.SemaphoreType.DMA
    return pl.pallas_call(
        front_kernel,
        out_shape=(
            shape((3, 8 * rows, head_width), low),
            shape((pairs, rows, rows), full),
            shape((8 * rows, head_width), low),
            shape((8 * rows, width), low),
            shape((rows, width), full),
            shape((rows, width), low),
            shape((8, 4, 16, rows), full),
            shape((16, rows), full),
            shape((16, width), low),
            shape((width, 4 * head_width), low),
            shape((head_width, width), low),
            shape((8, 4, rows, width), low),
            shape((3, routed_units, width), low),
            shape((4, 8, rows, width), low),
        ),
        in_specs=[vmem] * 10 + [any_space] * 4,
        out_specs=tuple([vmem] * 9 + [any_space] * 5),
        scratch_shapes=[
            pltpu.VMEM((8, rows, width), low),
            pltpu.VMEM((width, 4 * head_width), low),
            pltpu.VMEM((head_width, width), low),
            pltpu.VMEM((4, 16, shard_width), low),
            pltpu.VMEM((8, 8, rows), full),
            pltpu.VMEM((8, 4, 16, rows), full),
            pltpu.VMEM((8 * rows, head_width), full),
            pltpu.VMEM((4, rows, width), low),
            pltpu.VMEM((2, rows // 2, width), low),
            pltpu.VMEM((2, rows, width), low),
            dma((10,)),
            dma((10,)),
            dma((2, 3)),
            dma((2, 3)),
            dma((4,)),
            dma((4,)),
            dma((8,)),
            dma((8,)),
            dma((8,)),
            dma((8,)),
            dma((7,)),
            dma((7,)),
            dma((7, 10)),
            dma((7, 10)),
            dma((2, 3)),
            dma((2, 3)),
            dma((3, 4)),
            dma((3, 4)),
            dma((10,)),
            dma((10,)),
            dma((4,)),
            dma((4,)),
            dma((8,)),
            dma((8,)),
            dma((6,)),
        ],
        compiler_params=pltpu.CompilerParams(
            collective_id=2, has_side_effects=True, vmem_limit_bytes=60 * 2**20
        ),
        cost_estimate=pl.CostEstimate(
            flops=8 * 8 * rows * width * head_width, bytes_accessed=80 * 2**20, transcendentals=0
        ),
    )(
        tokens, docs, routes, router, gate_vector, gain_in, gain_out, bias_in, tables, cotangent, qkv_weight,
        out_weight, up_weight, down_weight,
    )


def widen_kernel(attn_all, shared_all, expert_all, qkv, out, shared, up, down):
    for part in range(3):
        width = attn_all.shape[2]
        qkv[:, part * width : (part + 1) * width] = attn_all[part].astype(jnp.float32)
        shared[part] = shared_all[part].astype(jnp.float32)
    out[...] = attn_all[3].astype(jnp.float32)
    for part in range(2):
        up[:, part, :] = expert_all[part].astype(jnp.float32)
    down[...] = expert_all[2].astype(jnp.float32)


def widen_call(attn_all, shared_all, expert_all):
    steps = 8
    _, depth, width = attn_all.shape
    units, routed, cols = shared_all.shape[1], expert_all.shape[1], expert_all.shape[2]
    full = jnp.float32
    shape = jax.ShapeDtypeStruct
    return pl.pallas_call(
        widen_kernel,
        grid=(steps,),
        out_shape=(
            shape((depth, 3 * width), full),
            shape((depth, width), full),
            shape(shared_all.shape, full),
            shape((routed, 2, cols), full),
            shape((routed, cols), full),
        ),
        in_specs=[
            pl.BlockSpec((4, depth // steps, width), lambda i: (0, i, 0)),
            pl.BlockSpec((3, units // steps, width), lambda i: (0, i, 0)),
            pl.BlockSpec((3, routed // steps, cols), lambda i: (0, i, 0)),
        ],
        out_specs=(
            pl.BlockSpec((depth // steps, 3 * width), lambda i: (i, 0)),
            pl.BlockSpec((depth // steps, width), lambda i: (i, 0)),
            pl.BlockSpec((3, units // steps, width), lambda i: (0, i, 0)),
            pl.BlockSpec((routed // steps, 2, cols), lambda i: (i, 0, 0)),
            pl.BlockSpec((routed // steps, cols), lambda i: (i, 0)),
        ),
        compiler_params=pltpu.CompilerParams(vmem_limit_bytes=60 * 2**20),
        cost_estimate=pl.CostEstimate(flops=0, bytes_accessed=96 * 2**20, transcendentals=0),
    )(attn_all, shared_all, expert_all)


def silu_parts(gate):
    logistic = jax.nn.sigmoid(gate)
    silu = gate * logistic
    return (silu, logistic * (1.0 + gate * (1.0 - logistic)))


def gather_all(rows):
    rows = lax.all_gather(rows, "dp", axis=0, tiled=True)
    return lax.all_gather(rows, "expert", axis=0, tiled=True)


def scatter_all(rows):
    rows = lax.psum_scatter(rows, "expert", scatter_dimension=0, tiled=True)
    return lax.psum_scatter(rows, "dp", scatter_dimension=0, tiled=True)


def shards(
    tokens,
    attn_gain,
    qkv_weight,
    qkv_bias,
    out_weight,
    ffn_gain,
    router_weight,
    shared_gate_weight,
    shared_weight,
    expert_up,
    expert_down,
    routes,
    segment_ids,
    cotangent,
):
    num_dp = lax.axis_size("dp")
    num_expert = lax.axis_size("expert")
    me_expert = lax.axis_index("expert")
    seq_len, model_width = tokens.shape
    shard_width = qkv_weight.shape[0]
    head_count = HEADS // num_expert
    head_width = head_count * HEAD
    plane_rows = seq_len * num_expert
    units = shared_weight.shape[0] // num_expert
    score_scale = HEAD ** (-0.5)

    small = jnp.concatenate(
        [
            attn_gain[None],
            ffn_gain[None],
            shared_gate_weight[None],
            qkv_bias,
            router_weight.T,
        ],
        axis=0,
    )
    small = lax.all_gather(small, "dp", axis=1, tiled=True)
    gain_one = small[0].astype(jnp.float32)
    gain_two = small[1].astype(jnp.float32)
    bias_cols = lax.dynamic_slice_in_dim(small[3:6], me_expert * head_width, head_width, 1)
    w_route = jnp.concatenate([small[6:], small[2:3]], axis=0)

    plane_tokens = lax.all_gather(tokens, "expert", axis=0, tiled=True)
    plane_docs = lax.all_gather(segment_ids, "expert", axis=0, tiled=True)
    cols_qkv = lax.dynamic_slice_in_dim(
        qkv_weight.reshape(shard_width, 3, model_width), me_expert * head_width, head_width, 2
    ).reshape(shard_width, 3 * head_width)
    cols_out = lax.dynamic_slice_in_dim(out_weight, me_expert * head_width, head_width, 1)
    attn_weights = lax.all_gather(
        jnp.concatenate([cols_qkv, cols_out], axis=1), "dp", axis=0, tiled=True
    )
    w_qkv = attn_weights[:, : 3 * head_width]
    w_out = lax.all_to_all(
        attn_weights[:, 3 * head_width :], "expert", split_axis=0, concat_axis=1, tiled=True
    )

    expert_full = jnp.concatenate([expert_up[0], expert_down[0][:, None, :]], axis=1)
    expert_units = lax.all_to_all(expert_full, "dp", split_axis=0, concat_axis=2, tiled=True)
    shared_units = lax.dynamic_slice_in_dim(shared_weight, me_expert * units, units, 0)
    mlp_weight = jnp.concatenate([expert_units, shared_units], axis=0)
    routed_units = expert_units.shape[0]
    all_units = routed_units + units

    all_cot = gather_all(cotangent)
    all_routes = gather_all(routes)

    plane_resid = plane_tokens.astype(jnp.float32)
    normed_one = (plane_resid * rms_scale(plane_resid) * gain_one).astype(jnp.bfloat16)
    qkv_rows = jnp.dot(normed_one, w_qkv, preferred_element_type=jnp.float32) + bias_cols.reshape(
        -1
    ).astype(jnp.float32)
    qkv_rows = qkv_rows.reshape(num_expert, seq_len, 3, head_count, HEAD)
    cosine_table, sine_table = rope_tables(seq_len, HEAD)
    query_rows = rotate(qkv_rows[:, :, 0], cosine_table, sine_table).astype(jnp.bfloat16)
    key_rows = rotate(qkv_rows[:, :, 1], cosine_table, sine_table).astype(jnp.bfloat16)
    value_rows = qkv_rows[:, :, 2].astype(jnp.bfloat16)
    positions = jnp.arange(seq_len)
    allowed = (
        (plane_docs[:, :, None] == plane_docs[:, None, :])
        & (positions[:, None] >= positions[None, :])[None]
    )[:, None]
    scores = (
        jnp.einsum("bthd,bshd->bhts", query_rows, key_rows, preferred_element_type=jnp.float32)
        * score_scale
    )
    scores = jnp.where(allowed, scores, NEGATIVE)
    exp_scores = jnp.exp(scores - jnp.max(scores, axis=-1, keepdims=True))
    attn_probs = exp_scores / jnp.sum(exp_scores, axis=-1, keepdims=True)
    probs_low = attn_probs.astype(jnp.bfloat16)
    mixed_heads = (
        jnp.einsum("bhts,bshd->bthd", probs_low, value_rows, preferred_element_type=jnp.float32)
        .reshape(plane_rows, head_width)
        .astype(jnp.bfloat16)
    )
    attn_part = jnp.dot(mixed_heads, w_out, preferred_element_type=jnp.float32)
    attn_out = lax.psum_scatter(
        attn_part.astype(jnp.bfloat16), "expert", scatter_dimension=0, tiled=True
    )

    resid_in = tokens.astype(jnp.float32)
    hidden_state = resid_in + attn_out.astype(jnp.float32)
    rms_two = rms_scale(hidden_state)
    normed_two = (hidden_state * rms_two * gain_two).astype(jnp.bfloat16)

    all_normed = gather_all(normed_two)
    all_logits = jnp.einsum(
        "td,ed->te", all_normed, w_route, preferred_element_type=jnp.float32
    )
    all_probs = jax.nn.softmax(all_logits[:, :num_expert], axis=-1)
    all_named = jnp.any(all_routes == me_expert, axis=1)
    my_prob = jnp.sum(
        jnp.where(jnp.arange(num_expert)[None, :] == me_expert, all_probs, 0.0), axis=1
    )
    gate_routed = jnp.where(all_named, my_prob, 0.0)
    gate_shared = jax.nn.sigmoid(all_logits[:, num_expert])
    is_routed = (jnp.arange(all_units) < routed_units)[None, :]
    row_gate = jnp.where(is_routed, gate_routed[:, None], gate_shared[:, None])

    gate_up = jnp.einsum(
        "td,fgd->gtf", all_normed, mlp_weight[:, :2], preferred_element_type=jnp.float32
    )
    silu, d_silu = silu_parts(gate_up[0])
    act = silu * gate_up[1]
    raw_act_grad = jnp.einsum(
        "td,fd->tf", all_cot, mlp_weight[:, 2], preferred_element_type=jnp.float32
    )
    gated_act = (row_gate * act).astype(jnp.bfloat16)
    act_dots = act * raw_act_grad
    d_gate_routed = jnp.where(
        all_named, jnp.sum(jnp.where(is_routed, act_dots, 0.0), axis=1), 0.0
    )
    d_gate_shared = jnp.sum(jnp.where(is_routed, 0.0, act_dots), axis=1)
    act_grad = raw_act_grad * row_gate
    d_gate_up = jnp.stack([act_grad * gate_up[1] * d_silu, act_grad * silu], axis=0).astype(
        jnp.bfloat16
    )
    d_rows = jnp.einsum(
        "gtf,fgd->td", d_gate_up, mlp_weight[:, :2], preferred_element_type=jnp.float32
    ).astype(jnp.bfloat16)
    gate_cols = jnp.concatenate(
        [
            jnp.where(
                jnp.arange(num_expert)[None, :] == me_expert, d_gate_routed[:, None], 0.0
            ),
            d_gate_shared[:, None],
        ],
        axis=1,
    )
    d_gate_cols = scatter_all(gate_cols)
    d_rows_sum = scatter_all(d_rows).astype(jnp.float32)

    up_grad = jnp.einsum(
        "gtf,td->fgd", d_gate_up, all_normed, preferred_element_type=jnp.float32
    ).astype(jnp.bfloat16)
    down_grad = jnp.einsum(
        "tf,td->fd", gated_act, all_cot, preferred_element_type=jnp.float32
    ).astype(jnp.bfloat16)
    out_rows = jnp.dot(gated_act, mlp_weight[:, 2], preferred_element_type=jnp.float32).astype(
        jnp.bfloat16
    )
    output = (hidden_state + scatter_all(out_rows).astype(jnp.float32)).astype(jnp.bfloat16)
    mlp_grad = jnp.concatenate([up_grad, down_grad[:, None, :]], axis=1)
    expert_grad = lax.all_to_all(
        mlp_grad[:routed_units], "dp", split_axis=2, concat_axis=0, tiled=True
    ).astype(jnp.float32)
    shared_grad = lax.all_gather(
        mlp_grad[routed_units:], "expert", axis=0, tiled=True
    ).astype(jnp.float32)

    back_grad = cotangent.astype(jnp.float32)
    logits = jnp.einsum("td,ed->te", normed_two, w_route, preferred_element_type=jnp.float32)
    router_probs = jax.nn.softmax(logits[:, :num_expert], axis=-1)
    logistic_gate = jax.nn.sigmoid(logits[:, num_expert:])
    d_router_probs = d_gate_cols[:, :num_expert]
    d_logits = router_probs * (
        d_router_probs - jnp.sum(router_probs * d_router_probs, axis=-1, keepdims=True)
    )
    d_gate_logit = d_gate_cols[:, num_expert:] * logistic_gate * (1.0 - logistic_gate)
    d_route = jnp.concatenate([d_logits, d_gate_logit], axis=1).astype(jnp.bfloat16)
    route_grad = jnp.einsum("td,te->ed", normed_two, d_route, preferred_element_type=jnp.float32)
    d_normed = d_rows_sum + jnp.dot(d_route, w_route, preferred_element_type=jnp.float32)
    ffn_gain_grad, d_hidden = norm_back(hidden_state, rms_two, gain_two, d_normed)
    d_hidden = back_grad + d_hidden

    d_attn_out = lax.all_gather(d_hidden.astype(jnp.bfloat16), "expert", axis=0, tiled=True)
    out_grad = jnp.einsum(
        "td,te->de", mixed_heads, d_attn_out, preferred_element_type=jnp.float32
    ).astype(jnp.bfloat16)
    out_grad = lax.all_to_all(out_grad, "expert", split_axis=1, concat_axis=0, tiled=True)
    d_mixed = (
        jnp.einsum("te,de->td", d_attn_out, w_out, preferred_element_type=jnp.float32)
        .astype(jnp.bfloat16)
        .reshape(num_expert, seq_len, head_count, HEAD)
    )
    values_grad = jnp.einsum(
        "bhts,bthd->bshd", probs_low, d_mixed, preferred_element_type=jnp.float32
    )
    d_probs = jnp.einsum("bthd,bshd->bhts", d_mixed, value_rows, preferred_element_type=jnp.float32)
    d_scores = (
        attn_probs * (d_probs - jnp.sum(attn_probs * d_probs, axis=-1, keepdims=True))
    ).astype(jnp.bfloat16)
    d_query = unrotate(
        jnp.einsum("bhts,bshd->bthd", d_scores, key_rows, preferred_element_type=jnp.float32)
        * score_scale,
        cosine_table,
        sine_table,
    )
    d_keys = unrotate(
        jnp.einsum("bhts,bthd->bshd", d_scores, query_rows, preferred_element_type=jnp.float32)
        * score_scale,
        cosine_table,
        sine_table,
    )
    d_qkv = (
        jnp.stack([d_query, d_keys, values_grad], axis=2)
        .reshape(plane_rows, 3 * head_width)
        .astype(jnp.bfloat16)
    )
    bias_part = jnp.sum(d_qkv.astype(jnp.float32), axis=0).reshape(3, head_width)
    bias_grad = lax.dynamic_update_slice_in_dim(
        jnp.zeros((3, model_width), jnp.float32), bias_part, me_expert * head_width, 1
    )
    d_normed_one = lax.psum_scatter(
        jnp.einsum("te,de->td", d_qkv, w_qkv, preferred_element_type=jnp.float32).astype(
            jnp.bfloat16
        ),
        "expert",
        scatter_dimension=0,
        tiled=True,
    ).astype(jnp.float32)
    qkv_grad = jnp.einsum(
        "td,te->de", normed_one, d_qkv, preferred_element_type=jnp.float32
    ).astype(jnp.bfloat16)
    attn_grad = lax.psum_scatter(
        jnp.concatenate([qkv_grad, out_grad], axis=1), "dp", scatter_dimension=0, tiled=True
    )
    attn_grad = lax.all_gather(attn_grad, "expert", axis=0).astype(jnp.float32)
    qkv_weight_grad = (
        attn_grad[:, :, : 3 * head_width]
        .reshape(num_expert, shard_width, 3, head_width)
        .transpose(1, 2, 0, 3)
        .reshape(shard_width, 3 * model_width)
    )
    out_weight_grad = (
        attn_grad[:, :, 3 * head_width :].transpose(1, 0, 2).reshape(shard_width, model_width)
    )
    attn_gain_grad, d_input = norm_back(resid_in, rms_scale(resid_in), gain_one, d_normed_one)
    tokens_grad = d_hidden + d_input

    small_grad = jnp.concatenate(
        [attn_gain_grad[None], ffn_gain_grad[None], bias_grad, route_grad], axis=0
    )
    small_grad = lax.psum_scatter(small_grad, "dp", scatter_dimension=1, tiled=True)
    small_grad = lax.psum(small_grad, "expert")
    return (
        output,
        tokens_grad,
        small_grad[0],
        qkv_weight_grad,
        small_grad[2:5],
        out_weight_grad,
        small_grad[1],
        small_grad[5 : 5 + num_expert].T,
        small_grad[5 + num_expert],
        shared_grad,
        expert_grad[None, :, :2],
        expert_grad[None, :, 2],
    )


def fast_shards(
    tokens,
    attn_gain,
    qkv_weight,
    qkv_bias,
    out_weight,
    ffn_gain,
    router_weight,
    shared_gate_weight,
    shared_weight,
    expert_up,
    expert_down,
    routes,
    segment_ids,
    cotangent,
):
    num_dp = lax.axis_size("dp")
    num_expert = lax.axis_size("expert")
    seq_len, model_width = tokens.shape
    up_weight = expert_up[0].transpose(1, 0, 2)
    low, full = jnp.bfloat16, jnp.float32

    positions = np.arange(seq_len, dtype=np.float32)[:, None]
    angles = positions * np.exp(np.arange(HEAD // 2) * (-2.0 * math.log(THETA) / HEAD)).astype(np.float32)
    sines = np.sin(angles)
    tables = jnp.asarray(
        np.stack([np.tile(np.cos(angles), 2), np.concatenate([-sines, sines], axis=1)]), full
    )
    (
        qkv,
        probs,
        mixed,
        normed_one,
        hidden_state,
        normed_two,
        gates_all,
        router_probs,
        params,
        attn_weights,
        w_out,
        all_cot,
        mlp_weight,
        x_all,
    ) = front_call(
        tokens,
        segment_ids,
        routes.T,
        router_weight.T,
        shared_gate_weight,
        attn_gain,
        ffn_gain,
        qkv_bias,
        tables,
        cotangent,
        qkv_weight,
        out_weight,
        up_weight,
        expert_down[0],
    )

    _, out_part, d_rows, d_gates, d_routed, shared_grad, expert_grad = mlp_call(
        x_all,
        gates_all,
        all_cot,
        mlp_weight,
        up_weight,
        expert_down[0],
        shared_weight.transpose(1, 0, 2),
    )

    output, tokens_grad, small_grad, attn_grad, shared_grad, expert_grad = tail_call(
        mixed,
        qkv,
        probs,
        normed_one,
        attn_weights,
        w_out,
        tables,
        tokens,
        params,
        d_rows,
        d_gates,
        routes.T,
        router_probs,
        normed_two,
        hidden_state,
        cotangent,
        out_part.reshape(num_expert // 2, 2, num_dp, seq_len, model_width),
        d_routed,
        shared_grad,
        expert_grad,
    )
    qkv_grad, out_grad, shared_grad, up_grad, down_grad = widen_call(
        attn_grad, shared_grad, expert_grad
    )
    return (
        output,
        tokens_grad,
        small_grad[num_expert + 1],
        qkv_grad,
        small_grad[num_expert + 3 : num_expert + 6],
        out_grad,
        small_grad[num_expert + 2],
        small_grad[:num_expert].T,
        small_grad[num_expert],
        shared_grad.transpose(1, 0, 2),
        up_grad[None],
        down_grad[None],
    )


def solution(mesh):
    cube = mesh.shape["expert"] == 8 and mesh.shape["dp"] == 4
    return jax.shard_map(
        fast_shards if cube else shards,
        mesh=mesh,
        in_specs=(
            P(("dp", "expert"), None),
            P("dp"),
            P("dp", None),
            P(None, "dp"),
            P("dp", None),
            P("dp"),
            P("dp", None),
            P("dp"),
            P("dp", None, None),
            P("expert", None, None, "dp"),
            P("expert", None, "dp"),
            P(("dp", "expert"), None),
            P(("dp", "expert"), None),
            P(("dp", "expert"), None),
        ),
        out_specs=(
            P(("dp", "expert"), None),
            P(("dp", "expert"), None),
            P("dp"),
            P("dp", None),
            P(None, "dp"),
            P("dp", None),
            P("dp"),
            P("dp", None),
            P("dp"),
            P("dp", None, None),
            P("expert", None, None, "dp"),
            P("expert", None, "dp"),
        ),
        check_vma=False,
    )
```

```python
import functools
import math

import jax
import jax.numpy as jnp
import numpy as np
from jax import lax
from jax.experimental import pallas as pl
from jax.experimental.pallas import tpu as pltpu
from jax.sharding import PartitionSpec as P

HEADS = 16
HEAD = 128


EPS = 1e-06
THETA = 1000000.0
NEGATIVE = -1e30


def rms_scale(values):
    return lax.rsqrt(jnp.mean(values * values, axis=-1, keepdims=True) + EPS)


def rope_tables(length, head_width):
    indices = jnp.arange(head_width // 2).astype(jnp.float32)
    frequency = jnp.exp(indices * (-2.0 * math.log(THETA) / head_width))
    angles = jnp.arange(length).astype(jnp.float32)[:, None] * frequency[None, :]
    return (jnp.cos(angles), jnp.sin(angles))


def rotate(values, cosine_table, sine_table):
    half_width = values.shape[-1] // 2
    lower_half = values[..., :half_width]
    upper_half = values[..., half_width:]
    cos_rows = cosine_table[:, None, :]
    sin_rows = sine_table[:, None, :]
    return jnp.concatenate(
        [
            lower_half * cos_rows - upper_half * sin_rows,
            upper_half * cos_rows + lower_half * sin_rows,
        ],
        axis=-1,
    )


def unrotate(values, cosine_table, sine_table):
    half_width = values.shape[-1] // 2
    lower_half = values[..., :half_width]
    upper_half = values[..., half_width:]
    cos_rows = cosine_table[:, None, :]
    sin_rows = sine_table[:, None, :]
    return jnp.concatenate(
        [
            lower_half * cos_rows + upper_half * sin_rows,
            upper_half * cos_rows - lower_half * sin_rows,
        ],
        axis=-1,
    )


def norm_back(values, scale_rows, gain_row, upstream):
    scaled = gain_row * upstream
    gain_grad = jnp.sum(upstream * values * scale_rows, axis=0)
    input_grad = scale_rows * scaled - values * scale_rows**3 * jnp.mean(
        scaled * values, axis=-1, keepdims=True
    )
    return (gain_grad, input_grad)


MESH = pl.DeviceIdType.MESH
NT = (((1,), (1,)), ((), ()))


def flip(index, step):
    return index + step - 2 * step * lax.rem(lax.div(index, step), 2)


def flip_pair(index, turn):
    return index + lax.rem(turn, 2) * (1 - 2 * lax.rem(index, 2)) + lax.div(turn, 2) * (
        2 - 4 * lax.rem(lax.div(index, 2), 2)
    )


def send(source, target, send_sem, recv_sem, device):
    return pltpu.make_async_remote_copy(
        src_ref=source,
        dst_ref=target,
        send_sem=send_sem,
        recv_sem=recv_sem,
        device_id=device,
        device_id_type=MESH,
    )


def greet(devices):
    barrier = pltpu.get_barrier_semaphore()
    for device in devices:
        pl.semaphore_signal(barrier, inc=1, device_id=device, device_id_type=MESH)
    pl.semaphore_wait(barrier, len(devices))

TN = (((0,), (0,)), ((), ()))


class PlaneGather:
    def __init__(self, region, send_sem, recv_sem, me_z, me_e, nbr):
        self.sems = send_sem, recv_sem
        self.region, self.me_z, self.nbr = region, me_z, nbr
        out = {1: (me_e, None, 1), 2: (me_e, None, 2), 3: (me_e, None, 4)}
        out.update({4: (nbr[2], 0, 4), 5: (nbr[4], 1, 2), 6: (nbr[2], None, 1), 7: (nbr[4], None, 1)})
        out.update({8: (nbr[6], 0, 1), 9: (nbr[6], 1, 1)})
        self.out = out
        self.into = {
            1: (nbr[1], None), 2: (nbr[2], None), 3: (nbr[4], None), 4: (nbr[6], 0), 5: (nbr[6], 1),
            6: (nbr[3], None), 7: (nbr[5], None), 8: (nbr[7], 0), 9: (nbr[7], 1),
        }

    def copy(self, channel):
        owner, half, step = self.out[channel]
        ref = self.region(owner, half)
        return send(
            ref, ref, self.sems[0].at[channel], self.sems[1].at[channel], (self.me_z, self.nbr[step])
        )

    def start(self, *channels):
        for channel in channels:
            self.copy(channel).start()

    def wait(self, *channels):
        for channel in channels:
            ref = self.region(*self.into[channel])
            send(
                ref, ref, self.sems[0].at[channel], self.sems[1].at[channel], (self.me_z, self.nbr[1])
            ).wait_recv()

    def begin(self):
        self.start(2, 3, 1)

    def relay(self):
        self.wait(2)
        self.start(4, 6)
        self.wait(3)
        self.start(5, 7)

    def relay_far(self):
        self.wait(4)
        self.start(8)
        self.wait(5)
        self.start(9)

    def finish(self):
        self.wait(1, 6, 7, 8, 9)

    def drain(self):
        for channel in range(1, 10):
            self.copy(channel).wait_send()


def add_rows(target, source, rows):
    @pl.loop(0, rows, step=32)
    def _(row):
        span = pl.ds(pl.multiple_of(row, 32), 32)
        target[span, :] = target[span, :] + source[span, :]


class PlaneScatter:
    def __init__(self, theirs, own, sib, relayed, crossed, sems, place, me_z, nbr):
        self.theirs, self.own, self.sib, self.relayed, self.crossed = theirs, own, sib, relayed, crossed
        self.sems, self.me_z, self.nbr = sems, me_z, nbr
        y, x = place
        self.own_block, self.far_block = 2 * y + x, 2 * (1 - y) + 1 - x
        self.x_block, self.y_block = 2 * y + 1 - x, 2 * (1 - y) + x
        self.rows = crossed.shape[1]

    def copy(self, channel):
        half = self.rows // 2
        low, high = pl.ds(0, half), pl.ds(half, half)
        own, x_block, y_block, far_block = self.own, self.x_block, self.y_block, self.far_block
        if channel == 0:
            source, target, step = self.theirs, self.sib, 1
        elif channel == 1:
            source, target, step = own.at[far_block, low], self.relayed.at[0], 2
        elif channel == 2:
            source, target, step = own.at[far_block, high], self.relayed.at[1], 4
        elif channel == 3:
            source, target, step = own.at[x_block, low], self.crossed.at[0, low], 2
        elif channel == 4:
            source, target, step = own.at[y_block, high], self.crossed.at[1, high], 4
        elif channel == 5:
            source, target, step = own.at[y_block, low], self.crossed.at[1, low], 4
        else:
            source, target, step = own.at[x_block, high], self.crossed.at[0, high], 2
        return send(
            source,
            target,
            self.sems[0].at[channel],
            self.sems[1].at[channel],
            (self.me_z, self.nbr[step]),
        )

    def first(self):
        self.copy(0).start()

    def second(self):
        self.copy(0).wait_recv()
        own, sib = self.own, self.sib
        add_rows(own.at[self.far_block], sib.at[self.far_block], self.rows)
        self.copy(1).start()
        self.copy(2).start()
        add_rows(own.at[self.x_block], sib.at[self.x_block], self.rows)
        self.copy(3).start()
        add_rows(own.at[self.y_block], sib.at[self.y_block], self.rows)
        self.copy(4).start()
        add_rows(own.at[self.own_block], sib.at[self.own_block], self.rows)

    def third(self):
        half = self.rows // 2
        self.copy(1).wait_recv()
        add_rows(self.own.at[self.y_block, pl.ds(0, half)], self.relayed.at[0], half)
        self.copy(2).wait_recv()
        add_rows(self.own.at[self.x_block, pl.ds(half, half)], self.relayed.at[1], half)
        self.copy(5).start()
        self.copy(6).start()

    def fourth(self, store):
        for channel in (3, 4, 5, 6):
            self.copy(channel).wait_recv()

        @pl.loop(0, self.rows, step=32)
        def _(row):
            span = pl.ds(pl.multiple_of(row, 32), 32)
            store(
                span,
                self.own[self.own_block, span, :].astype(jnp.float32)
                + self.crossed[0, span, :].astype(jnp.float32)
                + self.crossed[1, span, :].astype(jnp.float32),
            )

    def drain(self):
        for channel in range(7):
            self.copy(channel).wait_send()


class TileScatter(PlaneScatter):
    def copy(self, channel):
        if channel not in (0, 7):
            return super().copy(channel)
        part = channel // 7
        return send(
            self.theirs.at[part],
            self.sib.at[part],
            self.sems[0].at[channel],
            self.sems[1].at[channel],
            (self.me_z, self.nbr[1]),
        )

    def sum_near(self):
        self.copy(0).wait_recv()
        own, near = self.own, self.sib.at[0]
        add_rows(own.at[self.x_block], near.at[lax.rem(self.x_block, 2)], self.rows)
        self.copy(3).start()
        add_rows(own.at[self.own_block], near.at[lax.rem(self.own_block, 2)], self.rows)

    def sum_far(self):
        self.copy(7).wait_recv()
        own, other = self.own, self.sib.at[1]
        add_rows(own.at[self.far_block], other.at[lax.rem(self.far_block, 2)], self.rows)
        self.copy(1).start()
        self.copy(2).start()
        add_rows(own.at[self.y_block], other.at[lax.rem(self.y_block, 2)], self.rows)
        self.copy(4).start()

    def drain(self):
        for channel in range(1, 7):
            self.copy(channel).wait_send()


class ChainGather:
    def __init__(self, region, send_sem, recv_sem, me_z, me_e):
        self.region, self.sems, self.me_z, self.me_e = region, (send_sem, recv_sem), me_z, me_e

    def copy(self, way, hop):
        step = 1 - 2 * way
        ref = self.region(jnp.clip(self.me_z - step * hop, 0, 3))
        return send(
            ref,
            ref,
            self.sems[0].at[way, hop],
            self.sems[1].at[way, hop],
            (jnp.clip(self.me_z + step, 0, 3), self.me_e),
        )

    def sends(self, way, hop):
        z = self.me_z
        return (z < 3) & (z >= hop) if way == 0 else (z > 0) & (z <= 3 - hop)

    def takes(self, way, hop):
        z = self.me_z
        return z > hop if way == 0 else z < 3 - hop

    def begin(self):
        for way in range(2):
            pl.when(self.sends(way, 0))(self.copy(way, 0).start)

    def hop(self, hop):
        for way in range(2):
            step = 1 - 2 * way
            ref = self.region(jnp.clip(self.me_z - step * (hop + 1), 0, 3))
            arrived = send(
                ref,
                ref,
                self.sems[0].at[way, hop],
                self.sems[1].at[way, hop],
                (jnp.clip(self.me_z - step, 0, 3), self.me_e),
            )
            pl.when(self.takes(way, hop))(arrived.wait_recv)
            if hop < 2:
                pl.when(self.sends(way, hop + 1))(self.copy(way, hop + 1).start)

    def drain(self):
        for hop in range(3):
            for way in range(2):
                pl.when(self.sends(way, hop))(self.copy(way, hop).wait_send)


class ChainScatter:
    def __init__(self, part, landing, add, sems, me_z, me_e):
        self.part, self.landing, self.add = part, landing, add
        self.sems, self.me_z, self.me_e = sems, me_z, me_e

    def copy(self, way, hop, source, owner):
        slot = 4 if way == 1 and hop == 2 else owner
        return send(
            source,
            self.landing.at[slot],
            self.sems[0].at[way, hop],
            self.sems[1].at[way, hop],
            (jnp.clip(self.me_z + 1 - 2 * way, 0, 3), self.me_e),
        )

    def steps(self, hop):
        for way in range(2):
            place = self.me_z if way == 0 else 3 - self.me_z
            owner = jnp.clip(3 - hop + place if way == 0 else hop - place, 0, 3)
            yield way, place, owner

    def hop(self, hop):
        for way, place, owner in self.steps(hop):

            @pl.when(place == 0)
            def _(way=way, owner=owner):
                self.copy(way, hop, self.part(owner), owner).start()

            @pl.when((place > 0) & (place <= hop))
            def _(way=way, owner=owner):
                here = self.landing.at[owner]
                self.copy(way, hop - 1, here, owner).wait_recv()
                self.add(owner, owner)
                self.copy(way, hop, here, owner).start()

    def last(self, low, middle, high):
        up = self.copy(0, 2, self.landing.at[self.me_z], self.me_z)
        down = self.copy(1, 2, self.landing.at[4], 4)
        pl.when(self.me_z > 0)(up.wait_recv)
        pl.when(self.me_z < 3)(down.wait_recv)
        pl.when(self.me_z == 0)(low)
        pl.when((self.me_z > 0) & (self.me_z < 3))(middle)
        pl.when(self.me_z == 3)(high)

    def drain(self):
        for hop in range(3):
            for way, place, owner in self.steps(hop):
                pl.when(place <= hop)(self.copy(way, hop, self.part(owner), owner).wait_send)


def named_of(routes):
    expert = lax.broadcasted_iota(jnp.int32, (8, routes.shape[1]), 0)
    hits = jnp.zeros(expert.shape, jnp.float32)
    for way in range(routes.shape[0]):
        hits = hits + jnp.where(routes[way : way + 1, :] == expert, 1.0, 0.0)
    return hits


def mlp_kernel(
    routed_units,
    _x_in,
    g_all,
    cot,
    w_all,
    up_weight,
    down_weight,
    shared_weight,
    x_all,
    out_part,
    dx_own,
    dg_own,
    d_routed,
    shared_all,
    expert_all,
    w_gu,
    w_d,
    acc_gu,
    acc_d,
    stage,
    x_tile,
    c_tile,
    gu_buf,
    h_buf,
    dgu_buf,
    act_buf,
    out_buf,
    theirs,
    own,
    sib_x,
    relayed,
    crossed,
    sum_x,
    far_x,
    dg_all,
    dg_in,
    dg_sum,
    dg_far,
    a_send,
    a_recv,
    z_send,
    z_recv,
    r_send,
    r_recv,
    fz_send,
    fz_recv,
    dp_send,
    dp_recv,
    dz_send,
    dz_recv,
    local_sem,
):
    me_z = lax.axis_index("dp")
    me_e = lax.axis_index("expert")
    core = lax.rem(me_e, 2)
    me_x = lax.rem(lax.div(me_e, 2), 2)
    me_y = lax.div(me_e, 4)
    nbr = {1: flip(me_e, 1), 2: flip(me_e, 2), 4: flip(me_e, 4)}
    nbr[6] = flip(nbr[2], 4)
    nbr[3], nbr[5], nbr[7] = flip(nbr[2], 1), flip(nbr[4], 1), flip(nbr[6], 1)
    units, width = w_d.shape
    rows = x_all.shape[2]
    tile = 4 * rows
    chunk = 256

    def z_of(turn):
        return flip_pair(me_z, turn)

    def gather(turn):
        where = z_of(turn)

        def region(owner, half):
            if half is None:
                return x_all.at[where, owner]
            return x_all.at[where, owner, pl.ds(half * (rows // 2), rows // 2)]

        return PlaneGather(region, a_send.at[turn], a_recv.at[turn], me_z, me_e, nbr)

    def z_copy(turn, here):
        block = (z_of(turn) if here else me_z, me_e)
        return send(
            x_all.at[block], x_all.at[block], z_send.at[turn], z_recv.at[turn], (z_of(turn), me_e)
        )

    def slot_of(turn):
        return turn - 2 * lax.div(turn, 3)

    def scatter(turn):
        par = lax.rem(turn, 2)
        return TileScatter(
            theirs,
            own.at[slot_of(turn)],
            sib_x.at[par],
            relayed.at[par],
            crossed.at[slot_of(turn)],
            (r_send.at[turn], r_recv.at[turn]),
            (me_y, me_x),
            me_z,
            nbr,
        )

    def far_send(turn):
        return send(
            sum_x.at[turn], far_x.at[turn - 1], fz_send.at[turn], fz_recv.at[turn], (z_of(turn), me_e)
        )

    def plane_sum(turn):
        sums = scatter(turn)

        def store(span, total):
            sum_x[turn, span, :] = total.astype(jnp.bfloat16)

        sums.fourth(store)
        pl.when(turn > 0)(lambda: far_send(turn).start())
        sums.drain()

    greet([(z_of(turn), me_e) for turn in (1, 2, 3)] + [(me_z, nbr[k]) for k in range(1, 8)])
    z_copy(1, False).start()
    shard_width = width // 4
    shared_units = units - routed_units

    def lanes(index):
        return pl.ds(pl.multiple_of(index * shard_width, shard_width), shard_width)

    def lines(index, amount):
        return pl.ds(pl.multiple_of(index * amount, 16), amount)

    w_loads = []
    for part in range(3):
        target, base = (w_d, 0) if part == 2 else (w_gu, part * units)
        routed = pl.ds(base, routed_units)
        own_units = lines(me_z, routed_units)
        pairs = [
            (w_all.at[part, :, lanes(z_of(turn))], target.at[routed, lanes(z_of(turn))])
            for turn in (1, 2, 3)
        ]
        pairs.append(
            (
                down_weight.at[own_units] if part == 2 else up_weight.at[part, own_units],
                target.at[routed, lanes(me_z)],
            )
        )
        pairs.append(
            (
                shared_weight.at[part, lines(me_e, shared_units)],
                target.at[pl.ds(base + routed_units, shared_units)],
            )
        )
        for source, place in pairs:
            w_loads.append(
                pltpu.make_async_copy(source, place, local_sem.at[3 + len(w_loads)])
            )
    for copy in w_loads:
        copy.start()

    @pl.loop(0, 2 * units, step=48)
    def _(row):
        acc_gu[pl.ds(pl.multiple_of(row, 16), 48), :] = jnp.zeros((48, width), jnp.float32)

    @pl.loop(0, units, step=48)
    def _(row):
        acc_d[pl.ds(pl.multiple_of(row, 16), 48), :] = jnp.zeros((48, width), jnp.float32)

    def group_of(half):
        return lax.rem(me_y + half, 2)

    def place_of(index):
        turn = lax.rem(lax.div(index + 1, 2), 4)
        ends = 1 - lax.div(index + 6, 7) + lax.div(index, 7)
        return turn, lax.rem(index + 1 + ends, 2)

    def load(index):
        turn, half = place_of(index)
        block = pl.ds(pl.multiple_of(group_of(half) * 4, 4), 4)
        return (
            pltpu.make_async_copy(x_all.at[z_of(turn), block], x_tile, local_sem.at[0]),
            pltpu.make_async_copy(cot.at[block, z_of(turn)], c_tile, local_sem.at[1]),
        )


    for copy in load(0):
        copy.start()
    for copy in w_loads:
        copy.wait()

    def step(index, carry):
        turn, half = place_of(index)
        slot = slot_of(turn)
        pair, odd = lax.div(index, 2), lax.rem(index, 2)
        where = z_of(turn)
        group = group_of(half)
        block = pl.ds(pl.multiple_of(group * 4, 4), 4)

        for copy in load(index):
            copy.wait()
        for j in range(2):
            xs = x_tile[2 * j : 2 * j + 2].reshape(2 * rows, width)
            cs = c_tile[2 * j : 2 * j + 2].reshape(2 * rows, width)
            gu_buf[:, 2 * rows * j : 2 * rows * (j + 1)] = lax.dot_general(
                w_gu[...], xs, NT, preferred_element_type=jnp.float32
            )
            h_buf[:, 2 * rows * j : 2 * rows * (j + 1)] = lax.dot_general(
                w_d[...], cs, NT, preferred_element_type=jnp.float32
            )

        def gates(row):
            return jnp.concatenate(
                [g_all[group * 4 + j, where, pl.ds(row, 1), :] for j in range(4)], axis=1
            )

        dots = []
        for low, high, gate in (
            (0, routed_units, gates(me_e)),
            (routed_units, units, gates(8)),
        ):
            piece = 16

            def units_step(k, dot, low=low, gate=gate):
                at = pl.multiple_of(low + k * piece, 16)
                g = gu_buf[pl.ds(at, piece), :]
                u = gu_buf[pl.ds(pl.multiple_of(units + at, 16), piece), :]
                h = h_buf[pl.ds(at, piece), :]
                logistic = jax.nn.sigmoid(g)
                silu = g * logistic
                act = silu * u
                act_buf[pl.ds(at, piece), :] = (act * gate).astype(jnp.bfloat16)
                d_act = h * gate
                dgu_buf[pl.ds(at, piece), :] = (
                    d_act * u * (logistic * (1.0 + g * (1.0 - logistic)))
                ).astype(jnp.bfloat16)
                dgu_buf[pl.ds(pl.multiple_of(units + at, 16), piece), :] = (d_act * silu).astype(
                    jnp.bfloat16
                )
                return dot + jnp.sum(act * h, axis=0, keepdims=True)

            dots.append(
                lax.fori_loop(
                    0, (high - low) // piece, units_step, jnp.zeros((1, tile), jnp.float32)
                )
            )
        line = lax.broadcasted_iota(jnp.int32, (8, tile), 0)
        d_gates = jnp.where(line == 0, dots[0], 0.0) + jnp.where(line == 1, dots[1], 0.0)
        for j in range(4):
            dg_all[group * 4 + j, where] = d_gates[:, j * rows : (j + 1) * rows]

        @pl.when(index == 0)
        def _():
            z_copy(1, True).wait_recv()
            gather(1).begin()
            z_copy(2, False).start()

        @pl.when((odd == 1) & (index < 7))
        def _():
            gather(pair + 1).relay_far()

        @pl.when((odd == 1) & (index < 5))
        def _():
            z_copy(pair + 2, True).wait_recv()
            gather(pair + 2).begin()
            pl.when(index == 1)(lambda: z_copy(3, False).start())

        @pl.when((odd == 1) & (index > 4))
        def _():
            plane_sum(pair - 1)

        for n in range(width // chunk):
            cols = slice(n * chunk, (n + 1) * chunk)
            acc_gu[:, cols] += jnp.dot(
                dgu_buf[...], x_tile[:, :, cols].reshape(tile, chunk), preferred_element_type=jnp.float32
            )
            acc_d[:, cols] += jnp.dot(
                act_buf[...], c_tile[:, :, cols].reshape(tile, chunk), preferred_element_type=jnp.float32
            )

        @pl.when((odd == 0) & (index < 6))
        def _():
            gather(pair + 1).relay()
            gather(pair + 1).wait(1, 6)

        @pl.when((odd == 1) & (index < 7))
        def _():
            gather(pair + 1).wait(7, 8, 9)

        @pl.when(index < 7)
        def _():
            for copy in load(index + 1):
                copy.start()

        out_store = pltpu.make_async_copy(out_buf, out_part.at[block, where], local_sem.at[2])

        @pl.when(index > 0)
        def _():
            out_store.wait()

        @pl.when((odd == 1) & (index < 7))
        def _():
            scatter(turn - 1).copy(0).wait_send()

        @pl.when((odd == 0) & (index > 2))
        def _():
            scatter(turn - 1).copy(7).wait_send()

        @pl.when(index == 7)
        def _():
            scatter(3).copy(7).wait_send()

        dgu_t = dgu_buf[...].T
        act_t = act_buf[...].T
        for n in range(width // chunk):
            cols = slice(n * chunk, (n + 1) * chunk)
            dx = jnp.dot(dgu_t, w_gu[:, cols], preferred_element_type=jnp.float32).astype(jnp.bfloat16)
            out = jnp.dot(act_t, w_d[:, cols], preferred_element_type=jnp.float32).astype(jnp.bfloat16)
            for column in range(2):
                core_0 = dx[2 * column * rows : (2 * column + 1) * rows]
                core_1 = dx[(2 * column + 1) * rows : (2 * column + 2) * rows]
                own[slot, 2 * group + column, :, cols] = jnp.where(core == 0, core_0, core_1)
                theirs[half, column, :, cols] = jnp.where(core == 0, core_1, core_0)
            for j in range(4):
                out_buf[j, :, cols] = out[j * rows : (j + 1) * rows]
        out_store.start()

        @pl.when(odd == 1)
        def _():
            pl.when(index == 1)(lambda: scatter(0).sum_near())
            pl.when(index > 2)(lambda: scatter(pair).sum_far())

        @pl.when((odd == 0) & (index > 0))
        def _():
            pl.when(index > 2)(lambda: scatter(pair - 1).third())
            scatter(pair).sum_near()

        pl.when(half == 0)(lambda: scatter(turn).copy(0).start())
        pl.when(half == 1)(lambda: scatter(turn).copy(7).start())
        return carry

    lax.fori_loop(0, 8, step, 0)

    def dp_copy(step, here):
        return send(
            dg_all.at[nbr[step]],
            dg_in.at[nbr[step] if here else me_e],
            dp_send.at[step],
            dp_recv.at[step],
            (me_z, nbr[step]),
        )

    for step_to in range(1, 8):
        dp_copy(step_to, False).start()
    dg_in[me_e] = dg_all[me_e]
    scatter(3).third()
    scatter(0).sum_far()

    depth = stage.shape[1]
    stores = []

    def write_out(part):
        for piece in range(units // depth):
            row, slot = piece * depth, len(stores) % 2
            if len(stores) > 1:
                for copy in stores[-2]:
                    copy.wait()
            if part == 2:
                stage[slot] = acc_d[row : row + depth].astype(jnp.bfloat16)
            else:
                at = part * units + row
                stage[slot] = acc_gu[at : at + depth].astype(jnp.bfloat16)
            if row < routed_units:
                pairs = [
                    (stage.at[slot], d_routed.at[part, pl.ds(row, depth)]),
                    (
                        stage.at[slot, :, lanes(me_z)],
                        expert_all.at[
                            part, pl.ds(pl.multiple_of(me_z * routed_units + row, 16), depth)
                        ],
                    ),
                ]
            else:
                at = pl.multiple_of(me_e * shared_units + row - routed_units, 16)
                pairs = [(stage.at[slot], shared_all.at[part, pl.ds(at, depth)])]
            stores.append(
                [
                    pltpu.make_async_copy(source, place, local_sem.at[2 * slot + 3 + k])
                    for k, (source, place) in enumerate(pairs)
                ]
            )
            for copy in stores[-1]:
                copy.start()

    write_out(0)
    plane_sum(3)
    scatter(0).third()
    for step_to in range(1, 8):
        dp_copy(step_to, True).wait_recv()
    total_shared = dg_in[0, :, 1:2, :]
    for source in range(1, 8):
        total_shared = total_shared + dg_in[source, :, 1:2, :]
    dg_sum[...] = jnp.concatenate(
        [dg_in[source, :, 0:1, :] for source in range(8)]
        + [total_shared, jnp.zeros((4, 7, rows), jnp.float32)],
        axis=1,
    )

    def dz_copy(turn):
        return send(
            dg_sum.at[z_of(turn)],
            dg_far.at[turn - 1],
            dz_send.at[turn],
            dz_recv.at[turn],
            (z_of(turn), me_e),
        )

    for turn in (1, 2, 3):
        dz_copy(turn).start()
    write_out(1)
    plane_sum(0)
    write_out(2)
    pltpu.make_async_copy(out_buf, out_part.at[pl.ds(0, 4), me_z], local_sem.at[2]).wait()
    for turn in (1, 2, 3):
        dz_copy(turn).wait_recv()
    dg_own[...] = dg_sum[me_z] + dg_far[0] + dg_far[1] + dg_far[2]
    for turn in (1, 2, 3):
        far_send(turn).wait_recv()

    @pl.loop(0, rows, step=32)
    def _(row):
        span = pl.ds(pl.multiple_of(row, 32), 32)
        total = sum_x[0, span, :].astype(jnp.float32)
        for turn in range(3):
            total = total + far_x[turn, span, :].astype(jnp.float32)
        dx_own[span, :] = total

    for copy in stores[-2] + stores[-1]:
        copy.wait()
    scatter(3).copy(0).wait_send()
    scatter(0).copy(7).wait_send()
    for turn in (1, 2, 3):
        z_copy(turn, False).wait_send()
        dz_copy(turn).wait_send()
        far_send(turn).wait_send()
    for step_to in range(1, 8):
        dp_copy(step_to, False).wait_send()
    for turn in (1, 2, 3):
        gather(turn).drain()


def mlp_call(x_all, gates_all, all_cot, w_all, up_weight, down_weight, shared_weight):
    num_expert, num_dp, rows, width = all_cot.shape
    routed_units = w_all.shape[1]
    units = routed_units + shared_weight.shape[1] // num_expert
    low, full = jnp.bfloat16, jnp.float32
    shape = jax.ShapeDtypeStruct
    any_space = pl.BlockSpec(memory_space=pl.ANY)
    vmem = pl.BlockSpec(memory_space=pltpu.VMEM)
    dma = pltpu.SemaphoreType.DMA
    flops = 18 * num_expert * num_dp * rows * units * width
    return pl.pallas_call(
        functools.partial(mlp_kernel, routed_units),
        out_shape=(
            shape((num_dp, num_expert, rows, width), low),
            shape((num_expert, num_dp, rows, width), low),
            shape((rows, width), full),
            shape((16, rows), full),
            shape((3, routed_units, width), low),
            shape(shared_weight.shape, low),
            shape((3, num_dp * routed_units, width // num_dp), low),
        ),
        in_specs=[any_space, vmem] + [any_space] * 5,
        input_output_aliases={0: 0},
        out_specs=(any_space, any_space, vmem, vmem, any_space, any_space, any_space),
        scratch_shapes=[
            pltpu.VMEM((2 * units, width), low),
            pltpu.VMEM((units, width), low),
            pltpu.VMEM((2 * units, width), full),
            pltpu.VMEM((units, width), full),
            pltpu.VMEM((2, units - routed_units, width), low),
            pltpu.VMEM((4, rows, width), low),
            pltpu.VMEM((4, rows, width), low),
            pltpu.VMEM((2 * units, 4 * rows), full),
            pltpu.VMEM((units, 4 * rows), full),
            pltpu.VMEM((2 * units, 4 * rows), low),
            pltpu.VMEM((units, 4 * rows), low),
            pltpu.VMEM((4, rows, width), low),
            pltpu.VMEM((2, 2, rows, width), low),
            pltpu.VMEM((3, 4, rows, width), low),
            pltpu.VMEM((2, 2, 2, rows, width), low),
            pltpu.VMEM((2, 2, rows // 2, width), low),
            pltpu.VMEM((3, 2, rows, width), low),
            pltpu.VMEM((4, rows, width), low),
            pltpu.VMEM((3, rows, width), low),
            pltpu.VMEM((num_expert, num_dp, 8, rows), full),
            pltpu.VMEM((num_expert, num_dp, 8, rows), full),
            pltpu.VMEM((num_dp, 16, rows), full),
            pltpu.VMEM((3, 16, rows), full),
            dma((4, 10)),
            dma((4, 10)),
            dma((4,)),
            dma((4,)),
            dma((4, 8)),
            dma((4, 8)),
            dma((4,)),
            dma((4,)),
            dma((8,)),
            dma((8,)),
            dma((4,)),
            dma((4,)),
            dma((18,)),
        ],
        compiler_params=pltpu.CompilerParams(
            collective_id=0, has_side_effects=True, vmem_limit_bytes=63 * 2**20
        ),
        cost_estimate=pl.CostEstimate(flops=flops, bytes_accessed=80 * 2**20, transcendentals=0),
    )(x_all, gates_all, all_cot, w_all, up_weight, down_weight, shared_weight)


def swap_halves(values):
    half = values.shape[-1] // 2
    return jnp.concatenate([values[:, half:], values[:, :half]], axis=1)


def tail_kernel(
    mixed,
    qkv,
    probs,
    normed,
    w_qkv,
    w_out,
    tables,
    tokens,
    params,
    d_rows,
    d_gates,
    routes,
    router_probs,
    normed_two,
    hidden,
    cotangent,
    out_part,
    d_routed,
    _shared_in,
    _expert_in,
    output,
    tokens_grad,
    small_out,
    attn_all,
    shared_all,
    expert_all,
    rows_all,
    normed_part,
    d_mixed,
    d_qkv,
    out_grad,
    grads,
    grads_in,
    out_in,
    grads_sum,
    n_sib,
    n_relayed,
    n_crossed,
    f_own,
    f_sib,
    f_relayed,
    f_crossed,
    f_sum,
    f_far,
    d_normed,
    small,
    small_far,
    small_plane,
    e_send,
    e_recv,
    a_send,
    a_recv,
    o_send,
    o_recv,
    z_send,
    z_recv,
    y_send,
    y_recv,
    n_send,
    n_recv,
    f_send,
    f_recv,
    fz_send,
    fz_recv,
    s_send,
    s_recv,
    g_send,
    g_recv,
    h_send,
    h_recv,
    t_send,
    t_recv,
    p_send,
    p_recv,
    local_sem,
):
    me_z = lax.axis_index("dp")
    me_e = lax.axis_index("expert")
    core = lax.rem(me_e, 2)
    me_x = lax.rem(lax.div(me_e, 2), 2)
    me_y = lax.div(me_e, 4)
    nbr = {1: flip(me_e, 1), 2: flip(me_e, 2), 4: flip(me_e, 4)}
    nbr[6] = flip(nbr[2], 4)
    nbr[3], nbr[5], nbr[7] = flip(nbr[2], 1), flip(nbr[4], 1), flip(nbr[6], 1)
    far = {turn: flip_pair(me_z, turn) for turn in (1, 2, 3)}
    where = {0: me_z, **far}
    rows, width = tokens.shape
    head_width = mixed.shape[1]
    shard_width = width // 4
    routed_units = d_routed.shape[1]
    units = shared_all.shape[1] // 8
    heads = head_width // HEAD
    sequences = 8
    score_scale = HEAD ** (-0.5)

    greet([(far[turn], me_e) for turn in (1, 2, 3)] + [(me_z, nbr[k]) for k in range(1, 8)])

    def lanes(index, amount):
        return pl.ds(pl.multiple_of(index * amount, amount), amount)

    def expert_send(part, turn):
        return send(
            d_routed.at[part, :, lanes(far[turn], shard_width)],
            expert_all.at[part, pl.ds(pl.multiple_of(me_z * routed_units, 16), routed_units)],
            e_send.at[part, turn],
            e_recv.at[part, turn],
            (far[turn], me_e),
        )

    def expert_wait(part, turn):
        here = expert_all.at[part, pl.ds(pl.multiple_of(far[turn] * routed_units, 16), routed_units)]
        send(here, here, e_send.at[part, turn], e_recv.at[part, turn], (far[turn], me_e)).wait_recv()

    split = units // 32 * 16

    def shared_region(owner, half):
        base = pl.multiple_of(owner * units, 16)
        if half is None:
            return shared_all.at[:, pl.ds(base, units)]
        if half == 0:
            return shared_all.at[:, pl.ds(base, split)]
        return shared_all.at[:, pl.ds(pl.multiple_of(base + split, 16), units - split)]

    shared = PlaneGather(shared_region, s_send, s_recv, me_z, me_e, nbr)

    def rows_region(owner, half):
        if half is None:
            return rows_all.at[owner]
        return rows_all.at[owner, pl.ds(half * (rows // 2), rows // 2)]

    gather = PlaneGather(rows_region, a_send, a_recv, me_z, me_e, nbr)
    forward = {
        turn: PlaneScatter(
            out_part.at[:, 1 - core, where[turn]],
            f_own.at[turn % 2],
            f_sib.at[turn],
            f_relayed.at[turn],
            f_crossed.at[turn],
            (f_send.at[turn], f_recv.at[turn]),
            (me_y, me_x),
            me_z,
            nbr,
        )
        for turn in range(4)
    }

    def forward_load(turn):
        return pltpu.make_async_copy(
            out_part.at[:, core, where[turn]], f_own.at[turn % 2], local_sem.at[3 + turn % 2]
        )

    def far_send(turn):
        return send(
            f_sum.at[turn], f_far.at[turn - 1], fz_send.at[turn], fz_recv.at[turn], (where[turn], me_e)
        )

    def forward_last(turn):
        def store(span, total):
            f_sum[turn, span, :] = total.astype(jnp.bfloat16)

        forward[turn].fourth(store)
        if turn:
            far_send(turn).start()

    forward_load(1).start()
    forward_load(2).start()
    forward[1].first()
    forward[2].first()

    top, gate = router_probs[:8], router_probs[8:9]
    d_top = d_gates[:8] * named_of(routes)
    d_logits = top * (d_top - jnp.sum(top * d_top, axis=0, keepdims=True))
    line = lax.broadcasted_iota(jnp.int32, (8, rows), 0)
    d_rest = jnp.where(line == 0, d_gates[8:9] * gate * (1.0 - gate), 0.0)
    d_route = jnp.concatenate([d_logits, d_rest], axis=0).astype(jnp.bfloat16)
    small[...] = jnp.dot(d_route, normed_two[...], preferred_element_type=jnp.float32)
    d_normed[...] = d_rows[...] + lax.dot_general(
        d_route, params[...], TN, preferred_element_type=jnp.float32
    )
    gains = params[...].astype(jnp.float32)

    def norm_back_rows(value, up, gain):
        scale = lax.rsqrt(jnp.mean(value * value, axis=-1, keepdims=True) + EPS)
        scaled = gain * up
        grad = scale * scaled - value * (scale * scale * scale) * jnp.mean(
            scaled * value, axis=-1, keepdims=True
        )
        return grad, jnp.sum(up * value * scale, axis=0, keepdims=True)

    def hidden_step(index, gain_sum):
        span = pl.ds(pl.multiple_of(index * 16, 16), 16)
        grad, term = norm_back_rows(hidden[span, :], d_normed[span, :], gains[10:11])
        grad = cotangent[span, :].astype(jnp.float32) + grad
        tokens_grad[span, :] = grad
        rows_all[me_e, span, :] = grad.astype(jnp.bfloat16)
        return gain_sum + term

    small[10:11, :] = lax.fori_loop(0, rows // 16, hidden_step, jnp.zeros((1, width), jnp.float32))
    gather.begin()
    for part in range(3):
        for turn in (1, 2, 3):
            expert_send(part, turn).start()
    gather.relay()
    forward_load(1).wait()
    forward[1].second()
    gather.relay_far()
    gather.finish()
    forward[1].third()
    forward[3].first()
    forward[0].first()

    all_rows = sequences * rows
    d_mixed[...] = lax.dot_general(
        rows_all[...].reshape(all_rows, width), w_out[...], NT, preferred_element_type=jnp.float32
    ).astype(jnp.bfloat16)
    for n in range(4):
        cols = slice(n * shard_width, (n + 1) * shard_width)
        out_grad[:, cols] = lax.dot_general(
            mixed[...],
            rows_all[:, :, cols].reshape(all_rows, shard_width),
            TN,
            preferred_element_type=jnp.float32,
        ).astype(jnp.bfloat16)
    span_out = pl.ds(pl.multiple_of(me_e * head_width, head_width), head_width)

    def out_send(step):
        return send(
            out_grad.at[:, lanes(nbr[step], head_width)],
            grads.at[3, span_out],
            o_send.at[step],
            o_recv.at[step],
            (me_z, nbr[step]),
        )

    for step in range(1, 8):
        out_send(step).start()
    grads[3, span_out, :] = out_grad[:, lanes(me_e, head_width)]
    forward_load(2).wait()
    forward[2].second()
    forward_last(1)

    def chain_of(first, amount, landing, sems):
        def part(owner):
            return grads.at[
                pl.ds(first, amount), pl.ds(pl.multiple_of(owner * shard_width, shard_width), shard_width)
            ]

        def add(slot, owner):
            for index in range(amount):

                @pl.loop(0, shard_width, step=64)
                def _(row, index=index):
                    span = pl.ds(pl.multiple_of(row, 64), 64)
                    theirs = pl.ds(pl.multiple_of(owner * shard_width + row, 64), 64)
                    landing[slot, index, span, :] = (
                        landing[slot, index, span, :] + grads[first + index, theirs, :]
                    )

        def total(*slots):
            for index in range(amount):

                @pl.loop(0, shard_width, step=64)
                def _(row, index=index):
                    span = pl.ds(pl.multiple_of(row, 64), 64)
                    own = pl.ds(pl.multiple_of(me_z * shard_width + row, 64), 64)
                    value = grads[first + index, own, :].astype(jnp.float32)
                    for slot in slots:
                        value = value + landing[slot, index, span, :].astype(jnp.float32)
                    grads_sum[first + index, span, :] = value.astype(jnp.bfloat16)

        chain = ChainScatter(part, landing, add, sems, me_z, me_e)
        last = (lambda: total(4), lambda: total(me_z, 4), lambda: total(me_z))
        return chain, lambda: chain.last(*last)

    chain, chain_last = chain_of(0, 3, grads_in, (z_send, z_recv))
    out_chain, out_chain_last = chain_of(3, 1, out_in, (y_send, y_recv))

    def projections_of(first, amount, sems, place):
        def region(owner, half):
            cols = lanes(owner, head_width)
            if half is None:
                return attn_all.at[pl.ds(first, amount), :, cols]
            return attn_all.at[
                pl.ds(first, amount), pl.ds(half * (shard_width // 2), shard_width // 2), cols
            ]

        own = pltpu.make_async_copy(
            grads_sum.at[pl.ds(first, amount)], region(me_e, None), local_sem.at[place]
        )
        return own, PlaneGather(region, *sems, me_z, me_e, nbr)

    qkv_own, projections = projections_of(0, 3, (g_send, g_recv), 2)
    out_own, out_projection = projections_of(3, 1, (h_send, h_recv), 7)

    def sequence(index, carry):
        span = pl.ds(pl.multiple_of(index * rows, rows), rows)
        for head in range(heads):
            cols = slice(head * HEAD, (head + 1) * HEAD)
            query, key, value = qkv[0, span, cols], qkv[1, span, cols], qkv[2, span, cols]
            up = d_mixed[span, cols]
            weights = probs[index * heads + head]
            values_grad = lax.dot_general(
                weights.astype(jnp.bfloat16), up, TN, preferred_element_type=jnp.float32
            )
            d_probs = lax.dot_general(up, value, NT, preferred_element_type=jnp.float32)
            d_scores = (
                weights * (d_probs - jnp.sum(weights * d_probs, axis=-1, keepdims=True))
            ).astype(jnp.bfloat16)
            d_query = jnp.dot(d_scores, key, preferred_element_type=jnp.float32) * score_scale
            d_key = (
                lax.dot_general(d_scores, query, TN, preferred_element_type=jnp.float32)
                * score_scale
            )
            d_query = d_query * tables[0] - swap_halves(d_query) * tables[1]
            d_key = d_key * tables[0] - swap_halves(d_key) * tables[1]
            for part, value_of in enumerate((d_query, d_key, values_grad)):
                base = part * head_width + head * HEAD
                d_qkv[span, base : base + HEAD] = value_of.astype(jnp.bfloat16)
        return carry

    def normed_load(n):
        return pltpu.make_async_copy(
            normed.at[:, n * 256 : (n + 1) * 256], normed_part.at[n % 2], local_sem.at[5 + n % 2]
        )

    normed_load(0).start()
    lax.fori_loop(0, sequences // 2, sequence, 0)
    for step in range(1, 8):
        here = grads.at[3, pl.ds(pl.multiple_of(nbr[step] * head_width, head_width), head_width)]
        send(here, here, o_send.at[step], o_recv.at[step], (me_z, nbr[step])).wait_recv()
    out_chain.hop(0)
    shared.begin()
    forward[2].third()
    lax.fori_loop(sequences // 2, sequences, sequence, 0)

    for n in range(width // 256):
        cols = slice(n * 256, (n + 1) * 256)
        if n < width // 256 - 1:
            normed_load(n + 1).start()
        normed_load(n).wait()
        term = lax.dot_general(
            normed_part[n % 2], d_qkv[...], TN, preferred_element_type=jnp.float32
        ).astype(jnp.bfloat16)
        for part in range(3):
            grads[part, cols, :] = term[:, part * head_width : (part + 1) * head_width]
    chain.hop(0)
    out_chain.hop(1)
    gather.drain()

    for n in range(width // 256):
        cols = slice(n * 256, (n + 1) * 256)
        term = lax.dot_general(
            d_qkv[...], w_qkv[cols, : 3 * head_width], NT, preferred_element_type=jnp.float32
        ).astype(jnp.bfloat16)
        for owner in range(8):
            mine = lax.rem(owner + core + 1, 2)
            rows_all[4 * mine + owner // 2, :, cols] = term[owner * rows : (owner + 1) * rows]
    back = PlaneScatter(
        rows_all.at[pl.ds(0, 4)],
        rows_all.at[pl.ds(4, 4)],
        n_sib,
        n_relayed,
        n_crossed,
        (n_send, n_recv),
        (me_y, me_x),
        me_z,
        nbr,
    )
    def keep(span, total):
        d_normed[span, :] = total

    def norm_step(index, gain_sum):
        span = pl.ds(pl.multiple_of(index * 16, 16), 16)
        grad, term = norm_back_rows(
            tokens[span, :].astype(jnp.float32), d_normed[span, :], gains[9:10]
        )
        tokens_grad[span, :] = tokens_grad[span, :] + grad
        return gain_sum + term

    def small_send(turn):
        return send(
            small.at[:, lanes(far[turn], shard_width)],
            small_far.at[turn],
            t_send.at[turn],
            t_recv.at[turn],
            (far[turn], me_e),
        )

    def plane_send(step):
        return send(
            small_plane.at[me_e],
            small_plane.at[me_e],
            p_send.at[step],
            p_recv.at[step],
            (me_z, nbr[step]),
        )

    back.first()
    bias_terms = jnp.sum(d_qkv[...].astype(jnp.float32), axis=0, keepdims=True)
    for part in range(3):
        small[11 + part : 12 + part, lanes(me_e, head_width)] = bias_terms[
            :, part * head_width : (part + 1) * head_width
        ]
    back.second()
    out_chain.hop(2)
    chain.hop(1)
    out_chain_last()
    out_own.start()
    out_own.wait()
    out_projection.begin()
    back.third()
    out_projection.relay()
    chain.hop(2)
    out_projection.relay_far()
    shared.relay()
    back.fourth(keep)
    small[9:10, :] = lax.fori_loop(0, rows // 16, norm_step, jnp.zeros((1, width), jnp.float32))
    for turn in (1, 2, 3):
        small_send(turn).start()
    forward_last(2)
    forward[1].drain()
    forward_load(3).start()
    forward_load(3).wait()
    forward[3].second()
    forward[2].drain()
    forward_load(0).start()
    chain_last()
    qkv_own.start()
    qkv_own.wait()
    projections.begin()
    forward[3].third()
    forward_load(0).wait()
    forward[0].second()
    for turn in (1, 2, 3):
        small_send(turn).wait_recv()
    small_plane[me_e] = (
        small[:, lanes(me_z, shard_width)] + small_far[1] + small_far[2] + small_far[3]
    )
    for step in range(1, 8):
        plane_send(step).start()
    shared.relay_far()
    projections.relay()
    forward_last(3)
    forward[0].third()
    for step in range(1, 8):
        here = small_plane.at[nbr[step]]
        send(here, here, p_send.at[step], p_recv.at[step], (me_z, nbr[step])).wait_recv()
    total = small_plane[0]
    for index in range(1, 8):
        total = total + small_plane[index]
    small_out[...] = total
    forward_last(0)
    for turn in (1, 2, 3):
        far_send(turn).wait_recv()

    @pl.loop(0, rows, step=32)
    def _(row):
        span = pl.ds(pl.multiple_of(row, 32), 32)
        total = f_sum[0, span, :].astype(jnp.float32)
        for turn in (1, 2, 3):
            total = total + f_far[turn - 1, span, :].astype(jnp.float32)
        output[span, :] = (hidden[span, :] + total).astype(jnp.bfloat16)

    projections.relay_far()
    shared.finish()
    projections.finish()
    out_projection.finish()
    for turn in (1, 2, 3):
        for part in range(3):
            expert_wait(part, turn)
            expert_send(part, turn).wait_send()
        small_send(turn).wait_send()
        far_send(turn).wait_send()
    for step in range(1, 8):
        out_send(step).wait_send()
        plane_send(step).wait_send()
    for turn in (3, 0):
        forward[turn].drain()
    chain.drain()
    out_chain.drain()
    out_projection.drain()
    back.drain()
    shared.drain()
    projections.drain()


def tail_call(
    mixed, qkv, probs, normed, w_qkv, w_out, tables, tokens, params, d_rows, d_gates, routes, router_probs,
    normed_two, hidden, cotangent, out_part, d_routed, shared_all, expert_all,
):
    rows, width = tokens.shape
    head_width = mixed.shape[1]
    shard_width = width // 4
    low, full = jnp.bfloat16, jnp.float32
    shape = jax.ShapeDtypeStruct
    any_space = pl.BlockSpec(memory_space=pl.ANY)
    vmem = pl.BlockSpec(memory_space=pltpu.VMEM)
    dma = pltpu.SemaphoreType.DMA
    return pl.pallas_call(
        tail_kernel,
        out_shape=(
            shape((rows, width), low),
            shape((rows, width), full),
            shape((16, shard_width), full),
            shape((4, shard_width, width), low),
            shape(shared_all.shape, low),
            shape(expert_all.shape, low),
        ),
        in_specs=[vmem] * 3 + [any_space] + [vmem] * 12 + [any_space] * 4,
        input_output_aliases={18: 4, 19: 5},
        out_specs=(vmem, vmem, vmem, any_space, any_space, any_space),
        scratch_shapes=[
            pltpu.VMEM((8, rows, width), low),
            pltpu.VMEM((2, 8 * rows, 256), low),
            pltpu.VMEM((8 * rows, head_width), low),
            pltpu.VMEM((8 * rows, 3 * head_width), low),
            pltpu.VMEM((head_width, width), low),
            pltpu.VMEM((4, width, head_width), low),
            pltpu.VMEM((5, 3, shard_width, head_width), low),
            pltpu.VMEM((5, 1, shard_width, head_width), low),
            pltpu.VMEM((4, shard_width, head_width), low),
            pltpu.VMEM((4, rows, width), low),
            pltpu.VMEM((2, rows // 2, width), low),
            pltpu.VMEM((2, rows, width), low),
            pltpu.VMEM((2, 4, rows, width), low),
            pltpu.VMEM((4, 4, rows, width), low),
            pltpu.VMEM((4, 2, rows // 2, width), low),
            pltpu.VMEM((4, 2, rows, width), low),
            pltpu.VMEM((4, rows, width), low),
            pltpu.VMEM((3, rows, width), low),
            pltpu.VMEM((rows, width), full),
            pltpu.VMEM((16, width), full),
            pltpu.VMEM((4, 16, shard_width), full),
            pltpu.VMEM((8, 16, shard_width), full),
            dma((3, 4)),
            dma((3, 4)),
            dma((10,)),
            dma((10,)),
            dma((8,)),
            dma((8,)),
            dma((2, 3)),
            dma((2, 3)),
            dma((2, 3)),
            dma((2, 3)),
            dma((7,)),
            dma((7,)),
            dma((4, 7)),
            dma((4, 7)),
            dma((4,)),
            dma((4,)),
            dma((10,)),
            dma((10,)),
            dma((10,)),
            dma((10,)),
            dma((10,)),
            dma((10,)),
            dma((4,)),
            dma((4,)),
            dma((8,)),
            dma((8,)),
            dma((8,)),
        ],
        compiler_params=pltpu.CompilerParams(
            collective_id=1, has_side_effects=True, vmem_limit_bytes=63 * 2**20
        ),
        cost_estimate=pl.CostEstimate(
            flops=24 * 8 * rows * width * head_width, bytes_accessed=80 * 2**20, transcendentals=0
        ),
    )(
        mixed, qkv, probs, normed, w_qkv, w_out, tables, tokens, params, d_rows, d_gates, routes, router_probs,
        normed_two, hidden, cotangent, out_part, d_routed, shared_all, expert_all,
    )


def front_kernel(
    tokens,
    docs,
    routes,
    router,
    gate_vector,
    gain_in,
    gain_out,
    bias_in,
    tables,
    cotangent,
    qkv_weight,
    out_weight,
    up_weight,
    down_weight,
    qkv,
    probs,
    mixed,
    normed,
    hidden,
    normed_two,
    gates_all,
    router_probs,
    params_all,
    weights_out,
    w_out_out,
    cot_all,
    w_all,
    x_all,
    rows_all,
    weights,
    w_out,
    params_in,
    docs_all,
    gates_in,
    qkv_part,
    n_sib,
    n_relayed,
    n_crossed,
    a_send,
    a_recv,
    w_send,
    w_recv,
    p_send,
    p_recv,
    d_send,
    d_recv,
    o_send,
    o_recv,
    n_send,
    n_recv,
    c_send,
    c_recv,
    k_send,
    k_recv,
    e_send,
    e_recv,
    x_send,
    x_recv,
    y_send,
    y_recv,
    g_send,
    g_recv,
    local_sem,
):
    me_z = lax.axis_index("dp")
    me_e = lax.axis_index("expert")
    core = lax.rem(me_e, 2)
    me_x = lax.rem(lax.div(me_e, 2), 2)
    me_y = lax.div(me_e, 4)
    nbr = {1: flip(me_e, 1), 2: flip(me_e, 2), 4: flip(me_e, 4)}
    nbr[6] = flip(nbr[2], 4)
    nbr[3], nbr[5], nbr[7] = flip(nbr[2], 1), flip(nbr[4], 1), flip(nbr[6], 1)
    far = {turn: flip_pair(me_z, turn) for turn in (1, 2, 3)}
    rows, width = tokens.shape
    shard_width = qkv_weight.shape[0]
    head_width = w_out.shape[0]
    heads = head_width // HEAD
    routed_units = down_weight.shape[0] // 4
    sequences = 8
    score_scale = HEAD ** (-0.5)

    def lanes(index, amount):
        return pl.ds(pl.multiple_of(index * amount, amount), amount)

    def lines(index, amount, grain=16):
        return pl.ds(pl.multiple_of(index * amount, grain), amount)

    my_lines = lines(me_z, shard_width)
    own = [
        pltpu.make_async_copy(
            qkv_weight.at[:, pl.ds(pl.multiple_of(part * width + me_e * head_width, head_width), head_width)],
            weights.at[my_lines, part * head_width : (part + 1) * head_width],
            local_sem.at[part],
        )
        for part in range(3)
    ]
    own.append(
        pltpu.make_async_copy(
            out_weight.at[:, lanes(me_e, head_width)],
            weights.at[my_lines, 3 * head_width : 4 * head_width],
            local_sem.at[3],
        )
    )
    own.append(pltpu.make_async_copy(tokens, rows_all.at[me_e], local_sem.at[4]))
    own.append(pltpu.make_async_copy(cotangent, cot_all.at[me_e, me_z], local_sem.at[5]))
    for copy in own:
        copy.start()
    shards = [router[...]] + [ref[...].reshape(1, shard_width) for ref in (gate_vector, gain_in, gain_out)]
    shards = [part.astype(jnp.float32) for part in shards + [bias_in[...]]]
    shards.append(jnp.zeros((2, shard_width), jnp.float32))
    params_in[me_z] = jnp.concatenate(shards, axis=0).astype(jnp.bfloat16)
    docs_all[me_e] = jnp.broadcast_to(docs[...].astype(jnp.float32), docs_all.shape[1:])
    greet([(far[turn], me_e) for turn in (1, 2, 3)] + [(me_z, nbr[k]) for k in range(1, 8)])
    for copy in own:
        copy.wait()

    attn_weights = ChainGather(
        lambda z: weights.at[lines(z, shard_width)], w_send, w_recv, me_z, me_e
    )
    attn_weights.begin()
    cot_chain = ChainGather(lambda z: cot_all.at[me_e, z], k_send, k_recv, me_z, me_e)
    cot_chain.begin()

    def cot_gather(place, z):
        def region(owner, half):
            if half is None:
                return cot_all.at[owner, z]
            return cot_all.at[owner, z, pl.ds(half * (rows // 2), rows // 2)]

        return PlaneGather(region, c_send.at[place], c_recv.at[place], me_z, me_e, nbr)

    cot_own = cot_gather(6, me_z)

    def cot_step(hop, name):
        for way in range(2):
            z = jnp.clip(me_z - (1 - 2 * way) * (hop + 1), 0, 3)
            pl.when(cot_chain.takes(way, hop))(getattr(cot_gather(way * 3 + hop, z), name))

    def expert_copy(part, turn, here):
        source = down_weight if part == 2 else up_weight.at[part]
        z = far[turn] if here else me_z
        target = w_all.at[part, :, lanes(z, shard_width)]
        return send(
            target if here else source.at[lines(far[turn], routed_units)],
            target,
            e_send.at[part, turn],
            e_recv.at[part, turn],
            (far[turn], me_e),
        )

    ends = (me_z == 0) | (me_z == 3)

    def expert_start(turn, from_ends):
        @pl.when(ends if from_ends else jnp.logical_not(ends))
        def _():
            for part in range(3):
                expert_copy(part, turn, False).start()

    def rows_region(owner, half):
        if half is None:
            return rows_all.at[owner]
        return rows_all.at[owner, pl.ds(half * (rows // 2), rows // 2)]

    gather = PlaneGather(rows_region, a_send, a_recv, me_z, me_e, nbr)

    def params_send(turn):
        return send(
            params_in.at[me_z], params_in.at[me_z], p_send.at[turn], p_recv.at[turn], (far[turn], me_e)
        )

    def docs_send(step):
        return send(
            docs_all.at[me_e], docs_all.at[me_e], d_send.at[step], d_recv.at[step], (me_z, nbr[step])
        )

    for turn in (1, 2, 3):
        params_send(turn).start()
    gather.begin()
    for step in range(1, 8):
        docs_send(step).start()
    cot_own.begin()
    gather.relay()
    cot_chain.hop(0)
    cot_step(0, "begin")
    gather.relay_far()
    cot_own.relay()
    for turn in (1, 2, 3):
        here = params_in.at[far[turn]]
        send(here, here, p_send.at[turn], p_recv.at[turn], (far[turn], me_e)).wait_recv()
    params_all[...] = jnp.concatenate([params_in[z] for z in range(4)], axis=1)
    gather.finish()
    attn_weights.hop(0)
    cot_own.relay_far()
    cot_chain.hop(1)
    cot_step(0, "relay")
    cot_step(1, "begin")

    def norm_rows(value, gain):
        scale = lax.rsqrt(jnp.mean(value * value, axis=-1, keepdims=True) + EPS)
        return (value * scale * gain).astype(jnp.bfloat16)

    params_full = params_all[...].astype(jnp.float32)
    gain_one, gain_two = params_full[9:10], params_full[10:11]
    bias = params_all[:, lanes(me_e, head_width)].astype(jnp.float32)[11:14]

    for owner in range(8):

        @pl.loop(0, rows, step=16)
        def _(row, owner=owner):
            span = pl.ds(pl.multiple_of(row, 16), 16)
            normed[pl.ds(pl.multiple_of(owner * rows + row, 16), 16), :] = norm_rows(
                rows_all[owner, span, :].astype(jnp.float32), gain_one
            )

    cot_step(0, "relay_far")
    attn_weights.hop(1)
    expert_start(1, True)
    expert_start(2, True)
    expert_start(3, False)
    cot_chain.hop(2)

    cot_step(1, "relay")
    cot_step(2, "begin")
    attn_weights.hop(2)
    expert_start(1, False)
    expert_start(2, False)
    expert_start(3, True)

    def out_send(step):
        return send(
            weights.at[lines(nbr[step], head_width), 3 * head_width : 4 * head_width],
            w_out.at[:, lanes(me_e, head_width)],
            o_send.at[step],
            o_recv.at[step],
            (me_z, nbr[step]),
        )

    for step in range(1, 8):
        out_send(step).start()
    w_out[:, lanes(me_e, head_width)] = weights[lines(me_e, head_width), 3 * head_width :]
    weights_store = pltpu.make_async_copy(weights, weights_out, local_sem.at[0])
    weights_store.start()

    for part in range(3):
        cols = slice(part * head_width, (part + 1) * head_width)
        qkv_part[...] = (
            jnp.dot(normed[...], weights[:, cols], preferred_element_type=jnp.float32)
            + bias[part : part + 1]
        )
        if part == 2:
            qkv[part] = qkv_part[...].astype(jnp.bfloat16)
        else:

            @pl.loop(0, sequences)
            def _(index, part=part):
                span = pl.ds(pl.multiple_of(index * rows, rows), rows)
                for head in range(heads):
                    at = slice(head * HEAD, (head + 1) * HEAD)
                    value = qkv_part[span, at]
                    qkv[part, span, at] = (
                        value * tables[0] + swap_halves(value) * tables[1]
                    ).astype(jnp.bfloat16)

    order = lax.broadcasted_iota(jnp.int32, (rows, rows), 0) >= lax.broadcasted_iota(
        jnp.int32, (rows, rows), 1
    )

    def sequence(index, carry):
        span = pl.ds(pl.multiple_of(index * rows, rows), rows)
        doc = jnp.broadcast_to(docs_all[index, 0:1, :], (rows, rows))
        allowed = (doc == doc.T) & order
        for head in range(heads):
            at = slice(head * HEAD, (head + 1) * HEAD)
            scores = (
                lax.dot_general(
                    qkv[0, span, at], qkv[1, span, at], NT, preferred_element_type=jnp.float32
                )
                * score_scale
            )
            scores = jnp.where(allowed, scores, NEGATIVE)
            exp_scores = jnp.exp(scores - jnp.max(scores, axis=-1, keepdims=True))
            weight = exp_scores / jnp.sum(exp_scores, axis=-1, keepdims=True)
            probs[index * heads + head] = weight
            mixed[span, at] = jnp.dot(
                weight.astype(jnp.bfloat16), qkv[2, span, at], preferred_element_type=jnp.float32
            ).astype(jnp.bfloat16)
        return carry

    cot_step(1, "relay_far")
    cot_step(2, "relay")
    for step in range(1, 8):
        here = docs_all.at[nbr[step]]
        send(here, here, d_send.at[step], d_recv.at[step], (me_z, nbr[step])).wait_recv()
    lax.fori_loop(0, sequences // 2, sequence, 0)
    cot_step(2, "relay_far")
    lax.fori_loop(sequences // 2, sequences, sequence, 0)
    gather.drain()

    for step in range(1, 8):
        here = w_out.at[:, lanes(nbr[step], head_width)]
        send(here, here, o_send.at[step], o_recv.at[step], (me_z, nbr[step])).wait_recv()
    for n in range(width // shard_width):
        cols = slice(n * shard_width, (n + 1) * shard_width)
        term = jnp.dot(mixed[...], w_out[:, cols], preferred_element_type=jnp.float32).astype(
            jnp.bfloat16
        )
        for owner in range(8):
            mine = lax.rem(owner + core + 1, 2)
            rows_all[4 * mine + owner // 2, :, cols] = term[owner * rows : (owner + 1) * rows]
    sums = PlaneScatter(
        rows_all.at[pl.ds(0, 4)],
        rows_all.at[pl.ds(4, 4)],
        n_sib,
        n_relayed,
        n_crossed,
        (n_send, n_recv),
        (me_y, me_x),
        me_z,
        nbr,
    )
    sums.first()
    out_store = pltpu.make_async_copy(w_out, w_out_out, local_sem.at[1])
    out_store.start()
    sums.second()

    sums.third()

    def keep(span, total):
        hidden[span, :] = total + tokens[span, :].astype(jnp.float32)

    sums.fourth(keep)

    @pl.loop(0, rows, step=16)
    def _(row):
        span = pl.ds(pl.multiple_of(row, 16), 16)
        normed_two[span, :] = norm_rows(hidden[span, :], gain_two)

    logits = lax.dot_general(
        params_all[...], normed_two[...], NT, preferred_element_type=jnp.float32
    )
    top = jnp.exp(logits[:8] - jnp.max(logits[:8], axis=0, keepdims=True))
    top = top / jnp.sum(top, axis=0, keepdims=True)
    line = lax.broadcasted_iota(jnp.int32, (8, rows), 0)
    rest = jnp.where(line == 0, jax.nn.sigmoid(logits[8:]), 0.0)
    router_probs[...] = jnp.concatenate([top, rest], axis=0)
    x_own = pltpu.make_async_copy(normed_two, x_all.at[me_z, me_e], local_sem.at[2])
    x_own.start()
    gates_in[me_e, me_z] = jnp.concatenate([top * named_of(routes), rest], axis=0)

    def gates_far(turn, z):
        here = gates_in.at[me_e, z]
        return send(here, here, y_send.at[turn], y_recv.at[turn], (far[turn], me_e))

    def gates_near(step, owner):
        here = gates_in.at[owner]
        return send(here, here, g_send.at[step], g_recv.at[step], (me_z, nbr[step]))

    for turn in (1, 2, 3):
        gates_far(turn, me_z).start()

    def x_region(owner, half):
        if half is None:
            return x_all.at[me_z, owner]
        return x_all.at[me_z, owner, pl.ds(half * (rows // 2), rows // 2)]

    x_gather = PlaneGather(x_region, x_send, x_recv, me_z, me_e, nbr)
    x_own.wait()
    x_gather.begin()
    for turn in (1, 2, 3):
        gates_far(turn, far[turn]).wait_recv()
    for step in range(1, 8):
        gates_near(step, me_e).start()
    x_gather.relay()
    x_gather.relay_far()
    for step in range(1, 8):
        gates_near(step, nbr[step]).wait_recv()
    gates_all[...] = gates_in[...]
    x_gather.finish()

    cot_own.finish()
    for hop in range(3):
        cot_step(hop, "finish")
    for turn in (1, 2, 3):
        for part in range(3):
            expert_copy(part, turn, True).wait_recv()
            expert_copy(part, turn, False).wait_send()
        params_send(turn).wait_send()
        gates_far(turn, me_z).wait_send()
    for step in range(1, 8):
        docs_send(step).wait_send()
        gates_near(step, me_e).wait_send()
        out_send(step).wait_send()
    weights_store.wait()
    out_store.wait()
    attn_weights.drain()
    cot_chain.drain()
    sums.drain()
    x_gather.drain()
    cot_own.drain()
    for hop in range(3):
        cot_step(hop, "drain")


def front_call(
    tokens, docs, routes, router, gate_vector, gain_in, gain_out, bias_in, tables, cotangent, qkv_weight,
    out_weight, up_weight, down_weight,
):
    rows, width = tokens.shape
    shard_width = qkv_weight.shape[0]
    head_width = width // 8
    pairs = 8 * head_width // HEAD
    routed_units = down_weight.shape[0] // 4
    low, full = jnp.bfloat16, jnp.float32
    shape = jax.ShapeDtypeStruct
    any_space = pl.BlockSpec(memory_space=pl.ANY)
    vmem = pl.BlockSpec(memory_space=pltpu.VMEM)
    dma = pltpu.SemaphoreType.DMA
    return pl.pallas_call(
        front_kernel,
        out_shape=(
            shape((3, 8 * rows, head_width), low),
            shape((pairs, rows, rows), full),
            shape((8 * rows, head_width), low),
            shape((8 * rows, width), low),
            shape((rows, width), full),
            shape((rows, width), low),
            shape((8, 4, 16, rows), full),
            shape((16, rows), full),
            shape((16, width), low),
            shape((width, 4 * head_width), low),
            shape((head_width, width), low),
            shape((8, 4, rows, width), low),
            shape((3, routed_units, width), low),
            shape((4, 8, rows, width), low),
        ),
        in_specs=[vmem] * 10 + [any_space] * 4,
        out_specs=tuple([vmem] * 9 + [any_space] * 5),
        scratch_shapes=[
            pltpu.VMEM((8, rows, width), low),
            pltpu.VMEM((width, 4 * head_width), low),
            pltpu.VMEM((head_width, width), low),
            pltpu.VMEM((4, 16, shard_width), low),
            pltpu.VMEM((8, 8, rows), full),
            pltpu.VMEM((8, 4, 16, rows), full),
            pltpu.VMEM((8 * rows, head_width), full),
            pltpu.VMEM((4, rows, width), low),
            pltpu.VMEM((2, rows // 2, width), low),
            pltpu.VMEM((2, rows, width), low),
            dma((10,)),
            dma((10,)),
            dma((2, 3)),
            dma((2, 3)),
            dma((4,)),
            dma((4,)),
            dma((8,)),
            dma((8,)),
            dma((8,)),
            dma((8,)),
            dma((7,)),
            dma((7,)),
            dma((7, 10)),
            dma((7, 10)),
            dma((2, 3)),
            dma((2, 3)),
            dma((3, 4)),
            dma((3, 4)),
            dma((10,)),
            dma((10,)),
            dma((4,)),
            dma((4,)),
            dma((8,)),
            dma((8,)),
            dma((6,)),
        ],
        compiler_params=pltpu.CompilerParams(
            collective_id=2, has_side_effects=True, vmem_limit_bytes=60 * 2**20
        ),
        cost_estimate=pl.CostEstimate(
            flops=8 * 8 * rows * width * head_width, bytes_accessed=80 * 2**20, transcendentals=0
        ),
    )(
        tokens, docs, routes, router, gate_vector, gain_in, gain_out, bias_in, tables, cotangent, qkv_weight,
        out_weight, up_weight, down_weight,
    )


def widen_kernel(
    attn_all, shared_all, expert_all, small, qkv, out, shared, up, down, router, gate, gain_in, gain_out, bias
):
    for part in range(3):
        width = attn_all.shape[2]
        qkv[:, part * width : (part + 1) * width] = attn_all[part].astype(jnp.float32)
        shared[part] = shared_all[part].astype(jnp.float32)
    out[...] = attn_all[3].astype(jnp.float32)
    for part in range(2):
        up[:, part, :] = expert_all[part].astype(jnp.float32)
    down[...] = expert_all[2].astype(jnp.float32)

    @pl.when(pl.program_id(0) == 0)
    def _():
        router[...] = small[:8, :]
        for row, target in ((8, gate), (9, gain_in), (10, gain_out)):
            target[...] = small[row, :]
        bias[...] = small[11:14, :]


def widen_call(attn_all, shared_all, expert_all, small):
    steps = 8
    _, depth, width = attn_all.shape
    units, routed, cols = shared_all.shape[1], expert_all.shape[1], expert_all.shape[2]
    full = jnp.float32
    shape = jax.ShapeDtypeStruct
    return pl.pallas_call(
        widen_kernel,
        grid=(steps,),
        out_shape=(
            shape((depth, 3 * width), full),
            shape((depth, width), full),
            shape(shared_all.shape, full),
            shape((routed, 2, cols), full),
            shape((routed, cols), full),
            shape((8, depth), full),
            shape((depth,), full),
            shape((depth,), full),
            shape((depth,), full),
            shape((3, depth), full),
        ),
        in_specs=[
            pl.BlockSpec((4, depth // steps, width), lambda i: (0, i, 0)),
            pl.BlockSpec((3, units // steps, width), lambda i: (0, i, 0)),
            pl.BlockSpec((3, routed // steps, cols), lambda i: (0, i, 0)),
            pl.BlockSpec((16, depth), lambda i: (0, 0)),
        ],
        out_specs=(
            pl.BlockSpec((depth // steps, 3 * width), lambda i: (i, 0)),
            pl.BlockSpec((depth // steps, width), lambda i: (i, 0)),
            pl.BlockSpec((3, units // steps, width), lambda i: (0, i, 0)),
            pl.BlockSpec((routed // steps, 2, cols), lambda i: (i, 0, 0)),
            pl.BlockSpec((routed // steps, cols), lambda i: (i, 0)),
            pl.BlockSpec((8, depth), lambda i: (0, 0)),
            pl.BlockSpec((depth,), lambda i: (0,)),
            pl.BlockSpec((depth,), lambda i: (0,)),
            pl.BlockSpec((depth,), lambda i: (0,)),
            pl.BlockSpec((3, depth), lambda i: (0, 0)),
        ),
        compiler_params=pltpu.CompilerParams(vmem_limit_bytes=60 * 2**20),
        cost_estimate=pl.CostEstimate(flops=0, bytes_accessed=96 * 2**20, transcendentals=0),
    )(attn_all, shared_all, expert_all, small)


def silu_parts(gate):
    logistic = jax.nn.sigmoid(gate)
    silu = gate * logistic
    return (silu, logistic * (1.0 + gate * (1.0 - logistic)))


def gather_all(rows):
    rows = lax.all_gather(rows, "dp", axis=0, tiled=True)
    return lax.all_gather(rows, "expert", axis=0, tiled=True)


def scatter_all(rows):
    rows = lax.psum_scatter(rows, "expert", scatter_dimension=0, tiled=True)
    return lax.psum_scatter(rows, "dp", scatter_dimension=0, tiled=True)


def shards(
    tokens,
    attn_gain,
    qkv_weight,
    qkv_bias,
    out_weight,
    ffn_gain,
    router_weight,
    shared_gate_weight,
    shared_weight,
    expert_up,
    expert_down,
    routes,
    segment_ids,
    cotangent,
):
    num_dp = lax.axis_size("dp")
    num_expert = lax.axis_size("expert")
    me_expert = lax.axis_index("expert")
    seq_len, model_width = tokens.shape
    shard_width = qkv_weight.shape[0]
    head_count = HEADS // num_expert
    head_width = head_count * HEAD
    plane_rows = seq_len * num_expert
    units = shared_weight.shape[0] // num_expert
    score_scale = HEAD ** (-0.5)

    small = jnp.concatenate(
        [
            attn_gain[None],
            ffn_gain[None],
            shared_gate_weight[None],
            qkv_bias,
            router_weight.T,
        ],
        axis=0,
    )
    small = lax.all_gather(small, "dp", axis=1, tiled=True)
    gain_one = small[0].astype(jnp.float32)
    gain_two = small[1].astype(jnp.float32)
    bias_cols = lax.dynamic_slice_in_dim(small[3:6], me_expert * head_width, head_width, 1)
    w_route = jnp.concatenate([small[6:], small[2:3]], axis=0)

    plane_tokens = lax.all_gather(tokens, "expert", axis=0, tiled=True)
    plane_docs = lax.all_gather(segment_ids, "expert", axis=0, tiled=True)
    cols_qkv = lax.dynamic_slice_in_dim(
        qkv_weight.reshape(shard_width, 3, model_width), me_expert * head_width, head_width, 2
    ).reshape(shard_width, 3 * head_width)
    cols_out = lax.dynamic_slice_in_dim(out_weight, me_expert * head_width, head_width, 1)
    attn_weights = lax.all_gather(
        jnp.concatenate([cols_qkv, cols_out], axis=1), "dp", axis=0, tiled=True
    )
    w_qkv = attn_weights[:, : 3 * head_width]
    w_out = lax.all_to_all(
        attn_weights[:, 3 * head_width :], "expert", split_axis=0, concat_axis=1, tiled=True
    )

    expert_full = jnp.concatenate([expert_up[0], expert_down[0][:, None, :]], axis=1)
    expert_units = lax.all_to_all(expert_full, "dp", split_axis=0, concat_axis=2, tiled=True)
    shared_units = lax.dynamic_slice_in_dim(shared_weight, me_expert * units, units, 0)
    mlp_weight = jnp.concatenate([expert_units, shared_units], axis=0)
    routed_units = expert_units.shape[0]
    all_units = routed_units + units

    all_cot = gather_all(cotangent)
    all_routes = gather_all(routes)

    plane_resid = plane_tokens.astype(jnp.float32)
    normed_one = (plane_resid * rms_scale(plane_resid) * gain_one).astype(jnp.bfloat16)
    qkv_rows = jnp.dot(normed_one, w_qkv, preferred_element_type=jnp.float32) + bias_cols.reshape(
        -1
    ).astype(jnp.float32)
    qkv_rows = qkv_rows.reshape(num_expert, seq_len, 3, head_count, HEAD)
    cosine_table, sine_table = rope_tables(seq_len, HEAD)
    query_rows = rotate(qkv_rows[:, :, 0], cosine_table, sine_table).astype(jnp.bfloat16)
    key_rows = rotate(qkv_rows[:, :, 1], cosine_table, sine_table).astype(jnp.bfloat16)
    value_rows = qkv_rows[:, :, 2].astype(jnp.bfloat16)
    positions = jnp.arange(seq_len)
    allowed = (
        (plane_docs[:, :, None] == plane_docs[:, None, :])
        & (positions[:, None] >= positions[None, :])[None]
    )[:, None]
    scores = (
        jnp.einsum("bthd,bshd->bhts", query_rows, key_rows, preferred_element_type=jnp.float32)
        * score_scale
    )
    scores = jnp.where(allowed, scores, NEGATIVE)
    exp_scores = jnp.exp(scores - jnp.max(scores, axis=-1, keepdims=True))
    attn_probs = exp_scores / jnp.sum(exp_scores, axis=-1, keepdims=True)
    probs_low = attn_probs.astype(jnp.bfloat16)
    mixed_heads = (
        jnp.einsum("bhts,bshd->bthd", probs_low, value_rows, preferred_element_type=jnp.float32)
        .reshape(plane_rows, head_width)
        .astype(jnp.bfloat16)
    )
    attn_part = jnp.dot(mixed_heads, w_out, preferred_element_type=jnp.float32)
    attn_out = lax.psum_scatter(
        attn_part.astype(jnp.bfloat16), "expert", scatter_dimension=0, tiled=True
    )

    resid_in = tokens.astype(jnp.float32)
    hidden_state = resid_in + attn_out.astype(jnp.float32)
    rms_two = rms_scale(hidden_state)
    normed_two = (hidden_state * rms_two * gain_two).astype(jnp.bfloat16)

    all_normed = gather_all(normed_two)
    all_logits = jnp.einsum(
        "td,ed->te", all_normed, w_route, preferred_element_type=jnp.float32
    )
    all_probs = jax.nn.softmax(all_logits[:, :num_expert], axis=-1)
    all_named = jnp.any(all_routes == me_expert, axis=1)
    my_prob = jnp.sum(
        jnp.where(jnp.arange(num_expert)[None, :] == me_expert, all_probs, 0.0), axis=1
    )
    gate_routed = jnp.where(all_named, my_prob, 0.0)
    gate_shared = jax.nn.sigmoid(all_logits[:, num_expert])
    is_routed = (jnp.arange(all_units) < routed_units)[None, :]
    row_gate = jnp.where(is_routed, gate_routed[:, None], gate_shared[:, None])

    gate_up = jnp.einsum(
        "td,fgd->gtf", all_normed, mlp_weight[:, :2], preferred_element_type=jnp.float32
    )
    silu, d_silu = silu_parts(gate_up[0])
    act = silu * gate_up[1]
    raw_act_grad = jnp.einsum(
        "td,fd->tf", all_cot, mlp_weight[:, 2], preferred_element_type=jnp.float32
    )
    gated_act = (row_gate * act).astype(jnp.bfloat16)
    act_dots = act * raw_act_grad
    d_gate_routed = jnp.where(
        all_named, jnp.sum(jnp.where(is_routed, act_dots, 0.0), axis=1), 0.0
    )
    d_gate_shared = jnp.sum(jnp.where(is_routed, 0.0, act_dots), axis=1)
    act_grad = raw_act_grad * row_gate
    d_gate_up = jnp.stack([act_grad * gate_up[1] * d_silu, act_grad * silu], axis=0).astype(
        jnp.bfloat16
    )
    d_rows = jnp.einsum(
        "gtf,fgd->td", d_gate_up, mlp_weight[:, :2], preferred_element_type=jnp.float32
    ).astype(jnp.bfloat16)
    gate_cols = jnp.concatenate(
        [
            jnp.where(
                jnp.arange(num_expert)[None, :] == me_expert, d_gate_routed[:, None], 0.0
            ),
            d_gate_shared[:, None],
        ],
        axis=1,
    )
    d_gate_cols = scatter_all(gate_cols)
    d_rows_sum = scatter_all(d_rows).astype(jnp.float32)

    up_grad = jnp.einsum(
        "gtf,td->fgd", d_gate_up, all_normed, preferred_element_type=jnp.float32
    ).astype(jnp.bfloat16)
    down_grad = jnp.einsum(
        "tf,td->fd", gated_act, all_cot, preferred_element_type=jnp.float32
    ).astype(jnp.bfloat16)
    out_rows = jnp.dot(gated_act, mlp_weight[:, 2], preferred_element_type=jnp.float32).astype(
        jnp.bfloat16
    )
    output = (hidden_state + scatter_all(out_rows).astype(jnp.float32)).astype(jnp.bfloat16)
    mlp_grad = jnp.concatenate([up_grad, down_grad[:, None, :]], axis=1)
    expert_grad = lax.all_to_all(
        mlp_grad[:routed_units], "dp", split_axis=2, concat_axis=0, tiled=True
    ).astype(jnp.float32)
    shared_grad = lax.all_gather(
        mlp_grad[routed_units:], "expert", axis=0, tiled=True
    ).astype(jnp.float32)

    back_grad = cotangent.astype(jnp.float32)
    logits = jnp.einsum("td,ed->te", normed_two, w_route, preferred_element_type=jnp.float32)
    router_probs = jax.nn.softmax(logits[:, :num_expert], axis=-1)
    logistic_gate = jax.nn.sigmoid(logits[:, num_expert:])
    d_router_probs = d_gate_cols[:, :num_expert]
    d_logits = router_probs * (
        d_router_probs - jnp.sum(router_probs * d_router_probs, axis=-1, keepdims=True)
    )
    d_gate_logit = d_gate_cols[:, num_expert:] * logistic_gate * (1.0 - logistic_gate)
    d_route = jnp.concatenate([d_logits, d_gate_logit], axis=1).astype(jnp.bfloat16)
    route_grad = jnp.einsum("td,te->ed", normed_two, d_route, preferred_element_type=jnp.float32)
    d_normed = d_rows_sum + jnp.dot(d_route, w_route, preferred_element_type=jnp.float32)
    ffn_gain_grad, d_hidden = norm_back(hidden_state, rms_two, gain_two, d_normed)
    d_hidden = back_grad + d_hidden

    d_attn_out = lax.all_gather(d_hidden.astype(jnp.bfloat16), "expert", axis=0, tiled=True)
    out_grad = jnp.einsum(
        "td,te->de", mixed_heads, d_attn_out, preferred_element_type=jnp.float32
    ).astype(jnp.bfloat16)
    out_grad = lax.all_to_all(out_grad, "expert", split_axis=1, concat_axis=0, tiled=True)
    d_mixed = (
        jnp.einsum("te,de->td", d_attn_out, w_out, preferred_element_type=jnp.float32)
        .astype(jnp.bfloat16)
        .reshape(num_expert, seq_len, head_count, HEAD)
    )
    values_grad = jnp.einsum(
        "bhts,bthd->bshd", probs_low, d_mixed, preferred_element_type=jnp.float32
    )
    d_probs = jnp.einsum("bthd,bshd->bhts", d_mixed, value_rows, preferred_element_type=jnp.float32)
    d_scores = (
        attn_probs * (d_probs - jnp.sum(attn_probs * d_probs, axis=-1, keepdims=True))
    ).astype(jnp.bfloat16)
    d_query = unrotate(
        jnp.einsum("bhts,bshd->bthd", d_scores, key_rows, preferred_element_type=jnp.float32)
        * score_scale,
        cosine_table,
        sine_table,
    )
    d_keys = unrotate(
        jnp.einsum("bhts,bthd->bshd", d_scores, query_rows, preferred_element_type=jnp.float32)
        * score_scale,
        cosine_table,
        sine_table,
    )
    d_qkv = (
        jnp.stack([d_query, d_keys, values_grad], axis=2)
        .reshape(plane_rows, 3 * head_width)
        .astype(jnp.bfloat16)
    )
    bias_part = jnp.sum(d_qkv.astype(jnp.float32), axis=0).reshape(3, head_width)
    bias_grad = lax.dynamic_update_slice_in_dim(
        jnp.zeros((3, model_width), jnp.float32), bias_part, me_expert * head_width, 1
    )
    d_normed_one = lax.psum_scatter(
        jnp.einsum("te,de->td", d_qkv, w_qkv, preferred_element_type=jnp.float32).astype(
            jnp.bfloat16
        ),
        "expert",
        scatter_dimension=0,
        tiled=True,
    ).astype(jnp.float32)
    qkv_grad = jnp.einsum(
        "td,te->de", normed_one, d_qkv, preferred_element_type=jnp.float32
    ).astype(jnp.bfloat16)
    attn_grad = lax.psum_scatter(
        jnp.concatenate([qkv_grad, out_grad], axis=1), "dp", scatter_dimension=0, tiled=True
    )
    attn_grad = lax.all_gather(attn_grad, "expert", axis=0).astype(jnp.float32)
    qkv_weight_grad = (
        attn_grad[:, :, : 3 * head_width]
        .reshape(num_expert, shard_width, 3, head_width)
        .transpose(1, 2, 0, 3)
        .reshape(shard_width, 3 * model_width)
    )
    out_weight_grad = (
        attn_grad[:, :, 3 * head_width :].transpose(1, 0, 2).reshape(shard_width, model_width)
    )
    attn_gain_grad, d_input = norm_back(resid_in, rms_scale(resid_in), gain_one, d_normed_one)
    tokens_grad = d_hidden + d_input

    small_grad = jnp.concatenate(
        [attn_gain_grad[None], ffn_gain_grad[None], bias_grad, route_grad], axis=0
    )
    small_grad = lax.psum_scatter(small_grad, "dp", scatter_dimension=1, tiled=True)
    small_grad = lax.psum(small_grad, "expert")
    return (
        output,
        tokens_grad,
        small_grad[0],
        qkv_weight_grad,
        small_grad[2:5],
        out_weight_grad,
        small_grad[1],
        small_grad[5 : 5 + num_expert].T,
        small_grad[5 + num_expert],
        shared_grad,
        expert_grad[None, :, :2],
        expert_grad[None, :, 2],
    )


def fast_shards(
    tokens,
    attn_gain,
    qkv_weight,
    qkv_bias,
    out_weight,
    ffn_gain,
    router_weight,
    shared_gate_weight,
    shared_weight,
    expert_up,
    expert_down,
    routes,
    segment_ids,
    cotangent,
):
    num_dp = lax.axis_size("dp")
    num_expert = lax.axis_size("expert")
    seq_len, model_width = tokens.shape
    up_weight = expert_up[0].transpose(1, 0, 2)
    low, full = jnp.bfloat16, jnp.float32

    positions = np.arange(seq_len, dtype=np.float32)[:, None]
    angles = positions * np.exp(np.arange(HEAD // 2) * (-2.0 * math.log(THETA) / HEAD)).astype(np.float32)
    sines = np.sin(angles)
    tables = jnp.asarray(
        np.stack([np.tile(np.cos(angles), 2), np.concatenate([-sines, sines], axis=1)]), full
    )
    (
        qkv,
        probs,
        mixed,
        normed_one,
        hidden_state,
        normed_two,
        gates_all,
        router_probs,
        params,
        attn_weights,
        w_out,
        all_cot,
        mlp_weight,
        x_all,
    ) = front_call(
        tokens,
        segment_ids,
        routes.T,
        router_weight.T,
        shared_gate_weight,
        attn_gain,
        ffn_gain,
        qkv_bias,
        tables,
        cotangent,
        qkv_weight,
        out_weight,
        up_weight,
        expert_down[0],
    )

    _, out_part, d_rows, d_gates, d_routed, shared_grad, expert_grad = mlp_call(
        x_all,
        gates_all,
        all_cot,
        mlp_weight,
        up_weight,
        expert_down[0],
        shared_weight.transpose(1, 0, 2),
    )

    output, tokens_grad, small_grad, attn_grad, shared_grad, expert_grad = tail_call(
        mixed,
        qkv,
        probs,
        normed_one,
        attn_weights,
        w_out,
        tables,
        tokens,
        params,
        d_rows,
        d_gates,
        routes.T,
        router_probs,
        normed_two,
        hidden_state,
        cotangent,
        out_part.reshape(num_expert // 2, 2, num_dp, seq_len, model_width),
        d_routed,
        shared_grad,
        expert_grad,
    )
    (
        qkv_grad,
        out_grad,
        shared_grad,
        up_grad,
        down_grad,
        router_grad,
        gate_grad,
        attn_gain_grad,
        ffn_gain_grad,
        bias_grad,
    ) = widen_call(attn_grad, shared_grad, expert_grad, small_grad)
    return (
        output,
        tokens_grad,
        attn_gain_grad,
        qkv_grad,
        bias_grad,
        out_grad,
        ffn_gain_grad,
        router_grad.T,
        gate_grad,
        shared_grad.transpose(1, 0, 2),
        up_grad[None],
        down_grad[None],
    )


def solution(mesh):
    cube = mesh.shape["expert"] == 8 and mesh.shape["dp"] == 4
    return jax.shard_map(
        fast_shards if cube else shards,
        mesh=mesh,
        in_specs=(
            P(("dp", "expert"), None),
            P("dp"),
            P("dp", None),
            P(None, "dp"),
            P("dp", None),
            P("dp"),
            P("dp", None),
            P("dp"),
            P("dp", None, None),
            P("expert", None, None, "dp"),
            P("expert", None, "dp"),
            P(("dp", "expert"), None),
            P(("dp", "expert"), None),
            P(("dp", "expert"), None),
        ),
        out_specs=(
            P(("dp", "expert"), None),
            P(("dp", "expert"), None),
            P("dp"),
            P("dp", None),
            P(None, "dp"),
            P("dp", None),
            P("dp"),
            P("dp", None),
            P("dp"),
            P("dp", None, None),
            P("expert", None, None, "dp"),
            P("expert", None, "dp"),
        ),
        check_vma=False,
    )
```

```python
import functools
import math

import jax
import jax.numpy as jnp
import numpy as np
from jax import lax
from jax.experimental import pallas as pl
from jax.experimental.pallas import tpu as pltpu
from jax.sharding import PartitionSpec as P

HEADS = 16
HEAD = 128


EPS = 1e-06
THETA = 1000000.0
NEGATIVE = -1e30


def rms_scale(values):
    return lax.rsqrt(jnp.mean(values * values, axis=-1, keepdims=True) + EPS)


def rope_tables(length, head_width):
    indices = jnp.arange(head_width // 2).astype(jnp.float32)
    frequency = jnp.exp(indices * (-2.0 * math.log(THETA) / head_width))
    angles = jnp.arange(length).astype(jnp.float32)[:, None] * frequency[None, :]
    return (jnp.cos(angles), jnp.sin(angles))


def rotate(values, cosine_table, sine_table):
    half_width = values.shape[-1] // 2
    lower_half = values[..., :half_width]
    upper_half = values[..., half_width:]
    cos_rows = cosine_table[:, None, :]
    sin_rows = sine_table[:, None, :]
    return jnp.concatenate(
        [
            lower_half * cos_rows - upper_half * sin_rows,
            upper_half * cos_rows + lower_half * sin_rows,
        ],
        axis=-1,
    )


def unrotate(values, cosine_table, sine_table):
    half_width = values.shape[-1] // 2
    lower_half = values[..., :half_width]
    upper_half = values[..., half_width:]
    cos_rows = cosine_table[:, None, :]
    sin_rows = sine_table[:, None, :]
    return jnp.concatenate(
        [
            lower_half * cos_rows + upper_half * sin_rows,
            upper_half * cos_rows - lower_half * sin_rows,
        ],
        axis=-1,
    )


def norm_back(values, scale_rows, gain_row, upstream):
    scaled = gain_row * upstream
    gain_grad = jnp.sum(upstream * values * scale_rows, axis=0)
    input_grad = scale_rows * scaled - values * scale_rows**3 * jnp.mean(
        scaled * values, axis=-1, keepdims=True
    )
    return (gain_grad, input_grad)


MESH = pl.DeviceIdType.MESH
NT = (((1,), (1,)), ((), ()))


def flip(index, step):
    return index + step - 2 * step * lax.rem(lax.div(index, step), 2)


def flip_pair(index, turn):
    return index + lax.rem(turn, 2) * (1 - 2 * lax.rem(index, 2)) + lax.div(turn, 2) * (
        2 - 4 * lax.rem(lax.div(index, 2), 2)
    )


def send(source, target, send_sem, recv_sem, device):
    return pltpu.make_async_remote_copy(
        src_ref=source,
        dst_ref=target,
        send_sem=send_sem,
        recv_sem=recv_sem,
        device_id=device,
        device_id_type=MESH,
    )


def greet(devices):
    barrier = pltpu.get_barrier_semaphore()
    for device in devices:
        pl.semaphore_signal(barrier, inc=1, device_id=device, device_id_type=MESH)
    pl.semaphore_wait(barrier, len(devices))

TN = (((0,), (0,)), ((), ()))


class PlaneGather:
    def __init__(self, region, send_sem, recv_sem, me_z, me_e, nbr):
        self.sems = send_sem, recv_sem
        self.region, self.me_z, self.nbr = region, me_z, nbr
        out = {1: (me_e, None, 1), 2: (me_e, None, 2), 3: (me_e, None, 4)}
        out.update({4: (nbr[2], 0, 4), 5: (nbr[4], 1, 2), 6: (nbr[2], None, 1), 7: (nbr[4], None, 1)})
        out.update({8: (nbr[6], 0, 1), 9: (nbr[6], 1, 1)})
        self.out = out
        self.into = {
            1: (nbr[1], None), 2: (nbr[2], None), 3: (nbr[4], None), 4: (nbr[6], 0), 5: (nbr[6], 1),
            6: (nbr[3], None), 7: (nbr[5], None), 8: (nbr[7], 0), 9: (nbr[7], 1),
        }

    def copy(self, channel):
        owner, half, step = self.out[channel]
        ref = self.region(owner, half)
        return send(
            ref, ref, self.sems[0].at[channel], self.sems[1].at[channel], (self.me_z, self.nbr[step])
        )

    def start(self, *channels):
        for channel in channels:
            self.copy(channel).start()

    def wait(self, *channels):
        for channel in channels:
            ref = self.region(*self.into[channel])
            send(
                ref, ref, self.sems[0].at[channel], self.sems[1].at[channel], (self.me_z, self.nbr[1])
            ).wait_recv()

    def begin(self):
        self.start(2, 3, 1)

    def relay(self):
        self.wait(2)
        self.start(4, 6)
        self.wait(3)
        self.start(5, 7)

    def relay_far(self):
        self.wait(4)
        self.start(8)
        self.wait(5)
        self.start(9)

    def finish(self):
        self.wait(1, 6, 7, 8, 9)

    def drain(self):
        for channel in range(1, 10):
            self.copy(channel).wait_send()


def add_rows(target, source, rows):
    @pl.loop(0, rows, step=32)
    def _(row):
        span = pl.ds(pl.multiple_of(row, 32), 32)
        target[span, :] = target[span, :] + source[span, :]


class PlaneScatter:
    def __init__(self, theirs, own, sib, relayed, crossed, sems, place, me_z, nbr):
        self.theirs, self.own, self.sib, self.relayed, self.crossed = theirs, own, sib, relayed, crossed
        self.sems, self.me_z, self.nbr = sems, me_z, nbr
        y, x = place
        self.own_block, self.far_block = 2 * y + x, 2 * (1 - y) + 1 - x
        self.x_block, self.y_block = 2 * y + 1 - x, 2 * (1 - y) + x
        self.rows = crossed.shape[1]

    def copy(self, channel):
        half = self.rows // 2
        low, high = pl.ds(0, half), pl.ds(half, half)
        own, x_block, y_block, far_block = self.own, self.x_block, self.y_block, self.far_block
        if channel == 0:
            source, target, step = self.theirs, self.sib, 1
        elif channel == 1:
            source, target, step = own.at[far_block, low], self.relayed.at[0], 2
        elif channel == 2:
            source, target, step = own.at[far_block, high], self.relayed.at[1], 4
        elif channel == 3:
            source, target, step = own.at[x_block, low], self.crossed.at[0, low], 2
        elif channel == 4:
            source, target, step = own.at[y_block, high], self.crossed.at[1, high], 4
        elif channel == 5:
            source, target, step = own.at[y_block, low], self.crossed.at[1, low], 4
        else:
            source, target, step = own.at[x_block, high], self.crossed.at[0, high], 2
        return send(
            source,
            target,
            self.sems[0].at[channel],
            self.sems[1].at[channel],
            (self.me_z, self.nbr[step]),
        )

    def first(self):
        self.copy(0).start()

    def second(self):
        self.copy(0).wait_recv()
        own, sib = self.own, self.sib
        add_rows(own.at[self.far_block], sib.at[self.far_block], self.rows)
        self.copy(1).start()
        self.copy(2).start()
        add_rows(own.at[self.x_block], sib.at[self.x_block], self.rows)
        self.copy(3).start()
        add_rows(own.at[self.y_block], sib.at[self.y_block], self.rows)
        self.copy(4).start()
        add_rows(own.at[self.own_block], sib.at[self.own_block], self.rows)

    def third(self):
        half = self.rows // 2
        self.copy(1).wait_recv()
        add_rows(self.own.at[self.y_block, pl.ds(0, half)], self.relayed.at[0], half)
        self.copy(2).wait_recv()
        add_rows(self.own.at[self.x_block, pl.ds(half, half)], self.relayed.at[1], half)
        self.copy(5).start()
        self.copy(6).start()

    def fourth(self, store):
        for channel in (3, 4, 5, 6):
            self.copy(channel).wait_recv()

        @pl.loop(0, self.rows, step=32)
        def _(row):
            span = pl.ds(pl.multiple_of(row, 32), 32)
            store(
                span,
                self.own[self.own_block, span, :].astype(jnp.float32)
                + self.crossed[0, span, :].astype(jnp.float32)
                + self.crossed[1, span, :].astype(jnp.float32),
            )

    def drain(self):
        for channel in range(7):
            self.copy(channel).wait_send()


class TileScatter(PlaneScatter):
    def copy(self, channel):
        if channel not in (0, 7):
            return super().copy(channel)
        part = channel // 7
        return send(
            self.theirs.at[part],
            self.sib.at[part],
            self.sems[0].at[channel],
            self.sems[1].at[channel],
            (self.me_z, self.nbr[1]),
        )

    def sum_near(self):
        self.copy(0).wait_recv()
        own, near = self.own, self.sib.at[0]
        add_rows(own.at[self.x_block], near.at[lax.rem(self.x_block, 2)], self.rows)
        self.copy(3).start()
        add_rows(own.at[self.own_block], near.at[lax.rem(self.own_block, 2)], self.rows)

    def sum_far(self):
        self.copy(7).wait_recv()
        own, other = self.own, self.sib.at[1]
        add_rows(own.at[self.far_block], other.at[lax.rem(self.far_block, 2)], self.rows)
        self.copy(1).start()
        self.copy(2).start()
        add_rows(own.at[self.y_block], other.at[lax.rem(self.y_block, 2)], self.rows)
        self.copy(4).start()

    def drain(self):
        for channel in range(1, 7):
            self.copy(channel).wait_send()


class ChainGather:
    def __init__(self, region, send_sem, recv_sem, me_z, me_e):
        self.region, self.sems, self.me_z, self.me_e = region, (send_sem, recv_sem), me_z, me_e

    def copy(self, way, hop):
        step = 1 - 2 * way
        ref = self.region(jnp.clip(self.me_z - step * hop, 0, 3))
        return send(
            ref,
            ref,
            self.sems[0].at[way, hop],
            self.sems[1].at[way, hop],
            (jnp.clip(self.me_z + step, 0, 3), self.me_e),
        )

    def sends(self, way, hop):
        z = self.me_z
        return (z < 3) & (z >= hop) if way == 0 else (z > 0) & (z <= 3 - hop)

    def takes(self, way, hop):
        z = self.me_z
        return z > hop if way == 0 else z < 3 - hop

    def begin(self):
        for way in range(2):
            pl.when(self.sends(way, 0))(self.copy(way, 0).start)

    def hop(self, hop):
        for way in range(2):
            step = 1 - 2 * way
            ref = self.region(jnp.clip(self.me_z - step * (hop + 1), 0, 3))
            arrived = send(
                ref,
                ref,
                self.sems[0].at[way, hop],
                self.sems[1].at[way, hop],
                (jnp.clip(self.me_z - step, 0, 3), self.me_e),
            )
            pl.when(self.takes(way, hop))(arrived.wait_recv)
            if hop < 2:
                pl.when(self.sends(way, hop + 1))(self.copy(way, hop + 1).start)

    def drain(self):
        for hop in range(3):
            for way in range(2):
                pl.when(self.sends(way, hop))(self.copy(way, hop).wait_send)


class ChainScatter:
    def __init__(self, part, landing, add, sems, me_z, me_e):
        self.part, self.landing, self.add = part, landing, add
        self.sems, self.me_z, self.me_e = sems, me_z, me_e

    def copy(self, way, hop, source, owner):
        slot = 4 if way == 1 and hop == 2 else owner
        return send(
            source,
            self.landing.at[slot],
            self.sems[0].at[way, hop],
            self.sems[1].at[way, hop],
            (jnp.clip(self.me_z + 1 - 2 * way, 0, 3), self.me_e),
        )

    def steps(self, hop):
        for way in range(2):
            place = self.me_z if way == 0 else 3 - self.me_z
            owner = jnp.clip(3 - hop + place if way == 0 else hop - place, 0, 3)
            yield way, place, owner

    def hop(self, hop):
        for way, place, owner in self.steps(hop):

            @pl.when(place == 0)
            def _(way=way, owner=owner):
                self.copy(way, hop, self.part(owner), owner).start()

            @pl.when((place > 0) & (place <= hop))
            def _(way=way, owner=owner):
                here = self.landing.at[owner]
                self.copy(way, hop - 1, here, owner).wait_recv()
                self.add(owner, owner)
                self.copy(way, hop, here, owner).start()

    def last(self, low, middle, high):
        up = self.copy(0, 2, self.landing.at[self.me_z], self.me_z)
        down = self.copy(1, 2, self.landing.at[4], 4)
        pl.when(self.me_z > 0)(up.wait_recv)
        pl.when(self.me_z < 3)(down.wait_recv)
        pl.when(self.me_z == 0)(low)
        pl.when((self.me_z > 0) & (self.me_z < 3))(middle)
        pl.when(self.me_z == 3)(high)

    def drain(self):
        for hop in range(3):
            for way, place, owner in self.steps(hop):
                pl.when(place <= hop)(self.copy(way, hop, self.part(owner), owner).wait_send)


def named_of(routes):
    expert = lax.broadcasted_iota(jnp.int32, (8, routes.shape[1]), 0)
    hits = jnp.zeros(expert.shape, jnp.float32)
    for way in range(routes.shape[0]):
        hits = hits + jnp.where(routes[way : way + 1, :] == expert, 1.0, 0.0)
    return hits


def mlp_kernel(
    routed_units,
    _x_in,
    g_all,
    cot,
    w_all,
    up_weight,
    down_weight,
    shared_weight,
    x_all,
    out_part,
    dx_own,
    dg_own,
    d_routed,
    shared_all,
    expert_all,
    w_gu,
    w_d,
    acc_gu,
    acc_d,
    stage,
    x_tile,
    c_tile,
    gu_buf,
    h_buf,
    dgu_buf,
    act_buf,
    out_buf,
    theirs,
    own,
    sib_x,
    relayed,
    crossed,
    sum_x,
    far_x,
    dg_all,
    dg_in,
    dg_sum,
    dg_far,
    a_send,
    a_recv,
    z_send,
    z_recv,
    r_send,
    r_recv,
    fz_send,
    fz_recv,
    dp_send,
    dp_recv,
    dz_send,
    dz_recv,
    local_sem,
):
    me_z = lax.axis_index("dp")
    me_e = lax.axis_index("expert")
    core = lax.rem(me_e, 2)
    me_x = lax.rem(lax.div(me_e, 2), 2)
    me_y = lax.div(me_e, 4)
    nbr = {1: flip(me_e, 1), 2: flip(me_e, 2), 4: flip(me_e, 4)}
    nbr[6] = flip(nbr[2], 4)
    nbr[3], nbr[5], nbr[7] = flip(nbr[2], 1), flip(nbr[4], 1), flip(nbr[6], 1)
    units, width = w_d.shape
    rows = x_all.shape[2]
    tile = 4 * rows
    chunk = 256

    def z_of(turn):
        return flip_pair(me_z, turn)

    def gather(turn):
        where = z_of(turn)

        def region(owner, half):
            if half is None:
                return x_all.at[where, owner]
            return x_all.at[where, owner, pl.ds(half * (rows // 2), rows // 2)]

        return PlaneGather(region, a_send.at[turn], a_recv.at[turn], me_z, me_e, nbr)

    def z_copy(turn, here):
        block = (z_of(turn) if here else me_z, me_e)
        return send(
            x_all.at[block], x_all.at[block], z_send.at[turn], z_recv.at[turn], (z_of(turn), me_e)
        )

    def slot_of(turn):
        return turn - 2 * lax.div(turn, 3)

    def scatter(turn):
        par = lax.rem(turn, 2)
        return TileScatter(
            theirs,
            own.at[slot_of(turn)],
            sib_x.at[par],
            relayed.at[par],
            crossed.at[slot_of(turn)],
            (r_send.at[turn], r_recv.at[turn]),
            (me_y, me_x),
            me_z,
            nbr,
        )

    def far_send(turn):
        return send(
            sum_x.at[turn], far_x.at[turn - 1], fz_send.at[turn], fz_recv.at[turn], (z_of(turn), me_e)
        )

    def plane_sum(turn):
        sums = scatter(turn)

        def store(span, total):
            sum_x[turn, span, :] = total.astype(jnp.bfloat16)

        sums.fourth(store)
        pl.when(turn > 0)(lambda: far_send(turn).start())
        sums.drain()

    greet([(z_of(turn), me_e) for turn in (1, 2, 3)] + [(me_z, nbr[k]) for k in range(1, 8)])
    z_copy(1, False).start()
    shard_width = width // 4
    shared_units = units - routed_units

    def lanes(index):
        return pl.ds(pl.multiple_of(index * shard_width, shard_width), shard_width)

    def lines(index, amount):
        return pl.ds(pl.multiple_of(index * amount, 16), amount)

    w_loads = []
    for part in range(3):
        target, base = (w_d, 0) if part == 2 else (w_gu, part * units)
        routed = pl.ds(base, routed_units)
        own_units = lines(me_z, routed_units)
        pairs = [
            (w_all.at[part, :, lanes(z_of(turn))], target.at[routed, lanes(z_of(turn))])
            for turn in (1, 2, 3)
        ]
        pairs.append(
            (
                down_weight.at[own_units] if part == 2 else up_weight.at[part, own_units],
                target.at[routed, lanes(me_z)],
            )
        )
        pairs.append(
            (
                shared_weight.at[part, lines(me_e, shared_units)],
                target.at[pl.ds(base + routed_units, shared_units)],
            )
        )
        for source, place in pairs:
            w_loads.append(
                pltpu.make_async_copy(source, place, local_sem.at[3 + len(w_loads)])
            )
    for copy in w_loads:
        copy.start()

    @pl.loop(0, 2 * units, step=48)
    def _(row):
        acc_gu[pl.ds(pl.multiple_of(row, 16), 48), :] = jnp.zeros((48, width), jnp.float32)

    @pl.loop(0, units, step=48)
    def _(row):
        acc_d[pl.ds(pl.multiple_of(row, 16), 48), :] = jnp.zeros((48, width), jnp.float32)

    def group_of(half):
        return lax.rem(me_y + half, 2)

    def place_of(index):
        turn = lax.rem(lax.div(index + 1, 2), 4)
        ends = 1 - lax.div(index + 6, 7) + lax.div(index, 7)
        return turn, lax.rem(index + 1 + ends, 2)

    def load(index):
        turn, half = place_of(index)
        block = pl.ds(pl.multiple_of(group_of(half) * 4, 4), 4)
        return (
            pltpu.make_async_copy(x_all.at[z_of(turn), block], x_tile, local_sem.at[0]),
            pltpu.make_async_copy(cot.at[block, z_of(turn)], c_tile, local_sem.at[1]),
        )


    for copy in load(0):
        copy.start()
    for copy in w_loads:
        copy.wait()

    def step(index, carry):
        turn, half = place_of(index)
        slot = slot_of(turn)
        pair, odd = lax.div(index, 2), lax.rem(index, 2)
        where = z_of(turn)
        group = group_of(half)
        block = pl.ds(pl.multiple_of(group * 4, 4), 4)

        for copy in load(index):
            copy.wait()
        for j in range(2):
            xs = x_tile[2 * j : 2 * j + 2].reshape(2 * rows, width)
            cs = c_tile[2 * j : 2 * j + 2].reshape(2 * rows, width)
            gu_buf[:, 2 * rows * j : 2 * rows * (j + 1)] = lax.dot_general(
                w_gu[...], xs, NT, preferred_element_type=jnp.float32
            )
            h_buf[:, 2 * rows * j : 2 * rows * (j + 1)] = lax.dot_general(
                w_d[...], cs, NT, preferred_element_type=jnp.float32
            )

        def gates(row):
            return jnp.concatenate(
                [g_all[group * 4 + j, where, pl.ds(row, 1), :] for j in range(4)], axis=1
            )

        dots = []
        for low, high, gate in (
            (0, routed_units, gates(me_e)),
            (routed_units, units, gates(8)),
        ):
            piece = 16

            def units_step(k, dot, low=low, gate=gate):
                at = pl.multiple_of(low + k * piece, 16)
                g = gu_buf[pl.ds(at, piece), :]
                u = gu_buf[pl.ds(pl.multiple_of(units + at, 16), piece), :]
                h = h_buf[pl.ds(at, piece), :]
                logistic = jax.nn.sigmoid(g)
                silu = g * logistic
                act = silu * u
                act_buf[pl.ds(at, piece), :] = (act * gate).astype(jnp.bfloat16)
                d_act = h * gate
                dgu_buf[pl.ds(at, piece), :] = (
                    d_act * u * (logistic * (1.0 + g * (1.0 - logistic)))
                ).astype(jnp.bfloat16)
                dgu_buf[pl.ds(pl.multiple_of(units + at, 16), piece), :] = (d_act * silu).astype(
                    jnp.bfloat16
                )
                return dot + jnp.sum(act * h, axis=0, keepdims=True)

            dots.append(
                lax.fori_loop(
                    0, (high - low) // piece, units_step, jnp.zeros((1, tile), jnp.float32)
                )
            )
        line = lax.broadcasted_iota(jnp.int32, (8, tile), 0)
        d_gates = jnp.where(line == 0, dots[0], 0.0) + jnp.where(line == 1, dots[1], 0.0)
        for j in range(4):
            dg_all[group * 4 + j, where] = d_gates[:, j * rows : (j + 1) * rows]

        @pl.when(index == 0)
        def _():
            z_copy(1, True).wait_recv()
            gather(1).begin()
            z_copy(2, False).start()

        @pl.when((odd == 1) & (index < 7))
        def _():
            gather(pair + 1).relay_far()

        @pl.when((odd == 1) & (index < 5))
        def _():
            z_copy(pair + 2, True).wait_recv()
            gather(pair + 2).begin()
            pl.when(index == 1)(lambda: z_copy(3, False).start())

        @pl.when((odd == 1) & (index > 4))
        def _():
            plane_sum(pair - 1)

        for n in range(width // chunk):
            cols = slice(n * chunk, (n + 1) * chunk)
            acc_gu[:, cols] += jnp.dot(
                dgu_buf[...], x_tile[:, :, cols].reshape(tile, chunk), preferred_element_type=jnp.float32
            )
            acc_d[:, cols] += jnp.dot(
                act_buf[...], c_tile[:, :, cols].reshape(tile, chunk), preferred_element_type=jnp.float32
            )

        @pl.when((odd == 0) & (index < 6))
        def _():
            gather(pair + 1).relay()
            gather(pair + 1).wait(1, 6)

        @pl.when((odd == 1) & (index < 7))
        def _():
            gather(pair + 1).wait(7, 8, 9)

        @pl.when(index < 7)
        def _():
            for copy in load(index + 1):
                copy.start()

        out_store = pltpu.make_async_copy(out_buf, out_part.at[block, where], local_sem.at[2])

        @pl.when(index > 0)
        def _():
            out_store.wait()

        @pl.when((odd == 1) & (index < 7))
        def _():
            scatter(turn - 1).copy(0).wait_send()

        @pl.when((odd == 0) & (index > 2))
        def _():
            scatter(turn - 1).copy(7).wait_send()

        @pl.when(index == 7)
        def _():
            scatter(3).copy(7).wait_send()

        dgu_t = dgu_buf[...].T
        act_t = act_buf[...].T
        for n in range(width // chunk):
            cols = slice(n * chunk, (n + 1) * chunk)
            dx = jnp.dot(dgu_t, w_gu[:, cols], preferred_element_type=jnp.float32).astype(jnp.bfloat16)
            out = jnp.dot(act_t, w_d[:, cols], preferred_element_type=jnp.float32).astype(jnp.bfloat16)
            for column in range(2):
                core_0 = dx[2 * column * rows : (2 * column + 1) * rows]
                core_1 = dx[(2 * column + 1) * rows : (2 * column + 2) * rows]
                own[slot, 2 * group + column, :, cols] = jnp.where(core == 0, core_0, core_1)
                theirs[half, column, :, cols] = jnp.where(core == 0, core_1, core_0)
            for j in range(4):
                out_buf[j, :, cols] = out[j * rows : (j + 1) * rows]
        out_store.start()

        @pl.when(odd == 1)
        def _():
            pl.when(index == 1)(lambda: scatter(0).sum_near())
            pl.when(index > 2)(lambda: scatter(pair).sum_far())

        @pl.when((odd == 0) & (index > 0))
        def _():
            pl.when(index > 2)(lambda: scatter(pair - 1).third())
            scatter(pair).sum_near()

        pl.when(half == 0)(lambda: scatter(turn).copy(0).start())
        pl.when(half == 1)(lambda: scatter(turn).copy(7).start())
        return carry

    lax.fori_loop(0, 8, step, 0)

    def dp_copy(step, here):
        return send(
            dg_all.at[nbr[step]],
            dg_in.at[nbr[step] if here else me_e],
            dp_send.at[step],
            dp_recv.at[step],
            (me_z, nbr[step]),
        )

    for step_to in range(1, 8):
        dp_copy(step_to, False).start()
    dg_in[me_e] = dg_all[me_e]
    scatter(3).third()
    scatter(0).sum_far()

    depth = stage.shape[1]
    stores = []

    def write_out(part):
        for piece in range(units // depth):
            row, slot = piece * depth, len(stores) % 2
            if len(stores) > 1:
                for copy in stores[-2]:
                    copy.wait()
            if part == 2:
                stage[slot] = acc_d[row : row + depth].astype(jnp.bfloat16)
            else:
                at = part * units + row
                stage[slot] = acc_gu[at : at + depth].astype(jnp.bfloat16)
            if row < routed_units:
                pairs = [
                    (stage.at[slot], d_routed.at[part, pl.ds(row, depth)]),
                    (
                        stage.at[slot, :, lanes(me_z)],
                        expert_all.at[
                            part, pl.ds(pl.multiple_of(me_z * routed_units + row, 16), depth)
                        ],
                    ),
                ]
            else:
                at = pl.multiple_of(me_e * shared_units + row - routed_units, 16)
                pairs = [(stage.at[slot], shared_all.at[part, pl.ds(at, depth)])]
            stores.append(
                [
                    pltpu.make_async_copy(source, place, local_sem.at[2 * slot + 3 + k])
                    for k, (source, place) in enumerate(pairs)
                ]
            )
            for copy in stores[-1]:
                copy.start()

    write_out(0)
    plane_sum(3)
    scatter(0).third()
    for step_to in range(1, 8):
        dp_copy(step_to, True).wait_recv()
    total_shared = dg_in[0, :, 1:2, :]
    for source in range(1, 8):
        total_shared = total_shared + dg_in[source, :, 1:2, :]
    dg_sum[...] = jnp.concatenate(
        [dg_in[source, :, 0:1, :] for source in range(8)]
        + [total_shared, jnp.zeros((4, 7, rows), jnp.float32)],
        axis=1,
    )

    def dz_copy(turn):
        return send(
            dg_sum.at[z_of(turn)],
            dg_far.at[turn - 1],
            dz_send.at[turn],
            dz_recv.at[turn],
            (z_of(turn), me_e),
        )

    for turn in (1, 2, 3):
        dz_copy(turn).start()
    write_out(1)
    plane_sum(0)
    write_out(2)
    pltpu.make_async_copy(out_buf, out_part.at[pl.ds(0, 4), me_z], local_sem.at[2]).wait()
    for turn in (1, 2, 3):
        dz_copy(turn).wait_recv()
    dg_own[...] = dg_sum[me_z] + dg_far[0] + dg_far[1] + dg_far[2]
    for turn in (1, 2, 3):
        far_send(turn).wait_recv()

    @pl.loop(0, rows, step=32)
    def _(row):
        span = pl.ds(pl.multiple_of(row, 32), 32)
        total = sum_x[0, span, :].astype(jnp.float32)
        for turn in range(3):
            total = total + far_x[turn, span, :].astype(jnp.float32)
        dx_own[span, :] = total

    for copy in stores[-2] + stores[-1]:
        copy.wait()
    scatter(3).copy(0).wait_send()
    scatter(0).copy(7).wait_send()
    for turn in (1, 2, 3):
        z_copy(turn, False).wait_send()
        dz_copy(turn).wait_send()
        far_send(turn).wait_send()
    for step_to in range(1, 8):
        dp_copy(step_to, False).wait_send()
    for turn in (1, 2, 3):
        gather(turn).drain()


def mlp_call(x_all, gates_all, all_cot, w_all, up_weight, down_weight, shared_weight):
    num_expert, num_dp, rows, width = all_cot.shape
    routed_units = w_all.shape[1]
    units = routed_units + shared_weight.shape[1] // num_expert
    low, full = jnp.bfloat16, jnp.float32
    shape = jax.ShapeDtypeStruct
    any_space = pl.BlockSpec(memory_space=pl.ANY)
    vmem = pl.BlockSpec(memory_space=pltpu.VMEM)
    dma = pltpu.SemaphoreType.DMA
    flops = 18 * num_expert * num_dp * rows * units * width
    return pl.pallas_call(
        functools.partial(mlp_kernel, routed_units),
        out_shape=(
            shape((num_dp, num_expert, rows, width), low),
            shape((num_expert, num_dp, rows, width), low),
            shape((rows, width), full),
            shape((16, rows), full),
            shape((3, routed_units, width), low),
            shape(shared_weight.shape, low),
            shape((3, num_dp * routed_units, width // num_dp), low),
        ),
        in_specs=[any_space, vmem] + [any_space] * 5,
        input_output_aliases={0: 0},
        out_specs=(any_space, any_space, vmem, vmem, any_space, any_space, any_space),
        scratch_shapes=[
            pltpu.VMEM((2 * units, width), low),
            pltpu.VMEM((units, width), low),
            pltpu.VMEM((2 * units, width), full),
            pltpu.VMEM((units, width), full),
            pltpu.VMEM((2, units - routed_units, width), low),
            pltpu.VMEM((4, rows, width), low),
            pltpu.VMEM((4, rows, width), low),
            pltpu.VMEM((2 * units, 4 * rows), full),
            pltpu.VMEM((units, 4 * rows), full),
            pltpu.VMEM((2 * units, 4 * rows), low),
            pltpu.VMEM((units, 4 * rows), low),
            pltpu.VMEM((4, rows, width), low),
            pltpu.VMEM((2, 2, rows, width), low),
            pltpu.VMEM((3, 4, rows, width), low),
            pltpu.VMEM((2, 2, 2, rows, width), low),
            pltpu.VMEM((2, 2, rows // 2, width), low),
            pltpu.VMEM((3, 2, rows, width), low),
            pltpu.VMEM((4, rows, width), low),
            pltpu.VMEM((3, rows, width), low),
            pltpu.VMEM((num_expert, num_dp, 8, rows), full),
            pltpu.VMEM((num_expert, num_dp, 8, rows), full),
            pltpu.VMEM((num_dp, 16, rows), full),
            pltpu.VMEM((3, 16, rows), full),
            dma((4, 10)),
            dma((4, 10)),
            dma((4,)),
            dma((4,)),
            dma((4, 8)),
            dma((4, 8)),
            dma((4,)),
            dma((4,)),
            dma((8,)),
            dma((8,)),
            dma((4,)),
            dma((4,)),
            dma((18,)),
        ],
        compiler_params=pltpu.CompilerParams(
            collective_id=0, has_side_effects=True, vmem_limit_bytes=63 * 2**20
        ),
        cost_estimate=pl.CostEstimate(flops=flops, bytes_accessed=80 * 2**20, transcendentals=0),
    )(x_all, gates_all, all_cot, w_all, up_weight, down_weight, shared_weight)


def swap_halves(values):
    half = values.shape[-1] // 2
    return jnp.concatenate([values[:, half:], values[:, :half]], axis=1)


def tail_kernel(
    mixed,
    qkv,
    probs,
    normed,
    w_qkv,
    w_out,
    tables,
    tokens,
    params,
    d_rows,
    d_gates,
    routes,
    router_probs,
    normed_two,
    hidden,
    cotangent,
    out_part,
    d_routed,
    _shared_in,
    _expert_in,
    output,
    tokens_grad,
    small_out,
    attn_all,
    shared_all,
    expert_all,
    rows_all,
    normed_part,
    d_mixed,
    d_qkv,
    out_grad,
    grads,
    grads_in,
    out_in,
    grads_sum,
    n_sib,
    n_relayed,
    n_crossed,
    f_own,
    f_sib,
    f_relayed,
    f_crossed,
    f_sum,
    f_far,
    d_normed,
    small,
    small_far,
    small_plane,
    e_send,
    e_recv,
    a_send,
    a_recv,
    o_send,
    o_recv,
    z_send,
    z_recv,
    y_send,
    y_recv,
    n_send,
    n_recv,
    f_send,
    f_recv,
    fz_send,
    fz_recv,
    s_send,
    s_recv,
    g_send,
    g_recv,
    h_send,
    h_recv,
    t_send,
    t_recv,
    p_send,
    p_recv,
    local_sem,
):
    me_z = lax.axis_index("dp")
    me_e = lax.axis_index("expert")
    core = lax.rem(me_e, 2)
    me_x = lax.rem(lax.div(me_e, 2), 2)
    me_y = lax.div(me_e, 4)
    nbr = {1: flip(me_e, 1), 2: flip(me_e, 2), 4: flip(me_e, 4)}
    nbr[6] = flip(nbr[2], 4)
    nbr[3], nbr[5], nbr[7] = flip(nbr[2], 1), flip(nbr[4], 1), flip(nbr[6], 1)
    far = {turn: flip_pair(me_z, turn) for turn in (1, 2, 3)}
    where = {0: me_z, **far}
    rows, width = tokens.shape
    head_width = mixed.shape[1]
    shard_width = width // 4
    routed_units = d_routed.shape[1]
    units = shared_all.shape[1] // 8
    heads = head_width // HEAD
    sequences = 8
    score_scale = HEAD ** (-0.5)

    greet([(far[turn], me_e) for turn in (1, 2, 3)] + [(me_z, nbr[k]) for k in range(1, 8)])

    def lanes(index, amount):
        return pl.ds(pl.multiple_of(index * amount, amount), amount)

    def expert_send(part, turn):
        return send(
            d_routed.at[part, :, lanes(far[turn], shard_width)],
            expert_all.at[part, pl.ds(pl.multiple_of(me_z * routed_units, 16), routed_units)],
            e_send.at[part, turn],
            e_recv.at[part, turn],
            (far[turn], me_e),
        )

    def expert_wait(part, turn):
        here = expert_all.at[part, pl.ds(pl.multiple_of(far[turn] * routed_units, 16), routed_units)]
        send(here, here, e_send.at[part, turn], e_recv.at[part, turn], (far[turn], me_e)).wait_recv()

    split = units // 32 * 16

    def shared_region(owner, half):
        base = pl.multiple_of(owner * units, 16)
        if half is None:
            return shared_all.at[:, pl.ds(base, units)]
        if half == 0:
            return shared_all.at[:, pl.ds(base, split)]
        return shared_all.at[:, pl.ds(pl.multiple_of(base + split, 16), units - split)]

    shared = PlaneGather(shared_region, s_send, s_recv, me_z, me_e, nbr)

    def rows_region(owner, half):
        if half is None:
            return rows_all.at[owner]
        return rows_all.at[owner, pl.ds(half * (rows // 2), rows // 2)]

    gather = PlaneGather(rows_region, a_send, a_recv, me_z, me_e, nbr)
    forward = {
        turn: PlaneScatter(
            out_part.at[:, 1 - core, where[turn]],
            f_own.at[turn % 2],
            f_sib.at[turn],
            f_relayed.at[turn],
            f_crossed.at[turn],
            (f_send.at[turn], f_recv.at[turn]),
            (me_y, me_x),
            me_z,
            nbr,
        )
        for turn in range(4)
    }

    def forward_load(turn):
        return pltpu.make_async_copy(
            out_part.at[:, core, where[turn]], f_own.at[turn % 2], local_sem.at[3 + turn % 2]
        )

    def far_send(turn):
        return send(
            f_sum.at[turn], f_far.at[turn - 1], fz_send.at[turn], fz_recv.at[turn], (where[turn], me_e)
        )

    def forward_last(turn):
        def store(span, total):
            f_sum[turn, span, :] = total.astype(jnp.bfloat16)

        forward[turn].fourth(store)
        if turn:
            far_send(turn).start()

    forward_load(1).start()
    forward_load(2).start()
    forward[1].first()
    forward[2].first()

    top, gate = router_probs[:8], router_probs[8:9]
    d_top = d_gates[:8] * named_of(routes)
    d_logits = top * (d_top - jnp.sum(top * d_top, axis=0, keepdims=True))
    line = lax.broadcasted_iota(jnp.int32, (8, rows), 0)
    d_rest = jnp.where(line == 0, d_gates[8:9] * gate * (1.0 - gate), 0.0)
    d_route = jnp.concatenate([d_logits, d_rest], axis=0).astype(jnp.bfloat16)
    small[...] = jnp.dot(d_route, normed_two[...], preferred_element_type=jnp.float32)
    d_normed[...] = d_rows[...] + lax.dot_general(
        d_route, params[...], TN, preferred_element_type=jnp.float32
    )
    gains = params[...].astype(jnp.float32)

    def norm_back_rows(value, up, gain):
        scale = lax.rsqrt(jnp.mean(value * value, axis=-1, keepdims=True) + EPS)
        scaled = gain * up
        grad = scale * scaled - value * (scale * scale * scale) * jnp.mean(
            scaled * value, axis=-1, keepdims=True
        )
        return grad, jnp.sum(up * value * scale, axis=0, keepdims=True)

    def hidden_step(index, gain_sum):
        span = pl.ds(pl.multiple_of(index * 16, 16), 16)
        grad, term = norm_back_rows(hidden[span, :], d_normed[span, :], gains[10:11])
        grad = cotangent[span, :].astype(jnp.float32) + grad
        tokens_grad[span, :] = grad
        rows_all[me_e, span, :] = grad.astype(jnp.bfloat16)
        return gain_sum + term

    small[10:11, :] = lax.fori_loop(0, rows // 16, hidden_step, jnp.zeros((1, width), jnp.float32))
    gather.begin()
    for part in range(3):
        for turn in (1, 2, 3):
            expert_send(part, turn).start()
    gather.relay()
    forward_load(1).wait()
    forward[1].second()
    gather.relay_far()
    gather.finish()
    forward[1].third()
    forward[3].first()
    forward[0].first()

    all_rows = sequences * rows
    d_mixed[...] = lax.dot_general(
        rows_all[...].reshape(all_rows, width), w_out[...], NT, preferred_element_type=jnp.float32
    ).astype(jnp.bfloat16)
    for n in range(4):
        cols = slice(n * shard_width, (n + 1) * shard_width)
        out_grad[:, cols] = lax.dot_general(
            mixed[...],
            rows_all[:, :, cols].reshape(all_rows, shard_width),
            TN,
            preferred_element_type=jnp.float32,
        ).astype(jnp.bfloat16)
    span_out = pl.ds(pl.multiple_of(me_e * head_width, head_width), head_width)

    def out_send(step):
        return send(
            out_grad.at[:, lanes(nbr[step], head_width)],
            grads.at[3, span_out],
            o_send.at[step],
            o_recv.at[step],
            (me_z, nbr[step]),
        )

    for step in range(1, 8):
        out_send(step).start()
    grads[3, span_out, :] = out_grad[:, lanes(me_e, head_width)]
    forward_load(2).wait()
    forward[2].second()
    forward_last(1)

    def chain_of(first, amount, landing, sems):
        def part(owner):
            return grads.at[
                pl.ds(first, amount), pl.ds(pl.multiple_of(owner * shard_width, shard_width), shard_width)
            ]

        def add(slot, owner):
            for index in range(amount):

                @pl.loop(0, shard_width, step=64)
                def _(row, index=index):
                    span = pl.ds(pl.multiple_of(row, 64), 64)
                    theirs = pl.ds(pl.multiple_of(owner * shard_width + row, 64), 64)
                    landing[slot, index, span, :] = (
                        landing[slot, index, span, :] + grads[first + index, theirs, :]
                    )

        def total(*slots):
            for index in range(amount):

                @pl.loop(0, shard_width, step=64)
                def _(row, index=index):
                    span = pl.ds(pl.multiple_of(row, 64), 64)
                    own = pl.ds(pl.multiple_of(me_z * shard_width + row, 64), 64)
                    value = grads[first + index, own, :].astype(jnp.float32)
                    for slot in slots:
                        value = value + landing[slot, index, span, :].astype(jnp.float32)
                    grads_sum[first + index, span, :] = value.astype(jnp.bfloat16)

        chain = ChainScatter(part, landing, add, sems, me_z, me_e)
        last = (lambda: total(4), lambda: total(me_z, 4), lambda: total(me_z))
        return chain, lambda: chain.last(*last)

    chain, chain_last = chain_of(0, 3, grads_in, (z_send, z_recv))
    out_chain, out_chain_last = chain_of(3, 1, out_in, (y_send, y_recv))

    def projections_of(first, amount, sems, place):
        def region(owner, half):
            cols = lanes(owner, head_width)
            if half is None:
                return attn_all.at[pl.ds(first, amount), :, cols]
            return attn_all.at[
                pl.ds(first, amount), pl.ds(half * (shard_width // 2), shard_width // 2), cols
            ]

        own = pltpu.make_async_copy(
            grads_sum.at[pl.ds(first, amount)], region(me_e, None), local_sem.at[place]
        )
        return own, PlaneGather(region, *sems, me_z, me_e, nbr)

    qkv_own, projections = projections_of(0, 3, (g_send, g_recv), 2)
    out_own, out_projection = projections_of(3, 1, (h_send, h_recv), 7)

    def sequence(index, carry):
        span = pl.ds(pl.multiple_of(index * rows, rows), rows)
        for head in range(heads):
            cols = slice(head * HEAD, (head + 1) * HEAD)
            query, key, value = qkv[0, span, cols], qkv[1, span, cols], qkv[2, span, cols]
            up = d_mixed[span, cols]
            weights = probs[index * heads + head]
            values_grad = lax.dot_general(
                weights.astype(jnp.bfloat16), up, TN, preferred_element_type=jnp.float32
            )
            d_probs = lax.dot_general(up, value, NT, preferred_element_type=jnp.float32)
            d_scores = (
                weights * (d_probs - jnp.sum(weights * d_probs, axis=-1, keepdims=True))
            ).astype(jnp.bfloat16)
            d_query = jnp.dot(d_scores, key, preferred_element_type=jnp.float32) * score_scale
            d_key = (
                lax.dot_general(d_scores, query, TN, preferred_element_type=jnp.float32)
                * score_scale
            )
            d_query = d_query * tables[0] - swap_halves(d_query) * tables[1]
            d_key = d_key * tables[0] - swap_halves(d_key) * tables[1]
            for part, value_of in enumerate((d_query, d_key, values_grad)):
                base = part * head_width + head * HEAD
                d_qkv[span, base : base + HEAD] = value_of.astype(jnp.bfloat16)
        return carry

    def normed_load(n):
        return pltpu.make_async_copy(
            normed.at[:, n * 256 : (n + 1) * 256], normed_part.at[n % 2], local_sem.at[5 + n % 2]
        )

    normed_load(0).start()
    lax.fori_loop(0, sequences // 2, sequence, 0)
    for step in range(1, 8):
        here = grads.at[3, pl.ds(pl.multiple_of(nbr[step] * head_width, head_width), head_width)]
        send(here, here, o_send.at[step], o_recv.at[step], (me_z, nbr[step])).wait_recv()
    out_chain.hop(0)
    shared.begin()
    forward[2].third()
    lax.fori_loop(sequences // 2, sequences, sequence, 0)

    for n in range(width // 256):
        cols = slice(n * 256, (n + 1) * 256)
        if n < width // 256 - 1:
            normed_load(n + 1).start()
        normed_load(n).wait()
        term = lax.dot_general(
            normed_part[n % 2], d_qkv[...], TN, preferred_element_type=jnp.float32
        ).astype(jnp.bfloat16)
        for part in range(3):
            grads[part, cols, :] = term[:, part * head_width : (part + 1) * head_width]
    chain.hop(0)
    out_chain.hop(1)
    gather.drain()

    for n in range(width // 256):
        cols = slice(n * 256, (n + 1) * 256)
        term = lax.dot_general(
            d_qkv[...], w_qkv[cols, : 3 * head_width], NT, preferred_element_type=jnp.float32
        ).astype(jnp.bfloat16)
        for owner in range(8):
            mine = lax.rem(owner + core + 1, 2)
            rows_all[4 * mine + owner // 2, :, cols] = term[owner * rows : (owner + 1) * rows]
    back = PlaneScatter(
        rows_all.at[pl.ds(0, 4)],
        rows_all.at[pl.ds(4, 4)],
        n_sib,
        n_relayed,
        n_crossed,
        (n_send, n_recv),
        (me_y, me_x),
        me_z,
        nbr,
    )
    def keep(span, total):
        d_normed[span, :] = total

    def norm_step(index, gain_sum):
        span = pl.ds(pl.multiple_of(index * 16, 16), 16)
        grad, term = norm_back_rows(
            tokens[span, :].astype(jnp.float32), d_normed[span, :], gains[9:10]
        )
        tokens_grad[span, :] = tokens_grad[span, :] + grad
        return gain_sum + term

    def small_send(turn):
        return send(
            small.at[:, lanes(far[turn], shard_width)],
            small_far.at[turn],
            t_send.at[turn],
            t_recv.at[turn],
            (far[turn], me_e),
        )

    def plane_send(step):
        return send(
            small_plane.at[me_e],
            small_plane.at[me_e],
            p_send.at[step],
            p_recv.at[step],
            (me_z, nbr[step]),
        )

    back.first()
    bias_terms = jnp.sum(d_qkv[...].astype(jnp.float32), axis=0, keepdims=True)
    for part in range(3):
        small[11 + part : 12 + part, lanes(me_e, head_width)] = bias_terms[
            :, part * head_width : (part + 1) * head_width
        ]
    back.second()
    out_chain.hop(2)
    chain.hop(1)
    out_chain_last()
    out_own.start()
    out_own.wait()
    out_projection.begin()
    back.third()
    out_projection.relay()
    chain.hop(2)
    out_projection.relay_far()
    shared.relay()
    back.fourth(keep)
    small[9:10, :] = lax.fori_loop(0, rows // 16, norm_step, jnp.zeros((1, width), jnp.float32))
    for turn in (1, 2, 3):
        small_send(turn).start()
    forward_last(2)
    forward[1].drain()
    forward_load(3).start()
    forward_load(3).wait()
    forward[3].second()
    forward[2].drain()
    forward_load(0).start()
    chain_last()
    qkv_own.start()
    qkv_own.wait()
    projections.begin()
    forward[3].third()
    forward_load(0).wait()
    forward[0].second()
    for turn in (1, 2, 3):
        small_send(turn).wait_recv()
    small_plane[me_e] = (
        small[:, lanes(me_z, shard_width)] + small_far[1] + small_far[2] + small_far[3]
    )
    for step in range(1, 8):
        plane_send(step).start()
    shared.relay_far()
    projections.relay()
    forward_last(3)
    forward[0].third()
    for step in range(1, 8):
        here = small_plane.at[nbr[step]]
        send(here, here, p_send.at[step], p_recv.at[step], (me_z, nbr[step])).wait_recv()
    total = small_plane[0]
    for index in range(1, 8):
        total = total + small_plane[index]
    small_out[...] = total
    forward_last(0)
    for turn in (1, 2, 3):
        far_send(turn).wait_recv()

    @pl.loop(0, rows, step=32)
    def _(row):
        span = pl.ds(pl.multiple_of(row, 32), 32)
        total = f_sum[0, span, :].astype(jnp.float32)
        for turn in (1, 2, 3):
            total = total + f_far[turn - 1, span, :].astype(jnp.float32)
        output[span, :] = (hidden[span, :] + total).astype(jnp.bfloat16)

    projections.relay_far()
    shared.finish()
    projections.finish()
    out_projection.finish()
    for turn in (1, 2, 3):
        for part in range(3):
            expert_wait(part, turn)
            expert_send(part, turn).wait_send()
        small_send(turn).wait_send()
        far_send(turn).wait_send()
    for step in range(1, 8):
        out_send(step).wait_send()
        plane_send(step).wait_send()
    for turn in (3, 0):
        forward[turn].drain()
    chain.drain()
    out_chain.drain()
    out_projection.drain()
    back.drain()
    shared.drain()
    projections.drain()


def tail_call(
    mixed, qkv, probs, normed, w_qkv, w_out, tables, tokens, params, d_rows, d_gates, routes, router_probs,
    normed_two, hidden, cotangent, out_part, d_routed, shared_all, expert_all,
):
    rows, width = tokens.shape
    head_width = mixed.shape[1]
    shard_width = width // 4
    low, full = jnp.bfloat16, jnp.float32
    shape = jax.ShapeDtypeStruct
    any_space = pl.BlockSpec(memory_space=pl.ANY)
    vmem = pl.BlockSpec(memory_space=pltpu.VMEM)
    dma = pltpu.SemaphoreType.DMA
    return pl.pallas_call(
        tail_kernel,
        out_shape=(
            shape((rows, width), low),
            shape((rows, width), full),
            shape((16, shard_width), full),
            shape((4, shard_width, width), low),
            shape(shared_all.shape, low),
            shape(expert_all.shape, low),
        ),
        in_specs=[vmem] * 3 + [any_space] + [vmem] * 12 + [any_space] * 4,
        input_output_aliases={18: 4, 19: 5},
        out_specs=(vmem, vmem, vmem, any_space, any_space, any_space),
        scratch_shapes=[
            pltpu.VMEM((8, rows, width), low),
            pltpu.VMEM((2, 8 * rows, 256), low),
            pltpu.VMEM((8 * rows, head_width), low),
            pltpu.VMEM((8 * rows, 3 * head_width), low),
            pltpu.VMEM((head_width, width), low),
            pltpu.VMEM((4, width, head_width), low),
            pltpu.VMEM((5, 3, shard_width, head_width), low),
            pltpu.VMEM((5, 1, shard_width, head_width), low),
            pltpu.VMEM((4, shard_width, head_width), low),
            pltpu.VMEM((4, rows, width), low),
            pltpu.VMEM((2, rows // 2, width), low),
            pltpu.VMEM((2, rows, width), low),
            pltpu.VMEM((2, 4, rows, width), low),
            pltpu.VMEM((4, 4, rows, width), low),
            pltpu.VMEM((4, 2, rows // 2, width), low),
            pltpu.VMEM((4, 2, rows, width), low),
            pltpu.VMEM((4, rows, width), low),
            pltpu.VMEM((3, rows, width), low),
            pltpu.VMEM((rows, width), full),
            pltpu.VMEM((16, width), full),
            pltpu.VMEM((4, 16, shard_width), full),
            pltpu.VMEM((8, 16, shard_width), full),
            dma((3, 4)),
            dma((3, 4)),
            dma((10,)),
            dma((10,)),
            dma((8,)),
            dma((8,)),
            dma((2, 3)),
            dma((2, 3)),
            dma((2, 3)),
            dma((2, 3)),
            dma((7,)),
            dma((7,)),
            dma((4, 7)),
            dma((4, 7)),
            dma((4,)),
            dma((4,)),
            dma((10,)),
            dma((10,)),
            dma((10,)),
            dma((10,)),
            dma((10,)),
            dma((10,)),
            dma((4,)),
            dma((4,)),
            dma((8,)),
            dma((8,)),
            dma((8,)),
        ],
        compiler_params=pltpu.CompilerParams(
            collective_id=1, has_side_effects=True, vmem_limit_bytes=63 * 2**20
        ),
        cost_estimate=pl.CostEstimate(
            flops=24 * 8 * rows * width * head_width, bytes_accessed=80 * 2**20, transcendentals=0
        ),
    )(
        mixed, qkv, probs, normed, w_qkv, w_out, tables, tokens, params, d_rows, d_gates, routes, router_probs,
        normed_two, hidden, cotangent, out_part, d_routed, shared_all, expert_all,
    )


def front_kernel(
    tokens,
    docs,
    routes,
    router,
    gate_vector,
    gain_in,
    gain_out,
    bias_in,
    tables,
    cotangent,
    qkv_weight,
    out_weight,
    up_weight,
    down_weight,
    qkv,
    probs,
    mixed,
    normed,
    hidden,
    normed_two,
    gates_all,
    router_probs,
    params_all,
    weights_out,
    w_out_out,
    cot_all,
    w_all,
    x_all,
    rows_all,
    weights,
    w_out,
    params_in,
    docs_all,
    gates_in,
    qkv_part,
    n_sib,
    n_relayed,
    n_crossed,
    a_send,
    a_recv,
    w_send,
    w_recv,
    p_send,
    p_recv,
    d_send,
    d_recv,
    o_send,
    o_recv,
    n_send,
    n_recv,
    c_send,
    c_recv,
    k_send,
    k_recv,
    e_send,
    e_recv,
    x_send,
    x_recv,
    y_send,
    y_recv,
    g_send,
    g_recv,
    local_sem,
):
    me_z = lax.axis_index("dp")
    me_e = lax.axis_index("expert")
    core = lax.rem(me_e, 2)
    me_x = lax.rem(lax.div(me_e, 2), 2)
    me_y = lax.div(me_e, 4)
    nbr = {1: flip(me_e, 1), 2: flip(me_e, 2), 4: flip(me_e, 4)}
    nbr[6] = flip(nbr[2], 4)
    nbr[3], nbr[5], nbr[7] = flip(nbr[2], 1), flip(nbr[4], 1), flip(nbr[6], 1)
    far = {turn: flip_pair(me_z, turn) for turn in (1, 2, 3)}
    rows, width = tokens.shape
    shard_width = qkv_weight.shape[0]
    head_width = w_out.shape[0]
    heads = head_width // HEAD
    routed_units = down_weight.shape[0] // 4
    sequences = 8
    score_scale = HEAD ** (-0.5)

    def lanes(index, amount):
        return pl.ds(pl.multiple_of(index * amount, amount), amount)

    def lines(index, amount, grain=16):
        return pl.ds(pl.multiple_of(index * amount, grain), amount)

    my_lines = lines(me_z, shard_width)
    own = [
        pltpu.make_async_copy(
            qkv_weight.at[:, pl.ds(pl.multiple_of(part * width + me_e * head_width, head_width), head_width)],
            weights.at[my_lines, part * head_width : (part + 1) * head_width],
            local_sem.at[part],
        )
        for part in range(3)
    ]
    own.append(
        pltpu.make_async_copy(
            out_weight.at[:, lanes(me_e, head_width)],
            weights.at[my_lines, 3 * head_width : 4 * head_width],
            local_sem.at[3],
        )
    )
    own.append(pltpu.make_async_copy(tokens, rows_all.at[me_e], local_sem.at[4]))
    own.append(pltpu.make_async_copy(cotangent, cot_all.at[me_e, me_z], local_sem.at[5]))
    for copy in own:
        copy.start()
    shards = [router[...]] + [ref[...].reshape(1, shard_width) for ref in (gate_vector, gain_in, gain_out)]
    shards = [part.astype(jnp.float32) for part in shards + [bias_in[...]]]
    shards.append(jnp.zeros((2, shard_width), jnp.float32))
    params_in[me_z] = jnp.concatenate(shards, axis=0).astype(jnp.bfloat16)
    docs_all[me_e] = jnp.broadcast_to(docs[...].astype(jnp.float32), docs_all.shape[1:])
    greet([(far[turn], me_e) for turn in (1, 2, 3)] + [(me_z, nbr[k]) for k in range(1, 8)])
    for copy in own:
        copy.wait()

    attn_weights = ChainGather(
        lambda z: weights.at[lines(z, shard_width)], w_send, w_recv, me_z, me_e
    )
    attn_weights.begin()
    cot_chain = ChainGather(lambda z: cot_all.at[me_e, z], k_send, k_recv, me_z, me_e)
    cot_chain.begin()

    def cot_gather(place, z):
        def region(owner, half):
            if half is None:
                return cot_all.at[owner, z]
            return cot_all.at[owner, z, pl.ds(half * (rows // 2), rows // 2)]

        return PlaneGather(region, c_send.at[place], c_recv.at[place], me_z, me_e, nbr)

    cot_own = cot_gather(6, me_z)

    def cot_step(hop, name):
        for way in range(2):
            z = jnp.clip(me_z - (1 - 2 * way) * (hop + 1), 0, 3)
            pl.when(cot_chain.takes(way, hop))(getattr(cot_gather(way * 3 + hop, z), name))

    def expert_copy(part, turn, here):
        source = down_weight if part == 2 else up_weight.at[part]
        z = far[turn] if here else me_z
        target = w_all.at[part, :, lanes(z, shard_width)]
        return send(
            target if here else source.at[lines(far[turn], routed_units)],
            target,
            e_send.at[part, turn],
            e_recv.at[part, turn],
            (far[turn], me_e),
        )

    ends = (me_z == 0) | (me_z == 3)

    def expert_start(turn, from_ends):
        @pl.when(ends if from_ends else jnp.logical_not(ends))
        def _():
            for part in range(3):
                expert_copy(part, turn, False).start()

    def rows_region(owner, half):
        if half is None:
            return rows_all.at[owner]
        return rows_all.at[owner, pl.ds(half * (rows // 2), rows // 2)]

    gather = PlaneGather(rows_region, a_send, a_recv, me_z, me_e, nbr)

    def params_send(turn):
        return send(
            params_in.at[me_z], params_in.at[me_z], p_send.at[turn], p_recv.at[turn], (far[turn], me_e)
        )

    def docs_send(step):
        return send(
            docs_all.at[me_e], docs_all.at[me_e], d_send.at[step], d_recv.at[step], (me_z, nbr[step])
        )

    for turn in (1, 2, 3):
        params_send(turn).start()
    gather.begin()
    for step in range(1, 8):
        docs_send(step).start()
    cot_own.begin()
    gather.relay()
    cot_chain.hop(0)
    cot_step(0, "begin")
    gather.relay_far()
    cot_own.relay()
    for turn in (1, 2, 3):
        here = params_in.at[far[turn]]
        send(here, here, p_send.at[turn], p_recv.at[turn], (far[turn], me_e)).wait_recv()
    params_all[...] = jnp.concatenate([params_in[z] for z in range(4)], axis=1)
    gather.finish()
    attn_weights.hop(0)
    cot_own.relay_far()
    cot_chain.hop(1)
    cot_step(0, "relay")
    cot_step(1, "begin")

    def norm_rows(value, gain):
        scale = lax.rsqrt(jnp.mean(value * value, axis=-1, keepdims=True) + EPS)
        return (value * scale * gain).astype(jnp.bfloat16)

    params_full = params_all[...].astype(jnp.float32)
    gain_one, gain_two = params_full[9:10], params_full[10:11]
    bias = params_all[:, lanes(me_e, head_width)].astype(jnp.float32)[11:14]

    for owner in range(8):

        @pl.loop(0, rows, step=16)
        def _(row, owner=owner):
            span = pl.ds(pl.multiple_of(row, 16), 16)
            normed[pl.ds(pl.multiple_of(owner * rows + row, 16), 16), :] = norm_rows(
                rows_all[owner, span, :].astype(jnp.float32), gain_one
            )

    cot_step(0, "relay_far")
    attn_weights.hop(1)
    expert_start(1, True)
    expert_start(2, True)
    expert_start(3, False)
    cot_chain.hop(2)

    cot_step(1, "relay")
    cot_step(2, "begin")
    attn_weights.hop(2)
    expert_start(1, False)
    expert_start(2, False)
    expert_start(3, True)

    def out_send(step):
        return send(
            weights.at[lines(nbr[step], head_width), 3 * head_width : 4 * head_width],
            w_out.at[:, lanes(me_e, head_width)],
            o_send.at[step],
            o_recv.at[step],
            (me_z, nbr[step]),
        )

    for step in range(1, 8):
        out_send(step).start()
    w_out[:, lanes(me_e, head_width)] = weights[lines(me_e, head_width), 3 * head_width :]
    weights_store = pltpu.make_async_copy(weights, weights_out, local_sem.at[0])
    weights_store.start()

    for part in range(3):
        cols = slice(part * head_width, (part + 1) * head_width)
        qkv_part[...] = (
            jnp.dot(normed[...], weights[:, cols], preferred_element_type=jnp.float32)
            + bias[part : part + 1]
        )
        if part == 2:
            qkv[part] = qkv_part[...].astype(jnp.bfloat16)
        else:

            @pl.loop(0, sequences)
            def _(index, part=part):
                span = pl.ds(pl.multiple_of(index * rows, rows), rows)
                for head in range(heads):
                    at = slice(head * HEAD, (head + 1) * HEAD)
                    value = qkv_part[span, at]
                    qkv[part, span, at] = (
                        value * tables[0] + swap_halves(value) * tables[1]
                    ).astype(jnp.bfloat16)

    order = lax.broadcasted_iota(jnp.int32, (rows, rows), 0) >= lax.broadcasted_iota(
        jnp.int32, (rows, rows), 1
    )

    def sequence(index, carry):
        span = pl.ds(pl.multiple_of(index * rows, rows), rows)
        doc = jnp.broadcast_to(docs_all[index, 0:1, :], (rows, rows))
        allowed = (doc == doc.T) & order
        for head in range(heads):
            at = slice(head * HEAD, (head + 1) * HEAD)
            scores = (
                lax.dot_general(
                    qkv[0, span, at], qkv[1, span, at], NT, preferred_element_type=jnp.float32
                )
                * score_scale
            )
            scores = jnp.where(allowed, scores, NEGATIVE)
            exp_scores = jnp.exp(scores - jnp.max(scores, axis=-1, keepdims=True))
            weight = exp_scores / jnp.sum(exp_scores, axis=-1, keepdims=True)
            probs[index * heads + head] = weight
            mixed[span, at] = jnp.dot(
                weight.astype(jnp.bfloat16), qkv[2, span, at], preferred_element_type=jnp.float32
            ).astype(jnp.bfloat16)
        return carry

    cot_step(1, "relay_far")
    cot_step(2, "relay")
    for step in range(1, 8):
        here = docs_all.at[nbr[step]]
        send(here, here, d_send.at[step], d_recv.at[step], (me_z, nbr[step])).wait_recv()
    lax.fori_loop(0, sequences // 2, sequence, 0)
    cot_step(2, "relay_far")
    lax.fori_loop(sequences // 2, sequences, sequence, 0)
    gather.drain()

    for step in range(1, 8):
        here = w_out.at[:, lanes(nbr[step], head_width)]
        send(here, here, o_send.at[step], o_recv.at[step], (me_z, nbr[step])).wait_recv()
    for n in range(width // shard_width):
        cols = slice(n * shard_width, (n + 1) * shard_width)
        term = jnp.dot(mixed[...], w_out[:, cols], preferred_element_type=jnp.float32).astype(
            jnp.bfloat16
        )
        for owner in range(8):
            mine = lax.rem(owner + core + 1, 2)
            rows_all[4 * mine + owner // 2, :, cols] = term[owner * rows : (owner + 1) * rows]
    sums = PlaneScatter(
        rows_all.at[pl.ds(0, 4)],
        rows_all.at[pl.ds(4, 4)],
        n_sib,
        n_relayed,
        n_crossed,
        (n_send, n_recv),
        (me_y, me_x),
        me_z,
        nbr,
    )
    sums.first()
    out_store = pltpu.make_async_copy(w_out, w_out_out, local_sem.at[1])
    out_store.start()
    sums.second()

    sums.third()

    def keep(span, total):
        hidden[span, :] = total + tokens[span, :].astype(jnp.float32)

    sums.fourth(keep)

    @pl.loop(0, rows, step=16)
    def _(row):
        span = pl.ds(pl.multiple_of(row, 16), 16)
        normed_two[span, :] = norm_rows(hidden[span, :], gain_two)

    logits = lax.dot_general(
        params_all[...], normed_two[...], NT, preferred_element_type=jnp.float32
    )
    top = jnp.exp(logits[:8] - jnp.max(logits[:8], axis=0, keepdims=True))
    top = top / jnp.sum(top, axis=0, keepdims=True)
    line = lax.broadcasted_iota(jnp.int32, (8, rows), 0)
    rest = jnp.where(line == 0, jax.nn.sigmoid(logits[8:]), 0.0)
    router_probs[...] = jnp.concatenate([top, rest], axis=0)
    x_own = pltpu.make_async_copy(normed_two, x_all.at[me_z, me_e], local_sem.at[2])
    x_own.start()
    gates_in[me_e, me_z] = jnp.concatenate([top * named_of(routes), rest], axis=0)

    def gates_far(turn, z):
        here = gates_in.at[me_e, z]
        return send(here, here, y_send.at[turn], y_recv.at[turn], (far[turn], me_e))

    def gates_near(step, owner):
        here = gates_in.at[owner]
        return send(here, here, g_send.at[step], g_recv.at[step], (me_z, nbr[step]))

    for turn in (1, 2, 3):
        gates_far(turn, me_z).start()

    def x_region(owner, half):
        if half is None:
            return x_all.at[me_z, owner]
        return x_all.at[me_z, owner, pl.ds(half * (rows // 2), rows // 2)]

    x_gather = PlaneGather(x_region, x_send, x_recv, me_z, me_e, nbr)
    x_own.wait()
    x_gather.begin()
    for turn in (1, 2, 3):
        gates_far(turn, far[turn]).wait_recv()
    for step in range(1, 8):
        gates_near(step, me_e).start()
    x_gather.relay()
    x_gather.relay_far()
    for step in range(1, 8):
        gates_near(step, nbr[step]).wait_recv()
    gates_all[...] = gates_in[...]
    x_gather.finish()

    cot_own.finish()
    for hop in range(3):
        cot_step(hop, "finish")
    for turn in (1, 2, 3):
        for part in range(3):
            expert_copy(part, turn, True).wait_recv()
            expert_copy(part, turn, False).wait_send()
        params_send(turn).wait_send()
        gates_far(turn, me_z).wait_send()
    for step in range(1, 8):
        docs_send(step).wait_send()
        gates_near(step, me_e).wait_send()
        out_send(step).wait_send()
    weights_store.wait()
    out_store.wait()
    attn_weights.drain()
    cot_chain.drain()
    sums.drain()
    x_gather.drain()
    cot_own.drain()
    for hop in range(3):
        cot_step(hop, "drain")


def front_call(
    tokens, docs, routes, router, gate_vector, gain_in, gain_out, bias_in, tables, cotangent, qkv_weight,
    out_weight, up_weight, down_weight,
):
    rows, width = tokens.shape
    shard_width = qkv_weight.shape[0]
    head_width = width // 8
    pairs = 8 * head_width // HEAD
    routed_units = down_weight.shape[0] // 4
    low, full = jnp.bfloat16, jnp.float32
    shape = jax.ShapeDtypeStruct
    any_space = pl.BlockSpec(memory_space=pl.ANY)
    vmem = pl.BlockSpec(memory_space=pltpu.VMEM)
    dma = pltpu.SemaphoreType.DMA
    return pl.pallas_call(
        front_kernel,
        out_shape=(
            shape((3, 8 * rows, head_width), low),
            shape((pairs, rows, rows), full),
            shape((8 * rows, head_width), low),
            shape((8 * rows, width), low),
            shape((rows, width), full),
            shape((rows, width), low),
            shape((8, 4, 16, rows), full),
            shape((16, rows), full),
            shape((16, width), low),
            shape((width, 4 * head_width), low),
            shape((head_width, width), low),
            shape((8, 4, rows, width), low),
            shape((3, routed_units, width), low),
            shape((4, 8, rows, width), low),
        ),
        in_specs=[vmem] * 10 + [any_space] * 4,
        out_specs=tuple([vmem] * 9 + [any_space] * 5),
        scratch_shapes=[
            pltpu.VMEM((8, rows, width), low),
            pltpu.VMEM((width, 4 * head_width), low),
            pltpu.VMEM((head_width, width), low),
            pltpu.VMEM((4, 16, shard_width), low),
            pltpu.VMEM((8, 8, rows), full),
            pltpu.VMEM((8, 4, 16, rows), full),
            pltpu.VMEM((8 * rows, head_width), full),
            pltpu.VMEM((4, rows, width), low),
            pltpu.VMEM((2, rows // 2, width), low),
            pltpu.VMEM((2, rows, width), low),
            dma((10,)),
            dma((10,)),
            dma((2, 3)),
            dma((2, 3)),
            dma((4,)),
            dma((4,)),
            dma((8,)),
            dma((8,)),
            dma((8,)),
            dma((8,)),
            dma((7,)),
            dma((7,)),
            dma((7, 10)),
            dma((7, 10)),
            dma((2, 3)),
            dma((2, 3)),
            dma((3, 4)),
            dma((3, 4)),
            dma((10,)),
            dma((10,)),
            dma((4,)),
            dma((4,)),
            dma((8,)),
            dma((8,)),
            dma((6,)),
        ],
        compiler_params=pltpu.CompilerParams(
            collective_id=2, has_side_effects=True, vmem_limit_bytes=60 * 2**20
        ),
        cost_estimate=pl.CostEstimate(
            flops=8 * 8 * rows * width * head_width, bytes_accessed=80 * 2**20, transcendentals=0
        ),
    )(
        tokens, docs, routes, router, gate_vector, gain_in, gain_out, bias_in, tables, cotangent, qkv_weight,
        out_weight, up_weight, down_weight,
    )


def widen_kernel(
    attn_all, shared_all, expert_all, small, rows, rows_grad, qkv, out, shared, up, down, router, gate, gain_in,
    gain_out, bias, output, tokens_grad,
):
    output[...] = rows[...]
    tokens_grad[...] = rows_grad[...]
    for part in range(3):
        width = attn_all.shape[2]
        qkv[:, part * width : (part + 1) * width] = attn_all[part].astype(jnp.float32)
        shared[part] = shared_all[part].astype(jnp.float32)
    out[...] = attn_all[3].astype(jnp.float32)
    for part in range(2):
        up[:, part, :] = expert_all[part].astype(jnp.float32)
    down[...] = expert_all[2].astype(jnp.float32)

    @pl.when(pl.program_id(0) == 0)
    def _():
        router[...] = small[:8, :]
        for row, target in ((8, gate), (9, gain_in), (10, gain_out)):
            target[...] = small[row, :]
        bias[...] = small[11:14, :]


def widen_call(attn_all, shared_all, expert_all, small, rows, rows_grad):
    steps = 8
    _, depth, width = attn_all.shape
    units, routed, cols = shared_all.shape[1], expert_all.shape[1], expert_all.shape[2]
    full = jnp.float32
    shape = jax.ShapeDtypeStruct
    return pl.pallas_call(
        widen_kernel,
        grid=(steps,),
        out_shape=(
            shape((depth, 3 * width), full),
            shape((depth, width), full),
            shape(shared_all.shape, full),
            shape((routed, 2, cols), full),
            shape((routed, cols), full),
            shape((8, depth), full),
            shape((depth,), full),
            shape((depth,), full),
            shape((depth,), full),
            shape((3, depth), full),
            shape(rows.shape, rows.dtype),
            shape(rows.shape, full),
        ),
        in_specs=[
            pl.BlockSpec((4, depth // steps, width), lambda i: (0, i, 0)),
            pl.BlockSpec((3, units // steps, width), lambda i: (0, i, 0)),
            pl.BlockSpec((3, routed // steps, cols), lambda i: (0, i, 0)),
            pl.BlockSpec((16, depth), lambda i: (0, 0)),
            pl.BlockSpec((rows.shape[0] // steps, width), lambda i: (i, 0)),
            pl.BlockSpec((rows.shape[0] // steps, width), lambda i: (i, 0)),
        ],
        out_specs=(
            pl.BlockSpec((depth // steps, 3 * width), lambda i: (i, 0)),
            pl.BlockSpec((depth // steps, width), lambda i: (i, 0)),
            pl.BlockSpec((3, units // steps, width), lambda i: (0, i, 0)),
            pl.BlockSpec((routed // steps, 2, cols), lambda i: (i, 0, 0)),
            pl.BlockSpec((routed // steps, cols), lambda i: (i, 0)),
            pl.BlockSpec((8, depth), lambda i: (0, 0)),
            pl.BlockSpec((depth,), lambda i: (0,)),
            pl.BlockSpec((depth,), lambda i: (0,)),
            pl.BlockSpec((depth,), lambda i: (0,)),
            pl.BlockSpec((3, depth), lambda i: (0, 0)),
            pl.BlockSpec((rows.shape[0] // steps, width), lambda i: (i, 0)),
            pl.BlockSpec((rows.shape[0] // steps, width), lambda i: (i, 0)),
        ),
        compiler_params=pltpu.CompilerParams(vmem_limit_bytes=60 * 2**20),
        cost_estimate=pl.CostEstimate(flops=0, bytes_accessed=96 * 2**20, transcendentals=0),
    )(attn_all, shared_all, expert_all, small, rows, rows_grad)


def silu_parts(gate):
    logistic = jax.nn.sigmoid(gate)
    silu = gate * logistic
    return (silu, logistic * (1.0 + gate * (1.0 - logistic)))


def gather_all(rows):
    rows = lax.all_gather(rows, "dp", axis=0, tiled=True)
    return lax.all_gather(rows, "expert", axis=0, tiled=True)


def scatter_all(rows):
    rows = lax.psum_scatter(rows, "expert", scatter_dimension=0, tiled=True)
    return lax.psum_scatter(rows, "dp", scatter_dimension=0, tiled=True)


def shards(
    tokens,
    attn_gain,
    qkv_weight,
    qkv_bias,
    out_weight,
    ffn_gain,
    router_weight,
    shared_gate_weight,
    shared_weight,
    expert_up,
    expert_down,
    routes,
    segment_ids,
    cotangent,
):
    num_dp = lax.axis_size("dp")
    num_expert = lax.axis_size("expert")
    me_expert = lax.axis_index("expert")
    seq_len, model_width = tokens.shape
    shard_width = qkv_weight.shape[0]
    head_count = HEADS // num_expert
    head_width = head_count * HEAD
    plane_rows = seq_len * num_expert
    units = shared_weight.shape[0] // num_expert
    score_scale = HEAD ** (-0.5)

    small = jnp.concatenate(
        [
            attn_gain[None],
            ffn_gain[None],
            shared_gate_weight[None],
            qkv_bias,
            router_weight.T,
        ],
        axis=0,
    )
    small = lax.all_gather(small, "dp", axis=1, tiled=True)
    gain_one = small[0].astype(jnp.float32)
    gain_two = small[1].astype(jnp.float32)
    bias_cols = lax.dynamic_slice_in_dim(small[3:6], me_expert * head_width, head_width, 1)
    w_route = jnp.concatenate([small[6:], small[2:3]], axis=0)

    plane_tokens = lax.all_gather(tokens, "expert", axis=0, tiled=True)
    plane_docs = lax.all_gather(segment_ids, "expert", axis=0, tiled=True)
    cols_qkv = lax.dynamic_slice_in_dim(
        qkv_weight.reshape(shard_width, 3, model_width), me_expert * head_width, head_width, 2
    ).reshape(shard_width, 3 * head_width)
    cols_out = lax.dynamic_slice_in_dim(out_weight, me_expert * head_width, head_width, 1)
    attn_weights = lax.all_gather(
        jnp.concatenate([cols_qkv, cols_out], axis=1), "dp", axis=0, tiled=True
    )
    w_qkv = attn_weights[:, : 3 * head_width]
    w_out = lax.all_to_all(
        attn_weights[:, 3 * head_width :], "expert", split_axis=0, concat_axis=1, tiled=True
    )

    expert_full = jnp.concatenate([expert_up[0], expert_down[0][:, None, :]], axis=1)
    expert_units = lax.all_to_all(expert_full, "dp", split_axis=0, concat_axis=2, tiled=True)
    shared_units = lax.dynamic_slice_in_dim(shared_weight, me_expert * units, units, 0)
    mlp_weight = jnp.concatenate([expert_units, shared_units], axis=0)
    routed_units = expert_units.shape[0]
    all_units = routed_units + units

    all_cot = gather_all(cotangent)
    all_routes = gather_all(routes)

    plane_resid = plane_tokens.astype(jnp.float32)
    normed_one = (plane_resid * rms_scale(plane_resid) * gain_one).astype(jnp.bfloat16)
    qkv_rows = jnp.dot(normed_one, w_qkv, preferred_element_type=jnp.float32) + bias_cols.reshape(
        -1
    ).astype(jnp.float32)
    qkv_rows = qkv_rows.reshape(num_expert, seq_len, 3, head_count, HEAD)
    cosine_table, sine_table = rope_tables(seq_len, HEAD)
    query_rows = rotate(qkv_rows[:, :, 0], cosine_table, sine_table).astype(jnp.bfloat16)
    key_rows = rotate(qkv_rows[:, :, 1], cosine_table, sine_table).astype(jnp.bfloat16)
    value_rows = qkv_rows[:, :, 2].astype(jnp.bfloat16)
    positions = jnp.arange(seq_len)
    allowed = (
        (plane_docs[:, :, None] == plane_docs[:, None, :])
        & (positions[:, None] >= positions[None, :])[None]
    )[:, None]
    scores = (
        jnp.einsum("bthd,bshd->bhts", query_rows, key_rows, preferred_element_type=jnp.float32)
        * score_scale
    )
    scores = jnp.where(allowed, scores, NEGATIVE)
    exp_scores = jnp.exp(scores - jnp.max(scores, axis=-1, keepdims=True))
    attn_probs = exp_scores / jnp.sum(exp_scores, axis=-1, keepdims=True)
    probs_low = attn_probs.astype(jnp.bfloat16)
    mixed_heads = (
        jnp.einsum("bhts,bshd->bthd", probs_low, value_rows, preferred_element_type=jnp.float32)
        .reshape(plane_rows, head_width)
        .astype(jnp.bfloat16)
    )
    attn_part = jnp.dot(mixed_heads, w_out, preferred_element_type=jnp.float32)
    attn_out = lax.psum_scatter(
        attn_part.astype(jnp.bfloat16), "expert", scatter_dimension=0, tiled=True
    )

    resid_in = tokens.astype(jnp.float32)
    hidden_state = resid_in + attn_out.astype(jnp.float32)
    rms_two = rms_scale(hidden_state)
    normed_two = (hidden_state * rms_two * gain_two).astype(jnp.bfloat16)

    all_normed = gather_all(normed_two)
    all_logits = jnp.einsum(
        "td,ed->te", all_normed, w_route, preferred_element_type=jnp.float32
    )
    all_probs = jax.nn.softmax(all_logits[:, :num_expert], axis=-1)
    all_named = jnp.any(all_routes == me_expert, axis=1)
    my_prob = jnp.sum(
        jnp.where(jnp.arange(num_expert)[None, :] == me_expert, all_probs, 0.0), axis=1
    )
    gate_routed = jnp.where(all_named, my_prob, 0.0)
    gate_shared = jax.nn.sigmoid(all_logits[:, num_expert])
    is_routed = (jnp.arange(all_units) < routed_units)[None, :]
    row_gate = jnp.where(is_routed, gate_routed[:, None], gate_shared[:, None])

    gate_up = jnp.einsum(
        "td,fgd->gtf", all_normed, mlp_weight[:, :2], preferred_element_type=jnp.float32
    )
    silu, d_silu = silu_parts(gate_up[0])
    act = silu * gate_up[1]
    raw_act_grad = jnp.einsum(
        "td,fd->tf", all_cot, mlp_weight[:, 2], preferred_element_type=jnp.float32
    )
    gated_act = (row_gate * act).astype(jnp.bfloat16)
    act_dots = act * raw_act_grad
    d_gate_routed = jnp.where(
        all_named, jnp.sum(jnp.where(is_routed, act_dots, 0.0), axis=1), 0.0
    )
    d_gate_shared = jnp.sum(jnp.where(is_routed, 0.0, act_dots), axis=1)
    act_grad = raw_act_grad * row_gate
    d_gate_up = jnp.stack([act_grad * gate_up[1] * d_silu, act_grad * silu], axis=0).astype(
        jnp.bfloat16
    )
    d_rows = jnp.einsum(
        "gtf,fgd->td", d_gate_up, mlp_weight[:, :2], preferred_element_type=jnp.float32
    ).astype(jnp.bfloat16)
    gate_cols = jnp.concatenate(
        [
            jnp.where(
                jnp.arange(num_expert)[None, :] == me_expert, d_gate_routed[:, None], 0.0
            ),
            d_gate_shared[:, None],
        ],
        axis=1,
    )
    d_gate_cols = scatter_all(gate_cols)
    d_rows_sum = scatter_all(d_rows).astype(jnp.float32)

    up_grad = jnp.einsum(
        "gtf,td->fgd", d_gate_up, all_normed, preferred_element_type=jnp.float32
    ).astype(jnp.bfloat16)
    down_grad = jnp.einsum(
        "tf,td->fd", gated_act, all_cot, preferred_element_type=jnp.float32
    ).astype(jnp.bfloat16)
    out_rows = jnp.dot(gated_act, mlp_weight[:, 2], preferred_element_type=jnp.float32).astype(
        jnp.bfloat16
    )
    output = (hidden_state + scatter_all(out_rows).astype(jnp.float32)).astype(jnp.bfloat16)
    mlp_grad = jnp.concatenate([up_grad, down_grad[:, None, :]], axis=1)
    expert_grad = lax.all_to_all(
        mlp_grad[:routed_units], "dp", split_axis=2, concat_axis=0, tiled=True
    ).astype(jnp.float32)
    shared_grad = lax.all_gather(
        mlp_grad[routed_units:], "expert", axis=0, tiled=True
    ).astype(jnp.float32)

    back_grad = cotangent.astype(jnp.float32)
    logits = jnp.einsum("td,ed->te", normed_two, w_route, preferred_element_type=jnp.float32)
    router_probs = jax.nn.softmax(logits[:, :num_expert], axis=-1)
    logistic_gate = jax.nn.sigmoid(logits[:, num_expert:])
    d_router_probs = d_gate_cols[:, :num_expert]
    d_logits = router_probs * (
        d_router_probs - jnp.sum(router_probs * d_router_probs, axis=-1, keepdims=True)
    )
    d_gate_logit = d_gate_cols[:, num_expert:] * logistic_gate * (1.0 - logistic_gate)
    d_route = jnp.concatenate([d_logits, d_gate_logit], axis=1).astype(jnp.bfloat16)
    route_grad = jnp.einsum("td,te->ed", normed_two, d_route, preferred_element_type=jnp.float32)
    d_normed = d_rows_sum + jnp.dot(d_route, w_route, preferred_element_type=jnp.float32)
    ffn_gain_grad, d_hidden = norm_back(hidden_state, rms_two, gain_two, d_normed)
    d_hidden = back_grad + d_hidden

    d_attn_out = lax.all_gather(d_hidden.astype(jnp.bfloat16), "expert", axis=0, tiled=True)
    out_grad = jnp.einsum(
        "td,te->de", mixed_heads, d_attn_out, preferred_element_type=jnp.float32
    ).astype(jnp.bfloat16)
    out_grad = lax.all_to_all(out_grad, "expert", split_axis=1, concat_axis=0, tiled=True)
    d_mixed = (
        jnp.einsum("te,de->td", d_attn_out, w_out, preferred_element_type=jnp.float32)
        .astype(jnp.bfloat16)
        .reshape(num_expert, seq_len, head_count, HEAD)
    )
    values_grad = jnp.einsum(
        "bhts,bthd->bshd", probs_low, d_mixed, preferred_element_type=jnp.float32
    )
    d_probs = jnp.einsum("bthd,bshd->bhts", d_mixed, value_rows, preferred_element_type=jnp.float32)
    d_scores = (
        attn_probs * (d_probs - jnp.sum(attn_probs * d_probs, axis=-1, keepdims=True))
    ).astype(jnp.bfloat16)
    d_query = unrotate(
        jnp.einsum("bhts,bshd->bthd", d_scores, key_rows, preferred_element_type=jnp.float32)
        * score_scale,
        cosine_table,
        sine_table,
    )
    d_keys = unrotate(
        jnp.einsum("bhts,bthd->bshd", d_scores, query_rows, preferred_element_type=jnp.float32)
        * score_scale,
        cosine_table,
        sine_table,
    )
    d_qkv = (
        jnp.stack([d_query, d_keys, values_grad], axis=2)
        .reshape(plane_rows, 3 * head_width)
        .astype(jnp.bfloat16)
    )
    bias_part = jnp.sum(d_qkv.astype(jnp.float32), axis=0).reshape(3, head_width)
    bias_grad = lax.dynamic_update_slice_in_dim(
        jnp.zeros((3, model_width), jnp.float32), bias_part, me_expert * head_width, 1
    )
    d_normed_one = lax.psum_scatter(
        jnp.einsum("te,de->td", d_qkv, w_qkv, preferred_element_type=jnp.float32).astype(
            jnp.bfloat16
        ),
        "expert",
        scatter_dimension=0,
        tiled=True,
    ).astype(jnp.float32)
    qkv_grad = jnp.einsum(
        "td,te->de", normed_one, d_qkv, preferred_element_type=jnp.float32
    ).astype(jnp.bfloat16)
    attn_grad = lax.psum_scatter(
        jnp.concatenate([qkv_grad, out_grad], axis=1), "dp", scatter_dimension=0, tiled=True
    )
    attn_grad = lax.all_gather(attn_grad, "expert", axis=0).astype(jnp.float32)
    qkv_weight_grad = (
        attn_grad[:, :, : 3 * head_width]
        .reshape(num_expert, shard_width, 3, head_width)
        .transpose(1, 2, 0, 3)
        .reshape(shard_width, 3 * model_width)
    )
    out_weight_grad = (
        attn_grad[:, :, 3 * head_width :].transpose(1, 0, 2).reshape(shard_width, model_width)
    )
    attn_gain_grad, d_input = norm_back(resid_in, rms_scale(resid_in), gain_one, d_normed_one)
    tokens_grad = d_hidden + d_input

    small_grad = jnp.concatenate(
        [attn_gain_grad[None], ffn_gain_grad[None], bias_grad, route_grad], axis=0
    )
    small_grad = lax.psum_scatter(small_grad, "dp", scatter_dimension=1, tiled=True)
    small_grad = lax.psum(small_grad, "expert")
    return (
        output,
        tokens_grad,
        small_grad[0],
        qkv_weight_grad,
        small_grad[2:5],
        out_weight_grad,
        small_grad[1],
        small_grad[5 : 5 + num_expert].T,
        small_grad[5 + num_expert],
        shared_grad,
        expert_grad[None, :, :2],
        expert_grad[None, :, 2],
    )


def fast_shards(
    tokens,
    attn_gain,
    qkv_weight,
    qkv_bias,
    out_weight,
    ffn_gain,
    router_weight,
    shared_gate_weight,
    shared_weight,
    expert_up,
    expert_down,
    routes,
    segment_ids,
    cotangent,
):
    num_dp = lax.axis_size("dp")
    num_expert = lax.axis_size("expert")
    seq_len, model_width = tokens.shape
    up_weight = expert_up[0].transpose(1, 0, 2)
    low, full = jnp.bfloat16, jnp.float32

    positions = np.arange(seq_len, dtype=np.float32)[:, None]
    angles = positions * np.exp(np.arange(HEAD // 2) * (-2.0 * math.log(THETA) / HEAD)).astype(np.float32)
    sines = np.sin(angles)
    tables = jnp.asarray(
        np.stack([np.tile(np.cos(angles), 2), np.concatenate([-sines, sines], axis=1)]), full
    )
    (
        qkv,
        probs,
        mixed,
        normed_one,
        hidden_state,
        normed_two,
        gates_all,
        router_probs,
        params,
        attn_weights,
        w_out,
        all_cot,
        mlp_weight,
        x_all,
    ) = front_call(
        tokens,
        segment_ids,
        routes.T,
        router_weight.T,
        shared_gate_weight,
        attn_gain,
        ffn_gain,
        qkv_bias,
        tables,
        cotangent,
        qkv_weight,
        out_weight,
        up_weight,
        expert_down[0],
    )

    _, out_part, d_rows, d_gates, d_routed, shared_grad, expert_grad = mlp_call(
        x_all,
        gates_all,
        all_cot,
        mlp_weight,
        up_weight,
        expert_down[0],
        shared_weight.transpose(1, 0, 2),
    )

    output, tokens_grad, small_grad, attn_grad, shared_grad, expert_grad = tail_call(
        mixed,
        qkv,
        probs,
        normed_one,
        attn_weights,
        w_out,
        tables,
        tokens,
        params,
        d_rows,
        d_gates,
        routes.T,
        router_probs,
        normed_two,
        hidden_state,
        cotangent,
        out_part.reshape(num_expert // 2, 2, num_dp, seq_len, model_width),
        d_routed,
        shared_grad,
        expert_grad,
    )
    (
        qkv_grad,
        out_grad,
        shared_grad,
        up_grad,
        down_grad,
        router_grad,
        gate_grad,
        attn_gain_grad,
        ffn_gain_grad,
        bias_grad,
        output,
        tokens_grad,
    ) = widen_call(attn_grad, shared_grad, expert_grad, small_grad, output, tokens_grad)
    return (
        output,
        tokens_grad,
        attn_gain_grad,
        qkv_grad,
        bias_grad,
        out_grad,
        ffn_gain_grad,
        router_grad.T,
        gate_grad,
        shared_grad.transpose(1, 0, 2),
        up_grad[None],
        down_grad[None],
    )


def solution(mesh):
    cube = mesh.shape["expert"] == 8 and mesh.shape["dp"] == 4
    return jax.shard_map(
        fast_shards if cube else shards,
        mesh=mesh,
        in_specs=(
            P(("dp", "expert"), None),
            P("dp"),
            P("dp", None),
            P(None, "dp"),
            P("dp", None),
            P("dp"),
            P("dp", None),
            P("dp"),
            P("dp", None, None),
            P("expert", None, None, "dp"),
            P("expert", None, "dp"),
            P(("dp", "expert"), None),
            P(("dp", "expert"), None),
            P(("dp", "expert"), None),
        ),
        out_specs=(
            P(("dp", "expert"), None),
            P(("dp", "expert"), None),
            P("dp"),
            P("dp", None),
            P(None, "dp"),
            P("dp", None),
            P("dp"),
            P("dp", None),
            P("dp"),
            P("dp", None, None),
            P("expert", None, None, "dp"),
            P("expert", None, "dp"),
        ),
        check_vma=False,
    )
```
